32 devices in a mesh: frame: 4 (over x, core), clip: 8 (over z, y).
Axes of the slice: x: 2, y: 2, z: 4, core: 2. Of those that a mesh axis runs over, the one named last changes fastest.
Arguments:
- latents: float32 [8, 8, 256, 16], P('clip', 'frame'), may hold values from -6 to 6
- noise: float32 [8, 8, 256, 16], P('clip', 'frame'), may hold values from -6 to 6
- timesteps: int32 [8], P('clip'), may hold values from 0 to 999
- captions: bfloat16 [8, 120, 4096], P('clip'), may hold values from -6 to 6
- cap_lengths: int32 [8], P('clip'), may hold values from 30 to 120, as said below
- null_flags: int32 [8], P('clip'), may hold values 0 or 1
- sample_weight: float32 [8], P('clip'), may hold values from 0.8 to 6.25
- embed_w: float32 [16158720], P('clip'), may hold values from -3 to 3
- attend_w: float32 [15925248], P('clip'), may hold values from -3 to 3
- dense_w: float32 [10616832], P('clip'), may hold values from -3 to 3
- vector_w: float32 [38032], replicated, may hold values from -1 to 2
- embed_m: float32 [16158720], P('clip'), may hold values from -0.00390625 to 0.00390625
- attend_m: float32 [15925248], P('clip'), may hold values from -0.0009765625 to 0.0009765625
- dense_m: float32 [10616832], P('clip'), may hold values from -0.0009765625 to 0.0009765625
- vector_m: float32 [38032], replicated, may hold values from -0.009765625 to 0.009765625
- embed_v: float32 [16158720], P('clip'), may hold values from 7.019378e-07 to 2.8077511e-06
- attend_v: float32 [15925248], P('clip'), may hold values from 2.3397925e-08 to 9.35917e-08
- dense_v: float32 [10616832], P('clip'), may hold values from 2.3397925e-08 to 9.35917e-08
- vector_v: float32 [38032], replicated, may hold values from 2.3397924e-06 to 9.35917e-06
- embed_e: float32 [16158720], P('clip'), may hold values from -3 to 3
- attend_e: float32 [15925248], P('clip'), may hold values from -3 to 3
- dense_e: float32 [10616832], P('clip'), may hold values from -3 to 3
- vector_e: float32 [38032], replicated, may hold values from -1 to 2
Outputs:
- loss_sum: float32 [], replicated
- weight_total: float32 [], replicated
- grad_norm: float32 [], replicated
- embed_new: float32 [16158720], P('clip')
- attend_new: float32 [15925248], P('clip')
- dense_new: float32 [10616832], P('clip')
- vector_new: float32 [38032], replicated
- embed_first: float32 [16158720], P('clip')
- attend_first: float32 [15925248], P('clip')
- dense_first: float32 [10616832], P('clip')
- vector_first: float32 [38032], replicated
- embed_second: float32 [16158720], P('clip')
- attend_second: float32 [15925248], P('clip')
- dense_second: float32 [10616832], P('clip')
- vector_second: float32 [38032], replicated
- embed_average: float32 [16158720], P('clip')
- attend_average: float32 [15925248], P('clip')
- dense_average: float32 [10616832], P('clip')
- vector_average: float32 [38032], replicated
The draws below stay inside these ranges and needn't reach their ends.
Inputs may be any that keep to these rules, and one draw needn't show every extreme that they name: `cap_lengths`: in every draw one clip has 120 valid caption tokens and another has 30.
All inputs are finite; a program needn't handle non-finite values. No bound on the sum of `null_flags` on one device may be relied on, other than what follows from the above.
Results may differ from the reference program's by a relative error of at most 0.0017.
The reference program's roundings to bfloat16 on the way count: a program that leaves them out, or rounds other values in their place, can miss the bound.
Values may be sent and summed in bfloat16 or wider, within the bound.
A program may use at most 960 MiB of HBM per device.

```python
import math
import jax
import jax.numpy as jnp
from jax import lax

D = 1152
HEADS = 16
MLP = 4608
CAPW = 4096
L_CAP = 120
TFREQ = 256
PATCH_VALUES = 16
PGRID = 16
STEP = 10
HEAD_DIM = 72
PATCHES = 256
FRAMES = 8
CLIPS = 8
N_EMB = 16158720
N_ATT = 15925248
N_MLP = 10616832
N_VEC = 38032
NPARAM = 42738832


def embed_layout():
    return [(PATCH_VALUES * D, PATCH_VALUES ** (-0.5)), (TFREQ * D, TFREQ ** (-0.5)), (D * D, D ** (-0.5)), (6 * D * D, D ** (-0.5)), (CAPW * D, CAPW ** (-0.5)), (D * D, D ** (-0.5)), (D * PATCH_VALUES, D ** (-0.5)), (L_CAP * CAPW, 1.0)]


def attend_layout():
    return [(3 * D * D, D ** (-0.5)), (D * D, (D // 8) ** (-0.5)), (3 * D * D, D ** (-0.5)), (D * D, (D // 2) ** (-0.5)), (D * D, D ** (-0.5)), (2 * D * D, D ** (-0.5)), (D * D, (D // 4) ** (-0.5))]


def dense_layout():
    return [(D * MLP, D ** (-0.5)), (MLP * D, MLP ** (-0.5))]


def segment_draw(key, layout):
    pieces = []
    for number, entry in enumerate(layout):
        length, factor = entry
        subkey = jax.random.fold_in(key, number)
        gauss = jax.random.truncated_normal(subkey, -3.0, 3.0, (length,), jnp.float32)
        pieces.append(gauss * factor)
    return jnp.concatenate(pieces)


def vector_draw(key):
    biases = segment_draw(key, [(21 * D + MLP + PATCH_VALUES, 0.2)])
    table = segment_draw(jax.random.fold_in(key, 7), [(6 * D, 0.3)]).reshape(6, D)
    table = table + jnp.array([0.0, 0.0, 1.0, 0.0, 0.0, 1.0], jnp.float32)[:, None]
    final = segment_draw(jax.random.fold_in(key, 8), [(2 * D, 0.3)])
    return jnp.concatenate([biases, table.reshape(-1), final])


def draw_embed_w(key, part):
    key = jax.random.fold_in(key, 1)
    return segment_draw(key, embed_layout())


def draw_attend_w(key, part):
    key = jax.random.fold_in(key, 2)
    return segment_draw(key, attend_layout())


def draw_dense_w(key, part):
    key = jax.random.fold_in(key, 3)
    return segment_draw(key, dense_layout())


def draw_vector_w(key, part):
    key = jax.random.fold_in(key, 4)
    return vector_draw(key)


def draw_embed_e(key, part):
    key = jax.random.fold_in(key, 11)
    return segment_draw(key, embed_layout())


def draw_attend_e(key, part):
    key = jax.random.fold_in(key, 12)
    return segment_draw(key, attend_layout())


def draw_dense_e(key, part):
    key = jax.random.fold_in(key, 13)
    return segment_draw(key, dense_layout())


def draw_vector_e(key, part):
    key = jax.random.fold_in(key, 14)
    return vector_draw(key)


def draw_sample_weight(key, part):
    key = jax.random.fold_in(key, 21)
    ramp = jnp.arange(CLIPS, dtype=jnp.float32) / max(CLIPS - 1, 1)
    return 3.0 ** ramp * jnp.exp(jax.random.uniform(key, (CLIPS,), jnp.float32, math.log(0.8), math.log(1.25)))


def draw_cap_lengths(key, part):
    key = jax.random.fold_in(key, 31)
    base = jax.random.randint(key, (CLIPS,), L_CAP // 4, L_CAP + 1)
    chosen = jax.random.randint(jax.random.fold_in(key, 1), (), 0, CLIPS)
    places = jnp.arange(CLIPS)
    base = jnp.where(places == chosen, L_CAP, base)
    base = jnp.where(places == (chosen + 1) % CLIPS, L_CAP // 4, base)
    return base.astype(jnp.int32)


def set_ends(values, rng, low, largest):
    shape = values.shape
    index_at = [jax.random.randint(jax.random.fold_in(rng, axis), (), 0, shape[axis]) for axis in range(len(shape))]
    values = values.at[tuple(index_at)].set(low)
    longest = shape.index(max(shape))
    index_at[longest] = (index_at[longest] + 1) % shape[longest]
    return values.at[tuple(index_at)].set(largest)


def steps_of(stream_key, shape, cuts, least, high):
    def one(axis_at, parts):
        heights = jax.random.uniform(jax.random.fold_in(jax.random.fold_in(stream_key, 6), axis_at), (parts,), jnp.float32, least / len(cuts), high / len(cuts))
        return jnp.repeat(jnp.exp(heights), shape[axis_at] // parts).reshape((-1,) + (1,) * (len(shape) - axis_at - 1))

    loudness = one(*cuts[0])
    for cut in cuts[1:]:
        loudness = loudness * one(*cut)
    return loudness


def bell_draw(rng, dims, deviation, limit, split=(), kind=jnp.bfloat16):
    entries = jax.random.normal(rng, dims, jnp.float32) * deviation
    if len(split) > 0:
        entries = steps_of(rng, dims, split, -0.22, 0.18) * entries
    return jnp.clip(entries, min=-limit, max=limit).astype(kind)


def setup_inputs(seed: int = 0) -> dict:
    arg_keys = jax.random.split(jax.random.key(seed), 24)
    return {
        "latents": bell_draw(arg_keys[0], (CLIPS, FRAMES, PATCHES, PATCH_VALUES), 1.0, 6.0, ((0, 8), (1, 4)), jnp.float32),
        "noise": bell_draw(arg_keys[1], (CLIPS, FRAMES, PATCHES, PATCH_VALUES), 1.0, 6.0, ((0, 8), (1, 4)), jnp.float32),
        "timesteps": set_ends(jax.random.randint(arg_keys[2], (CLIPS,), 0, 1000), jax.random.fold_in(arg_keys[2], 1), 0, 999).astype(jnp.int32),
        "captions": bell_draw(arg_keys[3], (CLIPS, L_CAP, CAPW), 1.0, 6.0, ((0, 8),)),
        "cap_lengths": draw_cap_lengths(jax.random.fold_in(arg_keys[23], 71), 0),
        "null_flags": set_ends((jax.random.randint(arg_keys[5], (CLIPS,), 0, 4) < 1).astype(jnp.int32), jax.random.fold_in(arg_keys[5], 1), 0, 1),
        "sample_weight": draw_sample_weight(jax.random.fold_in(arg_keys[23], 71), 0),
        "embed_w": draw_embed_w(jax.random.fold_in(arg_keys[23], 71), 0),
        "attend_w": draw_attend_w(jax.random.fold_in(arg_keys[23], 71), 0),
        "dense_w": draw_dense_w(jax.random.fold_in(arg_keys[23], 71), 0),
        "vector_w": draw_vector_w(jax.random.fold_in(arg_keys[23], 71), 0),
        "embed_m": bell_draw(arg_keys[11], (N_EMB,), (4 * NPARAM ** -0.5), 0.00390625, ((0, 8),), jnp.float32),
        "attend_m": bell_draw(arg_keys[12], (N_ATT,), (NPARAM ** -0.5), 0.0009765625, ((0, 8),), jnp.float32),
        "dense_m": bell_draw(arg_keys[13], (N_MLP,), (NPARAM ** -0.5), 0.0009765625, ((0, 8),), jnp.float32),
        "vector_m": bell_draw(arg_keys[14], (N_VEC,), (10 * NPARAM ** -0.5), 0.009765625, (), jnp.float32),
        "embed_v": jnp.clip(jnp.exp(math.log(2.8077511160518043e-06) - 1.3862944 * jax.random.uniform(arg_keys[15], (N_EMB,), jnp.float32) ** steps_of(arg_keys[15], (N_EMB,), ((0, 8),), -0.2, 0.2)), 7.019377790129511e-07, 2.8077511160518043e-06),
        "attend_v": jnp.clip(jnp.exp(math.log(9.359170149991769e-08) - 1.3862944 * jax.random.uniform(arg_keys[16], (N_ATT,), jnp.float32) ** steps_of(arg_keys[16], (N_ATT,), ((0, 8),), -0.2, 0.2)), 2.3397925374979422e-08, 9.359170149991769e-08),
        "dense_v": jnp.clip(jnp.exp(math.log(9.359170149991769e-08) - 1.3862944 * jax.random.uniform(arg_keys[17], (N_MLP,), jnp.float32) ** steps_of(arg_keys[17], (N_MLP,), ((0, 8),), -0.2, 0.2)), 2.3397925374979422e-08, 9.359170149991769e-08),
        "vector_v": jnp.clip(jnp.exp(jax.random.uniform(arg_keys[18], (N_VEC,), jnp.float32, math.log(2.3397924451273866e-06), math.log(9.359169780509546e-06))), 2.3397924451273866e-06, 9.359169780509546e-06),
        "embed_e": draw_embed_e(jax.random.fold_in(arg_keys[23], 71), 0),
        "attend_e": draw_attend_e(jax.random.fold_in(arg_keys[23], 71), 0),
        "dense_e": draw_dense_e(jax.random.fold_in(arg_keys[23], 71), 0),
        "vector_e": draw_vector_e(jax.random.fold_in(arg_keys[23], 71), 0),
    }


HIGH = lax.Precision.HIGHEST
NORM_FLOOR = 1e-06
CLIP_LIMIT = 1.0
SNR_LIMIT = 5.0
BETA_FIRST = 0.5
BETA_SECOND = 0.5
LEARN_RATE = 0.02
WEIGHT_DECAY = 0.01
ADAM_FLOOR = 1e-08
AVERAGE_KEEP = 0.9999
MASKED_SCORE = -1e+30

@jax.custom_vjp
def low(v):
    return lax.optimization_barrier(v.astype(jnp.bfloat16)).astype(jnp.float32)

@jax.custom_vjp
def low_back(v):
    return v

def low_keep(v):
    return (low(v), None)

def low_pass(kept, grad):
    return (grad,)

def back_keep(v):
    return (v, None)

def back_low(kept, grad):
    return (low(grad),)
low.defvjp(low_keep, low_pass)
low_back.defvjp(back_keep, back_low)

def both_ways(value):
    return low(low_back(value))

def embed_shapes():
    return [(PATCH_VALUES, D), (TFREQ, D), (D, D), (D, 6 * D), (CAPW, D), (D, D), (D, PATCH_VALUES), (L_CAP, CAPW)]

def attend_shapes():
    return [(D, 3 * D), (D, D), (D, 3 * D), (D, D), (D, D), (D, 2 * D), (D, D)]

def dense_shapes():
    return [(D, MLP), (MLP, D)]

def vector_shapes():
    return [(D,)] * 3 + [(6 * D,)] + [(D,)] * 11 + [(MLP,), (D,), (PATCH_VALUES,), (6, D), (2, D)]

def split_flat(flat, shapes):
    pieces = []
    offset = 0
    for extent in shapes:
        length = math.prod(extent)
        pieces.append(flat[offset:offset + length].reshape(extent))
        offset += length
    return pieces

def sincos(places, width):
    half = width // 2
    omega = jnp.exp(-math.log(10000.0) * jnp.arange(half, dtype=jnp.float32) / half)
    angle = places.astype(jnp.float32)[..., None] * omega
    return jnp.concatenate([jnp.sin(angle), jnp.cos(angle)], -1)

def modulate(hidden, shift, scale):
    center = hidden - lax.optimization_barrier(jnp.mean(hidden, -1, keepdims=True))
    normed = center * lax.rsqrt(lax.optimization_barrier(jnp.mean(center * center, -1, keepdims=True)) + NORM_FLOOR)
    return normed * (1.0 + scale) + shift

def gelu_tanh(value):
    return jax.nn.gelu(value, approximate=True)

def matmul_high(left, right):
    return jnp.matmul(left, right, precision=HIGH)

def heads_of(tensor, batch):
    return tensor.reshape(batch, -1, HEADS, HEAD_DIM)

def attend(queries, key_rows, values, mask):
    scores = jnp.einsum('bqhe,bkhe->bhqk', queries, key_rows, precision=HIGH) * HEAD_DIM ** (-0.5)
    scores = low_back(scores)
    if mask is not None:
        scores = jnp.where(mask[:, None, None, :], scores, MASKED_SCORE)
    probs = low(jax.nn.softmax(scores, axis=-1))
    return jnp.einsum('bhqk,bkhe->bqhe', probs, values, precision=HIGH)

def split_qkv(merged, bias_q, bias_v):
    return (both_ways(merged[..., :D] + bias_q), both_ways(merged[..., D:2 * D]), both_ways(merged[..., 2 * D:] + bias_v))

def clip_error(weights, latent, noise_c, tstep, caption, length, flag):
    embeds, attends, denses, vectors = weights
    patch_w, time_one, time_two, block_w, cap_one, cap_two, final_w, null_caption = embeds
    space_qkv, space_out, time_qkv, time_out, cross_q, cross_kv, cross_out = attends
    fc_in, fc_out = denses
    patch_b, time_b1, time_b2, block_b, cap_b1, cap_b2, space_bq, space_bv, space_bo, time_bq, time_bv, time_bo, cross_bq, cross_bv, cross_bo, fc_in_b, fc_out_b, final_b, table, final_table = vectors
    frames = latent.shape[0]
    angle = (tstep.astype(jnp.float32) / 1000.0 + 0.008) / 1.008 * (math.pi / 2)
    signal = jnp.cos(angle) ** 2
    noisy = low(jnp.sqrt(signal) * latent + jnp.sqrt(1.0 - signal) * noise_c)
    patch_ids = jnp.arange(PATCHES)
    place = jnp.concatenate([sincos(patch_ids // PGRID, D // 2), sincos(patch_ids % PGRID, D // 2)], -1)[None]
    hidden = matmul_high(noisy, patch_w) + patch_b + place + sincos(jnp.arange(frames), D)[:, None]
    act_one = low(jax.nn.silu(matmul_high(low(sincos(tstep, TFREQ)), time_one) + time_b1))
    time_embed = matmul_high(act_one, time_two) + time_b2
    mods = table + (matmul_high(low(jax.nn.silu(time_embed)), block_w) + block_b).reshape(6, D)
    cap_in = jnp.where(flag == 1, null_caption, caption)
    cap_act = low(gelu_tanh(matmul_high(cap_in, cap_one) + cap_b1))
    cap_rows = low(matmul_high(cap_act, cap_two) + cap_b2)
    live = jnp.where(flag == 1, L_CAP, length)
    key_mask = (jnp.arange(L_CAP) < live)[None]
    space_in = low(modulate(hidden, mods[0], mods[1]))
    query, key_rows, values = (heads_of(piece, frames) for piece in split_qkv(matmul_high(space_in, space_qkv), space_bq, space_bv))
    space_o = both_ways(attend(query, key_rows, values, None)).reshape(frames, PATCHES, D)
    hidden = hidden + mods[2] * low_back(matmul_high(space_o, space_out) + space_bo)
    time_in = jnp.swapaxes(low(hidden), 0, 1)
    query, key_rows, values = (heads_of(piece, PATCHES) for piece in split_qkv(matmul_high(time_in, time_qkv), time_bq, time_bv))
    time_o = both_ways(attend(query, key_rows, values, None)).reshape(PATCHES, frames, D)
    hidden = hidden + mods[2] * low_back(matmul_high(jnp.swapaxes(time_o, 0, 1), time_out) + time_bo)
    query = heads_of(both_ways(matmul_high(low(hidden), cross_q) + cross_bq), 1)
    merged = matmul_high(cap_rows, cross_kv)
    key_rows = heads_of(low(merged[:, :D]), 1)
    values = heads_of(low(merged[:, D:] + cross_bv), 1)
    cross_o = both_ways(attend(query, key_rows, values, key_mask)).reshape(frames, PATCHES, D)
    hidden = hidden + low_back(matmul_high(cross_o, cross_out) + cross_bo)
    dense_in = low(modulate(hidden, mods[3], mods[4]))
    dense_pre = low_back(matmul_high(dense_in, fc_in) + fc_in_b)
    hidden = hidden + mods[5] * low_back(matmul_high(low(gelu_tanh(dense_pre)), fc_out) + fc_out_b)
    final_mod = final_table + time_embed[None]
    final_in = low(modulate(hidden, final_mod[0], final_mod[1]))
    predicted = low_back(matmul_high(final_in, final_w) + final_b)
    miss = predicted - noise_c
    return jnp.sum(lax.optimization_barrier(jnp.mean(miss * miss, -1)))

def adam_step(master, grad, first, second, average, factor):
    keep = min(AVERAGE_KEEP, (1.0 + STEP) / (10.0 + STEP))
    grad = grad * factor
    first = BETA_FIRST * first + (1.0 - BETA_FIRST) * grad
    second = BETA_SECOND * second + (1.0 - BETA_SECOND) * grad * grad
    moved = first / (1.0 - BETA_FIRST ** STEP) / (jnp.sqrt(second / (1.0 - BETA_SECOND ** STEP)) + ADAM_FLOOR)
    master = master - LEARN_RATE * (moved + WEIGHT_DECAY * master)
    return (master, first, second, keep * average + (1.0 - keep) * master)

def reference(latents, noise, timesteps, captions, cap_lengths, null_flags, sample_weight, embed_w, attend_w, dense_w, vector_w, embed_m, attend_m, dense_m, vector_m, embed_v, attend_v, dense_v, vector_v, embed_e, attend_e, dense_e, vector_e):
    angle = (timesteps.astype(jnp.float32) / 1000.0 + 0.008) / 1.008 * (math.pi / 2)
    signal = jnp.cos(angle) ** 2
    ratio = signal / (1.0 - signal)
    loss_weight = sample_weight * jnp.minimum(ratio, SNR_LIMIT) / ratio
    weight_total = jnp.sum(loss_weight)
    caption_float = captions.astype(jnp.float32)

    def objective(masters):
        weights = ([low(piece) for piece in split_flat(masters[0], embed_shapes())], [low(piece) for piece in split_flat(masters[1], attend_shapes())], [low(piece) for piece in split_flat(masters[2], dense_shapes())], split_flat(masters[3], vector_shapes()))
        error_fn = jax.checkpoint(lambda sample: clip_error(weights, *sample))
        errors = lax.map(error_fn, (latents, noise, timesteps, caption_float, cap_lengths, null_flags))
        loss_sum = jnp.sum(loss_weight * errors)
        return (loss_sum / weight_total, loss_sum)
    masters = (embed_w, attend_w, dense_w, vector_w)
    value, pullback, loss_sum = jax.vjp(objective, masters, has_aux=True)
    grads = pullback(jnp.ones_like(value))[0]
    grad_norm = jnp.sqrt(sum((jnp.sum(piece * piece) for piece in grads)))
    factor = jnp.minimum(1.0, CLIP_LIMIT / (grad_norm + NORM_FLOOR))
    embed_r = adam_step(embed_w, grads[0], embed_m, embed_v, embed_e, factor)
    attend_r = adam_step(attend_w, grads[1], attend_m, attend_v, attend_e, factor)
    dense_r = adam_step(dense_w, grads[2], dense_m, dense_v, dense_e, factor)
    vector_r = adam_step(vector_w, grads[3], vector_m, vector_v, vector_e, factor)
    return (loss_sum, weight_total, grad_norm, embed_r[0], attend_r[0], dense_r[0], vector_r[0], embed_r[1], attend_r[1], dense_r[1], vector_r[1], embed_r[2], attend_r[2], dense_r[2], vector_r[2], embed_r[3], attend_r[3], dense_r[3], vector_r[3])
```

```python
import math
from functools import partial

import jax
import jax.numpy as jnp
import numpy as np
from jax import lax
from jax.experimental import pallas as pl
from jax.experimental.pallas import tpu as pltpu
from jax.sharding import PartitionSpec as P

D = 1152
HEADS = 16
MLP = 4608
CAPW = 4096
L_CAP = 120
TFREQ = 256
PATCH_VALUES = 16
PGRID = 16
STEP = 10


NORM_FLOOR = 1e-06
CLIP_LIMIT = 1.0
SNR_LIMIT = 5.0
BETA_FIRST = 0.5
BETA_SECOND = 0.5
LEARN_RATE = 0.02
WEIGHT_DECAY = 0.01
ADAM_FLOOR = 1e-08
AVERAGE_KEEP = 0.9999
MASKED_SCORE = -1e30


def embed_shapes():
    return [
        (PATCH_VALUES, D),
        (TFREQ, D),
        (D, D),
        (D, 6 * D),
        (CAPW, D),
        (D, D),
        (D, PATCH_VALUES),
        (L_CAP, CAPW),
    ]


def attend_shapes():
    return [(D, 3 * D), (D, D), (D, 3 * D), (D, D), (D, D), (D, 2 * D), (D, D)]


def dense_shapes():
    return [(D, MLP), (MLP, D)]


def vector_shapes():
    return [(D,)] * 3 + [(6 * D,)] + [(D,)] * 11 + [(MLP,), (D,), (PATCH_VALUES,), (6, D), (2, D)]


def split_flat(flat, shapes):
    pieces = []
    offset = 0
    for extent in shapes:
        length = math.prod(extent)
        pieces.append(flat[offset : offset + length].reshape(extent))
        offset += length
    return pieces


def flatten_all(pieces):
    return jnp.concatenate([piece.reshape(-1) for piece in pieces])


def reduce_group(grad):
    n_clip = lax.axis_size("clip")
    n_frame = lax.axis_size("frame")
    reorder = grad.reshape(n_clip, n_frame, -1).swapaxes(0, 1).reshape(-1)
    share = lax.psum_scatter(reorder, ("frame", "clip"), scatter_dimension=0, tiled=True)
    return lax.all_gather(share, "frame", axis=0, tiled=True)


def sincos(places, width):
    half = width // 2
    omega = jnp.exp(-math.log(10000.0) * jnp.arange(half, dtype=jnp.float32) / half)
    angle = places.astype(jnp.float32)[..., None] * omega
    return jnp.concatenate([jnp.sin(angle), jnp.cos(angle)], -1)


def modulate(hidden, shift, scale):
    center = hidden - jnp.mean(hidden, -1, keepdims=True)
    normed = center * lax.rsqrt(jnp.mean(center * center, -1, keepdims=True) + NORM_FLOOR)
    return normed * (1.0 + scale) + shift


def gelu_tanh(value):
    return jax.nn.gelu(value, approximate=True)


def matmul_low(left, right):
    return lax.dot_general(
        left, right, (((left.ndim - 1,), (0,)), ((), ())), preferred_element_type=jnp.float32
    )


def halves(value):
    upper = value.astype(jnp.bfloat16)
    return (upper, (value - upper.astype(jnp.float32)).astype(jnp.bfloat16))


def back_low(grads, weight):
    return lax.dot_general(
        grads, weight, (((grads.ndim - 1,), (1,)), ((), ())), preferred_element_type=jnp.float32
    )


def back_split(grads, weight):
    upper, lower = halves(grads)
    return back_low(upper, weight) + back_low(lower, weight)


def weight_grad(inputs, grads):
    left = inputs.reshape(-1, inputs.shape[-1])
    right = grads.reshape(-1, grads.shape[-1])
    return lax.dot_general(
        left, right, (((0,), (0,)), ((), ())), preferred_element_type=jnp.float32
    )


def weight_split(inputs, grads):
    upper, lower = halves(grads)
    return weight_grad(inputs, upper) + weight_grad(inputs, lower)


def bias_grad(grads):
    return jnp.sum(grads.astype(jnp.float32).reshape(-1, grads.shape[-1]), 0)


def heads_of(tensor, batch):
    return tensor.reshape(batch, -1, HEADS, tensor.shape[-1] // HEADS)


def split_qkv(merged, bias_q, bias_v):
    width = merged.shape[-1] // 3
    return (
        (merged[..., :width] + bias_q).astype(jnp.bfloat16),
        merged[..., width : 2 * width].astype(jnp.bfloat16),
        (merged[..., 2 * width :] + bias_v).astype(jnp.bfloat16),
    )


def attend_scores(queries, key_rows, mask):
    scores = jnp.einsum("bqhe,bkhe->bhqk", queries, key_rows, preferred_element_type=jnp.float32)
    scores = scores * queries.shape[-1] ** (-0.5)
    if mask is not None:
        scores = jnp.where(mask[:, None, None, :], scores, MASKED_SCORE)
    return scores


def attend_forward(queries, key_rows, values, mask):
    scores = attend_scores(queries, key_rows, mask)
    summit = jnp.max(scores, -1, keepdims=True)
    powers = jnp.exp(scores - summit)
    totals = jnp.sum(powers, -1, keepdims=True)
    probs = (powers / totals).astype(jnp.bfloat16)
    output = jnp.einsum("bhqk,bkhe->bqhe", probs, values, preferred_element_type=jnp.float32)
    return (output.astype(jnp.bfloat16), summit + jnp.log(totals))


def attend_backward(queries, key_rows, values, mask, log_total, grad_out):
    scale = queries.shape[-1] ** (-0.5)
    probs = jnp.exp(attend_scores(queries, key_rows, mask) - log_total)
    grad_probs = jnp.einsum("bqhe,bkhe->bhqk", grad_out, values, preferred_element_type=jnp.float32)
    grad_scores = (probs * (grad_probs - jnp.sum(probs * grad_probs, -1, keepdims=True))).astype(
        jnp.bfloat16
    )
    grad_query = (
        jnp.einsum("bhqk,bkhe->bqhe", grad_scores, key_rows, preferred_element_type=jnp.float32)
        * scale
    )
    grad_keys = (
        jnp.einsum("bhqk,bqhe->bkhe", grad_scores, queries, preferred_element_type=jnp.float32)
        * scale
    )
    grad_values = jnp.einsum(
        "bhqk,bqhe->bkhe", probs.astype(jnp.bfloat16), grad_out, preferred_element_type=jnp.float32
    )
    return (grad_query, grad_keys, grad_values)


def unpack_all(gathered):
    return (
        split_flat(gathered[0], embed_shapes()),
        split_flat(gathered[1], attend_shapes()),
        split_flat(gathered[2], dense_shapes()),
    )


def adam_step(master, grad, first, second, average, factor):
    keep = min(AVERAGE_KEEP, (1.0 + STEP) / (10.0 + STEP))
    grad = grad * factor
    first = BETA_FIRST * first + (1.0 - BETA_FIRST) * grad
    second = BETA_SECOND * second + (1.0 - BETA_SECOND) * grad * grad
    moved = (
        first
        / (1.0 - BETA_FIRST**STEP)
        / (jnp.sqrt(second / (1.0 - BETA_SECOND**STEP)) + ADAM_FLOOR)
    )
    master = master - LEARN_RATE * (moved + WEIGHT_DECAY * master)
    return (master, first, second, keep * average + (1.0 - keep) * master)


def shards(
    latents,
    noise,
    timesteps,
    captions,
    cap_lengths,
    null_flags,
    sample_weight,
    embed_w,
    attend_w,
    dense_w,
    vector_w,
    embed_m,
    attend_m,
    dense_m,
    vector_m,
    embed_v,
    attend_v,
    dense_v,
    vector_v,
    embed_e,
    attend_e,
    dense_e,
    vector_e,
):
    clip_dev, frame_dev, patches = (latents.shape[0], latents.shape[1], latents.shape[2])
    n_frame = lax.axis_size("frame")
    n_clip = lax.axis_size("clip")
    local_pos = patches // n_frame
    gathered = (
        lax.all_gather(embed_w.astype(jnp.bfloat16), "clip", axis=0, tiled=True),
        lax.all_gather(attend_w.astype(jnp.bfloat16), "clip", axis=0, tiled=True),
        lax.all_gather(dense_w.astype(jnp.bfloat16), "clip", axis=0, tiled=True),
    )
    embeds, attends, denses = unpack_all(gathered)
    patch_w, time_one, time_two, block_w, cap_one, cap_two, final_w, null_caption = embeds
    space_qkv, space_out, time_qkv, time_out, cross_q, cross_kv, cross_out = attends
    fc_in, fc_out = denses
    (
        patch_b,
        time_b1,
        time_b2,
        block_b,
        cap_b1,
        cap_b2,
        space_bq,
        space_bv,
        space_bo,
        time_bq,
        time_bv,
        time_bo,
        cross_bq,
        cross_bv,
        cross_bo,
        fc_in_b,
        fc_out_b,
        final_b,
        table,
        final_table,
    ) = split_flat(vector_w, vector_shapes())
    angle = (timesteps.astype(jnp.float32) / 1000.0 + 0.008) / 1.008 * (math.pi / 2)
    signal = jnp.cos(angle) ** 2
    ratio = signal / (1.0 - signal)
    loss_weight = sample_weight * jnp.minimum(ratio, SNR_LIMIT) / ratio
    weight_total = lax.psum(jnp.sum(loss_weight), "clip")
    keep_part = jnp.sqrt(signal)[:, None, None, None]
    fade_part = jnp.sqrt(1.0 - signal)[:, None, None, None]
    noisy = (keep_part * latents + fade_part * noise).astype(jnp.bfloat16)
    frame_ids = lax.axis_index("frame") * frame_dev + jnp.arange(frame_dev)
    patch_ids = jnp.arange(patches)
    place = jnp.concatenate(
        [sincos(patch_ids // PGRID, D // 2), sincos(patch_ids % PGRID, D // 2)], -1
    )[None, None]
    hidden_zero = matmul_low(noisy, patch_w) + patch_b + place + sincos(frame_ids, D)[None, :, None]
    freq_in = sincos(timesteps, TFREQ).astype(jnp.bfloat16)
    pre_one = matmul_low(freq_in, time_one) + time_b1
    act_one = jax.nn.silu(pre_one).astype(jnp.bfloat16)
    time_embed = matmul_low(act_one, time_two) + time_b2
    silu_time = jax.nn.silu(time_embed).astype(jnp.bfloat16)
    mods = table[None] + (matmul_low(silu_time, block_w) + block_b).reshape(clip_dev, 6, D)

    def mod_row(number):
        return mods[:, number][:, None, None, :]

    is_null = null_flags == 1
    cap_in = jnp.where(is_null[:, None, None], null_caption[None], captions)
    cap_pre = matmul_low(cap_in, cap_one) + cap_b1
    cap_act = gelu_tanh(cap_pre).astype(jnp.bfloat16)
    cap_rows = (matmul_low(cap_act, cap_two) + cap_b2).astype(jnp.bfloat16)
    live_len = jnp.where(is_null, L_CAP, cap_lengths)
    key_mask = jnp.arange(L_CAP)[None, :] < live_len[:, None]
    space_in = modulate(hidden_zero, mod_row(0), mod_row(1)).astype(jnp.bfloat16)
    space_q, space_k, space_v = (
        heads_of(piece, clip_dev * frame_dev)
        for piece in split_qkv(matmul_low(space_in, space_qkv), space_bq, space_bv)
    )
    space_o, space_lse = attend_forward(space_q, space_k, space_v, None)
    space_flat = space_o.reshape(clip_dev, frame_dev, patches, D)
    space_res = matmul_low(space_flat, space_out) + space_bo
    hidden_one = hidden_zero + mod_row(2) * space_res
    time_in = lax.all_to_all(
        hidden_one.astype(jnp.bfloat16), "frame", split_axis=2, concat_axis=1, tiled=True
    )
    time_in = jnp.swapaxes(time_in, 1, 2)
    frames = time_in.shape[2]
    time_q, time_k, time_v = (
        heads_of(piece, clip_dev * local_pos)
        for piece in split_qkv(matmul_low(time_in, time_qkv), time_bq, time_bv)
    )
    time_o, time_lse = attend_forward(time_q, time_k, time_v, None)
    time_back = jnp.swapaxes(time_o.reshape(clip_dev, local_pos, frames, D), 1, 2)
    time_flat = lax.all_to_all(time_back, "frame", split_axis=1, concat_axis=2, tiled=True)
    time_res = matmul_low(time_flat, time_out) + time_bo
    hidden_two = hidden_one + mod_row(2) * time_res
    cross_in = hidden_two.astype(jnp.bfloat16)
    cross_query = heads_of(
        (matmul_low(cross_in, cross_q) + cross_bq).astype(jnp.bfloat16), clip_dev
    )
    cross_merged = matmul_low(cap_rows, cross_kv)
    cross_k = heads_of(cross_merged[..., :D].astype(jnp.bfloat16), clip_dev)
    cross_v = heads_of((cross_merged[..., D:] + cross_bv).astype(jnp.bfloat16), clip_dev)
    cross_o, cross_lse = attend_forward(cross_query, cross_k, cross_v, key_mask)
    cross_flat = cross_o.reshape(clip_dev, frame_dev, patches, D)
    hidden_three = hidden_two + matmul_low(cross_flat, cross_out) + cross_bo
    dense_in = modulate(hidden_three, mod_row(3), mod_row(4)).astype(jnp.bfloat16)
    dense_pre = matmul_low(dense_in, fc_in) + fc_in_b
    dense_act = gelu_tanh(dense_pre).astype(jnp.bfloat16)
    dense_res = matmul_low(dense_act, fc_out) + fc_out_b
    hidden_four = hidden_three + mod_row(5) * dense_res
    final_mod = final_table[None] + time_embed[:, None, :]
    final_shift = final_mod[:, 0][:, None, None, :]
    final_scale = final_mod[:, 1][:, None, None, :]
    final_in = modulate(hidden_four, final_shift, final_scale).astype(jnp.bfloat16)
    predicted = matmul_low(final_in, final_w) + final_b
    miss = predicted - noise
    clip_error = jnp.sum(jnp.mean(miss * miss, -1), (1, 2))
    local_loss = jnp.sum(loss_weight * clip_error)
    grad_pred = (
        2.0 / miss.shape[-1] * (loss_weight / weight_total)[:, None, None, None] * miss
    ).astype(jnp.bfloat16)
    g_final_w = weight_grad(final_in, grad_pred)
    g_final_b = bias_grad(grad_pred)
    unused, pullback = jax.vjp(modulate, hidden_four, final_shift, final_scale)
    grad_hidden, grad_fshift, grad_fscale = pullback(back_low(grad_pred, final_w))
    grad_fmod = jnp.stack([grad_fshift.reshape(clip_dev, D), grad_fscale.reshape(clip_dev, D)], 1)
    g_final_table = jnp.sum(grad_fmod, 0)
    grad_time_embed = grad_fmod[:, 0] + grad_fmod[:, 1]
    grad_dense = (grad_hidden * mod_row(5)).astype(jnp.bfloat16)
    grad_gate_b = jnp.sum(grad_hidden * dense_res, (1, 2))
    g_fc_out = weight_grad(dense_act, grad_dense)
    g_fc_out_b = bias_grad(grad_dense)
    unused, pullback = jax.vjp(gelu_tanh, dense_pre)
    grad_pre = pullback(back_low(grad_dense, fc_out))[0].astype(jnp.bfloat16)
    g_fc_in = weight_grad(dense_in, grad_pre)
    g_fc_in_b = bias_grad(grad_pre)
    dense_owned = reduce_group(flatten_all([g_fc_in, g_fc_out]))
    unused, pullback = jax.vjp(modulate, hidden_three, mod_row(3), mod_row(4))
    grad_input, grad_shift_b, grad_scale_b = pullback(back_low(grad_pre, fc_in))
    grad_hidden = grad_hidden + grad_input
    grad_cross = grad_hidden.astype(jnp.bfloat16)
    g_cross_out = weight_grad(cross_flat, grad_cross)
    g_cross_bo = bias_grad(grad_cross)
    grad_cross_o = heads_of(back_low(grad_cross, cross_out).astype(jnp.bfloat16), clip_dev)
    grad_cq, grad_ck, grad_cv = attend_backward(
        cross_query, cross_k, cross_v, key_mask, cross_lse, grad_cross_o
    )
    grad_cq = grad_cq.astype(jnp.bfloat16).reshape(clip_dev, frame_dev, patches, D)
    g_cross_q = weight_grad(cross_in, grad_cq)
    g_cross_bq = bias_grad(grad_cq)
    grad_hidden = grad_hidden + back_low(grad_cq, cross_q)
    grad_cv = grad_cv.reshape(clip_dev, L_CAP, D)
    grad_ckv = jnp.concatenate([grad_ck.reshape(clip_dev, L_CAP, D), grad_cv], -1)
    g_cross_kv = weight_split(cap_rows, grad_ckv)
    g_cross_bv = bias_grad(grad_cv)
    grad_cap_rows = back_split(grad_ckv, cross_kv)
    grad_time = (grad_hidden * mod_row(2)).astype(jnp.bfloat16)
    g_time_out = weight_grad(time_flat, grad_time)
    g_time_bo = bias_grad(grad_time)
    grad_time_o = lax.all_to_all(
        back_low(grad_time, time_out).astype(jnp.bfloat16),
        "frame",
        split_axis=2,
        concat_axis=1,
        tiled=True,
    )
    grad_time_o = heads_of(jnp.swapaxes(grad_time_o, 1, 2), clip_dev * local_pos)
    grad_tq, grad_tk, grad_tv = attend_backward(time_q, time_k, time_v, None, time_lse, grad_time_o)
    grad_tqkv = jnp.concatenate(
        [
            piece.astype(jnp.bfloat16).reshape(clip_dev, local_pos, frames, D)
            for piece in (grad_tq, grad_tk, grad_tv)
        ],
        -1,
    )
    g_time_qkv = weight_grad(time_in, grad_tqkv)
    g_time_bq = bias_grad(grad_tqkv[..., :D])
    g_time_bv = bias_grad(grad_tqkv[..., 2 * D :])
    grad_tqkv = lax.all_to_all(
        jnp.swapaxes(grad_tqkv, 1, 2), "frame", split_axis=1, concat_axis=2, tiled=True
    )
    grad_gate_a = jnp.sum(grad_hidden * time_res, (1, 2))
    grad_hidden = grad_hidden + back_low(grad_tqkv, time_qkv)
    grad_gate_a = grad_gate_a + jnp.sum(grad_hidden * space_res, (1, 2))
    grad_space = (grad_hidden * mod_row(2)).astype(jnp.bfloat16)
    g_space_out = weight_grad(space_flat, grad_space)
    g_space_bo = bias_grad(grad_space)
    grad_space_o = heads_of(
        back_low(grad_space, space_out).astype(jnp.bfloat16), clip_dev * frame_dev
    )
    grad_sq, grad_sk, grad_sv = attend_backward(
        space_q, space_k, space_v, None, space_lse, grad_space_o
    )
    grad_sqkv = jnp.concatenate(
        [
            piece.astype(jnp.bfloat16).reshape(clip_dev, frame_dev, patches, D)
            for piece in (grad_sq, grad_sk, grad_sv)
        ],
        -1,
    )
    g_space_qkv = weight_grad(space_in, grad_sqkv)
    g_space_bq = bias_grad(grad_sqkv[..., :D])
    g_space_bv = bias_grad(grad_sqkv[..., 2 * D :])
    attend_owned = reduce_group(
        flatten_all(
            [g_space_qkv, g_space_out, g_time_qkv, g_time_out, g_cross_q, g_cross_kv, g_cross_out]
        )
    )
    unused, pullback = jax.vjp(modulate, hidden_zero, mod_row(0), mod_row(1))
    grad_input, grad_shift_a, grad_scale_a = pullback(back_low(grad_sqkv, space_qkv))
    grad_hidden = grad_hidden + grad_input
    g_patch_w = weight_split(noisy, grad_hidden)
    g_patch_b = bias_grad(grad_hidden)
    grad_mods = jnp.stack(
        [
            grad_shift_a.reshape(clip_dev, D),
            grad_scale_a.reshape(clip_dev, D),
            grad_gate_a,
            grad_shift_b.reshape(clip_dev, D),
            grad_scale_b.reshape(clip_dev, D),
            grad_gate_b,
        ],
        1,
    )
    g_table = jnp.sum(grad_mods, 0)
    grad_zero = grad_mods.reshape(clip_dev, 6 * D)
    g_block_b = jnp.sum(grad_zero, 0)
    g_block_w = weight_split(silu_time, grad_zero)
    unused, pullback = jax.vjp(jax.nn.silu, time_embed)
    grad_time_embed = grad_time_embed + pullback(back_split(grad_zero, block_w))[0]
    g_time_b2 = jnp.sum(grad_time_embed, 0)
    g_time_two = weight_split(act_one, grad_time_embed)
    unused, pullback = jax.vjp(jax.nn.silu, pre_one)
    grad_pre_one = pullback(back_split(grad_time_embed, time_two))[0]
    g_time_b1 = jnp.sum(grad_pre_one, 0)
    g_time_one = weight_split(freq_in, grad_pre_one)
    g_cap_b2 = bias_grad(grad_cap_rows)
    g_cap_two = weight_split(cap_act, grad_cap_rows)
    unused, pullback = jax.vjp(gelu_tanh, cap_pre)
    grad_cap_pre = pullback(back_split(grad_cap_rows, cap_two))[0]
    g_cap_b1 = bias_grad(grad_cap_pre)
    g_cap_one = weight_split(cap_in, grad_cap_pre)
    grad_cap_in = back_split(grad_cap_pre, cap_one)
    g_null = jnp.sum(jnp.where(is_null[:, None, None], grad_cap_in, 0.0), 0)
    embed_owned = reduce_group(
        flatten_all(
            [g_patch_w, g_time_one, g_time_two, g_block_w, g_cap_one, g_cap_two, g_final_w, g_null]
        )
    )
    vector_grad = flatten_all(
        [
            g_patch_b,
            g_time_b1,
            g_time_b2,
            g_block_b,
            g_cap_b1,
            g_cap_b2,
            g_space_bq,
            g_space_bv,
            g_space_bo,
            g_time_bq,
            g_time_bv,
            g_time_bo,
            g_cross_bq,
            g_cross_bv,
            g_cross_bo,
            g_fc_in_b,
            g_fc_out_b,
            g_final_b,
            g_table,
            g_final_table,
        ]
    )
    vector_sum, loss_sum = lax.psum((vector_grad, local_loss), ("frame", "clip"))
    owned = (embed_owned, attend_owned, dense_owned)
    local_square = (
        sum((jnp.sum(shard_piece * shard_piece) for shard_piece in owned))
        + jnp.sum(vector_sum * vector_sum) / n_clip
    )
    grad_norm = jnp.sqrt(lax.psum(local_square, "clip"))
    factor = jnp.minimum(1.0, CLIP_LIMIT / (grad_norm + NORM_FLOOR))
    embed_r = adam_step(embed_w, owned[0], embed_m, embed_v, embed_e, factor)
    attend_r = adam_step(attend_w, owned[1], attend_m, attend_v, attend_e, factor)
    dense_r = adam_step(dense_w, owned[2], dense_m, dense_v, dense_e, factor)
    vector_r = adam_step(vector_w, vector_sum, vector_m, vector_v, vector_e, factor)
    return (
        loss_sum,
        weight_total,
        grad_norm,
        embed_r[0],
        attend_r[0],
        dense_r[0],
        vector_r[0],
        embed_r[1],
        attend_r[1],
        dense_r[1],
        vector_r[1],
        embed_r[2],
        attend_r[2],
        dense_r[2],
        vector_r[2],
        embed_r[3],
        attend_r[3],
        dense_r[3],
        vector_r[3],
    )


AXES = ("frame", "clip")
LANES = 128
LANE_TILES = D // LANES
EMB_PAD = 1792


X_SIZE, CORES, Z_SIZE, Y_SIZE = 2, 2, 4, 2
N_OWN = Z_SIZE * Y_SIZE
RING = [(0, 0), (1, 0), (2, 0), (3, 0), (3, 1), (2, 1), (1, 1), (0, 1)]
RING_CLIP = [z * Y_SIZE + y for z, y in RING]
CLIP_RING = [RING_CLIP.index(c) for c in range(N_OWN)]


def pairs(move):
    out = []
    for x in range(X_SIZE):
        for core in range(CORES):
            for z in range(Z_SIZE):
                for y in range(Y_SIZE):
                    to = move(x, core, z, y)
                    if to is not None:
                        rank = lambda a, b, c, d: (a * CORES + b) * N_OWN + c * Y_SIZE + d
                        out.append((rank(x, core, z, y), rank(*to)))
    return out


SWAP_X = pairs(lambda x, c, z, y: (1 - x, c, z, y))
SWAP_CORE = pairs(lambda x, c, z, y: (x, 1 - c, z, y))
SWAP_Y = pairs(lambda x, c, z, y: (x, c, z, 1 - y))
SWAP_Z1 = pairs(lambda x, c, z, y: (x, c, z ^ 1, y))
SWAP_Z2 = pairs(lambda x, c, z, y: (x, c, z ^ 2, y))


def hop_z(source, to):
    return pairs(lambda x, c, z, y: (x, c, to, y) if z == source else None)


def ring_move(step, keep, seen):
    def move(x, c, z, y):
        place = CLIP_RING[z * Y_SIZE + y]
        origin = RING_CLIP[(place + seen) % N_OWN]
        if origin not in keep:
            return None
        to = RING[(place + step) % N_OWN]
        return (x, c) + to

    return pairs(move)


def swap_move(flip_x, flip_core, keep, seen):
    def move(x, c, z, y):
        place = CLIP_RING[z * Y_SIZE + y]
        if RING_CLIP[(place + seen) % N_OWN] not in keep:
            return None
        return (x ^ flip_x, c ^ flip_core, z, y)

    return pairs(move)


def shift(value, perm):
    return lax.ppermute(value, AXES, perm)


def sum_clips(value):
    for perm in (SWAP_Y, SWAP_Z1, SWAP_Z2):
        value = value + shift(value, perm)
    return value


def sum_frames(value):
    for perm in (SWAP_CORE, SWAP_X):
        value = value + shift(value, perm)
    return value


def shard_segments(matrices, n_rows):
    spans, offset = [], 0
    for name, rows, wide in matrices:
        spans.append((name, offset, rows, wide))
        offset += rows * wide
    out = []
    for owner in range(N_OWN):
        low, high = owner * n_rows, (owner + 1) * n_rows
        mine = []
        for name, start, rows, wide in spans:
            begin, end = max(low, start), min(high, start + rows * wide)
            if begin < end:
                mine.append((name, (begin - start) // wide, (end - begin) // wide, wide))
        out.append(mine)
    return out


ATTEND = [
    ("space_qkv", D, 3),
    ("space_out", D, 1),
    ("time_qkv", D, 3),
    ("time_out", D, 1),
    ("cross_q", D, 1),
    ("cross_kv", D, 2),
    ("cross_out", D, 1),
]
DENSE = [("fc_in", D, 4), ("fc_out", MLP, 1)]
ATTEND_ROWS = 13824 // N_OWN
DENSE_ROWS = 9216 // N_OWN
ATTEND_SEGS = shard_segments(ATTEND, ATTEND_ROWS)
DENSE_SEGS = shard_segments(DENSE, DENSE_ROWS)


def cast_table(segments, block):
    out = []
    for mine in segments:
        rows, offset = [], 0
        for name, first, count, wide in mine:
            for start in range(0, count * wide, block):
                rows.append((wide, offset + start // wide, count))
            offset += count * wide
        out.append(rows)
    return np.array(out, np.int32)


def step_table(segments, block, n_rows):
    out = []
    for mine in segments:
        rows, offset = [], 0
        for name, first, count, wide in mine:
            half = count // 2
            for start in range(0, count * wide, block):
                core, inner = divmod(start // wide, half)
                rows.append((wide, core * (n_rows // 2) + offset + inner, half))
            offset += half * wide
        out.append(rows)
    return np.array(out, np.int32)


CAST_BLOCK = 576
STEP_BLOCK = 288


def cast_kernel(widths, table, flat, out):
    block = pl.program_id(0)
    for wide in widths:
        count = CAST_BLOCK // wide

        @pl.when(table[block, 0] == wide)
        def _():
            for slab in range(wide):
                row = pl.multiple_of(table[block, 1] + slab * table[block, 2], 16)
                for tile in range(LANE_TILES):
                    piece = flat[pl.ds(LANE_TILES * slab + tile, count, stride=LANE_TILES * wide), :]
                    out[pl.ds(row, count), tile * LANES : (tile + 1) * LANES] = piece.astype(jnp.bfloat16)


def cast_shard(flat, table, widths, n_rows):
    units = CAST_BLOCK * LANE_TILES
    return pl.pallas_call(
        partial(cast_kernel, widths),
        grid_spec=pltpu.PrefetchScalarGridSpec(
            num_scalar_prefetch=1,
            grid=(n_rows // CAST_BLOCK,),
            in_specs=[pl.BlockSpec((units, LANES), lambda b, t: (b, 0))],
            out_specs=pl.BlockSpec((n_rows, D), lambda b, t: (0, 0)),
        ),
        out_shape=jax.ShapeDtypeStruct((n_rows, D), jnp.bfloat16),
        compiler_params=pltpu.CompilerParams(vmem_limit_bytes=40 * 1024 * 1024),
    )(table, flat.reshape(-1, LANES))


def rows_kernel(flat, out):
    count = out.shape[0]
    for tile in range(LANE_TILES):
        piece = flat[pl.ds(tile, count, stride=LANE_TILES), :]
        out[:, tile * LANES : (tile + 1) * LANES] = piece.astype(out.dtype)


def flat_to_rows(flat, dtype):
    rows = flat.shape[0] // LANE_TILES
    block = rows // 8
    return pl.pallas_call(
        rows_kernel,
        grid=(8,),
        in_specs=[pl.BlockSpec((block * LANE_TILES, LANES), lambda b: (b, 0))],
        out_specs=pl.BlockSpec((block, D), lambda b: (b, 0)),
        out_shape=jax.ShapeDtypeStruct((rows, D), dtype),
        compiler_params=pltpu.CompilerParams(vmem_limit_bytes=32 * 1024 * 1024),
    )(flat)


def flat_kernel(rows, out):
    count = rows.shape[0]
    for tile in range(LANE_TILES):
        out[pl.ds(tile, count, stride=LANE_TILES), :] = rows[:, tile * LANES : (tile + 1) * LANES]


def rows_to_flat(rows):
    block = rows.shape[0] // 8
    return pl.pallas_call(
        flat_kernel,
        grid=(8,),
        in_specs=[pl.BlockSpec((block, D), lambda b: (b, 0))],
        out_specs=pl.BlockSpec((block * LANE_TILES, LANES), lambda b: (b, 0)),
        out_shape=jax.ShapeDtypeStruct((rows.shape[0] * LANE_TILES, LANES), rows.dtype),
        compiler_params=pltpu.CompilerParams(vmem_limit_bytes=32 * 1024 * 1024),
    )(rows)


def place_kernel(n_pieces, keep, stores, slots, own, *refs):
    pieces, outs, (held, sems, out_sem) = refs[:n_pieces], refs[n_pieces:-3], refs[-3:]
    low = min(keep)

    def copies():
        yield slots[0, 0], pltpu.make_async_copy(own, held.at[slots[0, 0] - low], sems.at[n_pieces])
        for number in range(n_pieces):
            owner = slots[number + 1, 0]
            yield owner, pltpu.make_async_copy(
                pieces[number], held.at[owner - low, slots[number + 1, 1]], sems.at[number]
            )

    for action in ("start", "wait"):
        for owner, copy in copies():
            if len(keep) == N_OWN:
                getattr(copy, action)()
            else:

                @pl.when(owner >= low)
                def _():
                    getattr(copy, action)()

    rows = held.shape[1] * held.shape[2]
    done = []
    for number, (out, row, column, owner, first, count) in enumerate(stores):
        quarter = rows // 4
        while count > 0:
            part, inner = divmod(first, quarter)
            some = min(count, quarter - inner)
            copy = pltpu.make_async_copy(
                held.at[owner - low, part, pl.ds(inner, some)],
                outs[out].at[pl.ds(row, some), pl.ds(column, D)],
                out_sem.at[len(done)],
            )
            copy.start()
            done.append(copy)
            first, row, count = first + some, row + some, count - some
    for copy in done:
        copy.wait()


def place_pieces(own, pieces, slots, keep, shapes, stores):
    rows = own.shape[0]
    spec = pl.BlockSpec(memory_space=pl.ANY)
    return pl.pallas_call(
        partial(place_kernel, len(pieces), keep, stores),
        in_specs=[pl.BlockSpec(memory_space=pltpu.SMEM)] + [spec] * (len(pieces) + 1),
        out_specs=[spec] * len(shapes),
        out_shape=[jax.ShapeDtypeStruct(shape, own.dtype) for shape in shapes],
        scratch_shapes=[
            pltpu.VMEM((len(keep), 4, rows // 4, D), own.dtype),
            pltpu.SemaphoreType.DMA((len(pieces) + 1,)),
            pltpu.SemaphoreType.DMA((4 * len(stores),)),
        ],
        compiler_params=pltpu.CompilerParams(vmem_limit_bytes=48 * 1024 * 1024),
    )(slots, own.reshape(4, rows // 4, D), *pieces)


def gather_shards(own, clip_id, frame_id, keep, shapes, stores):
    rows = own.shape[0]
    quarter = lax.dynamic_slice_in_dim(own, frame_id * (rows // 4), rows // 4, 0)
    place = jnp.asarray(CLIP_RING, jnp.int32)[clip_id]
    ring_clip = jnp.asarray(RING_CLIP, jnp.int32)
    pieces, slots = [], [jnp.stack([clip_id, 0 * clip_id])]
    ahead, behind = quarter, quarter
    arrived = []
    for step in range(1, N_OWN // 2 + 1):
        ahead = shift(ahead, ring_move(1, keep, 1 - step))
        arrived.append((ahead, -step))
        if step < N_OWN // 2:
            behind = shift(behind, ring_move(-1, keep, step - 1))
            arrived.append((behind, step))
    for piece, seen in arrived:
        source = ring_clip[(place + seen) % N_OWN]
        over_x = shift(piece, swap_move(1, 0, keep, seen))
        over_core = shift(piece, swap_move(0, 1, keep, seen))
        both = shift(over_x, swap_move(0, 1, keep, seen))
        for value, flip in ((piece, 0), (over_x, 2), (over_core, 1), (both, 3)):
            pieces.append(value)
            slots.append(jnp.stack([source, frame_id ^ flip]))
    return place_pieces(own, pieces, jnp.stack(slots).astype(jnp.int32), keep, shapes, stores)


def matrix_plan(matrices, segments):
    shapes = [(rows, wide * D) for name, rows, wide in matrices]
    names = [name for name, rows, wide in matrices]
    stores = []
    for owner in range(N_OWN):
        offset = 0
        for name, first, count, wide in segments[owner]:
            for j in range(wide):
                stores.append((names.index(name), first, j * D, owner, offset, count))
                offset += count
    return shapes, stores


def half_rows(segments, name):
    rows = [[], []]
    for mine in segments:
        for label, first, count, wide in mine:
            if label == name:
                for core in range(2):
                    begin = first + core * (count // 2)
                    rows[core].extend(range(begin, begin + count // 2))
    return np.array(rows, np.int32)


def pick_columns(values, rows, core):
    wanted = jnp.asarray(rows)[core]
    chooser = (jnp.arange(values.shape[1], dtype=jnp.int32)[:, None] == wanted[None]).astype(jnp.bfloat16)
    return matmul_low(values, chooser).astype(jnp.bfloat16)


def both_cores(value):
    return jnp.concatenate([value, shift(value, SWAP_CORE)], 0)


def reduce_pair(pair, owner_z, x_first, x_id, y_id):
    def fold(value, axis, place, perm):
        mine = lax.dynamic_index_in_dim(value, place, axis, keepdims=False)
        other = lax.dynamic_index_in_dim(value, 1 - place, axis, keepdims=False)
        return mine + shift(other, perm)

    if x_first:
        part = fold(fold(pair, 1, x_id, SWAP_X), 0, y_id, SWAP_Y)
    else:
        part = fold(fold(pair, 0, y_id, SWAP_Y), 0, x_id, SWAP_X)
    for source in range(Z_SIZE - 1, owner_z, -1):
        part = part + shift(part, hop_z(source, source - 1))
    for source in range(owner_z):
        part = part + shift(part, hop_z(source, source + 1))
    return part


def pair_chunks(grads, segments, owner_z):
    chunks = []
    for owner in (2 * owner_z, 2 * owner_z + 1):
        parts = []
        for label, first, count, wide in segments[owner]:
            begin = sum(
                seg[2] // 2 for mine in segments[:owner] for seg in mine if seg[0] == label
            )
            for j in range(wide):
                parts.append(grads[label][j][begin : begin + count // 2])
        chunks.append(jnp.concatenate(parts, 0) if len(parts) > 1 else parts[0])
    pair = jnp.stack(chunks)
    return pair.reshape(2, 2, pair.shape[1] // 2, D)


def choose_z(parts, z_id):
    out = parts[0]
    for number in range(1, Z_SIZE):
        out = jnp.where(z_id == number, parts[number], out)
    return out


def step_values(master, grad, first, second, average):
    keep = min(AVERAGE_KEEP, (1.0 + STEP) / (10.0 + STEP))
    first = BETA_FIRST * first + (1.0 - BETA_FIRST) * grad
    second = BETA_SECOND * second + (1.0 - BETA_SECOND) * grad * grad
    moved = (
        first
        / (1.0 - BETA_FIRST**STEP)
        / (jnp.sqrt(second / (1.0 - BETA_SECOND**STEP)) + ADAM_FLOOR)
    )
    master = master - LEARN_RATE * (moved + WEIGHT_DECAY * master)
    return (master, first, second, keep * average + (1.0 - keep) * master)


STEP_ROWS = 144


def step_kernel(widths, n_rows, table, places, factor, *refs):
    quarters, olds, news = refs[:4], refs[4:8], refs[8:12]
    shard, flat, sems = refs[12:]
    block = pl.program_id(0)
    per = n_rows // 4

    @pl.when(block == 0)
    def _():
        copies = [
            pltpu.make_async_copy(
                quarters[k],
                shard.at[pl.ds(pl.multiple_of(places[k] * per, 8), per)],
                sems.at[k],
            )
            for k in range(4)
        ]
        for copy in copies:
            copy.start()
        for copy in copies:
            copy.wait()

    for wide in widths:
        count = STEP_BLOCK // wide

        @pl.when(table[block, 0] == wide)
        def _():
            for slab in range(wide):
                row = pl.multiple_of(table[block, 1] + slab * table[block, 2], 8)
                for tile in range(LANE_TILES):
                    flat[pl.ds(LANE_TILES * slab + tile, count, stride=LANE_TILES * wide), :] = shard[
                        pl.ds(row, count), tile * LANES : (tile + 1) * LANES
                    ]

    scale = factor[0]

    def some_rows(number, carry):
        at = pl.ds(pl.multiple_of(number * STEP_ROWS, 8), STEP_ROWS)
        old = [ref[at, :] for ref in olds]
        made = step_values(old[0], flat[at, :] * scale, old[1], old[2], old[3])
        for ref, value in zip(news, made):
            ref[at, :] = value
        return carry

    lax.fori_loop(0, STEP_BLOCK * LANE_TILES // STEP_ROWS, some_rows, 0)


def step_shard(quarters, places, table, widths, n_rows, factor, olds):
    units = STEP_BLOCK * LANE_TILES
    block_spec = pl.BlockSpec((units, LANES), lambda b, t, p, f: (b, 0))
    whole = pl.BlockSpec(memory_space=pl.ANY)
    flat_shape = jax.ShapeDtypeStruct((n_rows * LANE_TILES, LANES), jnp.float32)
    made = pl.pallas_call(
        partial(step_kernel, widths, n_rows),
        grid_spec=pltpu.PrefetchScalarGridSpec(
            num_scalar_prefetch=3,
            grid=(n_rows // STEP_BLOCK,),
            in_specs=[whole] * 4 + [block_spec] * 4,
            out_specs=[block_spec] * 4,
            scratch_shapes=[
                pltpu.VMEM((n_rows, D), jnp.float32),
                pltpu.VMEM((units, LANES), jnp.float32),
                pltpu.SemaphoreType.DMA((4,)),
            ],
        ),
        out_shape=[flat_shape] * 4,
        compiler_params=pltpu.CompilerParams(vmem_limit_bytes=50 * 1024 * 1024),
    )(table, places, factor, *quarters, *[old.reshape(-1, LANES) for old in olds])
    return [value.reshape(-1) for value in made]


ROW_TIME_ONE = PATCH_VALUES
ROW_TIME_TWO = ROW_TIME_ONE + TFREQ
ROW_BLOCK = ROW_TIME_TWO + D
ROW_CAP_ONE = ROW_BLOCK + 6 * D
ROW_CAP_TWO = ROW_CAP_ONE + CAPW
ROW_FINAL = ROW_CAP_TWO + D
ROW_NULL = ROW_FINAL + PATCH_VALUES
EMB_UNITS = 16158720 // LANES // N_OWN
EMB_FIRST = [EMB_UNITS * c // LANE_TILES for c in range(N_OWN)]
EMB_SHIFT = [EMB_UNITS * c % LANE_TILES for c in range(N_OWN)]


def two_parts(product, value):
    upper, lower = halves(value)
    return product(upper) + product(lower)


def shards_block(
    latents,
    noise,
    timesteps,
    captions,
    cap_lengths,
    null_flags,
    sample_weight,
    embed_w,
    attend_w,
    dense_w,
    vector_w,
    embed_m,
    attend_m,
    dense_m,
    vector_m,
    embed_v,
    attend_v,
    dense_v,
    vector_v,
    embed_e,
    attend_e,
    dense_e,
    vector_e,
):
    clip_dev, frame_dev, patches = (latents.shape[0], latents.shape[1], latents.shape[2])
    n_frame = lax.axis_size("frame")
    n_clip = lax.axis_size("clip")
    local_pos = patches // n_frame
    tokens = frame_dev * patches
    frame_id = lax.axis_index("frame")
    clip_id = lax.axis_index("clip")
    x_id, core_id = frame_id // CORES, frame_id % CORES
    z_id, y_id = clip_id // Y_SIZE, clip_id % Y_SIZE

    attend_cast = cast_shard(
        attend_w, jnp.asarray(cast_table(ATTEND_SEGS, CAST_BLOCK))[clip_id], (1, 2, 3), ATTEND_ROWS
    )
    space_qkv, space_out, time_qkv, time_out, cross_q, cross_kv, cross_out = gather_shards(
        attend_cast, clip_id, frame_id, range(N_OWN), *matrix_plan(ATTEND, ATTEND_SEGS)
    )
    emb_first = jnp.asarray(EMB_FIRST, jnp.int32)[clip_id]
    emb_shift = jnp.asarray(EMB_SHIFT, jnp.int32)[clip_id]
    emb_flat = lax.dynamic_update_slice(
        jnp.zeros((EMB_PAD * LANE_TILES, LANES), jnp.float32),
        embed_w.reshape(-1, LANES),
        (emb_shift, 0 * emb_shift),
    )
    emb_rows = flat_to_rows(emb_flat, jnp.bfloat16)
    cap_owners = range(4, N_OWN)
    cap_weights = gather_shards(
        emb_rows,
        clip_id,
        frame_id,
        cap_owners,
        [(EMB_PAD * len(cap_owners), D)],
        [(0, EMB_PAD * k, 0, owner, 0, EMB_PAD) for k, owner in enumerate(cap_owners)],
    )[0]
    dense_cast = cast_shard(
        dense_w, jnp.asarray(cast_table(DENSE_SEGS, CAST_BLOCK))[clip_id], (1, 4), DENSE_ROWS
    )
    fc_in, fc_out = gather_shards(
        dense_cast, clip_id, frame_id, range(N_OWN), *matrix_plan(DENSE, DENSE_SEGS)
    )

    last = N_OWN - 1
    cap_last = cap_weights[EMB_PAD * (len(cap_owners) - 1) :]
    null_end = 16158720 - ROW_NULL * D
    null_first, final_first = ROW_NULL - EMB_FIRST[last], ROW_FINAL - EMB_FIRST[last]
    null_caption = (
        cap_last[null_first : null_first - (-null_end // D)]
        .reshape(-1)[:null_end]
        .reshape(L_CAP, CAPW)
    )
    final_w = cap_last[final_first : final_first + PATCH_VALUES].reshape(D, PATCH_VALUES)
    two_first = ROW_CAP_TWO - EMB_FIRST[last]

    def to_cap_rows(value):
        padded = jnp.pad(value, ((0, 0), (EMB_PAD, EMB_PAD)))
        starts = [EMB_FIRST[owner] - ROW_CAP_ONE + EMB_PAD for owner in cap_owners]
        return jnp.concatenate([padded[:, start : start + EMB_PAD] for start in starts], 1)

    def from_cap_rows(value):
        total = 0.0
        for k, owner in enumerate(cap_owners):
            start = EMB_FIRST[owner] - ROW_CAP_ONE
            low, high = max(0, -start), min(EMB_PAD, CAPW - start)
            part = value[:, EMB_PAD * k + low : EMB_PAD * k + high]
            total = total + jnp.pad(part, ((0, 0), (start + low, CAPW - start - high)))
        return total

    (
        patch_b,
        time_b1,
        time_b2,
        block_b,
        cap_b1,
        cap_b2,
        space_bq,
        space_bv,
        space_bo,
        time_bq,
        time_bv,
        time_bo,
        cross_bq,
        cross_bv,
        cross_bo,
        fc_in_b,
        fc_out_b,
        final_b,
        table,
        final_table,
    ) = split_flat(vector_w, vector_shapes())

    own_clip = jnp.arange(n_clip) == clip_id
    facts = jnp.stack([timesteps.astype(jnp.float32)[0], sample_weight[0]])
    facts = sum_clips(jnp.where(own_clip[:, None], facts[None], 0.0))
    all_steps = facts[:, 0]
    angle = (all_steps / 1000.0 + 0.008) / 1.008 * (math.pi / 2)
    signal = jnp.cos(angle) ** 2
    ratio = signal / (1.0 - signal)
    all_weights = facts[:, 1] * jnp.minimum(ratio, SNR_LIMIT) / ratio
    weight_total = jnp.sum(all_weights)
    signal = lax.dynamic_slice_in_dim(signal, clip_id, 1, 0)
    loss_weight = lax.dynamic_slice_in_dim(all_weights, clip_id, 1, 0)

    freq_in = sincos(all_steps, TFREQ).astype(jnp.bfloat16)
    at_start = clip_id == 0
    time_one = emb_rows[ROW_TIME_ONE:ROW_TIME_TWO]
    time_two = emb_rows[ROW_TIME_TWO:ROW_BLOCK]
    pre_one = matmul_low(freq_in, time_one) + time_b1
    act_one = jax.nn.silu(pre_one).astype(jnp.bfloat16)
    time_embed = matmul_low(act_one, time_two) + time_b2
    early = jnp.concatenate(
        [pre_one, time_embed, emb_rows[:ROW_TIME_ONE].astype(jnp.float32)], 0
    )
    early = sum_clips(jnp.where(at_start, early, 0.0))
    pre_one, time_embed = early[:n_clip], early[n_clip : 2 * n_clip]
    patch_w = early[2 * n_clip :].astype(jnp.bfloat16)
    act_one = jax.nn.silu(pre_one).astype(jnp.bfloat16)
    silu_time = jax.nn.silu(time_embed).astype(jnp.bfloat16)
    local_row = emb_first + jnp.arange(EMB_PAD, dtype=jnp.int32)
    block_row = local_row - ROW_BLOCK
    in_block = (block_row >= 0) & (block_row < 6 * D)
    block_part = jnp.where(in_block, block_row % 6, -1)
    block_line = jnp.where(in_block, block_row // 6, -1)
    chooser = jnp.arange(D, dtype=jnp.int32)[:, None] == block_line[None]
    silu_rows = matmul_low(silu_time, chooser.astype(jnp.bfloat16)).astype(jnp.bfloat16)
    part_mask = jnp.arange(6, dtype=jnp.int32)[:, None] == block_part[None]
    block_left = jnp.where(part_mask[None], silu_rows[:, None], 0).reshape(n_clip * 6, EMB_PAD)
    block_out = sum_clips(matmul_low(block_left, emb_rows)).reshape(n_clip, 6, D)
    all_mods = table[None] + (block_out + block_b.reshape(6, D))
    mods = lax.dynamic_slice_in_dim(all_mods, clip_id, 1, 0)
    my_embed = lax.dynamic_slice_in_dim(time_embed, clip_id, 1, 0)

    keep_part = jnp.sqrt(signal)[:, None, None, None]
    fade_part = jnp.sqrt(1.0 - signal)[:, None, None, None]
    noisy = (keep_part * latents + fade_part * noise).astype(jnp.bfloat16)
    frame_ids = frame_id * frame_dev + jnp.arange(frame_dev)
    patch_ids = jnp.arange(patches)
    place = jnp.concatenate(
        [sincos(patch_ids // PGRID, D // 2), sincos(patch_ids % PGRID, D // 2)], -1
    )[None, None]
    hidden_zero = matmul_low(noisy, patch_w) + patch_b + place + sincos(frame_ids, D)[None, :, None]

    def mod_row(number):
        return mods[:, number][:, None, None, :]

    is_null = null_flags == 1
    cap_in = jnp.where(is_null[:, None, None], null_caption[None], captions)
    cap_pre = (matmul_low(to_cap_rows(cap_in[0]), cap_weights) + cap_b1)[None]
    cap_act = gelu_tanh(cap_pre).astype(jnp.bfloat16)
    act_rows = jnp.pad(cap_act[0], ((0, 0), (two_first, EMB_PAD - two_first - D)))
    cap_rows = (matmul_low(act_rows, cap_last) + cap_b2).astype(jnp.bfloat16)[None]
    live_len = jnp.where(is_null, L_CAP, cap_lengths)
    key_mask = jnp.arange(L_CAP)[None, :] < live_len[:, None]
    cap_wide = jnp.concatenate([cap_in[0], cap_act[0]], -1)
    cap_wide = jnp.pad(cap_wide, ((0, 0), (EMB_PAD, EMB_PAD)))
    wanted = []
    for owner in range(n_clip):
        start = EMB_FIRST[owner] - ROW_CAP_ONE + EMB_PAD
        if start + EMB_PAD <= EMB_PAD:
            wanted.append(jnp.zeros((L_CAP, EMB_PAD // 4), jnp.bfloat16))
        else:
            wanted.append(
                lax.dynamic_slice_in_dim(cap_wide, start + frame_id * (EMB_PAD // 4), EMB_PAD // 4, 1)
            )
    cap_left = lax.all_to_all(jnp.stack(wanted), "clip", split_axis=0, concat_axis=0, tiled=True)
    cap_left = cap_left.reshape(n_clip * L_CAP, EMB_PAD // 4)

    def flat2(value):
        return value.reshape(-1, value.shape[-1])

    space_in = modulate(hidden_zero, mod_row(0), mod_row(1)).astype(jnp.bfloat16)
    space_q, space_k, space_v = (
        heads_of(piece, clip_dev * frame_dev)
        for piece in split_qkv(matmul_low(space_in, space_qkv), space_bq, space_bv)
    )
    space_o, space_lse = attend_forward(space_q, space_k, space_v, None)
    space_flat = space_o.reshape(clip_dev, frame_dev, patches, D)
    space_res = matmul_low(space_flat, space_out) + space_bo
    hidden_one = hidden_zero + mod_row(2) * space_res
    time_in = lax.all_to_all(
        hidden_one.astype(jnp.bfloat16), "frame", split_axis=2, concat_axis=1, tiled=True
    )
    time_in = jnp.swapaxes(time_in, 1, 2)
    frames = time_in.shape[2]
    time_q, time_k, time_v = (
        heads_of(piece, clip_dev * local_pos)
        for piece in split_qkv(matmul_low(time_in, time_qkv), time_bq, time_bv)
    )
    time_o, time_lse = attend_forward(time_q, time_k, time_v, None)
    time_back = jnp.swapaxes(time_o.reshape(clip_dev, local_pos, frames, D), 1, 2)
    time_flat = lax.all_to_all(time_back, "frame", split_axis=1, concat_axis=2, tiled=True)
    time_res = matmul_low(time_flat, time_out) + time_bo
    hidden_two = hidden_one + mod_row(2) * time_res
    cross_in = hidden_two.astype(jnp.bfloat16)
    cross_query = heads_of(
        (matmul_low(cross_in, cross_q) + cross_bq).astype(jnp.bfloat16), clip_dev
    )
    cross_merged = matmul_low(cap_rows, cross_kv)
    cross_k = heads_of(cross_merged[..., :D].astype(jnp.bfloat16), clip_dev)
    cross_v = heads_of((cross_merged[..., D:] + cross_bv).astype(jnp.bfloat16), clip_dev)
    cross_o, cross_lse = attend_forward(cross_query, cross_k, cross_v, key_mask)
    cross_flat = cross_o.reshape(clip_dev, frame_dev, patches, D)
    hidden_three = hidden_two + matmul_low(cross_flat, cross_out) + cross_bo
    dense_in = modulate(hidden_three, mod_row(3), mod_row(4)).astype(jnp.bfloat16)
    dense_pre = matmul_low(dense_in, fc_in) + fc_in_b
    dense_act = gelu_tanh(dense_pre).astype(jnp.bfloat16)
    dense_res = matmul_low(dense_act, fc_out) + fc_out_b
    hidden_four = hidden_three + mod_row(5) * dense_res
    final_mod = final_table[None] + my_embed[:, None, :]
    final_shift = final_mod[:, 0][:, None, None, :]
    final_scale = final_mod[:, 1][:, None, None, :]
    final_in = modulate(hidden_four, final_shift, final_scale).astype(jnp.bfloat16)
    predicted = matmul_low(final_in, final_w) + final_b
    miss = predicted - noise
    clip_error = jnp.sum(jnp.mean(miss * miss, -1), (1, 2))
    local_loss = jnp.sum(loss_weight * clip_error)

    inputs = {}
    for label, value in (
        ("space_qkv", space_in),
        ("space_out", space_flat),
        ("time_qkv", time_in),
        ("time_out", time_flat),
        ("cross_q", cross_in),
        ("cross_out", cross_flat),
        ("fc_in", dense_in),
    ):
        segments = DENSE_SEGS if label == "fc_in" else ATTEND_SEGS
        inputs[label] = pick_columns(both_cores(flat2(value)), half_rows(segments, label), core_id)
    act_both = both_cores(flat2(dense_act))
    half = half_rows([[("square", 0, D, 1)]], "square")
    for block in range(MLP // D):
        inputs["fc_out", block] = pick_columns(act_both[:, block * D : (block + 1) * D], half, core_id)

    def core_grad(left, outs):
        return [weight_grad(left, both_cores(flat2(out))) for out in outs]

    def columns(value):
        return [value[..., j * D : (j + 1) * D] for j in range(value.shape[-1] // D)]

    grad_pred = (
        2.0 / miss.shape[-1] * (loss_weight / weight_total)[:, None, None, None] * miss
    ).astype(jnp.bfloat16)
    g_final_w = weight_grad(final_in, grad_pred)
    g_final_b = bias_grad(grad_pred)
    unused, pullback = jax.vjp(modulate, hidden_four, final_shift, final_scale)
    grad_hidden, grad_fshift, grad_fscale = pullback(back_low(grad_pred, final_w))
    grad_fmod = jnp.concatenate([grad_fshift.reshape(1, D), grad_fscale.reshape(1, D)], 0)
    grad_dense = (grad_hidden * mod_row(5)).astype(jnp.bfloat16)
    grad_gate_b = jnp.sum(grad_hidden * dense_res, (1, 2))
    grads = {}
    dense_both = both_cores(flat2(grad_dense))
    g_fc_out = [weight_grad(inputs["fc_out", block], dense_both) for block in range(MLP // D)]
    grads["fc_out"] = [jnp.concatenate(g_fc_out, 0)]
    g_fc_out_b = bias_grad(grad_dense)
    unused, pullback = jax.vjp(gelu_tanh, dense_pre)
    grad_pre = pullback(back_low(grad_dense, fc_out))[0].astype(jnp.bfloat16)
    grads["fc_in"] = core_grad(inputs["fc_in"], columns(grad_pre))
    g_fc_in_b = bias_grad(grad_pre)
    dense_parts = [
        reduce_pair(pair_chunks(grads, DENSE_SEGS, z), z, z % 2 == 1, x_id, y_id)
        for z in (3, 2, 1, 0)
    ][::-1]
    unused, pullback = jax.vjp(modulate, hidden_three, mod_row(3), mod_row(4))
    grad_input, grad_shift_b, grad_scale_b = pullback(back_low(grad_pre, fc_in))
    grad_hidden = grad_hidden + grad_input
    grad_cross = grad_hidden.astype(jnp.bfloat16)
    grads["cross_out"] = core_grad(inputs["cross_out"], [grad_cross])
    g_cross_bo = bias_grad(grad_cross)
    grad_cross_o = heads_of(back_low(grad_cross, cross_out).astype(jnp.bfloat16), clip_dev)
    grad_cq, grad_ck, grad_cv = attend_backward(
        cross_query, cross_k, cross_v, key_mask, cross_lse, grad_cross_o
    )
    grad_cq = grad_cq.astype(jnp.bfloat16).reshape(clip_dev, frame_dev, patches, D)
    grads["cross_q"] = core_grad(inputs["cross_q"], [grad_cq])
    g_cross_bq = bias_grad(grad_cq)
    grad_hidden = grad_hidden + back_low(grad_cq, cross_q)
    grad_cv = grad_cv.reshape(clip_dev, L_CAP, D)
    grad_ckv = jnp.concatenate([grad_ck.reshape(clip_dev, L_CAP, D), grad_cv], -1)[0]
    g_cross_bv = bias_grad(grad_cv)
    grad_ckv = grad_ckv + shift(grad_ckv, SWAP_CORE)
    cap_half = pick_columns(cap_rows[0], half_rows(ATTEND_SEGS, "cross_kv"), core_id)
    grads["cross_kv"] = [weight_split(cap_half, part) for part in columns(grad_ckv)]
    grad_ckv = grad_ckv + shift(grad_ckv, SWAP_X)
    grad_cap_rows = back_split(grad_ckv, cross_kv)

    def reduce_attend(z, x_first):
        return reduce_pair(pair_chunks(grads, ATTEND_SEGS, z), z, x_first, x_id, y_id)

    attend_parts = [None] * Z_SIZE
    attend_parts[3] = reduce_attend(3, True)
    grad_time = (grad_hidden * mod_row(2)).astype(jnp.bfloat16)
    grads["time_out"] = core_grad(inputs["time_out"], [grad_time])
    g_time_bo = bias_grad(grad_time)
    grad_time_o = lax.all_to_all(
        back_low(grad_time, time_out).astype(jnp.bfloat16),
        "frame",
        split_axis=2,
        concat_axis=1,
        tiled=True,
    )
    grad_time_o = heads_of(jnp.swapaxes(grad_time_o, 1, 2), clip_dev * local_pos)
    grad_tq, grad_tk, grad_tv = attend_backward(time_q, time_k, time_v, None, time_lse, grad_time_o)
    grad_tqkv = [
        piece.astype(jnp.bfloat16).reshape(clip_dev, local_pos, frames, D)
        for piece in (grad_tq, grad_tk, grad_tv)
    ]
    grads["time_qkv"] = core_grad(inputs["time_qkv"], grad_tqkv)
    g_time_bq = bias_grad(grad_tqkv[0])
    g_time_bv = bias_grad(grad_tqkv[2])
    grad_tqkv = lax.all_to_all(
        jnp.swapaxes(jnp.concatenate(grad_tqkv, -1), 1, 2), "frame", split_axis=1, concat_axis=2, tiled=True
    )
    attend_parts[2] = reduce_attend(2, False)
    grad_gate_a = jnp.sum(grad_hidden * time_res, (1, 2))
    grad_hidden = grad_hidden + back_low(grad_tqkv, time_qkv)
    grad_gate_a = grad_gate_a + jnp.sum(grad_hidden * space_res, (1, 2))
    grad_space = (grad_hidden * mod_row(2)).astype(jnp.bfloat16)
    grads["space_out"] = core_grad(inputs["space_out"], [grad_space])
    g_space_bo = bias_grad(grad_space)
    attend_parts[1] = reduce_attend(1, True)
    grad_space_o = heads_of(
        back_low(grad_space, space_out).astype(jnp.bfloat16), clip_dev * frame_dev
    )
    grad_sqkv = [
        piece.astype(jnp.bfloat16).reshape(clip_dev, frame_dev, patches, D)
        for piece in attend_backward(space_q, space_k, space_v, None, space_lse, grad_space_o)
    ]
    grads["space_qkv"] = core_grad(inputs["space_qkv"], grad_sqkv)
    attend_parts[0] = reduce_attend(0, False)
    g_space_bq = bias_grad(grad_sqkv[0])
    g_space_bv = bias_grad(grad_sqkv[2])
    grad_sqkv = jnp.concatenate(grad_sqkv, -1)
    unused, pullback = jax.vjp(modulate, hidden_zero, mod_row(0), mod_row(1))
    grad_input, grad_shift_a, grad_scale_a = pullback(back_low(grad_sqkv, space_qkv))
    grad_hidden = grad_hidden + grad_input
    g_patch_w = weight_split(noisy, grad_hidden)
    g_patch_b = bias_grad(grad_hidden)
    grad_mods = jnp.concatenate(
        [
            grad_shift_a.reshape(clip_dev, D),
            grad_scale_a.reshape(clip_dev, D),
            grad_gate_a,
            grad_shift_b.reshape(clip_dev, D),
            grad_scale_b.reshape(clip_dev, D),
            grad_gate_b,
            grad_fmod,
        ],
        0,
    )

    unused, pullback = jax.vjp(gelu_tanh, cap_pre[0])
    grad_cap_pre = pullback(back_split(grad_cap_rows, cap_last)[:, two_first : two_first + D])[0]
    cap_right = lax.all_gather(
        jnp.stack([grad_cap_pre, grad_cap_rows]), "clip", axis=1, tiled=True
    )
    null_sum = jnp.where(is_null[0], grad_cap_pre, 0.0)
    g_cap_b1 = bias_grad(grad_cap_pre)
    g_cap_b2 = bias_grad(grad_cap_rows)

    once = frame_id == 0
    gathered_mods = jnp.where(own_clip[:, None, None], grad_mods[None], 0.0)
    zero_d = jnp.zeros((D,), jnp.float32)
    vector_grad = flatten_all(
        [
            g_patch_b,
            jnp.where(once, g_cap_b1, 0.0),
            jnp.where(once, g_cap_b2, 0.0),
            g_space_bq,
            g_space_bv,
            g_space_bo,
            g_time_bq,
            g_time_bv,
            g_time_bo,
            g_cross_bq,
            g_cross_bv,
            g_cross_bo,
            g_fc_in_b,
            g_fc_out_b,
            g_final_b,
        ]
    )
    vector_grad, gathered_mods, g_patch_w, g_final_w, loss_sum, null_sum = lax.psum(
        (
            vector_grad,
            gathered_mods,
            g_patch_w,
            g_final_w,
            local_loss,
            jnp.where(once, null_sum, 0.0),
        ),
        AXES,
    )

    grad_zero = gathered_mods[:, :6]
    grad_final = gathered_mods[:, 6:]
    zero_rows = grad_zero.reshape(n_clip * 6, D)
    back_rows = two_parts(lambda part: back_low(part, emb_rows), zero_rows)
    back_rows = jnp.sum(jnp.where(part_mask[None], back_rows.reshape(n_clip, 6, EMB_PAD), 0.0), 1)
    grad_silu = lax.dot_general(
        back_rows,
        chooser.astype(jnp.float32),
        (((1,), (1,)), ((), ())),
        precision=lax.Precision.HIGHEST,
        preferred_element_type=jnp.float32,
    )
    grad_silu = sum_clips(grad_silu)
    unused, pullback = jax.vjp(jax.nn.silu, time_embed)
    grad_embed = grad_final[:, 0] + grad_final[:, 1] + pullback(grad_silu)[0]
    grad_act = two_parts(lambda part: back_low(part, time_two), grad_embed)
    grad_act = sum_clips(jnp.where(at_start, grad_act, 0.0))
    unused, pullback = jax.vjp(jax.nn.silu, pre_one)
    grad_one = pullback(grad_act)[0]
    g_table = jnp.sum(grad_zero, 0)
    vector_sum = flatten_all(
        [
            vector_grad[:D],
            jnp.sum(grad_one, 0),
            jnp.sum(grad_embed, 0),
            g_table,
            vector_grad[D:],
            g_table,
            jnp.sum(grad_final, 0),
        ]
    )

    per = EMB_PAD // 4
    quarter_row = emb_first + frame_id * per + jnp.arange(per, dtype=jnp.int32)
    time_left = jnp.concatenate(
        [
            jnp.pad(freq_in, ((0, 0), (ROW_TIME_ONE, EMB_PAD - ROW_TIME_TWO))),
            jnp.pad(act_one, ((0, 0), (ROW_TIME_TWO, EMB_PAD - ROW_BLOCK))),
        ],
        0,
    )
    time_left = jnp.where(at_start, time_left, jnp.zeros_like(time_left))
    small_left = lax.dynamic_slice_in_dim(
        jnp.concatenate([time_left, block_left], 0), frame_id * per, per, 1
    )
    small_right = jnp.concatenate([grad_one, grad_embed, zero_rows], 0)
    first_kind = (quarter_row < ROW_CAP_TWO)[None]
    no_left = jnp.zeros_like(cap_left)
    emb_left = jnp.concatenate(
        [
            small_left,
            jnp.where(first_kind, cap_left, no_left),
            jnp.where(first_kind, no_left, cap_left),
        ],
        0,
    )
    emb_right = jnp.concatenate([small_right, cap_right[0], cap_right[1]], 0)
    emb_grad = two_parts(lambda part: weight_grad(emb_left, part), emb_right)
    g_null = from_cap_rows(two_parts(lambda part: back_low(part, cap_weights), null_sum))
    null_rows = jnp.pad(g_null.reshape(-1), (0, (EMB_PAD - (ROW_NULL - EMB_FIRST[last])) * D - null_end))
    tail_rows = jnp.concatenate(
        [
            jnp.zeros((ROW_FINAL - EMB_FIRST[last], D), jnp.float32),
            g_final_w.reshape(PATCH_VALUES, D),
            null_rows.reshape(-1, D),
        ],
        0,
    )
    head_rows = jnp.pad(g_patch_w, ((0, EMB_PAD - PATCH_VALUES), (0, 0)))
    extra = jnp.where(clip_id == last, tail_rows, jnp.where(at_start, head_rows, 0.0))
    emb_grad = emb_grad + lax.dynamic_slice_in_dim(extra, frame_id * per, per, 0)
    unit = (
        LANE_TILES * (frame_id * per + jnp.arange(per, dtype=jnp.int32))[:, None]
        + jnp.arange(D, dtype=jnp.int32)[None] // LANES
        - emb_shift
    )
    emb_grad = jnp.where((unit >= 0) & (unit < EMB_UNITS), emb_grad, 0.0)

    attend_part = choose_z(attend_parts, z_id).reshape(-1, D)
    dense_part = choose_z(dense_parts, z_id).reshape(-1, D)
    local_square = sum(jnp.sum(part * part) for part in (attend_part, dense_part, emb_grad))
    grad_norm = jnp.sqrt(lax.psum(local_square, AXES) + jnp.sum(vector_sum * vector_sum))
    factor = jnp.minimum(1.0, CLIP_LIMIT / (grad_norm + NORM_FLOOR))

    def four_parts(part):
        over_x = shift(part, SWAP_X)
        return [part, over_x, shift(part, SWAP_CORE), shift(over_x, SWAP_CORE)]

    spots = jnp.stack(
        [
            core_id * 2 + x_id,
            core_id * 2 + 1 - x_id,
            (1 - core_id) * 2 + x_id,
            (1 - core_id) * 2 + 1 - x_id,
        ]
    ).astype(jnp.int32)
    scale = factor.reshape(1)
    dense_r = step_shard(
        four_parts(dense_part),
        spots,
        jnp.asarray(step_table(DENSE_SEGS, STEP_BLOCK, DENSE_ROWS))[clip_id],
        (1, 4),
        DENSE_ROWS,
        scale,
        (dense_w, dense_m, dense_v, dense_e),
    )
    attend_r = step_shard(
        four_parts(attend_part),
        spots,
        jnp.asarray(step_table(ATTEND_SEGS, STEP_BLOCK, ATTEND_ROWS))[clip_id],
        (1, 2, 3),
        ATTEND_ROWS,
        scale,
        (attend_w, attend_m, attend_v, attend_e),
    )
    emb_parts = four_parts(emb_grad)
    emb_whole = jnp.zeros((4, per, D), jnp.float32)
    for part, flip in zip(emb_parts, (0, 2, 1, 3)):
        emb_whole = lax.dynamic_update_index_in_dim(emb_whole, part, frame_id ^ flip, 0)
    emb_flat = rows_to_flat(emb_whole.reshape(EMB_PAD, D))
    emb_owned = lax.dynamic_slice_in_dim(emb_flat, emb_shift, EMB_UNITS, 0).reshape(-1)
    embed_r = adam_step(embed_w, emb_owned, embed_m, embed_v, embed_e, factor)
    vector_r = adam_step(vector_w, vector_sum, vector_m, vector_v, vector_e, factor)
    return (
        loss_sum,
        weight_total,
        grad_norm,
        embed_r[0],
        attend_r[0],
        dense_r[0],
        vector_r[0],
        embed_r[1],
        attend_r[1],
        dense_r[1],
        vector_r[1],
        embed_r[2],
        attend_r[2],
        dense_r[2],
        vector_r[2],
        embed_r[3],
        attend_r[3],
        dense_r[3],
        vector_r[3],
    )


def pick_plan(mesh):
    if mesh.shape["frame"] == X_SIZE * CORES and mesh.shape["clip"] == N_OWN:
        return shards_block
    return shards


def solution(mesh):
    in_specs = (
        P("clip", "frame", None, None),
        P("clip", "frame", None, None),
        P("clip"),
        P("clip", None, None),
        P("clip"),
        P("clip"),
        P("clip"),
        P("clip"),
        P("clip"),
        P("clip"),
        P(),
        P("clip"),
        P("clip"),
        P("clip"),
        P(),
        P("clip"),
        P("clip"),
        P("clip"),
        P(),
        P("clip"),
        P("clip"),
        P("clip"),
        P(),
    )
    out_specs = (
        P(),
        P(),
        P(),
        P("clip"),
        P("clip"),
        P("clip"),
        P(),
        P("clip"),
        P("clip"),
        P("clip"),
        P(),
        P("clip"),
        P("clip"),
        P("clip"),
        P(),
        P("clip"),
        P("clip"),
        P("clip"),
        P(),
    )
    return jax.shard_map(pick_plan(mesh), mesh=mesh, in_specs=in_specs, out_specs=out_specs, check_vma=False)
```

```python
import math
from functools import partial

import jax
import jax.numpy as jnp
import numpy as np
from jax import lax
from jax.experimental import pallas as pl
from jax.experimental.pallas import tpu as pltpu
from jax.sharding import PartitionSpec as P

D = 1152
HEADS = 16
MLP = 4608
CAPW = 4096
L_CAP = 120
TFREQ = 256
PATCH_VALUES = 16
PGRID = 16
STEP = 10


NORM_FLOOR = 1e-06
CLIP_LIMIT = 1.0
SNR_LIMIT = 5.0
BETA_FIRST = 0.5
BETA_SECOND = 0.5
LEARN_RATE = 0.02
WEIGHT_DECAY = 0.01
ADAM_FLOOR = 1e-08
AVERAGE_KEEP = 0.9999
MASKED_SCORE = -1e30


def embed_shapes():
    return [
        (PATCH_VALUES, D),
        (TFREQ, D),
        (D, D),
        (D, 6 * D),
        (CAPW, D),
        (D, D),
        (D, PATCH_VALUES),
        (L_CAP, CAPW),
    ]


def attend_shapes():
    return [(D, 3 * D), (D, D), (D, 3 * D), (D, D), (D, D), (D, 2 * D), (D, D)]


def dense_shapes():
    return [(D, MLP), (MLP, D)]


def vector_shapes():
    return [(D,)] * 3 + [(6 * D,)] + [(D,)] * 11 + [(MLP,), (D,), (PATCH_VALUES,), (6, D), (2, D)]


def split_flat(flat, shapes):
    pieces = []
    offset = 0
    for extent in shapes:
        length = math.prod(extent)
        pieces.append(flat[offset : offset + length].reshape(extent))
        offset += length
    return pieces


def flatten_all(pieces):
    return jnp.concatenate([piece.reshape(-1) for piece in pieces])


def reduce_group(grad):
    n_clip = lax.axis_size("clip")
    n_frame = lax.axis_size("frame")
    reorder = grad.reshape(n_clip, n_frame, -1).swapaxes(0, 1).reshape(-1)
    share = lax.psum_scatter(reorder, ("frame", "clip"), scatter_dimension=0, tiled=True)
    return lax.all_gather(share, "frame", axis=0, tiled=True)


def sincos(places, width):
    half = width // 2
    omega = jnp.exp(-math.log(10000.0) * jnp.arange(half, dtype=jnp.float32) / half)
    angle = places.astype(jnp.float32)[..., None] * omega
    return jnp.concatenate([jnp.sin(angle), jnp.cos(angle)], -1)


def modulate(hidden, shift, scale):
    center = hidden - jnp.mean(hidden, -1, keepdims=True)
    normed = center * lax.rsqrt(jnp.mean(center * center, -1, keepdims=True) + NORM_FLOOR)
    return normed * (1.0 + scale) + shift


def gelu_tanh(value):
    return jax.nn.gelu(value, approximate=True)


def matmul_low(left, right):
    return lax.dot_general(
        left, right, (((left.ndim - 1,), (0,)), ((), ())), preferred_element_type=jnp.float32
    )


def halves(value):
    upper = lax.optimization_barrier(value.astype(jnp.bfloat16))
    return (upper, (value - upper.astype(jnp.float32)).astype(jnp.bfloat16))


def back_low(grads, weight):
    return lax.dot_general(
        grads, weight, (((grads.ndim - 1,), (1,)), ((), ())), preferred_element_type=jnp.float32
    )


def back_split(grads, weight):
    upper, lower = halves(grads)
    return back_low(upper, weight) + back_low(lower, weight)


def weight_grad(inputs, grads):
    left = inputs.reshape(-1, inputs.shape[-1])
    right = grads.reshape(-1, grads.shape[-1])
    return lax.dot_general(
        left, right, (((0,), (0,)), ((), ())), preferred_element_type=jnp.float32
    )


def weight_split(inputs, grads):
    upper, lower = halves(grads)
    return weight_grad(inputs, upper) + weight_grad(inputs, lower)


def bias_grad(grads):
    return jnp.sum(grads.astype(jnp.float32).reshape(-1, grads.shape[-1]), 0)


def heads_of(tensor, batch):
    return tensor.reshape(batch, -1, HEADS, tensor.shape[-1] // HEADS)


def split_qkv(merged, bias_q, bias_v):
    width = merged.shape[-1] // 3
    return (
        (merged[..., :width] + bias_q).astype(jnp.bfloat16),
        merged[..., width : 2 * width].astype(jnp.bfloat16),
        (merged[..., 2 * width :] + bias_v).astype(jnp.bfloat16),
    )


def attend_scores(queries, key_rows, mask):
    scores = jnp.einsum("bqhe,bkhe->bhqk", queries, key_rows, preferred_element_type=jnp.float32)
    scores = scores * queries.shape[-1] ** (-0.5)
    if mask is not None:
        scores = jnp.where(mask[:, None, None, :], scores, MASKED_SCORE)
    return scores


def attend_forward(queries, key_rows, values, mask):
    scores = attend_scores(queries, key_rows, mask)
    summit = jnp.max(scores, -1, keepdims=True)
    powers = jnp.exp(scores - summit)
    totals = jnp.sum(powers, -1, keepdims=True)
    probs = (powers / totals).astype(jnp.bfloat16)
    output = jnp.einsum("bhqk,bkhe->bqhe", probs, values, preferred_element_type=jnp.float32)
    return (output.astype(jnp.bfloat16), summit + jnp.log(totals))


def attend_backward(queries, key_rows, values, mask, log_total, grad_out):
    scale = queries.shape[-1] ** (-0.5)
    probs = jnp.exp(attend_scores(queries, key_rows, mask) - log_total)
    grad_probs = jnp.einsum("bqhe,bkhe->bhqk", grad_out, values, preferred_element_type=jnp.float32)
    grad_scores = (probs * (grad_probs - jnp.sum(probs * grad_probs, -1, keepdims=True))).astype(
        jnp.bfloat16
    )
    grad_query = (
        jnp.einsum("bhqk,bkhe->bqhe", grad_scores, key_rows, preferred_element_type=jnp.float32)
        * scale
    )
    grad_keys = (
        jnp.einsum("bhqk,bqhe->bkhe", grad_scores, queries, preferred_element_type=jnp.float32)
        * scale
    )
    grad_values = jnp.einsum(
        "bhqk,bqhe->bkhe", probs.astype(jnp.bfloat16), grad_out, preferred_element_type=jnp.float32
    )
    return (grad_query, grad_keys, grad_values)


def unpack_all(gathered):
    return (
        split_flat(gathered[0], embed_shapes()),
        split_flat(gathered[1], attend_shapes()),
        split_flat(gathered[2], dense_shapes()),
    )


def adam_step(master, grad, first, second, average, factor):
    keep = min(AVERAGE_KEEP, (1.0 + STEP) / (10.0 + STEP))
    grad = grad * factor
    first = BETA_FIRST * first + (1.0 - BETA_FIRST) * grad
    second = BETA_SECOND * second + (1.0 - BETA_SECOND) * grad * grad
    moved = (
        first
        / (1.0 - BETA_FIRST**STEP)
        / (jnp.sqrt(second / (1.0 - BETA_SECOND**STEP)) + ADAM_FLOOR)
    )
    master = master - LEARN_RATE * (moved + WEIGHT_DECAY * master)
    return (master, first, second, keep * average + (1.0 - keep) * master)


def shards(
    latents,
    noise,
    timesteps,
    captions,
    cap_lengths,
    null_flags,
    sample_weight,
    embed_w,
    attend_w,
    dense_w,
    vector_w,
    embed_m,
    attend_m,
    dense_m,
    vector_m,
    embed_v,
    attend_v,
    dense_v,
    vector_v,
    embed_e,
    attend_e,
    dense_e,
    vector_e,
):
    clip_dev, frame_dev, patches = (latents.shape[0], latents.shape[1], latents.shape[2])
    n_frame = lax.axis_size("frame")
    n_clip = lax.axis_size("clip")
    local_pos = patches // n_frame
    gathered = (
        lax.all_gather(embed_w.astype(jnp.bfloat16), "clip", axis=0, tiled=True),
        lax.all_gather(attend_w.astype(jnp.bfloat16), "clip", axis=0, tiled=True),
        lax.all_gather(dense_w.astype(jnp.bfloat16), "clip", axis=0, tiled=True),
    )
    embeds, attends, denses = unpack_all(gathered)
    patch_w, time_one, time_two, block_w, cap_one, cap_two, final_w, null_caption = embeds
    space_qkv, space_out, time_qkv, time_out, cross_q, cross_kv, cross_out = attends
    fc_in, fc_out = denses
    (
        patch_b,
        time_b1,
        time_b2,
        block_b,
        cap_b1,
        cap_b2,
        space_bq,
        space_bv,
        space_bo,
        time_bq,
        time_bv,
        time_bo,
        cross_bq,
        cross_bv,
        cross_bo,
        fc_in_b,
        fc_out_b,
        final_b,
        table,
        final_table,
    ) = split_flat(vector_w, vector_shapes())
    angle = (timesteps.astype(jnp.float32) / 1000.0 + 0.008) / 1.008 * (math.pi / 2)
    signal = jnp.cos(angle) ** 2
    ratio = signal / (1.0 - signal)
    loss_weight = sample_weight * jnp.minimum(ratio, SNR_LIMIT) / ratio
    weight_total = lax.psum(jnp.sum(loss_weight), "clip")
    keep_part = jnp.sqrt(signal)[:, None, None, None]
    fade_part = jnp.sqrt(1.0 - signal)[:, None, None, None]
    noisy = (keep_part * latents + fade_part * noise).astype(jnp.bfloat16)
    frame_ids = lax.axis_index("frame") * frame_dev + jnp.arange(frame_dev)
    patch_ids = jnp.arange(patches)
    place = jnp.concatenate(
        [sincos(patch_ids // PGRID, D // 2), sincos(patch_ids % PGRID, D // 2)], -1
    )[None, None]
    hidden_zero = matmul_low(noisy, patch_w) + patch_b + place + sincos(frame_ids, D)[None, :, None]
    freq_in = sincos(timesteps, TFREQ).astype(jnp.bfloat16)
    pre_one = matmul_low(freq_in, time_one) + time_b1
    act_one = jax.nn.silu(pre_one).astype(jnp.bfloat16)
    time_embed = matmul_low(act_one, time_two) + time_b2
    silu_time = jax.nn.silu(time_embed).astype(jnp.bfloat16)
    mods = table[None] + (matmul_low(silu_time, block_w) + block_b).reshape(clip_dev, 6, D)

    def mod_row(number):
        return mods[:, number][:, None, None, :]

    is_null = null_flags == 1
    cap_in = jnp.where(is_null[:, None, None], null_caption[None], captions)
    cap_pre = matmul_low(cap_in, cap_one) + cap_b1
    cap_act = gelu_tanh(cap_pre).astype(jnp.bfloat16)
    cap_rows = (matmul_low(cap_act, cap_two) + cap_b2).astype(jnp.bfloat16)
    live_len = jnp.where(is_null, L_CAP, cap_lengths)
    key_mask = jnp.arange(L_CAP)[None, :] < live_len[:, None]
    space_in = modulate(hidden_zero, mod_row(0), mod_row(1)).astype(jnp.bfloat16)
    space_q, space_k, space_v = (
        heads_of(piece, clip_dev * frame_dev)
        for piece in split_qkv(matmul_low(space_in, space_qkv), space_bq, space_bv)
    )
    space_o, space_lse = attend_forward(space_q, space_k, space_v, None)
    space_flat = space_o.reshape(clip_dev, frame_dev, patches, D)
    space_res = matmul_low(space_flat, space_out) + space_bo
    hidden_one = hidden_zero + mod_row(2) * space_res
    time_in = lax.all_to_all(
        hidden_one.astype(jnp.bfloat16), "frame", split_axis=2, concat_axis=1, tiled=True
    )
    time_in = jnp.swapaxes(time_in, 1, 2)
    frames = time_in.shape[2]
    time_q, time_k, time_v = (
        heads_of(piece, clip_dev * local_pos)
        for piece in split_qkv(matmul_low(time_in, time_qkv), time_bq, time_bv)
    )
    time_o, time_lse = attend_forward(time_q, time_k, time_v, None)
    time_back = jnp.swapaxes(time_o.reshape(clip_dev, local_pos, frames, D), 1, 2)
    time_flat = lax.all_to_all(time_back, "frame", split_axis=1, concat_axis=2, tiled=True)
    time_res = matmul_low(time_flat, time_out) + time_bo
    hidden_two = hidden_one + mod_row(2) * time_res
    cross_in = hidden_two.astype(jnp.bfloat16)
    cross_query = heads_of(
        (matmul_low(cross_in, cross_q) + cross_bq).astype(jnp.bfloat16), clip_dev
    )
    cross_merged = matmul_low(cap_rows, cross_kv)
    cross_k = heads_of(cross_merged[..., :D].astype(jnp.bfloat16), clip_dev)
    cross_v = heads_of((cross_merged[..., D:] + cross_bv).astype(jnp.bfloat16), clip_dev)
    cross_o, cross_lse = attend_forward(cross_query, cross_k, cross_v, key_mask)
    cross_flat = cross_o.reshape(clip_dev, frame_dev, patches, D)
    hidden_three = hidden_two + matmul_low(cross_flat, cross_out) + cross_bo
    dense_in = modulate(hidden_three, mod_row(3), mod_row(4)).astype(jnp.bfloat16)
    dense_pre = matmul_low(dense_in, fc_in) + fc_in_b
    dense_act = gelu_tanh(dense_pre).astype(jnp.bfloat16)
    dense_res = matmul_low(dense_act, fc_out) + fc_out_b
    hidden_four = hidden_three + mod_row(5) * dense_res
    final_mod = final_table[None] + time_embed[:, None, :]
    final_shift = final_mod[:, 0][:, None, None, :]
    final_scale = final_mod[:, 1][:, None, None, :]
    final_in = modulate(hidden_four, final_shift, final_scale).astype(jnp.bfloat16)
    predicted = matmul_low(final_in, final_w) + final_b
    miss = predicted - noise
    clip_error = jnp.sum(jnp.mean(miss * miss, -1), (1, 2))
    local_loss = jnp.sum(loss_weight * clip_error)
    grad_pred = (
        2.0 / miss.shape[-1] * (loss_weight / weight_total)[:, None, None, None] * miss
    ).astype(jnp.bfloat16)
    g_final_w = weight_grad(final_in, grad_pred)
    g_final_b = bias_grad(grad_pred)
    unused, pullback = jax.vjp(modulate, hidden_four, final_shift, final_scale)
    grad_hidden, grad_fshift, grad_fscale = pullback(back_low(grad_pred, final_w))
    grad_fmod = jnp.stack([grad_fshift.reshape(clip_dev, D), grad_fscale.reshape(clip_dev, D)], 1)
    g_final_table = jnp.sum(grad_fmod, 0)
    grad_time_embed = grad_fmod[:, 0] + grad_fmod[:, 1]
    grad_dense = (grad_hidden * mod_row(5)).astype(jnp.bfloat16)
    grad_gate_b = jnp.sum(grad_hidden * dense_res, (1, 2))
    g_fc_out = weight_grad(dense_act, grad_dense)
    g_fc_out_b = bias_grad(grad_dense)
    unused, pullback = jax.vjp(gelu_tanh, dense_pre)
    grad_pre = pullback(back_low(grad_dense, fc_out))[0].astype(jnp.bfloat16)
    g_fc_in = weight_grad(dense_in, grad_pre)
    g_fc_in_b = bias_grad(grad_pre)
    dense_owned = reduce_group(flatten_all([g_fc_in, g_fc_out]))
    unused, pullback = jax.vjp(modulate, hidden_three, mod_row(3), mod_row(4))
    grad_input, grad_shift_b, grad_scale_b = pullback(back_low(grad_pre, fc_in))
    grad_hidden = grad_hidden + grad_input
    grad_cross = grad_hidden.astype(jnp.bfloat16)
    g_cross_out = weight_grad(cross_flat, grad_cross)
    g_cross_bo = bias_grad(grad_cross)
    grad_cross_o = heads_of(back_low(grad_cross, cross_out).astype(jnp.bfloat16), clip_dev)
    grad_cq, grad_ck, grad_cv = attend_backward(
        cross_query, cross_k, cross_v, key_mask, cross_lse, grad_cross_o
    )
    grad_cq = grad_cq.astype(jnp.bfloat16).reshape(clip_dev, frame_dev, patches, D)
    g_cross_q = weight_grad(cross_in, grad_cq)
    g_cross_bq = bias_grad(grad_cq)
    grad_hidden = grad_hidden + back_low(grad_cq, cross_q)
    grad_cv = grad_cv.reshape(clip_dev, L_CAP, D)
    grad_ckv = jnp.concatenate([grad_ck.reshape(clip_dev, L_CAP, D), grad_cv], -1)
    g_cross_kv = weight_split(cap_rows, grad_ckv)
    g_cross_bv = bias_grad(grad_cv)
    grad_cap_rows = back_split(grad_ckv, cross_kv)
    grad_time = (grad_hidden * mod_row(2)).astype(jnp.bfloat16)
    g_time_out = weight_grad(time_flat, grad_time)
    g_time_bo = bias_grad(grad_time)
    grad_time_o = lax.all_to_all(
        back_low(grad_time, time_out).astype(jnp.bfloat16),
        "frame",
        split_axis=2,
        concat_axis=1,
        tiled=True,
    )
    grad_time_o = heads_of(jnp.swapaxes(grad_time_o, 1, 2), clip_dev * local_pos)
    grad_tq, grad_tk, grad_tv = attend_backward(time_q, time_k, time_v, None, time_lse, grad_time_o)
    grad_tqkv = jnp.concatenate(
        [
            piece.astype(jnp.bfloat16).reshape(clip_dev, local_pos, frames, D)
            for piece in (grad_tq, grad_tk, grad_tv)
        ],
        -1,
    )
    g_time_qkv = weight_grad(time_in, grad_tqkv)
    g_time_bq = bias_grad(grad_tqkv[..., :D])
    g_time_bv = bias_grad(grad_tqkv[..., 2 * D :])
    grad_tqkv = lax.all_to_all(
        jnp.swapaxes(grad_tqkv, 1, 2), "frame", split_axis=1, concat_axis=2, tiled=True
    )
    grad_gate_a = jnp.sum(grad_hidden * time_res, (1, 2))
    grad_hidden = grad_hidden + back_low(grad_tqkv, time_qkv)
    grad_gate_a = grad_gate_a + jnp.sum(grad_hidden * space_res, (1, 2))
    grad_space = (grad_hidden * mod_row(2)).astype(jnp.bfloat16)
    g_space_out = weight_grad(space_flat, grad_space)
    g_space_bo = bias_grad(grad_space)
    grad_space_o = heads_of(
        back_low(grad_space, space_out).astype(jnp.bfloat16), clip_dev * frame_dev
    )
    grad_sq, grad_sk, grad_sv = attend_backward(
        space_q, space_k, space_v, None, space_lse, grad_space_o
    )
    grad_sqkv = jnp.concatenate(
        [
            piece.astype(jnp.bfloat16).reshape(clip_dev, frame_dev, patches, D)
            for piece in (grad_sq, grad_sk, grad_sv)
        ],
        -1,
    )
    g_space_qkv = weight_grad(space_in, grad_sqkv)
    g_space_bq = bias_grad(grad_sqkv[..., :D])
    g_space_bv = bias_grad(grad_sqkv[..., 2 * D :])
    attend_owned = reduce_group(
        flatten_all(
            [g_space_qkv, g_space_out, g_time_qkv, g_time_out, g_cross_q, g_cross_kv, g_cross_out]
        )
    )
    unused, pullback = jax.vjp(modulate, hidden_zero, mod_row(0), mod_row(1))
    grad_input, grad_shift_a, grad_scale_a = pullback(back_low(grad_sqkv, space_qkv))
    grad_hidden = grad_hidden + grad_input
    g_patch_w = weight_split(noisy, grad_hidden)
    g_patch_b = bias_grad(grad_hidden)
    grad_mods = jnp.stack(
        [
            grad_shift_a.reshape(clip_dev, D),
            grad_scale_a.reshape(clip_dev, D),
            grad_gate_a,
            grad_shift_b.reshape(clip_dev, D),
            grad_scale_b.reshape(clip_dev, D),
            grad_gate_b,
        ],
        1,
    )
    g_table = jnp.sum(grad_mods, 0)
    grad_zero = grad_mods.reshape(clip_dev, 6 * D)
    g_block_b = jnp.sum(grad_zero, 0)
    g_block_w = weight_split(silu_time, grad_zero)
    unused, pullback = jax.vjp(jax.nn.silu, time_embed)
    grad_time_embed = grad_time_embed + pullback(back_split(grad_zero, block_w))[0]
    g_time_b2 = jnp.sum(grad_time_embed, 0)
    g_time_two = weight_split(act_one, grad_time_embed)
    unused, pullback = jax.vjp(jax.nn.silu, pre_one)
    grad_pre_one = pullback(back_split(grad_time_embed, time_two))[0]
    g_time_b1 = jnp.sum(grad_pre_one, 0)
    g_time_one = weight_split(freq_in, grad_pre_one)
    g_cap_b2 = bias_grad(grad_cap_rows)
    g_cap_two = weight_split(cap_act, grad_cap_rows)
    unused, pullback = jax.vjp(gelu_tanh, cap_pre)
    grad_cap_pre = pullback(back_split(grad_cap_rows, cap_two))[0]
    g_cap_b1 = bias_grad(grad_cap_pre)
    g_cap_one = weight_split(cap_in, grad_cap_pre)
    grad_cap_in = back_split(grad_cap_pre, cap_one)
    g_null = jnp.sum(jnp.where(is_null[:, None, None], grad_cap_in, 0.0), 0)
    embed_owned = reduce_group(
        flatten_all(
            [g_patch_w, g_time_one, g_time_two, g_block_w, g_cap_one, g_cap_two, g_final_w, g_null]
        )
    )
    vector_grad = flatten_all(
        [
            g_patch_b,
            g_time_b1,
            g_time_b2,
            g_block_b,
            g_cap_b1,
            g_cap_b2,
            g_space_bq,
            g_space_bv,
            g_space_bo,
            g_time_bq,
            g_time_bv,
            g_time_bo,
            g_cross_bq,
            g_cross_bv,
            g_cross_bo,
            g_fc_in_b,
            g_fc_out_b,
            g_final_b,
            g_table,
            g_final_table,
        ]
    )
    vector_sum, loss_sum = lax.psum((vector_grad, local_loss), ("frame", "clip"))
    owned = (embed_owned, attend_owned, dense_owned)
    local_square = (
        sum((jnp.sum(shard_piece * shard_piece) for shard_piece in owned))
        + jnp.sum(vector_sum * vector_sum) / n_clip
    )
    grad_norm = jnp.sqrt(lax.psum(local_square, "clip"))
    factor = jnp.minimum(1.0, CLIP_LIMIT / (grad_norm + NORM_FLOOR))
    embed_r = adam_step(embed_w, owned[0], embed_m, embed_v, embed_e, factor)
    attend_r = adam_step(attend_w, owned[1], attend_m, attend_v, attend_e, factor)
    dense_r = adam_step(dense_w, owned[2], dense_m, dense_v, dense_e, factor)
    vector_r = adam_step(vector_w, vector_sum, vector_m, vector_v, vector_e, factor)
    return (
        loss_sum,
        weight_total,
        grad_norm,
        embed_r[0],
        attend_r[0],
        dense_r[0],
        vector_r[0],
        embed_r[1],
        attend_r[1],
        dense_r[1],
        vector_r[1],
        embed_r[2],
        attend_r[2],
        dense_r[2],
        vector_r[2],
        embed_r[3],
        attend_r[3],
        dense_r[3],
        vector_r[3],
    )


AXES = ("frame", "clip")
LANES = 128
LANE_TILES = D // LANES
EMB_PAD = 1856


X_SIZE, CORES, Z_SIZE, Y_SIZE = 2, 2, 4, 2
N_OWN = Z_SIZE * Y_SIZE
RING = [(0, 0), (1, 0), (2, 0), (3, 0), (3, 1), (2, 1), (1, 1), (0, 1)]
RING_CLIP = [z * Y_SIZE + y for z, y in RING]
CLIP_RING = [RING_CLIP.index(c) for c in range(N_OWN)]


def pairs(move):
    out = []
    for x in range(X_SIZE):
        for core in range(CORES):
            for z in range(Z_SIZE):
                for y in range(Y_SIZE):
                    to = move(x, core, z, y)
                    if to is not None:
                        rank = lambda a, b, c, d: (a * CORES + b) * N_OWN + c * Y_SIZE + d
                        out.append((rank(x, core, z, y), rank(*to)))
    return out


SWAP_X = pairs(lambda x, c, z, y: (1 - x, c, z, y))
SWAP_CORE = pairs(lambda x, c, z, y: (x, 1 - c, z, y))
SWAP_Y = pairs(lambda x, c, z, y: (x, c, z, 1 - y))
SWAP_Z1 = pairs(lambda x, c, z, y: (x, c, z ^ 1, y))
SWAP_Z2 = pairs(lambda x, c, z, y: (x, c, z ^ 2, y))


def shift(value, perm):
    return lax.ppermute(value, AXES, perm)


def sum_clips(value):
    for perm in (SWAP_Y, SWAP_Z1, SWAP_Z2):
        value = value + shift(value, perm)
    return value


def sum_frames(value):
    for perm in (SWAP_CORE, SWAP_X):
        value = value + shift(value, perm)
    return value


def shard_segments(matrices, n_rows):
    spans, offset = [], 0
    for name, rows, wide in matrices:
        spans.append((name, offset, rows, wide))
        offset += rows * wide
    out = []
    for owner in range(N_OWN):
        low, high = owner * n_rows, (owner + 1) * n_rows
        mine = []
        for name, start, rows, wide in spans:
            begin, end = max(low, start), min(high, start + rows * wide)
            if begin < end:
                mine.append((name, (begin - start) // wide, (end - begin) // wide, wide))
        out.append(mine)
    return out


ATTEND = [
    ("space_qkv", D, 3),
    ("space_out", D, 1),
    ("time_qkv", D, 3),
    ("time_out", D, 1),
    ("cross_q", D, 1),
    ("cross_kv", D, 2),
    ("cross_out", D, 1),
]
DENSE = [("fc_in", D, 4), ("fc_out", MLP, 1)]
ATTEND_ROWS = 13824 // N_OWN
DENSE_ROWS = 9216 // N_OWN
ATTEND_SEGS = shard_segments(ATTEND, ATTEND_ROWS)
DENSE_SEGS = shard_segments(DENSE, DENSE_ROWS)


def cast_table(segments, block):
    out = []
    for mine in segments:
        rows, offset = [], 0
        for name, first, count, wide in mine:
            for start in range(0, count * wide, block):
                rows.append((wide, offset + start // wide, count))
            offset += count * wide
        out.append(rows)
    return np.array(out, np.int32)


def step_table(segments, block, n_rows):
    out = []
    for mine in segments:
        rows, offset = [], 0
        for name, first, count, wide in mine:
            half = count // 2
            for start in range(0, count * wide, block):
                core, inner = divmod(start // wide, half)
                rows.append((wide, core * (n_rows // 2) + offset + inner, half))
            offset += half * wide
        out.append(rows)
    return np.array(out, np.int32)


CAST_BLOCK = 576
STEP_BLOCK = 288


def cast_kernel(widths, table, flat, out):
    block = pl.program_id(0)
    for wide in widths:
        count = CAST_BLOCK // wide

        @pl.when(table[block, 0] == wide)
        def _():
            for slab in range(wide):
                row = pl.multiple_of(table[block, 1] + slab * table[block, 2], 16)
                for tile in range(LANE_TILES):
                    piece = flat[pl.ds(LANE_TILES * slab + tile, count, stride=LANE_TILES * wide), :]
                    out[pl.ds(row, count), tile * LANES : (tile + 1) * LANES] = piece.astype(jnp.bfloat16)


def cast_shard(flat, table, widths, n_rows):
    units = CAST_BLOCK * LANE_TILES
    return pl.pallas_call(
        partial(cast_kernel, widths),
        grid_spec=pltpu.PrefetchScalarGridSpec(
            num_scalar_prefetch=1,
            grid=(n_rows // CAST_BLOCK,),
            in_specs=[pl.BlockSpec((units, LANES), lambda b, t: (b, 0))],
            out_specs=pl.BlockSpec((n_rows, D), lambda b, t: (0, 0)),
        ),
        out_shape=jax.ShapeDtypeStruct((n_rows, D), jnp.bfloat16),
        compiler_params=pltpu.CompilerParams(vmem_limit_bytes=40 * 1024 * 1024),
    )(table, flat.reshape(-1, LANES))


ROWS_AHEAD = 16


def rows_kernel(shift_ref, flat, out, held, sem):
    units, count = flat.shape[0], out.shape[0]
    block = pl.program_id(0)

    @pl.when(block == 0)
    def _():
        end = (ROWS_AHEAD + units) // 8 * 8
        held[pl.ds(0, ROWS_AHEAD), :] = jnp.zeros((ROWS_AHEAD, LANES), jnp.float32)
        held[pl.ds(end, held.shape[0] - end), :] = jnp.zeros((held.shape[0] - end, LANES), jnp.float32)
        copy = pltpu.make_async_copy(flat, held.at[pl.ds(ROWS_AHEAD, units)], sem)
        copy.start()
        copy.wait()

    begin = ROWS_AHEAD + block * (count * LANE_TILES) - shift_ref[0]
    for tile in range(LANE_TILES):
        piece = held[pl.ds(begin + tile, count, stride=LANE_TILES), :]
        out[:, tile * LANES : (tile + 1) * LANES] = piece.astype(out.dtype)


def flat_to_rows(flat, rows, shift, dtype):
    block = rows // 4
    return pl.pallas_call(
        rows_kernel,
        grid_spec=pltpu.PrefetchScalarGridSpec(
            num_scalar_prefetch=1,
            grid=(4,),
            in_specs=[pl.BlockSpec(memory_space=pl.ANY)],
            out_specs=pl.BlockSpec((block, D), lambda b, t: (b, 0)),
            scratch_shapes=[
                pltpu.VMEM((ROWS_AHEAD + rows * LANE_TILES + 8, LANES), jnp.float32),
                pltpu.SemaphoreType.DMA,
            ],
        ),
        out_shape=jax.ShapeDtypeStruct((rows, D), dtype),
        compiler_params=pltpu.CompilerParams(vmem_limit_bytes=32 * 1024 * 1024),
    )(shift.reshape(1), flat)


def flat_kernel(rows, out):
    count = rows.shape[0]
    for tile in range(LANE_TILES):
        out[pl.ds(tile, count, stride=LANE_TILES), :] = rows[:, tile * LANES : (tile + 1) * LANES]


def rows_to_flat(rows):
    block = rows.shape[0] // 4
    return pl.pallas_call(
        flat_kernel,
        grid=(4,),
        in_specs=[pl.BlockSpec((block, D), lambda b: (b, 0))],
        out_specs=pl.BlockSpec((block * LANE_TILES, LANES), lambda b: (b, 0)),
        out_shape=jax.ShapeDtypeStruct((rows.shape[0] * LANE_TILES, LANES), rows.dtype),
        compiler_params=pltpu.CompilerParams(vmem_limit_bytes=32 * 1024 * 1024),
    )(rows)


def ring_place(clip):
    return jnp.where(clip % 2 == 0, clip // 2, N_OWN - 1 - clip // 2)


def clip_at(place):
    return jnp.where(place < N_OWN // 2, 2 * place, 2 * N_OWN - 1 - 2 * place)


def partners(frame, clip):
    place = ring_place(clip)
    x, core = frame // CORES, frame % CORES
    return (
        {"clip": clip_at((place + 1) % N_OWN)},
        {"clip": clip_at((place + N_OWN - 1) % N_OWN)},
        {"frame": (1 - x) * CORES + core},
        {"frame": x * CORES + 1 - core},
    )


def greet(devices):
    barrier = pltpu.get_barrier_semaphore()
    for device in devices:
        pl.semaphore_signal(barrier, inc=1, device_id=device, device_id_type=pl.DeviceIdType.MESH)
    pl.semaphore_wait(barrier, len(devices))


def spread_kernel(groups, modes, *refs):
    n, m = len(groups), len(modes)
    counts = [len(shapes) for keep, shapes, stores, common in groups]
    refs = list(refs)
    take = lambda number: [refs.pop(0) for _ in range(number)]
    owns, given, outs, given_outs = take(n), take(m), take(sum(counts)), take(m)
    helds, sources, landings = take(n), take(m), take(m)
    load_sem, send_sem, recv_sem, out_sem, peer_sem, peer_send, peer_recv = refs
    frame, clip = lax.axis_index("frame"), lax.axis_index("clip")
    x, core = frame // CORES, frame % CORES
    place = ring_place(clip)
    right, left, over_x, other = partners(frame, clip)
    half = N_OWN // 2
    owners = [clip_at((place + N_OWN - k) % N_OWN) for k in range(half + 1)]
    owners += [clip_at((place + k) % N_OWN) for k in range(1, half)]
    flip_x = (1 - x) * CORES + core
    mine = [core, frame, flip_x]
    theirs = [1 - core, x * CORES + 1 - core, (1 - x) * CORES + 1 - core]
    landing = mine + theirs

    def block_of(group, kinds, kind):
        return kinds[kind] + (2 if groups[group][3] and kind % 3 else 0)

    def held_at(group, slot):
        return helds[group].at[owners[slot] - min(groups[group][0])]

    def where_kept(group, slot, action):
        keep = groups[group][0]
        if len(keep) == N_OWN:
            action()
        else:
            pl.when(owners[slot] >= min(keep))(action)

    def load(group):
        return pltpu.make_async_copy(owns[group], held_at(group, 0), load_sem.at[group])

    def copy_of(group, slot, block, device, to_slot, kind):
        return pltpu.make_async_remote_copy(
            src_ref=held_at(group, slot).at[block],
            dst_ref=held_at(group, slot).at[block],
            send_sem=send_sem.at[group, to_slot, kind],
            recv_sem=recv_sem.at[group, to_slot, kind],
            device_id=device,
            device_id_type=pl.DeviceIdType.MESH,
        )

    sent = []

    def send(group, slot, from_kind, device, to_slot, kind):
        if from_kind == 0 and not groups[group][3]:
            return
        args = (group, slot, block_of(group, mine, from_kind), device, to_slot, kind)
        where_kept(group, slot, lambda: copy_of(*args).start())
        sent.append(args)

    def arrive(group, slot, kind):
        if kind % 3 == 0 and not groups[group][3]:
            return
        block = block_of(group, landing, kind)
        where_kept(group, slot, lambda: copy_of(group, slot, block, other, slot, kind).wait_recv())

    def onward(group, slot, kind):
        if slot < half:
            send(group, slot, kind, right, slot + 1, kind)
        if slot == 0:
            send(group, slot, kind, left, half + 1, kind)
        elif half < slot < N_OWN - 1:
            send(group, slot, kind, left, slot + 1, kind)

    def peer_load(item):
        return pltpu.make_async_copy(given[item], sources[item], peer_sem.at[item, 0])

    def peer_own(item):
        source = sources[item].at[clip] if modes[item] == "swap" else sources[item]
        return pltpu.make_async_copy(source, landings[item].at[clip], peer_sem.at[item, 1])

    def peer_copy(item, k):
        to = (clip + k) % N_OWN
        return pltpu.make_async_remote_copy(
            src_ref=sources[item].at[to] if modes[item] == "swap" else sources[item],
            dst_ref=landings[item].at[clip],
            send_sem=peer_send.at[item, k - 1],
            recv_sem=peer_recv.at[item, k - 1],
            device_id={"clip": to},
            device_id_type=pl.DeviceIdType.MESH,
        )

    def peers(item, arriving, action):
        for k in range(1, N_OWN):
            if modes[item] != "first":
                action(k)
            else:
                pl.when(clip == (k if arriving else 0))(lambda: action(k))

    for group in range(n):
        where_kept(group, 0, lambda: load(group).start())
    for item in range(m):
        peer_load(item).start()
    everyone = tuple({"clip": (clip + k) % N_OWN} for k in range(1, N_OWN)) if m else ()
    greet((right, left, over_x, other) + everyone)
    for group in range(n):
        where_kept(group, 0, lambda: load(group).wait())
        onward(group, 0, 1)
        onward(group, 0, 0)
    for item in range(m):
        peer_load(item).wait()
        peer_own(item).start()
        peers(item, False, lambda k: peer_copy(item, k).start())
    waiting = []
    for step in range(1, half + 1):
        slots = [step] + ([half + step] if step < half else [])
        pairs_now = [(group, slot) for group in range(n) for slot in slots]
        for group, slot in pairs_now:
            arrive(group, slot, 1)
            onward(group, slot, 1)
            send(group, slot, 1, over_x, slot, 2)
            send(group, slot, 1, other, slot, 4)
            arrive(group, slot, 0)
            onward(group, slot, 0)
            send(group, slot, 0, other, slot, 3)
        for group, slot in waiting:
            arrive(group, slot, 2)
            send(group, slot, 2, other, slot, 5)
        waiting = pairs_now
    for group, slot in waiting:
        arrive(group, slot, 2)
        send(group, slot, 2, other, slot, 5)
    for group in range(n):
        for slot in range(1, N_OWN):
            for kind in (3, 4, 5):
                arrive(group, slot, kind)
    done, base = [], 0
    for group, (keep, shapes, stores, common) in enumerate(groups):
        held = helds[group]
        rows = held.shape[2]
        for out, row, column, owner, first, count in stores:
            while count > 0:
                part, inner = divmod(first, rows)
                some = min(count, rows - inner)
                copy = pltpu.make_async_copy(
                    held.at[owner - min(keep), part, pl.ds(inner, some)],
                    outs[base + out].at[pl.ds(row, some), pl.ds(column, D)],
                    out_sem.at[len(done)],
                )
                copy.start()
                done.append(copy)
                first, row, count = first + some, row + some, count - some
        base += counts[group]
    for item in range(m):
        peer_own(item).wait()
        peers(item, True, lambda k: peer_copy(item, k).wait_recv())
        copy = pltpu.make_async_copy(landings[item], given_outs[item], peer_sem.at[item, 2])
        copy.start()
        done.append(copy)
    for item in range(m):
        peers(item, False, lambda k: peer_copy(item, k).wait_send())
    for args in sent:
        where_kept(args[0], args[1], lambda: copy_of(*args).wait_send())
    for copy in done:
        copy.wait()


def spread_shards(owns, groups, collective, given=()):
    spec = pl.BlockSpec(memory_space=pl.ANY)
    shapes = [shape for keep, some, stores, common in groups for shape in some]
    n_stores = sum(6 * len(stores) for keep, some, stores, common in groups)
    blocks = [6 if group[3] else 4 for group in groups]
    modes = [mode for value, mode in given]
    values = [value for value, mode in given]
    landed = [
        value.shape if mode == "swap" else (N_OWN,) + value.shape for value, mode in given
    ]
    many = max(len(given), 1)
    return pl.pallas_call(
        partial(spread_kernel, groups, modes),
        in_specs=[spec] * (len(owns) + len(given)),
        out_specs=[spec] * (len(shapes) + len(given)),
        out_shape=[jax.ShapeDtypeStruct(shape, jnp.bfloat16) for shape in shapes]
        + [jax.ShapeDtypeStruct(shape, value.dtype) for shape, value in zip(landed, values)],
        scratch_shapes=[
            pltpu.VMEM((len(group[0]), count, own.shape[0] // count, D), jnp.bfloat16)
            for own, group, count in zip(owns, groups, blocks)
        ]
        + [pltpu.VMEM(value.shape, value.dtype) for value in values]
        + [pltpu.VMEM(shape, value.dtype) for shape, value in zip(landed, values)]
        + [
            pltpu.SemaphoreType.DMA((len(owns),)),
            pltpu.SemaphoreType.DMA((len(owns), N_OWN, 6)),
            pltpu.SemaphoreType.DMA((len(owns), N_OWN, 6)),
            pltpu.SemaphoreType.DMA((n_stores,)),
            pltpu.SemaphoreType.DMA((many, 3)),
            pltpu.SemaphoreType.DMA((many, N_OWN - 1)),
            pltpu.SemaphoreType.DMA((many, N_OWN - 1)),
        ],
        compiler_params=pltpu.CompilerParams(
            collective_id=collective, has_side_effects=True, vmem_limit_bytes=50 * 1024 * 1024
        ),
        cost_estimate=pl.CostEstimate(
            flops=0, bytes_accessed=200 * 1000 * 1000, transcendentals=0
        ),
    )(*[own.reshape(count, own.shape[0] // count, D) for own, count in zip(owns, blocks)], *values)


LAG = 5


def collect_kernel(first, last, chunks, small, part, out, small_out, part_out, scratch):
    bufs, extra, locals_, finals, result = scratch[:2], scratch[2], scratch[3:5], scratch[5:7], scratch[7]
    ring_send, ring_recv, x_send, x_recv, end_send, end_recv, load_sem, own_sem = scratch[8:16]
    if small is not None:
        sums, arrived, small_send, small_recv = scratch[16:]
    if part is not None:
        frames, part_send, part_recv = scratch[16:]
    frame, clip = lax.axis_index("frame"), lax.axis_index("clip")
    x, core = frame // CORES, frame % CORES
    place = ring_place(clip)
    right, left, over_x, other = partners(frame, clip)
    swaps = [
        other,
        over_x,
        {"clip": clip + 1 - 2 * (clip % 2)},
        {"clip": clip + 2 - 4 * (clip // 2 % 2)},
        {"clip": clip + 4 - 8 * (clip // 4)},
    ]
    greet((right, left) + (tuple(swaps) if small is not None else (over_x, other)))
    f, l = first // 2, last // 2
    toward = (right, left)

    def owner(way, step):
        moved = N_OWN - 1 - step if way == 0 else 1 + step
        return clip_at((place + moved) % N_OWN)

    def f_rows(side, way):
        return pl.ds(pl.multiple_of(side * first + way * f, 8), f)

    def l_rows(way):
        return pl.ds(2 * first + way * l, l)

    def remote(src, dst, send_sem, recv_sem, device):
        return pltpu.make_async_remote_copy(
            src_ref=src,
            dst_ref=dst,
            send_sem=send_sem,
            recv_sem=recv_sem,
            device_id=device,
            device_id_type=pl.DeviceIdType.MESH,
        )

    def x_copy(way, step):
        return remote(
            chunks.at[owner(way, step), f_rows(1 - x, way)],
            extra.at[way, step],
            x_send.at[way, step],
            x_recv.at[way, step],
            over_x,
        )

    def load(kind, way, step):
        to = bufs[kind].at[way, 0] if step == 0 else locals_[kind].at[way, step % 2]
        rows = l_rows(way) if kind == 0 else f_rows(x, way)
        return pltpu.make_async_copy(
            chunks.at[owner(way, step), rows], to, load_sem.at[kind, way, step % 2]
        )

    def ring_copy(kind, way, step):
        return remote(
            bufs[kind].at[way, step],
            bufs[kind].at[way, step + 1],
            ring_send.at[kind, way, step],
            ring_recv.at[kind, way, step],
            toward[way],
        )

    def final_copy(kind, way):
        return remote(
            bufs[kind].at[way, N_OWN - 1],
            finals[kind].at[way],
            end_send.at[kind, way],
            end_recv.at[kind, way],
            over_x,
        )

    def small_copy(stage):
        return remote(
            sums.at[stage], arrived.at[stage], small_send.at[stage], small_recv.at[stage], swaps[stage]
        )

    flip_x = (1 - x) * CORES + core

    def part_copy(number, block=None):
        block = (frame, frame, flip_x)[number] if block is None else block
        return remote(
            frames.at[block],
            frames.at[block],
            part_send.at[number],
            part_recv.at[number],
            (over_x, other, other)[number],
        )

    def over_rows(start, count, work):
        def body(number, carry):
            work(pl.multiple_of(start + number * 8, 8))
            return carry

        lax.fori_loop(0, count // 8, body, 0)

    def small_load():
        return pltpu.make_async_copy(small, sums.at[0], own_sem.at[7])

    def part_load():
        return pltpu.make_async_copy(part, frames.at[frame], own_sem.at[7])

    for kind in range(2):
        for way in range(2):
            load(kind, way, 0).start()
    for way in range(2):
        x_copy(way, 0).start()
    if small is not None:
        small_load().start()
    if part is not None:
        part_load().start()

    def ring_step(kind, way, step):
        load(kind, way, step).wait()
        if step + 1 < N_OWN:
            load(kind, way, step + 1).start()
        if kind == 1:
            x_copy(way, step).wait_recv()
        if step > 0:
            ring_copy(kind, way, step - 1).wait_recv()
        buf, local = bufs[kind], locals_[kind]

        def add(row):
            at = pl.ds(row, 8)
            total = buf[way, step, at]
            if kind == 1:
                total = total + extra[way, step, at]
            if step > 0:
                total = total + local[way, step % 2, at]
            buf[way, step, at] = total

        if kind == 1 or step > 0:
            over_rows(0, f if kind == 1 else l, add)
        if step + 1 < N_OWN:
            ring_copy(kind, way, step).start()
        else:
            final_copy(kind, way).start()

    def own_half(kind):
        return pl.ds(2 * first, last) if kind == 0 else pl.ds(0, 2 * first)

    def core_swap(kind, to):
        return remote(
            result.at[own_half(kind)],
            out.at[to, own_half(kind)],
            own_sem.at[kind],
            own_sem.at[2 + kind],
            other,
        )

    def own_store(kind):
        return pltpu.make_async_copy(
            result.at[own_half(kind)], out.at[core, own_half(kind)], own_sem.at[4 + kind]
        )

    def finish(kind):
        for way in range(2):
            final_copy(kind, way).wait_recv()
            buf, final = bufs[kind], finals[kind]

            def put(row):
                at = pl.ds(row, 8)
                if kind == 0:
                    to = pl.multiple_of(2 * first + way * l + row, 8)
                    result[pl.ds(to, 8)] = buf[way, N_OWN - 1, at] + final[way, at]
                else:
                    to = pl.multiple_of(x * first + way * f + row, 8)
                    back = pl.multiple_of((1 - x) * first + way * f + row, 8)
                    result[pl.ds(to, 8)] = buf[way, N_OWN - 1, at]
                    result[pl.ds(back, 8)] = final[way, at]

            over_rows(0, l if kind == 0 else f, put)
        core_swap(kind, core).start()
        own_store(kind).start()

    for tick in range(N_OWN + LAG):
        if small is not None and tick < len(swaps) + 1:
            if tick == 0:
                small_load().wait()
            else:
                small_copy(tick - 1).wait_recv()

                def add_small(row):
                    at = pl.ds(row, 8)
                    sums[tick, at] = sums[tick - 1, at] + arrived[tick - 1, at]

                over_rows(0, small.shape[0], add_small)
            if tick < len(swaps):
                small_copy(tick).start()
        if 0 < tick < N_OWN:
            for way in range(2):
                x_copy(way, tick).start()
        if part is not None and tick == N_OWN - 1:
            part_load().wait()
            part_copy(0).start()
            part_copy(1).start()
        for way in range(2):
            if tick < N_OWN:
                ring_step(0, way, tick)
            if tick >= LAG:
                ring_step(1, way, tick - LAG)
    if small is not None:
        small_store = pltpu.make_async_copy(sums.at[len(swaps)], small_out, own_sem.at[6])
        small_store.start()
    finish(0)
    if part is not None:
        part_copy(0, flip_x).wait_recv()
        part_copy(2).start()
    finish(1)
    if part is not None:
        part_copy(1, x * CORES + 1 - core).wait_recv()
        part_copy(2, (1 - x) * CORES + 1 - core).wait_recv()
        part_store = pltpu.make_async_copy(frames, part_out, own_sem.at[6])
        part_store.start()
        part_store.wait()
        for number in range(3):
            part_copy(number).wait_send()
    if small is not None:
        small_store.wait()
        for stage in range(len(swaps)):
            small_copy(stage).wait_send()
    for way in range(2):
        for step in range(N_OWN):
            x_copy(way, step).wait_send()
    for kind in range(2):
        for way in range(2):
            for step in range(N_OWN - 1):
                ring_copy(kind, way, step).wait_send()
            final_copy(kind, way).wait_send()
        core_swap(kind, 1 - core).wait_recv()
        core_swap(kind, core).wait_send()
        own_store(kind).wait()


def collect_shard(chunks, first, collective, small=None, part=None):
    rows = chunks.shape[1]
    last = rows - 2 * first
    spec = pl.BlockSpec(memory_space=pl.ANY)
    out_shape = [jax.ShapeDtypeStruct((2, rows, D), jnp.float32)]
    beside = small if part is None else part
    if part is None:
        out_shape.append(jax.ShapeDtypeStruct(small.shape, jnp.float32))
        more = [
            pltpu.VMEM((6,) + small.shape, jnp.float32),
            pltpu.VMEM((5,) + small.shape, jnp.float32),
            pltpu.SemaphoreType.DMA((5,)),
            pltpu.SemaphoreType.DMA((5,)),
        ]
    else:
        out_shape.append(jax.ShapeDtypeStruct((4,) + part.shape, jnp.float32))
        more = [
            pltpu.VMEM((4,) + part.shape, jnp.float32),
            pltpu.SemaphoreType.DMA((3,)),
            pltpu.SemaphoreType.DMA((3,)),
        ]

    def kernel(chunks, beside, out, beside_out, *scratch):
        if part is None:
            collect_kernel(first, last, chunks, beside, None, out, beside_out, None, scratch)
        else:
            collect_kernel(first, last, chunks, None, beside, out, None, beside_out, scratch)

    return pl.pallas_call(
        kernel,
        in_specs=[spec] * 2,
        out_specs=[spec] * 2,
        out_shape=out_shape,
        scratch_shapes=[
            pltpu.VMEM((2, N_OWN, last // 2, D), jnp.float32),
            pltpu.VMEM((2, N_OWN, first // 2, D), jnp.float32),
            pltpu.VMEM((2, N_OWN, first // 2, D), jnp.float32),
            pltpu.VMEM((2, 2, last // 2, D), jnp.float32),
            pltpu.VMEM((2, 2, first // 2, D), jnp.float32),
            pltpu.VMEM((2, last // 2, D), jnp.float32),
            pltpu.VMEM((2, first // 2, D), jnp.float32),
            pltpu.VMEM((rows, D), jnp.float32),
            pltpu.SemaphoreType.DMA((2, 2, N_OWN)),
            pltpu.SemaphoreType.DMA((2, 2, N_OWN)),
            pltpu.SemaphoreType.DMA((2, N_OWN)),
            pltpu.SemaphoreType.DMA((2, N_OWN)),
            pltpu.SemaphoreType.DMA((2, 2)),
            pltpu.SemaphoreType.DMA((2, 2)),
            pltpu.SemaphoreType.DMA((2, 2, 2)),
            pltpu.SemaphoreType.DMA((8,)),
        ]
        + more,
        compiler_params=pltpu.CompilerParams(
            collective_id=collective, has_side_effects=True, vmem_limit_bytes=58 * 1024 * 1024
        ),
        cost_estimate=pl.CostEstimate(
            flops=0, bytes_accessed=800 * 1000 * 1000, transcendentals=0
        ),
    )(chunks, beside)


def matrix_plan(matrices, segments):
    shapes = [(rows, wide * D) for name, rows, wide in matrices]
    names = [name for name, rows, wide in matrices]
    stores = []
    for owner in range(N_OWN):
        offset = 0
        for name, first, count, wide in segments[owner]:
            for j in range(wide):
                stores.append((names.index(name), first, j * D, owner, offset, count))
                offset += count
    return shapes, stores


def half_rows(segments, name):
    rows = [[], []]
    for mine in segments:
        for label, first, count, wide in mine:
            if label == name:
                for core in range(2):
                    begin = first + core * (count // 2)
                    rows[core].extend(range(begin, begin + count // 2))
    return np.array(rows, np.int32)


def pick_columns(values, rows, core):
    wanted = jnp.asarray(rows)[core]
    chooser = (jnp.arange(values.shape[1], dtype=jnp.int32)[:, None] == wanted[None]).astype(jnp.bfloat16)
    return matmul_low(values, chooser).astype(jnp.bfloat16)


def both_cores(value):
    return jnp.concatenate([value, shift(value, SWAP_CORE)], 0)


def owner_chunk(grads, segments, owner):
    parts = []
    for label, first, count, wide in segments[owner]:
        begin = sum(seg[2] // 2 for mine in segments[:owner] for seg in mine if seg[0] == label)
        for j in range(wide):
            parts.append(grads[label][j][begin : begin + count // 2])
    return jnp.concatenate(parts, 0) if len(parts) > 1 else parts[0]


def step_values(master, grad, first, second, average):
    keep = min(AVERAGE_KEEP, (1.0 + STEP) / (10.0 + STEP))
    first = BETA_FIRST * first + (1.0 - BETA_FIRST) * grad
    second = BETA_SECOND * second + (1.0 - BETA_SECOND) * grad * grad
    moved = (
        first
        / (1.0 - BETA_FIRST**STEP)
        / (jnp.sqrt(second / (1.0 - BETA_SECOND**STEP)) + ADAM_FLOOR)
    )
    master = master - LEARN_RATE * (moved + WEIGHT_DECAY * master)
    return (master, first, second, keep * average + (1.0 - keep) * master)


STEP_ROWS = 144


def step_kernel(widths, table, factor, grad, *refs):
    olds, news, (shard, flat, sem) = refs[:4], refs[4:8], refs[8:]
    block = pl.program_id(0)

    @pl.when(block == 0)
    def _():
        copy = pltpu.make_async_copy(grad, shard, sem)
        copy.start()
        copy.wait()

    for wide in widths:
        count = STEP_BLOCK // wide

        @pl.when(table[block, 0] == wide)
        def _():
            for slab in range(wide):
                row = pl.multiple_of(table[block, 1] + slab * table[block, 2], 8)
                for tile in range(LANE_TILES):
                    flat[pl.ds(LANE_TILES * slab + tile, count, stride=LANE_TILES * wide), :] = shard[
                        pl.ds(row, count), tile * LANES : (tile + 1) * LANES
                    ]

    scale = factor[0]

    def some_rows(number, carry):
        at = pl.ds(pl.multiple_of(number * STEP_ROWS, 8), STEP_ROWS)
        old = [ref[at, :] for ref in olds]
        made = step_values(old[0], flat[at, :] * scale, old[1], old[2], old[3])
        for ref, value in zip(news, made):
            ref[at, :] = value
        return carry

    lax.fori_loop(0, STEP_BLOCK * LANE_TILES // STEP_ROWS, some_rows, 0)


def step_shard(grad, table, widths, n_rows, factor, olds):
    units = STEP_BLOCK * LANE_TILES
    block_spec = pl.BlockSpec((units, LANES), lambda b, t, f: (b, 0))
    flat_shape = jax.ShapeDtypeStruct((n_rows * LANE_TILES, LANES), jnp.float32)
    made = pl.pallas_call(
        partial(step_kernel, widths),
        grid_spec=pltpu.PrefetchScalarGridSpec(
            num_scalar_prefetch=2,
            grid=(n_rows // STEP_BLOCK,),
            in_specs=[pl.BlockSpec(memory_space=pl.ANY)] + [block_spec] * 4,
            out_specs=[block_spec] * 4,
            scratch_shapes=[
                pltpu.VMEM((n_rows, D), jnp.float32),
                pltpu.VMEM((units, LANES), jnp.float32),
                pltpu.SemaphoreType.DMA,
            ],
        ),
        out_shape=[flat_shape] * 4,
        compiler_params=pltpu.CompilerParams(vmem_limit_bytes=50 * 1024 * 1024),
    )(table, factor, grad, *[old.reshape(-1, LANES) for old in olds])
    return [value.reshape(-1) for value in made]


ROW_TIME_ONE = PATCH_VALUES
ROW_TIME_TWO = ROW_TIME_ONE + TFREQ
ROW_BLOCK = ROW_TIME_TWO + D
ROW_CAP_ONE = ROW_BLOCK + 6 * D
ROW_CAP_TWO = ROW_CAP_ONE + CAPW
ROW_FINAL = ROW_CAP_TWO + D
ROW_NULL = ROW_FINAL + PATCH_VALUES
EMB_UNITS = 16158720 // LANES // N_OWN
EMB_FIRST = [EMB_UNITS * c // LANE_TILES for c in range(N_OWN)]
EMB_SHIFT = [EMB_UNITS * c % LANE_TILES for c in range(N_OWN)]


def two_parts(product, value):
    both = product(jnp.concatenate(halves(value), 0))
    return both[: value.shape[0]] + both[value.shape[0] :]


def grad_two_parts(left, value):
    return weight_grad(jnp.concatenate([left, left], 0), jnp.concatenate(halves(value), 0))


def shards_block(
    latents,
    noise,
    timesteps,
    captions,
    cap_lengths,
    null_flags,
    sample_weight,
    embed_w,
    attend_w,
    dense_w,
    vector_w,
    embed_m,
    attend_m,
    dense_m,
    vector_m,
    embed_v,
    attend_v,
    dense_v,
    vector_v,
    embed_e,
    attend_e,
    dense_e,
    vector_e,
):
    clip_dev, frame_dev, patches = (latents.shape[0], latents.shape[1], latents.shape[2])
    n_frame = lax.axis_size("frame")
    n_clip = lax.axis_size("clip")
    local_pos = patches // n_frame
    tokens = frame_dev * patches
    frame_id = lax.axis_index("frame")
    clip_id = lax.axis_index("clip")
    x_id, core_id = frame_id // CORES, frame_id % CORES
    z_id, y_id = clip_id // Y_SIZE, clip_id % Y_SIZE

    emb_first = jnp.asarray(EMB_FIRST, jnp.int32)[clip_id]
    emb_shift = jnp.asarray(EMB_SHIFT, jnp.int32)[clip_id]
    emb_rows = flat_to_rows(embed_w.reshape(-1, LANES), EMB_PAD, emb_shift, jnp.bfloat16)
    dense_cast = cast_shard(
        dense_w, jnp.asarray(cast_table(DENSE_SEGS, CAST_BLOCK))[clip_id], (1, 4), DENSE_ROWS
    )
    cap_owners = range(4, N_OWN)
    cap_plan = (
        [(EMB_PAD * len(cap_owners), D)],
        [(0, EMB_PAD * k, 0, owner, 0, EMB_PAD) for k, owner in enumerate(cap_owners)],
    )
    own_clip = jnp.arange(n_clip) == clip_id
    facts = jnp.stack([timesteps.astype(jnp.float32)[0], sample_weight[0], null_flags.astype(jnp.float32)[0]])
    facts = jnp.broadcast_to(jnp.pad(facts, (0, LANES - 3))[None], (8, LANES))
    cap_weights, fc_in, fc_out, facts = spread_shards(
        [emb_rows, dense_cast],
        [(cap_owners,) + cap_plan + (False,), (range(N_OWN),) + matrix_plan(DENSE, DENSE_SEGS) + (True,)],
        2,
        given=[(facts, "gather")],
    )
    facts = facts[:, 0, :3]
    last = N_OWN - 1
    cap_last = cap_weights[EMB_PAD * (len(cap_owners) - 1) :]
    null_end = 16158720 - ROW_NULL * D
    null_first, final_first = ROW_NULL - EMB_FIRST[last], ROW_FINAL - EMB_FIRST[last]
    null_caption = (
        cap_last[null_first : null_first - (-null_end // D)]
        .reshape(-1)[:null_end]
        .reshape(L_CAP, CAPW)
    )
    final_w = cap_last[final_first : final_first + PATCH_VALUES].reshape(D, PATCH_VALUES)
    two_first = ROW_CAP_TWO - EMB_FIRST[last]

    def to_cap_rows(value):
        padded = jnp.pad(value, ((0, 0), (EMB_PAD, EMB_PAD)))
        starts = [EMB_FIRST[owner] - ROW_CAP_ONE + EMB_PAD for owner in cap_owners]
        return jnp.concatenate([padded[:, start : start + EMB_PAD] for start in starts], 1)

    def from_cap_rows(value):
        total = 0.0
        for k, owner in enumerate(cap_owners):
            start = EMB_FIRST[owner] - ROW_CAP_ONE
            low, high = max(0, -start), min(EMB_PAD, CAPW - start)
            part = value[:, EMB_PAD * k + low : EMB_PAD * k + high]
            total = total + jnp.pad(part, ((0, 0), (start + low, CAPW - start - high)))
        return total

    (
        patch_b,
        time_b1,
        time_b2,
        block_b,
        cap_b1,
        cap_b2,
        space_bq,
        space_bv,
        space_bo,
        time_bq,
        time_bv,
        time_bo,
        cross_bq,
        cross_bv,
        cross_bo,
        fc_in_b,
        fc_out_b,
        final_b,
        table,
        final_table,
    ) = split_flat(vector_w, vector_shapes())

    all_steps, all_null = facts[:, 0], facts[:, 2] == 1.0
    angle = (all_steps / 1000.0 + 0.008) / 1.008 * (math.pi / 2)
    signal = jnp.cos(angle) ** 2
    ratio = signal / (1.0 - signal)
    all_weights = facts[:, 1] * jnp.minimum(ratio, SNR_LIMIT) / ratio
    weight_total = jnp.sum(all_weights)
    signal = lax.dynamic_slice_in_dim(signal, clip_id, 1, 0)
    loss_weight = lax.dynamic_slice_in_dim(all_weights, clip_id, 1, 0)

    freq_in = sincos(all_steps, TFREQ).astype(jnp.bfloat16)
    at_start = clip_id == 0
    time_one = emb_rows[ROW_TIME_ONE:ROW_TIME_TWO]
    time_two = emb_rows[ROW_TIME_TWO:ROW_BLOCK]
    pre_one = matmul_low(freq_in, time_one) + time_b1
    act_one = jax.nn.silu(pre_one).astype(jnp.bfloat16)
    time_embed = matmul_low(act_one, time_two) + time_b2
    early = jnp.concatenate(
        [pre_one, time_embed, emb_rows[:ROW_TIME_ONE].astype(jnp.float32)], 0
    )
    is_null = null_flags == 1
    cap_in = jnp.where(is_null[:, None, None], null_caption[None], captions)
    cap_pre = (matmul_low(to_cap_rows(cap_in[0]), cap_weights) + cap_b1)[None]
    cap_act = gelu_tanh(cap_pre).astype(jnp.bfloat16)
    act_rows = jnp.pad(cap_act[0], ((0, 0), (two_first, EMB_PAD - two_first - D)))
    cap_rows = (matmul_low(act_rows, cap_last) + cap_b2).astype(jnp.bfloat16)[None]
    live_len = jnp.where(is_null, L_CAP, cap_lengths)
    key_mask = jnp.arange(L_CAP)[None, :] < live_len[:, None]
    cap_wide = jnp.concatenate([cap_in[0], cap_act[0]], -1)
    cap_wide = jnp.pad(cap_wide, ((0, 0), (EMB_PAD, EMB_PAD)))
    wanted = []
    for owner in range(n_clip):
        start = EMB_FIRST[owner] - ROW_CAP_ONE + EMB_PAD
        if start + EMB_PAD <= EMB_PAD:
            wanted.append(jnp.zeros((L_CAP, EMB_PAD // 4), jnp.bfloat16))
        else:
            wanted.append(
                lax.dynamic_slice_in_dim(cap_wide, start + frame_id * (EMB_PAD // 4), EMB_PAD // 4, 1)
            )
    attend_cast = cast_shard(
        attend_w, jnp.asarray(cast_table(ATTEND_SEGS, CAST_BLOCK))[clip_id], (1, 2, 3), ATTEND_ROWS
    )
    space_qkv, space_out, time_qkv, time_out, cross_q, cross_kv, cross_out, early, cap_left = spread_shards(
        [attend_cast],
        [(range(N_OWN),) + matrix_plan(ATTEND, ATTEND_SEGS) + (True,)],
        1,
        given=[(early, "first"), (jnp.pad(jnp.stack(wanted), ((0, 0), (0, 128 - L_CAP), (0, 0))), "swap")],
    )
    early = early[0]
    cap_left = cap_left[:, :L_CAP].reshape(n_clip * L_CAP, EMB_PAD // 4)
    pre_one, time_embed = early[:n_clip], early[n_clip : 2 * n_clip]
    patch_w = early[2 * n_clip :].astype(jnp.bfloat16)
    act_one = jax.nn.silu(pre_one).astype(jnp.bfloat16)
    silu_time = jax.nn.silu(time_embed).astype(jnp.bfloat16)
    local_row = emb_first + jnp.arange(EMB_PAD, dtype=jnp.int32)
    block_row = local_row - ROW_BLOCK
    in_block = (block_row >= 0) & (block_row < 6 * D)
    block_part = jnp.where(in_block, block_row % 6, -1)
    block_line = jnp.where(in_block, block_row // 6, -1)
    chooser = jnp.arange(D, dtype=jnp.int32)[:, None] == block_line[None]
    silu_rows = matmul_low(silu_time, chooser.astype(jnp.bfloat16)).astype(jnp.bfloat16)
    part_mask = jnp.arange(6, dtype=jnp.int32)[:, None] == block_part[None]
    block_left = jnp.where(part_mask[None], silu_rows[:, None], 0).reshape(n_clip * 6, EMB_PAD)
    block_out = sum_clips(matmul_low(block_left, emb_rows)).reshape(n_clip, 6, D)
    all_mods = table[None] + (block_out + block_b.reshape(6, D))
    mods = lax.dynamic_slice_in_dim(all_mods, clip_id, 1, 0)
    my_embed = lax.dynamic_slice_in_dim(time_embed, clip_id, 1, 0)

    keep_part = jnp.sqrt(signal)[:, None, None, None]
    fade_part = jnp.sqrt(1.0 - signal)[:, None, None, None]
    noisy = (keep_part * latents + fade_part * noise).astype(jnp.bfloat16)
    frame_ids = frame_id * frame_dev + jnp.arange(frame_dev)
    patch_ids = jnp.arange(patches)
    place = jnp.concatenate(
        [sincos(patch_ids // PGRID, D // 2), sincos(patch_ids % PGRID, D // 2)], -1
    )[None, None]
    hidden_zero = matmul_low(noisy, patch_w) + patch_b + place + sincos(frame_ids, D)[None, :, None]

    def mod_row(number):
        return mods[:, number][:, None, None, :]

    def flat2(value):
        return value.reshape(-1, value.shape[-1])

    space_in = modulate(hidden_zero, mod_row(0), mod_row(1)).astype(jnp.bfloat16)
    space_q, space_k, space_v = (
        heads_of(piece, clip_dev * frame_dev)
        for piece in split_qkv(matmul_low(space_in, space_qkv), space_bq, space_bv)
    )
    space_o, space_lse = attend_forward(space_q, space_k, space_v, None)
    space_flat = space_o.reshape(clip_dev, frame_dev, patches, D)
    space_res = matmul_low(space_flat, space_out) + space_bo
    hidden_one = hidden_zero + mod_row(2) * space_res
    time_in = lax.all_to_all(
        hidden_one.astype(jnp.bfloat16), "frame", split_axis=2, concat_axis=1, tiled=True
    )
    time_in = jnp.swapaxes(time_in, 1, 2)
    frames = time_in.shape[2]
    time_q, time_k, time_v = (
        heads_of(piece, clip_dev * local_pos)
        for piece in split_qkv(matmul_low(time_in, time_qkv), time_bq, time_bv)
    )
    time_o, time_lse = attend_forward(time_q, time_k, time_v, None)
    time_back = jnp.swapaxes(time_o.reshape(clip_dev, local_pos, frames, D), 1, 2)
    time_flat = lax.all_to_all(time_back, "frame", split_axis=1, concat_axis=2, tiled=True)
    time_res = matmul_low(time_flat, time_out) + time_bo
    hidden_two = hidden_one + mod_row(2) * time_res
    cross_in = hidden_two.astype(jnp.bfloat16)
    cross_query = heads_of(
        (matmul_low(cross_in, cross_q) + cross_bq).astype(jnp.bfloat16), clip_dev
    )
    cross_merged = matmul_low(cap_rows, cross_kv)
    cross_k = heads_of(cross_merged[..., :D].astype(jnp.bfloat16), clip_dev)
    cross_v = heads_of((cross_merged[..., D:] + cross_bv).astype(jnp.bfloat16), clip_dev)
    cross_o, cross_lse = attend_forward(cross_query, cross_k, cross_v, key_mask)
    cross_flat = cross_o.reshape(clip_dev, frame_dev, patches, D)
    hidden_three = hidden_two + matmul_low(cross_flat, cross_out) + cross_bo
    dense_in = modulate(hidden_three, mod_row(3), mod_row(4)).astype(jnp.bfloat16)
    dense_pre = matmul_low(dense_in, fc_in) + fc_in_b
    dense_act = gelu_tanh(dense_pre).astype(jnp.bfloat16)
    dense_res = matmul_low(dense_act, fc_out) + fc_out_b
    hidden_four = hidden_three + mod_row(5) * dense_res
    final_mod = final_table[None] + my_embed[:, None, :]
    final_shift = final_mod[:, 0][:, None, None, :]
    final_scale = final_mod[:, 1][:, None, None, :]
    final_in = modulate(hidden_four, final_shift, final_scale).astype(jnp.bfloat16)
    predicted = matmul_low(final_in, final_w) + final_b
    miss = predicted - noise
    clip_error = jnp.sum(jnp.mean(miss * miss, -1), (1, 2))
    local_loss = jnp.sum(loss_weight * clip_error)

    inputs = {}
    for label, value in (
        ("space_qkv", space_in),
        ("space_out", space_flat),
        ("time_qkv", time_in),
        ("time_out", time_flat),
        ("cross_q", cross_in),
        ("cross_out", cross_flat),
        ("fc_in", dense_in),
    ):
        segments = DENSE_SEGS if label == "fc_in" else ATTEND_SEGS
        inputs[label] = pick_columns(both_cores(flat2(value)), half_rows(segments, label), core_id)
    act_both = both_cores(flat2(dense_act))
    half = half_rows([[("square", 0, D, 1)]], "square")
    for block in range(MLP // D):
        inputs["fc_out", block] = pick_columns(act_both[:, block * D : (block + 1) * D], half, core_id)

    def core_grad(left, outs):
        return [weight_grad(left, both_cores(flat2(out))) for out in outs]

    def columns(value):
        return [value[..., j * D : (j + 1) * D] for j in range(value.shape[-1] // D)]

    grad_pred = (
        2.0 / miss.shape[-1] * (loss_weight / weight_total)[:, None, None, None] * miss
    ).astype(jnp.bfloat16)
    g_final_w = weight_grad(final_in, grad_pred)
    g_final_b = bias_grad(grad_pred)
    unused, pullback = jax.vjp(modulate, hidden_four, final_shift, final_scale)
    grad_hidden, grad_fshift, grad_fscale = pullback(back_low(grad_pred, final_w))
    grad_fmod = jnp.concatenate([grad_fshift.reshape(1, D), grad_fscale.reshape(1, D)], 0)
    grad_dense = (grad_hidden * mod_row(5)).astype(jnp.bfloat16)
    grad_gate_b = jnp.sum(grad_hidden * dense_res, (1, 2))
    grads = {}
    dense_both = both_cores(flat2(grad_dense))
    g_fc_out = [weight_grad(inputs["fc_out", block], dense_both) for block in range(MLP // D)]
    grads["fc_out"] = [jnp.concatenate(g_fc_out, 0)]
    g_fc_out_b = bias_grad(grad_dense)
    unused, pullback = jax.vjp(gelu_tanh, dense_pre)
    grad_pre = pullback(back_low(grad_dense, fc_out))[0].astype(jnp.bfloat16)
    grads["fc_in"] = core_grad(inputs["fc_in"], columns(grad_pre))
    g_fc_in_b = bias_grad(grad_pre)
    unused, pullback = jax.vjp(modulate, hidden_three, mod_row(3), mod_row(4))
    grad_input, grad_shift_b, grad_scale_b = pullback(back_low(grad_pre, fc_in))
    grad_hidden = grad_hidden + grad_input
    grad_cross = grad_hidden.astype(jnp.bfloat16)
    grads["cross_out"] = core_grad(inputs["cross_out"], [grad_cross])
    g_cross_bo = bias_grad(grad_cross)
    grad_cross_o = heads_of(back_low(grad_cross, cross_out).astype(jnp.bfloat16), clip_dev)
    grad_cq, grad_ck, grad_cv = attend_backward(
        cross_query, cross_k, cross_v, key_mask, cross_lse, grad_cross_o
    )
    grad_cq = grad_cq.astype(jnp.bfloat16).reshape(clip_dev, frame_dev, patches, D)
    grads["cross_q"] = core_grad(inputs["cross_q"], [grad_cq])
    g_cross_bq = bias_grad(grad_cq)
    grad_hidden = grad_hidden + back_low(grad_cq, cross_q)
    grad_cv = grad_cv.reshape(clip_dev, L_CAP, D)
    grad_ckv = jnp.concatenate([grad_ck.reshape(clip_dev, L_CAP, D), grad_cv], -1)[0]
    g_cross_bv = bias_grad(grad_cv)
    grad_ckv = grad_ckv + shift(grad_ckv, SWAP_CORE)
    cap_half = pick_columns(cap_rows[0], half_rows(ATTEND_SEGS, "cross_kv"), core_id)
    grads["cross_kv"] = [grad_two_parts(cap_half, part) for part in columns(grad_ckv)]
    grad_ckv = grad_ckv + shift(grad_ckv, SWAP_X)
    grad_cap_rows = two_parts(lambda part: back_low(part, cross_kv), grad_ckv)

    grad_time = (grad_hidden * mod_row(2)).astype(jnp.bfloat16)
    grads["time_out"] = core_grad(inputs["time_out"], [grad_time])
    g_time_bo = bias_grad(grad_time)
    grad_time_o = lax.all_to_all(
        back_low(grad_time, time_out).astype(jnp.bfloat16),
        "frame",
        split_axis=2,
        concat_axis=1,
        tiled=True,
    )
    grad_time_o = heads_of(jnp.swapaxes(grad_time_o, 1, 2), clip_dev * local_pos)
    grad_tq, grad_tk, grad_tv = attend_backward(time_q, time_k, time_v, None, time_lse, grad_time_o)
    grad_tqkv = [
        piece.astype(jnp.bfloat16).reshape(clip_dev, local_pos, frames, D)
        for piece in (grad_tq, grad_tk, grad_tv)
    ]
    grads["time_qkv"] = core_grad(inputs["time_qkv"], grad_tqkv)
    g_time_bq = bias_grad(grad_tqkv[0])
    g_time_bv = bias_grad(grad_tqkv[2])
    grad_tqkv = lax.all_to_all(
        jnp.swapaxes(jnp.concatenate(grad_tqkv, -1), 1, 2), "frame", split_axis=1, concat_axis=2, tiled=True
    )
    grad_gate_a = jnp.sum(grad_hidden * time_res, (1, 2))
    grad_hidden = grad_hidden + back_low(grad_tqkv, time_qkv)
    grad_gate_a = grad_gate_a + jnp.sum(grad_hidden * space_res, (1, 2))
    grad_space = (grad_hidden * mod_row(2)).astype(jnp.bfloat16)
    grads["space_out"] = core_grad(inputs["space_out"], [grad_space])
    g_space_bo = bias_grad(grad_space)
    grad_space_o = heads_of(
        back_low(grad_space, space_out).astype(jnp.bfloat16), clip_dev * frame_dev
    )
    grad_sqkv = [
        piece.astype(jnp.bfloat16).reshape(clip_dev, frame_dev, patches, D)
        for piece in attend_backward(space_q, space_k, space_v, None, space_lse, grad_space_o)
    ]
    grads["space_qkv"] = core_grad(inputs["space_qkv"], grad_sqkv)
    g_space_bq = bias_grad(grad_sqkv[0])
    g_space_bv = bias_grad(grad_sqkv[2])
    grad_sqkv = jnp.concatenate(grad_sqkv, -1)
    unused, pullback = jax.vjp(modulate, hidden_zero, mod_row(0), mod_row(1))
    grad_input, grad_shift_a, grad_scale_a = pullback(back_low(grad_sqkv, space_qkv))
    grad_hidden = grad_hidden + grad_input
    g_patch_w = weight_split(noisy, grad_hidden)
    g_patch_b = bias_grad(grad_hidden)
    grad_mods = jnp.concatenate(
        [
            grad_shift_a.reshape(clip_dev, D),
            grad_scale_a.reshape(clip_dev, D),
            grad_gate_a,
            grad_shift_b.reshape(clip_dev, D),
            grad_scale_b.reshape(clip_dev, D),
            grad_gate_b,
            grad_fmod,
        ],
        0,
    )

    unused, pullback = jax.vjp(gelu_tanh, cap_pre[0])
    grad_cap_act = two_parts(lambda part: back_low(part, cap_last), grad_cap_rows)
    grad_cap_pre = pullback(grad_cap_act[:, two_first : two_first + D])[0]
    cap_right = lax.all_gather(
        jnp.stack([grad_cap_pre, grad_cap_rows]), "clip", axis=1, tiled=True
    )
    null_sum = jnp.sum(jnp.where(all_null[:, None, None], cap_right[0].reshape(n_clip, L_CAP, D), 0.0), 0)
    g_cap_b1 = bias_grad(grad_cap_pre)
    g_cap_b2 = bias_grad(grad_cap_rows)

    once = frame_id == 0
    gathered_mods = jnp.where(own_clip[:, None, None], grad_mods[None], 0.0)
    zero_d = jnp.zeros((D,), jnp.float32)
    vector_grad = flatten_all(
        [
            g_patch_b,
            jnp.where(once, g_cap_b1, 0.0),
            jnp.where(once, g_cap_b2, 0.0),
            g_space_bq,
            g_space_bv,
            g_space_bo,
            g_time_bq,
            g_time_bv,
            g_time_bo,
            g_cross_bq,
            g_cross_bv,
            g_cross_bo,
            g_fc_in_b,
            g_fc_out_b,
            g_final_b,
        ]
    )
    n_vector = vector_grad.shape[0]
    small = flatten_all([gathered_mods, g_patch_w, g_final_w, vector_grad, local_loss])
    small_rows = -(-small.shape[0] // (8 * D)) * 8
    small = jnp.pad(small, (0, small_rows * D - small.shape[0])).reshape(small_rows, D)
    dense_grad, small = collect_shard(
        jnp.stack([owner_chunk(grads, DENSE_SEGS, owner) for owner in range(N_OWN)]),
        144,
        3,
        small=small,
    )
    dense_grad = dense_grad.reshape(DENSE_ROWS, D)
    at = 8 * n_clip
    gathered_mods = small[:at].reshape(n_clip, 8, D)
    g_patch_w = small[at : at + PATCH_VALUES]
    g_final_w = small[at + PATCH_VALUES : at + 2 * PATCH_VALUES]
    rest = small[at + 2 * PATCH_VALUES :].reshape(-1)
    vector_grad, loss_sum = rest[:n_vector], rest[n_vector]

    grad_zero = gathered_mods[:, :6]
    grad_final = gathered_mods[:, 6:]
    zero_rows = grad_zero.reshape(n_clip * 6, D)
    back_rows = two_parts(lambda part: back_low(part, emb_rows), zero_rows)
    back_rows = jnp.sum(jnp.where(part_mask[None], back_rows.reshape(n_clip, 6, EMB_PAD), 0.0), 1)
    grad_silu = lax.dot_general(
        back_rows,
        chooser.astype(jnp.float32),
        (((1,), (1,)), ((), ())),
        precision=lax.Precision.HIGHEST,
        preferred_element_type=jnp.float32,
    )
    grad_silu = sum_clips(grad_silu)
    unused, pullback = jax.vjp(jax.nn.silu, time_embed)
    grad_embed = grad_final[:, 0] + grad_final[:, 1] + pullback(grad_silu)[0]
    grad_act = two_parts(lambda part: back_low(part, time_two), grad_embed)
    grad_act = sum_clips(jnp.where(at_start, grad_act, 0.0))
    unused, pullback = jax.vjp(jax.nn.silu, pre_one)
    grad_one = pullback(grad_act)[0]
    g_table = jnp.sum(grad_zero, 0)
    vector_sum = flatten_all(
        [
            vector_grad[:D],
            jnp.sum(grad_one, 0),
            jnp.sum(grad_embed, 0),
            g_table,
            vector_grad[D:],
            g_table,
            jnp.sum(grad_final, 0),
        ]
    )

    per = EMB_PAD // 4
    quarter_row = emb_first + frame_id * per + jnp.arange(per, dtype=jnp.int32)
    time_left = jnp.concatenate(
        [
            jnp.pad(freq_in, ((0, 0), (ROW_TIME_ONE, EMB_PAD - ROW_TIME_TWO))),
            jnp.pad(act_one, ((0, 0), (ROW_TIME_TWO, EMB_PAD - ROW_BLOCK))),
        ],
        0,
    )
    time_left = jnp.where(at_start, time_left, jnp.zeros_like(time_left))
    small_left = lax.dynamic_slice_in_dim(
        jnp.concatenate([time_left, block_left], 0), frame_id * per, per, 1
    )
    small_right = jnp.concatenate([grad_one, grad_embed, zero_rows], 0)
    first_kind = (quarter_row < ROW_CAP_TWO)[None]
    no_left = jnp.zeros_like(cap_left)
    g_null = from_cap_rows(two_parts(lambda part: back_low(part, cap_weights), null_sum))
    n_null = -(-null_end // D)
    n_known = -(-(2 * PATCH_VALUES + n_null) // 16) * 16
    null_rows = jnp.pad(g_null.reshape(-1), (0, (n_known - 2 * PATCH_VALUES) * D - null_end))
    known = jnp.concatenate([g_patch_w, g_final_w, null_rows.reshape(-1, D)], 0)
    known_row = np.concatenate(
        [np.arange(PATCH_VALUES), ROW_FINAL + np.arange(n_known - PATCH_VALUES)]
    ).astype(np.int32)
    known_left = (jnp.asarray(known_row)[:, None] == quarter_row[None]).astype(jnp.bfloat16)
    emb_left = jnp.concatenate(
        [
            small_left,
            jnp.where(first_kind, cap_left, no_left),
            jnp.where(first_kind, no_left, cap_left),
            known_left,
        ],
        0,
    )
    emb_right = jnp.concatenate([small_right, cap_right[0], cap_right[1], known], 0)
    emb_grad = weight_split(emb_left, emb_right)
    unit = (
        LANE_TILES * (frame_id * per + jnp.arange(per, dtype=jnp.int32))[:, None]
        + jnp.arange(D, dtype=jnp.int32)[None] // LANES
        - emb_shift
    )
    emb_grad = jnp.where((unit >= 0) & (unit < EMB_UNITS), emb_grad, 0.0)

    attend_grad, emb_whole = collect_shard(
        jnp.stack([owner_chunk(grads, ATTEND_SEGS, owner) for owner in range(N_OWN)]),
        176,
        4,
        part=emb_grad,
    )
    attend_grad = attend_grad.reshape(ATTEND_ROWS, D)
    local_square = sum(jnp.sum(value * value) for value in (dense_grad, attend_grad, emb_whole))
    vector_square = jnp.sum(vector_sum * vector_sum)
    grad_norm = jnp.sqrt(sum_clips(local_square.reshape(1))[0] + vector_square)
    factor = jnp.minimum(1.0, CLIP_LIMIT / (grad_norm + NORM_FLOOR))
    scale = factor.reshape(1)
    dense_r = step_shard(
        dense_grad,
        jnp.asarray(step_table(DENSE_SEGS, STEP_BLOCK, DENSE_ROWS))[clip_id],
        (1, 4),
        DENSE_ROWS,
        scale,
        (dense_w, dense_m, dense_v, dense_e),
    )
    attend_r = step_shard(
        attend_grad,
        jnp.asarray(step_table(ATTEND_SEGS, STEP_BLOCK, ATTEND_ROWS))[clip_id],
        (1, 2, 3),
        ATTEND_ROWS,
        scale,
        (attend_w, attend_m, attend_v, attend_e),
    )
    emb_flat = rows_to_flat(emb_whole.reshape(EMB_PAD, D))
    emb_owned = lax.dynamic_slice_in_dim(emb_flat, emb_shift, EMB_UNITS, 0).reshape(-1)
    embed_r = adam_step(embed_w, emb_owned, embed_m, embed_v, embed_e, factor)
    vector_r = adam_step(vector_w, vector_sum, vector_m, vector_v, vector_e, factor)
    return (
        loss_sum,
        weight_total,
        grad_norm,
        embed_r[0],
        attend_r[0],
        dense_r[0],
        vector_r[0],
        embed_r[1],
        attend_r[1],
        dense_r[1],
        vector_r[1],
        embed_r[2],
        attend_r[2],
        dense_r[2],
        vector_r[2],
        embed_r[3],
        attend_r[3],
        dense_r[3],
        vector_r[3],
    )


def pick_plan(mesh):
    if mesh.shape["frame"] == X_SIZE * CORES and mesh.shape["clip"] == N_OWN:
        return shards_block
    return shards


def solution(mesh):
    in_specs = (
        P("clip", "frame", None, None),
        P("clip", "frame", None, None),
        P("clip"),
        P("clip", None, None),
        P("clip"),
        P("clip"),
        P("clip"),
        P("clip"),
        P("clip"),
        P("clip"),
        P(),
        P("clip"),
        P("clip"),
        P("clip"),
        P(),
        P("clip"),
        P("clip"),
        P("clip"),
        P(),
        P("clip"),
        P("clip"),
        P("clip"),
        P(),
    )
    out_specs = (
        P(),
        P(),
        P(),
        P("clip"),
        P("clip"),
        P("clip"),
        P(),
        P("clip"),
        P("clip"),
        P("clip"),
        P(),
        P("clip"),
        P("clip"),
        P("clip"),
        P(),
        P("clip"),
        P("clip"),
        P("clip"),
        P(),
    )
    return jax.shard_map(pick_plan(mesh), mesh=mesh, in_specs=in_specs, out_specs=out_specs, check_vma=False)
```

```python
import math
from functools import partial

import jax
import jax.numpy as jnp
import numpy as np
from jax import lax
from jax.experimental import pallas as pl
from jax.experimental.pallas import tpu as pltpu
from jax.sharding import PartitionSpec as P

D = 1152
HEADS = 16
MLP = 4608
CAPW = 4096
L_CAP = 120
TFREQ = 256
PATCH_VALUES = 16
PGRID = 16
STEP = 10


NORM_FLOOR = 1e-06
CLIP_LIMIT = 1.0
SNR_LIMIT = 5.0
BETA_FIRST = 0.5
BETA_SECOND = 0.5
LEARN_RATE = 0.02
WEIGHT_DECAY = 0.01
ADAM_FLOOR = 1e-08
AVERAGE_KEEP = 0.9999
MASKED_SCORE = -1e30


def embed_shapes():
    return [
        (PATCH_VALUES, D),
        (TFREQ, D),
        (D, D),
        (D, 6 * D),
        (CAPW, D),
        (D, D),
        (D, PATCH_VALUES),
        (L_CAP, CAPW),
    ]


def attend_shapes():
    return [(D, 3 * D), (D, D), (D, 3 * D), (D, D), (D, D), (D, 2 * D), (D, D)]


def dense_shapes():
    return [(D, MLP), (MLP, D)]


def vector_shapes():
    return [(D,)] * 3 + [(6 * D,)] + [(D,)] * 11 + [(MLP,), (D,), (PATCH_VALUES,), (6, D), (2, D)]


def split_flat(flat, shapes):
    pieces = []
    offset = 0
    for extent in shapes:
        length = math.prod(extent)
        pieces.append(flat[offset : offset + length].reshape(extent))
        offset += length
    return pieces


def flatten_all(pieces):
    return jnp.concatenate([piece.reshape(-1) for piece in pieces])


def reduce_group(grad):
    n_clip = lax.axis_size("clip")
    n_frame = lax.axis_size("frame")
    reorder = grad.reshape(n_clip, n_frame, -1).swapaxes(0, 1).reshape(-1)
    share = lax.psum_scatter(reorder, ("frame", "clip"), scatter_dimension=0, tiled=True)
    return lax.all_gather(share, "frame", axis=0, tiled=True)


def sincos(places, width):
    half = width // 2
    omega = jnp.exp(-math.log(10000.0) * jnp.arange(half, dtype=jnp.float32) / half)
    angle = places.astype(jnp.float32)[..., None] * omega
    return jnp.concatenate([jnp.sin(angle), jnp.cos(angle)], -1)


def modulate(hidden, shift, scale):
    center = hidden - jnp.mean(hidden, -1, keepdims=True)
    normed = center * lax.rsqrt(jnp.mean(center * center, -1, keepdims=True) + NORM_FLOOR)
    return normed * (1.0 + scale) + shift


def gelu_tanh(value):
    return jax.nn.gelu(value, approximate=True)


def matmul_low(left, right):
    return lax.dot_general(
        left, right, (((left.ndim - 1,), (0,)), ((), ())), preferred_element_type=jnp.float32
    )


def halves(value):
    upper = lax.optimization_barrier(value.astype(jnp.bfloat16))
    return (upper, (value - upper.astype(jnp.float32)).astype(jnp.bfloat16))


def back_low(grads, weight):
    return lax.dot_general(
        grads, weight, (((grads.ndim - 1,), (1,)), ((), ())), preferred_element_type=jnp.float32
    )


def back_split(grads, weight):
    upper, lower = halves(grads)
    return back_low(upper, weight) + back_low(lower, weight)


def weight_grad(inputs, grads):
    left = inputs.reshape(-1, inputs.shape[-1])
    right = grads.reshape(-1, grads.shape[-1])
    return lax.dot_general(
        left, right, (((0,), (0,)), ((), ())), preferred_element_type=jnp.float32
    )


def weight_split(inputs, grads):
    upper, lower = halves(grads)
    return weight_grad(inputs, upper) + weight_grad(inputs, lower)


def bias_grad(grads):
    return jnp.sum(grads.astype(jnp.float32).reshape(-1, grads.shape[-1]), 0)


def heads_of(tensor, batch):
    return tensor.reshape(batch, -1, HEADS, tensor.shape[-1] // HEADS)


def split_qkv(merged, bias_q, bias_v):
    width = merged.shape[-1] // 3
    return (
        (merged[..., :width] + bias_q).astype(jnp.bfloat16),
        merged[..., width : 2 * width].astype(jnp.bfloat16),
        (merged[..., 2 * width :] + bias_v).astype(jnp.bfloat16),
    )


def attend_scores(queries, key_rows, mask):
    scores = jnp.einsum("bqhe,bkhe->bhqk", queries, key_rows, preferred_element_type=jnp.float32)
    scores = scores * queries.shape[-1] ** (-0.5)
    if mask is not None:
        scores = jnp.where(mask[:, None, None, :], scores, MASKED_SCORE)
    return scores


def attend_forward(queries, key_rows, values, mask):
    scores = attend_scores(queries, key_rows, mask)
    summit = jnp.max(scores, -1, keepdims=True)
    powers = jnp.exp(scores - summit)
    totals = jnp.sum(powers, -1, keepdims=True)
    probs = (powers / totals).astype(jnp.bfloat16)
    output = jnp.einsum("bhqk,bkhe->bqhe", probs, values, preferred_element_type=jnp.float32)
    return (output.astype(jnp.bfloat16), summit + jnp.log(totals))


def attend_backward(queries, key_rows, values, mask, log_total, grad_out):
    scale = queries.shape[-1] ** (-0.5)
    probs = jnp.exp(attend_scores(queries, key_rows, mask) - log_total)
    grad_probs = jnp.einsum("bqhe,bkhe->bhqk", grad_out, values, preferred_element_type=jnp.float32)
    grad_scores = (probs * (grad_probs - jnp.sum(probs * grad_probs, -1, keepdims=True))).astype(
        jnp.bfloat16
    )
    grad_query = (
        jnp.einsum("bhqk,bkhe->bqhe", grad_scores, key_rows, preferred_element_type=jnp.float32)
        * scale
    )
    grad_keys = (
        jnp.einsum("bhqk,bqhe->bkhe", grad_scores, queries, preferred_element_type=jnp.float32)
        * scale
    )
    grad_values = jnp.einsum(
        "bhqk,bqhe->bkhe", probs.astype(jnp.bfloat16), grad_out, preferred_element_type=jnp.float32
    )
    return (grad_query, grad_keys, grad_values)


def unpack_all(gathered):
    return (
        split_flat(gathered[0], embed_shapes()),
        split_flat(gathered[1], attend_shapes()),
        split_flat(gathered[2], dense_shapes()),
    )


def adam_step(master, grad, first, second, average, factor):
    keep = min(AVERAGE_KEEP, (1.0 + STEP) / (10.0 + STEP))
    grad = grad * factor
    first = BETA_FIRST * first + (1.0 - BETA_FIRST) * grad
    second = BETA_SECOND * second + (1.0 - BETA_SECOND) * grad * grad
    moved = (
        first
        / (1.0 - BETA_FIRST**STEP)
        / (jnp.sqrt(second / (1.0 - BETA_SECOND**STEP)) + ADAM_FLOOR)
    )
    master = master - LEARN_RATE * (moved + WEIGHT_DECAY * master)
    return (master, first, second, keep * average + (1.0 - keep) * master)


def shards(
    latents,
    noise,
    timesteps,
    captions,
    cap_lengths,
    null_flags,
    sample_weight,
    embed_w,
    attend_w,
    dense_w,
    vector_w,
    embed_m,
    attend_m,
    dense_m,
    vector_m,
    embed_v,
    attend_v,
    dense_v,
    vector_v,
    embed_e,
    attend_e,
    dense_e,
    vector_e,
):
    clip_dev, frame_dev, patches = (latents.shape[0], latents.shape[1], latents.shape[2])
    n_frame = lax.axis_size("frame")
    n_clip = lax.axis_size("clip")
    local_pos = patches // n_frame
    gathered = (
        lax.all_gather(embed_w.astype(jnp.bfloat16), "clip", axis=0, tiled=True),
        lax.all_gather(attend_w.astype(jnp.bfloat16), "clip", axis=0, tiled=True),
        lax.all_gather(dense_w.astype(jnp.bfloat16), "clip", axis=0, tiled=True),
    )
    embeds, attends, denses = unpack_all(gathered)
    patch_w, time_one, time_two, block_w, cap_one, cap_two, final_w, null_caption = embeds
    space_qkv, space_out, time_qkv, time_out, cross_q, cross_kv, cross_out = attends
    fc_in, fc_out = denses
    (
        patch_b,
        time_b1,
        time_b2,
        block_b,
        cap_b1,
        cap_b2,
        space_bq,
        space_bv,
        space_bo,
        time_bq,
        time_bv,
        time_bo,
        cross_bq,
        cross_bv,
        cross_bo,
        fc_in_b,
        fc_out_b,
        final_b,
        table,
        final_table,
    ) = split_flat(vector_w, vector_shapes())
    angle = (timesteps.astype(jnp.float32) / 1000.0 + 0.008) / 1.008 * (math.pi / 2)
    signal = jnp.cos(angle) ** 2
    ratio = signal / (1.0 - signal)
    loss_weight = sample_weight * jnp.minimum(ratio, SNR_LIMIT) / ratio
    weight_total = lax.psum(jnp.sum(loss_weight), "clip")
    keep_part = jnp.sqrt(signal)[:, None, None, None]
    fade_part = jnp.sqrt(1.0 - signal)[:, None, None, None]
    noisy = (keep_part * latents + fade_part * noise).astype(jnp.bfloat16)
    frame_ids = lax.axis_index("frame") * frame_dev + jnp.arange(frame_dev)
    patch_ids = jnp.arange(patches)
    place = jnp.concatenate(
        [sincos(patch_ids // PGRID, D // 2), sincos(patch_ids % PGRID, D // 2)], -1
    )[None, None]
    hidden_zero = matmul_low(noisy, patch_w) + patch_b + place + sincos(frame_ids, D)[None, :, None]
    freq_in = sincos(timesteps, TFREQ).astype(jnp.bfloat16)
    pre_one = matmul_low(freq_in, time_one) + time_b1
    act_one = jax.nn.silu(pre_one).astype(jnp.bfloat16)
    time_embed = matmul_low(act_one, time_two) + time_b2
    silu_time = jax.nn.silu(time_embed).astype(jnp.bfloat16)
    mods = table[None] + (matmul_low(silu_time, block_w) + block_b).reshape(clip_dev, 6, D)

    def mod_row(number):
        return mods[:, number][:, None, None, :]

    is_null = null_flags == 1
    cap_in = jnp.where(is_null[:, None, None], null_caption[None], captions)
    cap_pre = matmul_low(cap_in, cap_one) + cap_b1
    cap_act = gelu_tanh(cap_pre).astype(jnp.bfloat16)
    cap_rows = (matmul_low(cap_act, cap_two) + cap_b2).astype(jnp.bfloat16)
    live_len = jnp.where(is_null, L_CAP, cap_lengths)
    key_mask = jnp.arange(L_CAP)[None, :] < live_len[:, None]
    space_in = modulate(hidden_zero, mod_row(0), mod_row(1)).astype(jnp.bfloat16)
    space_q, space_k, space_v = (
        heads_of(piece, clip_dev * frame_dev)
        for piece in split_qkv(matmul_low(space_in, space_qkv), space_bq, space_bv)
    )
    space_o, space_lse = attend_forward(space_q, space_k, space_v, None)
    space_flat = space_o.reshape(clip_dev, frame_dev, patches, D)
    space_res = matmul_low(space_flat, space_out) + space_bo
    hidden_one = hidden_zero + mod_row(2) * space_res
    time_in = lax.all_to_all(
        hidden_one.astype(jnp.bfloat16), "frame", split_axis=2, concat_axis=1, tiled=True
    )
    time_in = jnp.swapaxes(time_in, 1, 2)
    frames = time_in.shape[2]
    time_q, time_k, time_v = (
        heads_of(piece, clip_dev * local_pos)
        for piece in split_qkv(matmul_low(time_in, time_qkv), time_bq, time_bv)
    )
    time_o, time_lse = attend_forward(time_q, time_k, time_v, None)
    time_back = jnp.swapaxes(time_o.reshape(clip_dev, local_pos, frames, D), 1, 2)
    time_flat = lax.all_to_all(time_back, "frame", split_axis=1, concat_axis=2, tiled=True)
    time_res = matmul_low(time_flat, time_out) + time_bo
    hidden_two = hidden_one + mod_row(2) * time_res
    cross_in = hidden_two.astype(jnp.bfloat16)
    cross_query = heads_of(
        (matmul_low(cross_in, cross_q) + cross_bq).astype(jnp.bfloat16), clip_dev
    )
    cross_merged = matmul_low(cap_rows, cross_kv)
    cross_k = heads_of(cross_merged[..., :D].astype(jnp.bfloat16), clip_dev)
    cross_v = heads_of((cross_merged[..., D:] + cross_bv).astype(jnp.bfloat16), clip_dev)
    cross_o, cross_lse = attend_forward(cross_query, cross_k, cross_v, key_mask)
    cross_flat = cross_o.reshape(clip_dev, frame_dev, patches, D)
    hidden_three = hidden_two + matmul_low(cross_flat, cross_out) + cross_bo
    dense_in = modulate(hidden_three, mod_row(3), mod_row(4)).astype(jnp.bfloat16)
    dense_pre = matmul_low(dense_in, fc_in) + fc_in_b
    dense_act = gelu_tanh(dense_pre).astype(jnp.bfloat16)
    dense_res = matmul_low(dense_act, fc_out) + fc_out_b
    hidden_four = hidden_three + mod_row(5) * dense_res
    final_mod = final_table[None] + time_embed[:, None, :]
    final_shift = final_mod[:, 0][:, None, None, :]
    final_scale = final_mod[:, 1][:, None, None, :]
    final_in = modulate(hidden_four, final_shift, final_scale).astype(jnp.bfloat16)
    predicted = matmul_low(final_in, final_w) + final_b
    miss = predicted - noise
    clip_error = jnp.sum(jnp.mean(miss * miss, -1), (1, 2))
    local_loss = jnp.sum(loss_weight * clip_error)
    grad_pred = (
        2.0 / miss.shape[-1] * (loss_weight / weight_total)[:, None, None, None] * miss
    ).astype(jnp.bfloat16)
    g_final_w = weight_grad(final_in, grad_pred)
    g_final_b = bias_grad(grad_pred)
    unused, pullback = jax.vjp(modulate, hidden_four, final_shift, final_scale)
    grad_hidden, grad_fshift, grad_fscale = pullback(back_low(grad_pred, final_w))
    grad_fmod = jnp.stack([grad_fshift.reshape(clip_dev, D), grad_fscale.reshape(clip_dev, D)], 1)
    g_final_table = jnp.sum(grad_fmod, 0)
    grad_time_embed = grad_fmod[:, 0] + grad_fmod[:, 1]
    grad_dense = (grad_hidden * mod_row(5)).astype(jnp.bfloat16)
    grad_gate_b = jnp.sum(grad_hidden * dense_res, (1, 2))
    g_fc_out = weight_grad(dense_act, grad_dense)
    g_fc_out_b = bias_grad(grad_dense)
    unused, pullback = jax.vjp(gelu_tanh, dense_pre)
    grad_pre = pullback(back_low(grad_dense, fc_out))[0].astype(jnp.bfloat16)
    g_fc_in = weight_grad(dense_in, grad_pre)
    g_fc_in_b = bias_grad(grad_pre)
    dense_owned = reduce_group(flatten_all([g_fc_in, g_fc_out]))
    unused, pullback = jax.vjp(modulate, hidden_three, mod_row(3), mod_row(4))
    grad_input, grad_shift_b, grad_scale_b = pullback(back_low(grad_pre, fc_in))
    grad_hidden = grad_hidden + grad_input
    grad_cross = grad_hidden.astype(jnp.bfloat16)
    g_cross_out = weight_grad(cross_flat, grad_cross)
    g_cross_bo = bias_grad(grad_cross)
    grad_cross_o = heads_of(back_low(grad_cross, cross_out).astype(jnp.bfloat16), clip_dev)
    grad_cq, grad_ck, grad_cv = attend_backward(
        cross_query, cross_k, cross_v, key_mask, cross_lse, grad_cross_o
    )
    grad_cq = grad_cq.astype(jnp.bfloat16).reshape(clip_dev, frame_dev, patches, D)
    g_cross_q = weight_grad(cross_in, grad_cq)
    g_cross_bq = bias_grad(grad_cq)
    grad_hidden = grad_hidden + back_low(grad_cq, cross_q)
    grad_cv = grad_cv.reshape(clip_dev, L_CAP, D)
    grad_ckv = jnp.concatenate([grad_ck.reshape(clip_dev, L_CAP, D), grad_cv], -1)
    g_cross_kv = weight_split(cap_rows, grad_ckv)
    g_cross_bv = bias_grad(grad_cv)
    grad_cap_rows = back_split(grad_ckv, cross_kv)
    grad_time = (grad_hidden * mod_row(2)).astype(jnp.bfloat16)
    g_time_out = weight_grad(time_flat, grad_time)
    g_time_bo = bias_grad(grad_time)
    grad_time_o = lax.all_to_all(
        back_low(grad_time, time_out).astype(jnp.bfloat16),
        "frame",
        split_axis=2,
        concat_axis=1,
        tiled=True,
    )
    grad_time_o = heads_of(jnp.swapaxes(grad_time_o, 1, 2), clip_dev * local_pos)
    grad_tq, grad_tk, grad_tv = attend_backward(time_q, time_k, time_v, None, time_lse, grad_time_o)
    grad_tqkv = jnp.concatenate(
        [
            piece.astype(jnp.bfloat16).reshape(clip_dev, local_pos, frames, D)
            for piece in (grad_tq, grad_tk, grad_tv)
        ],
        -1,
    )
    g_time_qkv = weight_grad(time_in, grad_tqkv)
    g_time_bq = bias_grad(grad_tqkv[..., :D])
    g_time_bv = bias_grad(grad_tqkv[..., 2 * D :])
    grad_tqkv = lax.all_to_all(
        jnp.swapaxes(grad_tqkv, 1, 2), "frame", split_axis=1, concat_axis=2, tiled=True
    )
    grad_gate_a = jnp.sum(grad_hidden * time_res, (1, 2))
    grad_hidden = grad_hidden + back_low(grad_tqkv, time_qkv)
    grad_gate_a = grad_gate_a + jnp.sum(grad_hidden * space_res, (1, 2))
    grad_space = (grad_hidden * mod_row(2)).astype(jnp.bfloat16)
    g_space_out = weight_grad(space_flat, grad_space)
    g_space_bo = bias_grad(grad_space)
    grad_space_o = heads_of(
        back_low(grad_space, space_out).astype(jnp.bfloat16), clip_dev * frame_dev
    )
    grad_sq, grad_sk, grad_sv = attend_backward(
        space_q, space_k, space_v, None, space_lse, grad_space_o
    )
    grad_sqkv = jnp.concatenate(
        [
            piece.astype(jnp.bfloat16).reshape(clip_dev, frame_dev, patches, D)
            for piece in (grad_sq, grad_sk, grad_sv)
        ],
        -1,
    )
    g_space_qkv = weight_grad(space_in, grad_sqkv)
    g_space_bq = bias_grad(grad_sqkv[..., :D])
    g_space_bv = bias_grad(grad_sqkv[..., 2 * D :])
    attend_owned = reduce_group(
        flatten_all(
            [g_space_qkv, g_space_out, g_time_qkv, g_time_out, g_cross_q, g_cross_kv, g_cross_out]
        )
    )
    unused, pullback = jax.vjp(modulate, hidden_zero, mod_row(0), mod_row(1))
    grad_input, grad_shift_a, grad_scale_a = pullback(back_low(grad_sqkv, space_qkv))
    grad_hidden = grad_hidden + grad_input
    g_patch_w = weight_split(noisy, grad_hidden)
    g_patch_b = bias_grad(grad_hidden)
    grad_mods = jnp.stack(
        [
            grad_shift_a.reshape(clip_dev, D),
            grad_scale_a.reshape(clip_dev, D),
            grad_gate_a,
            grad_shift_b.reshape(clip_dev, D),
            grad_scale_b.reshape(clip_dev, D),
            grad_gate_b,
        ],
        1,
    )
    g_table = jnp.sum(grad_mods, 0)
    grad_zero = grad_mods.reshape(clip_dev, 6 * D)
    g_block_b = jnp.sum(grad_zero, 0)
    g_block_w = weight_split(silu_time, grad_zero)
    unused, pullback = jax.vjp(jax.nn.silu, time_embed)
    grad_time_embed = grad_time_embed + pullback(back_split(grad_zero, block_w))[0]
    g_time_b2 = jnp.sum(grad_time_embed, 0)
    g_time_two = weight_split(act_one, grad_time_embed)
    unused, pullback = jax.vjp(jax.nn.silu, pre_one)
    grad_pre_one = pullback(back_split(grad_time_embed, time_two))[0]
    g_time_b1 = jnp.sum(grad_pre_one, 0)
    g_time_one = weight_split(freq_in, grad_pre_one)
    g_cap_b2 = bias_grad(grad_cap_rows)
    g_cap_two = weight_split(cap_act, grad_cap_rows)
    unused, pullback = jax.vjp(gelu_tanh, cap_pre)
    grad_cap_pre = pullback(back_split(grad_cap_rows, cap_two))[0]
    g_cap_b1 = bias_grad(grad_cap_pre)
    g_cap_one = weight_split(cap_in, grad_cap_pre)
    grad_cap_in = back_split(grad_cap_pre, cap_one)
    g_null = jnp.sum(jnp.where(is_null[:, None, None], grad_cap_in, 0.0), 0)
    embed_owned = reduce_group(
        flatten_all(
            [g_patch_w, g_time_one, g_time_two, g_block_w, g_cap_one, g_cap_two, g_final_w, g_null]
        )
    )
    vector_grad = flatten_all(
        [
            g_patch_b,
            g_time_b1,
            g_time_b2,
            g_block_b,
            g_cap_b1,
            g_cap_b2,
            g_space_bq,
            g_space_bv,
            g_space_bo,
            g_time_bq,
            g_time_bv,
            g_time_bo,
            g_cross_bq,
            g_cross_bv,
            g_cross_bo,
            g_fc_in_b,
            g_fc_out_b,
            g_final_b,
            g_table,
            g_final_table,
        ]
    )
    vector_sum, loss_sum = lax.psum((vector_grad, local_loss), ("frame", "clip"))
    owned = (embed_owned, attend_owned, dense_owned)
    local_square = (
        sum((jnp.sum(shard_piece * shard_piece) for shard_piece in owned))
        + jnp.sum(vector_sum * vector_sum) / n_clip
    )
    grad_norm = jnp.sqrt(lax.psum(local_square, "clip"))
    factor = jnp.minimum(1.0, CLIP_LIMIT / (grad_norm + NORM_FLOOR))
    embed_r = adam_step(embed_w, owned[0], embed_m, embed_v, embed_e, factor)
    attend_r = adam_step(attend_w, owned[1], attend_m, attend_v, attend_e, factor)
    dense_r = adam_step(dense_w, owned[2], dense_m, dense_v, dense_e, factor)
    vector_r = adam_step(vector_w, vector_sum, vector_m, vector_v, vector_e, factor)
    return (
        loss_sum,
        weight_total,
        grad_norm,
        embed_r[0],
        attend_r[0],
        dense_r[0],
        vector_r[0],
        embed_r[1],
        attend_r[1],
        dense_r[1],
        vector_r[1],
        embed_r[2],
        attend_r[2],
        dense_r[2],
        vector_r[2],
        embed_r[3],
        attend_r[3],
        dense_r[3],
        vector_r[3],
    )


AXES = ("frame", "clip")
LANES = 128
LANE_TILES = D // LANES
EMB_PAD = 1856


X_SIZE, CORES, Z_SIZE, Y_SIZE = 2, 2, 4, 2
N_OWN = Z_SIZE * Y_SIZE
RING = [(0, 0), (1, 0), (2, 0), (3, 0), (3, 1), (2, 1), (1, 1), (0, 1)]
RING_CLIP = [z * Y_SIZE + y for z, y in RING]
CLIP_RING = [RING_CLIP.index(c) for c in range(N_OWN)]


def pairs(move):
    out = []
    for x in range(X_SIZE):
        for core in range(CORES):
            for z in range(Z_SIZE):
                for y in range(Y_SIZE):
                    to = move(x, core, z, y)
                    if to is not None:
                        rank = lambda a, b, c, d: (a * CORES + b) * N_OWN + c * Y_SIZE + d
                        out.append((rank(x, core, z, y), rank(*to)))
    return out


SWAP_X = pairs(lambda x, c, z, y: (1 - x, c, z, y))
SWAP_CORE = pairs(lambda x, c, z, y: (x, 1 - c, z, y))
SWAP_Y = pairs(lambda x, c, z, y: (x, c, z, 1 - y))
SWAP_Z1 = pairs(lambda x, c, z, y: (x, c, z ^ 1, y))
SWAP_Z2 = pairs(lambda x, c, z, y: (x, c, z ^ 2, y))


def shift(value, perm):
    return lax.ppermute(value, AXES, perm)


def sum_clips(value):
    for perm in (SWAP_Y, SWAP_Z1, SWAP_Z2):
        value = value + shift(value, perm)
    return value


def sum_frames(value):
    for perm in (SWAP_CORE, SWAP_X):
        value = value + shift(value, perm)
    return value


def shard_segments(matrices, n_rows):
    spans, offset = [], 0
    for name, rows, wide in matrices:
        spans.append((name, offset, rows, wide))
        offset += rows * wide
    out = []
    for owner in range(N_OWN):
        low, high = owner * n_rows, (owner + 1) * n_rows
        mine = []
        for name, start, rows, wide in spans:
            begin, end = max(low, start), min(high, start + rows * wide)
            if begin < end:
                mine.append((name, (begin - start) // wide, (end - begin) // wide, wide))
        out.append(mine)
    return out


ATTEND = [
    ("space_qkv", D, 3),
    ("space_out", D, 1),
    ("time_qkv", D, 3),
    ("time_out", D, 1),
    ("cross_q", D, 1),
    ("cross_kv", D, 2),
    ("cross_out", D, 1),
]
DENSE = [("fc_in", D, 4), ("fc_out", MLP, 1)]
ATTEND_ROWS = 13824 // N_OWN
DENSE_ROWS = 9216 // N_OWN
ATTEND_SEGS = shard_segments(ATTEND, ATTEND_ROWS)
DENSE_SEGS = shard_segments(DENSE, DENSE_ROWS)


def cast_table(segments, block):
    out = []
    for mine in segments:
        rows, offset = [], 0
        for name, first, count, wide in mine:
            for start in range(0, count * wide, block):
                rows.append((wide, offset + start // wide, count))
            offset += count * wide
        out.append(rows)
    return np.array(out, np.int32)


def step_table(segments, block, n_rows):
    out = []
    for mine in segments:
        rows, offset = [], 0
        for name, first, count, wide in mine:
            half = count // 2
            for start in range(0, count * wide, block):
                core, inner = divmod(start // wide, half)
                rows.append((wide, core * (n_rows // 2) + offset + inner, half))
            offset += half * wide
        out.append(rows)
    return np.array(out, np.int32)


CAST_BLOCK = 576
STEP_BLOCK = 288


def cast_kernel(widths, table, flat, out):
    block = pl.program_id(0)
    for wide in widths:
        count = CAST_BLOCK // wide

        @pl.when(table[block, 0] == wide)
        def _():
            for slab in range(wide):
                row = pl.multiple_of(table[block, 1] + slab * table[block, 2], 16)
                for tile in range(LANE_TILES):
                    piece = flat[pl.ds(LANE_TILES * slab + tile, count, stride=LANE_TILES * wide), :]
                    out[pl.ds(row, count), tile * LANES : (tile + 1) * LANES] = piece.astype(jnp.bfloat16)


def cast_shard(flat, table, widths, n_rows):
    units = CAST_BLOCK * LANE_TILES
    return pl.pallas_call(
        partial(cast_kernel, widths),
        grid_spec=pltpu.PrefetchScalarGridSpec(
            num_scalar_prefetch=1,
            grid=(n_rows // CAST_BLOCK,),
            in_specs=[pl.BlockSpec((units, LANES), lambda b, t: (b, 0))],
            out_specs=pl.BlockSpec((n_rows, D), lambda b, t: (0, 0)),
        ),
        out_shape=jax.ShapeDtypeStruct((n_rows, D), jnp.bfloat16),
        compiler_params=pltpu.CompilerParams(vmem_limit_bytes=40 * 1024 * 1024),
    )(table, flat.reshape(-1, LANES))


ROWS_AHEAD = 16


def rows_kernel(shift_ref, flat, out, held, sem):
    units, count = flat.shape[0], out.shape[0]
    block = pl.program_id(0)

    @pl.when(block == 0)
    def _():
        end = (ROWS_AHEAD + units) // 8 * 8
        held[pl.ds(0, ROWS_AHEAD), :] = jnp.zeros((ROWS_AHEAD, LANES), jnp.float32)
        held[pl.ds(end, held.shape[0] - end), :] = jnp.zeros((held.shape[0] - end, LANES), jnp.float32)
        copy = pltpu.make_async_copy(flat, held.at[pl.ds(ROWS_AHEAD, units)], sem)
        copy.start()
        copy.wait()

    begin = ROWS_AHEAD + block * (count * LANE_TILES) - shift_ref[0]
    for tile in range(LANE_TILES):
        piece = held[pl.ds(begin + tile, count, stride=LANE_TILES), :]
        out[:, tile * LANES : (tile + 1) * LANES] = piece.astype(out.dtype)


def flat_to_rows(flat, rows, shift, dtype):
    block = rows // 4
    return pl.pallas_call(
        rows_kernel,
        grid_spec=pltpu.PrefetchScalarGridSpec(
            num_scalar_prefetch=1,
            grid=(4,),
            in_specs=[pl.BlockSpec(memory_space=pl.ANY)],
            out_specs=pl.BlockSpec((block, D), lambda b, t: (b, 0)),
            scratch_shapes=[
                pltpu.VMEM((ROWS_AHEAD + rows * LANE_TILES + 8, LANES), jnp.float32),
                pltpu.SemaphoreType.DMA,
            ],
        ),
        out_shape=jax.ShapeDtypeStruct((rows, D), dtype),
        compiler_params=pltpu.CompilerParams(vmem_limit_bytes=32 * 1024 * 1024),
    )(shift.reshape(1), flat)


def flat_kernel(rows, out):
    count = rows.shape[0]
    for tile in range(LANE_TILES):
        out[pl.ds(tile, count, stride=LANE_TILES), :] = rows[:, tile * LANES : (tile + 1) * LANES]


def rows_to_flat(rows):
    block = rows.shape[0] // 4
    return pl.pallas_call(
        flat_kernel,
        grid=(4,),
        in_specs=[pl.BlockSpec((block, D), lambda b: (b, 0))],
        out_specs=pl.BlockSpec((block * LANE_TILES, LANES), lambda b: (b, 0)),
        out_shape=jax.ShapeDtypeStruct((rows.shape[0] * LANE_TILES, LANES), rows.dtype),
        compiler_params=pltpu.CompilerParams(vmem_limit_bytes=32 * 1024 * 1024),
    )(rows)


def ring_place(clip):
    return jnp.where(clip % 2 == 0, clip // 2, N_OWN - 1 - clip // 2)


def clip_at(place):
    return jnp.where(place < N_OWN // 2, 2 * place, 2 * N_OWN - 1 - 2 * place)


def partners(frame, clip):
    place = ring_place(clip)
    x, core = frame // CORES, frame % CORES
    return (
        {"clip": clip_at((place + 1) % N_OWN)},
        {"clip": clip_at((place + N_OWN - 1) % N_OWN)},
        {"frame": (1 - x) * CORES + core},
        {"frame": x * CORES + 1 - core},
    )


def greet(devices):
    barrier = pltpu.get_barrier_semaphore()
    for device in devices:
        pl.semaphore_signal(barrier, inc=1, device_id=device, device_id_type=pl.DeviceIdType.MESH)
    pl.semaphore_wait(barrier, len(devices))


def spread_kernel(groups, modes, *refs):
    n, m = len(groups), len(modes)
    counts = [len(shapes) for keep, shapes, stores, common in groups]
    refs = list(refs)
    take = lambda number: [refs.pop(0) for _ in range(number)]
    owns, given, outs, given_outs = take(n), take(m), take(sum(counts)), take(m)
    helds, sources, landings = take(n), take(m), take(m)
    load_sem, send_sem, recv_sem, out_sem, peer_sem, peer_send, peer_recv = refs
    frame, clip = lax.axis_index("frame"), lax.axis_index("clip")
    x, core = frame // CORES, frame % CORES
    place = ring_place(clip)
    right, left, over_x, other = partners(frame, clip)
    half = N_OWN // 2
    owners = [clip_at((place + N_OWN - k) % N_OWN) for k in range(half + 1)]
    owners += [clip_at((place + k) % N_OWN) for k in range(1, half)]
    flip_x = (1 - x) * CORES + core
    mine = [core, frame, flip_x]
    theirs = [1 - core, x * CORES + 1 - core, (1 - x) * CORES + 1 - core]
    landing = mine + theirs

    def block_of(group, kinds, kind):
        return kinds[kind] + (2 if groups[group][3] and kind % 3 else 0)

    def held_at(group, slot):
        return helds[group].at[owners[slot] - min(groups[group][0])]

    def where_kept(group, slot, action):
        keep = groups[group][0]
        if len(keep) == N_OWN:
            action()
        else:
            pl.when(owners[slot] >= min(keep))(action)

    def load(group):
        return pltpu.make_async_copy(owns[group], held_at(group, 0), load_sem.at[group])

    def copy_of(group, slot, block, device, to_slot, kind):
        return pltpu.make_async_remote_copy(
            src_ref=held_at(group, slot).at[block],
            dst_ref=held_at(group, slot).at[block],
            send_sem=send_sem.at[group, to_slot, kind],
            recv_sem=recv_sem.at[group, to_slot, kind],
            device_id=device,
            device_id_type=pl.DeviceIdType.MESH,
        )

    sent = []

    def send(group, slot, from_kind, device, to_slot, kind):
        if from_kind == 0 and not groups[group][3]:
            return
        args = (group, slot, block_of(group, mine, from_kind), device, to_slot, kind)
        where_kept(group, slot, lambda: copy_of(*args).start())
        sent.append(args)

    def arrive(group, slot, kind):
        if kind % 3 == 0 and not groups[group][3]:
            return
        block = block_of(group, landing, kind)
        where_kept(group, slot, lambda: copy_of(group, slot, block, other, slot, kind).wait_recv())

    def onward(group, slot, kind):
        if slot < half:
            send(group, slot, kind, right, slot + 1, kind)
        if slot == 0:
            send(group, slot, kind, left, half + 1, kind)
        elif half < slot < N_OWN - 1:
            send(group, slot, kind, left, slot + 1, kind)

    def peer_load(item):
        return pltpu.make_async_copy(given[item], sources[item], peer_sem.at[item, 0])

    def peer_own(item):
        source = sources[item].at[clip] if modes[item] == "swap" else sources[item]
        return pltpu.make_async_copy(source, landings[item].at[clip], peer_sem.at[item, 1])

    def peer_copy(item, k):
        to = (clip + k) % N_OWN
        return pltpu.make_async_remote_copy(
            src_ref=sources[item].at[to] if modes[item] == "swap" else sources[item],
            dst_ref=landings[item].at[clip],
            send_sem=peer_send.at[item, k - 1],
            recv_sem=peer_recv.at[item, k - 1],
            device_id={"clip": to},
            device_id_type=pl.DeviceIdType.MESH,
        )

    def peers(item, arriving, action):
        for k in range(1, N_OWN):
            if modes[item] != "first":
                action(k)
            else:
                pl.when(clip == (k if arriving else 0))(lambda: action(k))

    for group in range(n):
        where_kept(group, 0, lambda: load(group).start())
    for item in range(m):
        peer_load(item).start()
    everyone = tuple({"clip": (clip + k) % N_OWN} for k in range(1, N_OWN)) if m else ()
    greet((right, left, over_x, other) + everyone)
    for group in range(n):
        where_kept(group, 0, lambda: load(group).wait())
        onward(group, 0, 1)
        onward(group, 0, 0)
    for item in range(m):
        peer_load(item).wait()
        peer_own(item).start()
        peers(item, False, lambda k: peer_copy(item, k).start())
    waiting = []
    for step in range(1, half + 1):
        slots = [step] + ([half + step] if step < half else [])
        pairs_now = [(group, slot) for group in range(n) for slot in slots]
        for group, slot in pairs_now:
            arrive(group, slot, 1)
            onward(group, slot, 1)
            send(group, slot, 1, over_x, slot, 2)
            send(group, slot, 1, other, slot, 4)
            arrive(group, slot, 0)
            onward(group, slot, 0)
            send(group, slot, 0, other, slot, 3)
        for group, slot in waiting:
            arrive(group, slot, 2)
            send(group, slot, 2, other, slot, 5)
        waiting = pairs_now
    for group, slot in waiting:
        arrive(group, slot, 2)
        send(group, slot, 2, other, slot, 5)
    for group in range(n):
        for slot in range(1, N_OWN):
            for kind in (3, 4, 5):
                arrive(group, slot, kind)
    done, base = [], 0
    for group, (keep, shapes, stores, common) in enumerate(groups):
        held = helds[group]
        rows = held.shape[2]
        for out, row, column, owner, first, count in stores:
            while count > 0:
                part, inner = divmod(first, rows)
                some = min(count, rows - inner)
                copy = pltpu.make_async_copy(
                    held.at[owner - min(keep), part, pl.ds(inner, some)],
                    outs[base + out].at[pl.ds(row, some), pl.ds(column, D)],
                    out_sem.at[len(done)],
                )
                copy.start()
                done.append(copy)
                first, row, count = first + some, row + some, count - some
        base += counts[group]
    for item in range(m):
        peer_own(item).wait()
        peers(item, True, lambda k: peer_copy(item, k).wait_recv())
        copy = pltpu.make_async_copy(landings[item], given_outs[item], peer_sem.at[item, 2])
        copy.start()
        done.append(copy)
    for item in range(m):
        peers(item, False, lambda k: peer_copy(item, k).wait_send())
    for args in sent:
        where_kept(args[0], args[1], lambda: copy_of(*args).wait_send())
    for copy in done:
        copy.wait()


def spread_shards(owns, groups, collective, given=()):
    spec = pl.BlockSpec(memory_space=pl.ANY)
    shapes = [shape for keep, some, stores, common in groups for shape in some]
    n_stores = sum(6 * len(stores) for keep, some, stores, common in groups)
    blocks = [6 if group[3] else 4 for group in groups]
    modes = [mode for value, mode in given]
    values = [value for value, mode in given]
    landed = [
        value.shape if mode == "swap" else (N_OWN,) + value.shape for value, mode in given
    ]
    many = max(len(given), 1)
    return pl.pallas_call(
        partial(spread_kernel, groups, modes),
        in_specs=[spec] * (len(owns) + len(given)),
        out_specs=[spec] * (len(shapes) + len(given)),
        out_shape=[jax.ShapeDtypeStruct(shape, jnp.bfloat16) for shape in shapes]
        + [jax.ShapeDtypeStruct(shape, value.dtype) for shape, value in zip(landed, values)],
        scratch_shapes=[
            pltpu.VMEM((len(group[0]), count, own.shape[0] // count, D), jnp.bfloat16)
            for own, group, count in zip(owns, groups, blocks)
        ]
        + [pltpu.VMEM(value.shape, value.dtype) for value in values]
        + [pltpu.VMEM(shape, value.dtype) for shape, value in zip(landed, values)]
        + [
            pltpu.SemaphoreType.DMA((len(owns),)),
            pltpu.SemaphoreType.DMA((len(owns), N_OWN, 6)),
            pltpu.SemaphoreType.DMA((len(owns), N_OWN, 6)),
            pltpu.SemaphoreType.DMA((n_stores,)),
            pltpu.SemaphoreType.DMA((many, 3)),
            pltpu.SemaphoreType.DMA((many, N_OWN - 1)),
            pltpu.SemaphoreType.DMA((many, N_OWN - 1)),
        ],
        compiler_params=pltpu.CompilerParams(
            collective_id=collective, has_side_effects=True, vmem_limit_bytes=50 * 1024 * 1024
        ),
        cost_estimate=pl.CostEstimate(
            flops=0, bytes_accessed=200 * 1000 * 1000, transcendentals=0
        ),
    )(*[own.reshape(count, own.shape[0] // count, D) for own, count in zip(owns, blocks)], *values)


LAG = 5


def collect_kernel(first, last, chunks, small, part, out, small_out, part_out, scratch):
    bufs, extra, locals_, finals, result = scratch[:2], scratch[2], scratch[3:5], scratch[5:7], scratch[7]
    ring_send, ring_recv, x_send, x_recv, end_send, end_recv, load_sem, own_sem = scratch[8:16]
    if small is not None:
        sums, arrived, small_send, small_recv = scratch[16:]
    if part is not None:
        frames, part_send, part_recv = scratch[16:]
    frame, clip = lax.axis_index("frame"), lax.axis_index("clip")
    x, core = frame // CORES, frame % CORES
    place = ring_place(clip)
    right, left, over_x, other = partners(frame, clip)
    swaps = [
        other,
        over_x,
        {"clip": clip + 1 - 2 * (clip % 2)},
        {"clip": clip + 2 - 4 * (clip // 2 % 2)},
        {"clip": clip + 4 - 8 * (clip // 4)},
    ]
    greet((right, left) + (tuple(swaps) if small is not None else (over_x, other)))
    f, l = first // 2, last // 2
    toward = (right, left)

    def owner(way, step):
        moved = N_OWN - 1 - step if way == 0 else 1 + step
        return clip_at((place + moved) % N_OWN)

    def f_rows(side, way):
        return pl.ds(pl.multiple_of(side * first + way * f, 8), f)

    def l_rows(way):
        return pl.ds(2 * first + way * l, l)

    def remote(src, dst, send_sem, recv_sem, device):
        return pltpu.make_async_remote_copy(
            src_ref=src,
            dst_ref=dst,
            send_sem=send_sem,
            recv_sem=recv_sem,
            device_id=device,
            device_id_type=pl.DeviceIdType.MESH,
        )

    def x_copy(way, step):
        return remote(
            chunks.at[owner(way, step), f_rows(1 - x, way)],
            extra.at[way, step],
            x_send.at[way, step],
            x_recv.at[way, step],
            over_x,
        )

    def load(kind, way, step):
        to = bufs[kind].at[way, 0] if step == 0 else locals_[kind].at[way, step % 2]
        rows = l_rows(way) if kind == 0 else f_rows(x, way)
        return pltpu.make_async_copy(
            chunks.at[owner(way, step), rows], to, load_sem.at[kind, way, step % 2]
        )

    def ring_copy(kind, way, step):
        return remote(
            bufs[kind].at[way, step],
            bufs[kind].at[way, step + 1],
            ring_send.at[kind, way, step],
            ring_recv.at[kind, way, step],
            toward[way],
        )

    def final_copy(kind, way):
        return remote(
            bufs[kind].at[way, N_OWN - 1],
            finals[kind].at[way],
            end_send.at[kind, way],
            end_recv.at[kind, way],
            over_x,
        )

    def small_copy(stage):
        return remote(
            sums.at[stage], arrived.at[stage], small_send.at[stage], small_recv.at[stage], swaps[stage]
        )

    flip_x = (1 - x) * CORES + core

    def part_copy(number, block=None):
        block = (frame, frame, flip_x)[number] if block is None else block
        return remote(
            frames.at[block],
            frames.at[block],
            part_send.at[number],
            part_recv.at[number],
            (over_x, other, other)[number],
        )

    def over_rows(start, count, work):
        def body(number, carry):
            work(pl.multiple_of(start + number * 8, 8))
            return carry

        lax.fori_loop(0, count // 8, body, 0)

    def small_load():
        return pltpu.make_async_copy(small, sums.at[0], own_sem.at[7])

    def part_load():
        return pltpu.make_async_copy(part, frames.at[frame], own_sem.at[7])

    for kind in range(2):
        for way in range(2):
            load(kind, way, 0).start()
    for way in range(2):
        x_copy(way, 0).start()
    if small is not None:
        small_load().start()
    if part is not None:
        part_load().start()

    def ring_step(kind, way, step):
        load(kind, way, step).wait()
        if step + 1 < N_OWN:
            load(kind, way, step + 1).start()
        if kind == 1:
            x_copy(way, step).wait_recv()
        if step > 0:
            ring_copy(kind, way, step - 1).wait_recv()
        buf, local = bufs[kind], locals_[kind]

        def add(row):
            at = pl.ds(row, 8)
            total = buf[way, step, at]
            if kind == 1:
                total = total + extra[way, step, at]
            if step > 0:
                total = total + local[way, step % 2, at]
            buf[way, step, at] = total

        if kind == 1 or step > 0:
            over_rows(0, f if kind == 1 else l, add)
        if step + 1 < N_OWN:
            ring_copy(kind, way, step).start()
        else:
            final_copy(kind, way).start()

    def own_half(kind):
        return pl.ds(2 * first, last) if kind == 0 else pl.ds(0, 2 * first)

    def core_swap(kind, to):
        return remote(
            result.at[own_half(kind)],
            out.at[to, own_half(kind)],
            own_sem.at[kind],
            own_sem.at[2 + kind],
            other,
        )

    def own_store(kind):
        return pltpu.make_async_copy(
            result.at[own_half(kind)], out.at[core, own_half(kind)], own_sem.at[4 + kind]
        )

    def finish(kind):
        for way in range(2):
            final_copy(kind, way).wait_recv()
            buf, final = bufs[kind], finals[kind]

            def put(row):
                at = pl.ds(row, 8)
                if kind == 0:
                    to = pl.multiple_of(2 * first + way * l + row, 8)
                    result[pl.ds(to, 8)] = buf[way, N_OWN - 1, at] + final[way, at]
                else:
                    to = pl.multiple_of(x * first + way * f + row, 8)
                    back = pl.multiple_of((1 - x) * first + way * f + row, 8)
                    result[pl.ds(to, 8)] = buf[way, N_OWN - 1, at]
                    result[pl.ds(back, 8)] = final[way, at]

            over_rows(0, l if kind == 0 else f, put)
        core_swap(kind, core).start()
        own_store(kind).start()

    for tick in range(N_OWN + LAG):
        if small is not None and tick < len(swaps) + 1:
            if tick == 0:
                small_load().wait()
            else:
                small_copy(tick - 1).wait_recv()

                def add_small(row):
                    at = pl.ds(row, 8)
                    sums[tick, at] = sums[tick - 1, at] + arrived[tick - 1, at]

                over_rows(0, small.shape[0], add_small)
            if tick < len(swaps):
                small_copy(tick).start()
        if 0 < tick < N_OWN:
            for way in range(2):
                x_copy(way, tick).start()
        if part is not None and tick == N_OWN - 1:
            part_load().wait()
            part_copy(0).start()
            part_copy(1).start()
        for way in range(2):
            if tick < N_OWN:
                ring_step(0, way, tick)
            if tick >= LAG:
                ring_step(1, way, tick - LAG)
    if small is not None:
        small_store = pltpu.make_async_copy(sums.at[len(swaps)], small_out, own_sem.at[6])
        small_store.start()
    finish(0)
    if part is not None:
        part_copy(0, flip_x).wait_recv()
        part_copy(2).start()
    finish(1)
    if part is not None:
        part_copy(1, x * CORES + 1 - core).wait_recv()
        part_copy(2, (1 - x) * CORES + 1 - core).wait_recv()
        part_store = pltpu.make_async_copy(frames, part_out, own_sem.at[6])
        part_store.start()
        part_store.wait()
        for number in range(3):
            part_copy(number).wait_send()
    if small is not None:
        small_store.wait()
        for stage in range(len(swaps)):
            small_copy(stage).wait_send()
    for way in range(2):
        for step in range(N_OWN):
            x_copy(way, step).wait_send()
    for kind in range(2):
        for way in range(2):
            for step in range(N_OWN - 1):
                ring_copy(kind, way, step).wait_send()
            final_copy(kind, way).wait_send()
        core_swap(kind, 1 - core).wait_recv()
        core_swap(kind, core).wait_send()
        own_store(kind).wait()


def collect_shard(chunks, first, collective, small=None, part=None):
    rows = chunks.shape[1]
    last = rows - 2 * first
    spec = pl.BlockSpec(memory_space=pl.ANY)
    out_shape = [jax.ShapeDtypeStruct((2, rows, D), jnp.float32)]
    beside = small if part is None else part
    if part is None:
        out_shape.append(jax.ShapeDtypeStruct(small.shape, jnp.float32))
        more = [
            pltpu.VMEM((6,) + small.shape, jnp.float32),
            pltpu.VMEM((5,) + small.shape, jnp.float32),
            pltpu.SemaphoreType.DMA((5,)),
            pltpu.SemaphoreType.DMA((5,)),
        ]
    else:
        out_shape.append(jax.ShapeDtypeStruct((4,) + part.shape, jnp.float32))
        more = [
            pltpu.VMEM((4,) + part.shape, jnp.float32),
            pltpu.SemaphoreType.DMA((3,)),
            pltpu.SemaphoreType.DMA((3,)),
        ]

    def kernel(chunks, beside, out, beside_out, *scratch):
        if part is None:
            collect_kernel(first, last, chunks, beside, None, out, beside_out, None, scratch)
        else:
            collect_kernel(first, last, chunks, None, beside, out, None, beside_out, scratch)

    return pl.pallas_call(
        kernel,
        in_specs=[spec] * 2,
        out_specs=[spec] * 2,
        out_shape=out_shape,
        scratch_shapes=[
            pltpu.VMEM((2, N_OWN, last // 2, D), jnp.float32),
            pltpu.VMEM((2, N_OWN, first // 2, D), jnp.float32),
            pltpu.VMEM((2, N_OWN, first // 2, D), jnp.float32),
            pltpu.VMEM((2, 2, last // 2, D), jnp.float32),
            pltpu.VMEM((2, 2, first // 2, D), jnp.float32),
            pltpu.VMEM((2, last // 2, D), jnp.float32),
            pltpu.VMEM((2, first // 2, D), jnp.float32),
            pltpu.VMEM((rows, D), jnp.float32),
            pltpu.SemaphoreType.DMA((2, 2, N_OWN)),
            pltpu.SemaphoreType.DMA((2, 2, N_OWN)),
            pltpu.SemaphoreType.DMA((2, N_OWN)),
            pltpu.SemaphoreType.DMA((2, N_OWN)),
            pltpu.SemaphoreType.DMA((2, 2)),
            pltpu.SemaphoreType.DMA((2, 2)),
            pltpu.SemaphoreType.DMA((2, 2, 2)),
            pltpu.SemaphoreType.DMA((8,)),
        ]
        + more,
        compiler_params=pltpu.CompilerParams(
            collective_id=collective, has_side_effects=True, vmem_limit_bytes=58 * 1024 * 1024
        ),
        cost_estimate=pl.CostEstimate(
            flops=0, bytes_accessed=800 * 1000 * 1000, transcendentals=0
        ),
    )(chunks, beside)


def matrix_plan(matrices, segments):
    shapes = [(rows, wide * D) for name, rows, wide in matrices]
    names = [name for name, rows, wide in matrices]
    stores = []
    for owner in range(N_OWN):
        offset = 0
        for name, first, count, wide in segments[owner]:
            for j in range(wide):
                stores.append((names.index(name), first, j * D, owner, offset, count))
                offset += count
    return shapes, stores


def half_rows(segments, name):
    rows = [[], []]
    for mine in segments:
        for label, first, count, wide in mine:
            if label == name:
                for core in range(2):
                    begin = first + core * (count // 2)
                    rows[core].extend(range(begin, begin + count // 2))
    return np.array(rows, np.int32)


def pick_columns(values, rows, core):
    wanted = jnp.asarray(rows)[core]
    chooser = (jnp.arange(values.shape[1], dtype=jnp.int32)[:, None] == wanted[None]).astype(jnp.bfloat16)
    return matmul_low(values, chooser).astype(jnp.bfloat16)


def both_cores(value):
    return jnp.concatenate([value, shift(value, SWAP_CORE)], 0)


def owner_chunk(grads, segments, owner):
    parts = []
    for label, first, count, wide in segments[owner]:
        begin = sum(seg[2] // 2 for mine in segments[:owner] for seg in mine if seg[0] == label)
        for j in range(wide):
            parts.append(grads[label][j][begin : begin + count // 2])
    return jnp.concatenate(parts, 0) if len(parts) > 1 else parts[0]


def step_values(master, grad, first, second, average):
    keep = min(AVERAGE_KEEP, (1.0 + STEP) / (10.0 + STEP))
    first = BETA_FIRST * first + (1.0 - BETA_FIRST) * grad
    second = BETA_SECOND * second + (1.0 - BETA_SECOND) * grad * grad
    moved = (
        first
        / (1.0 - BETA_FIRST**STEP)
        / (jnp.sqrt(second / (1.0 - BETA_SECOND**STEP)) + ADAM_FLOOR)
    )
    master = master - LEARN_RATE * (moved + WEIGHT_DECAY * master)
    return (master, first, second, keep * average + (1.0 - keep) * master)


STEP_ROWS = 144


def step_kernel(widths, table, factor, grad, *refs):
    olds, news, (shard, flat, sem) = refs[:4], refs[4:8], refs[8:]
    block = pl.program_id(0)

    @pl.when(block == 0)
    def _():
        copy = pltpu.make_async_copy(grad, shard, sem)
        copy.start()
        copy.wait()

    for wide in widths:
        count = STEP_BLOCK // wide

        @pl.when(table[block, 0] == wide)
        def _():
            for slab in range(wide):
                row = pl.multiple_of(table[block, 1] + slab * table[block, 2], 8)
                for tile in range(LANE_TILES):
                    flat[pl.ds(LANE_TILES * slab + tile, count, stride=LANE_TILES * wide), :] = shard[
                        pl.ds(row, count), tile * LANES : (tile + 1) * LANES
                    ]

    scale = factor[0]

    def some_rows(number, carry):
        at = pl.ds(pl.multiple_of(number * STEP_ROWS, 8), STEP_ROWS)
        old = [ref[at, :] for ref in olds]
        made = step_values(old[0], flat[at, :] * scale, old[1], old[2], old[3])
        for ref, value in zip(news, made):
            ref[at, :] = value
        return carry

    lax.fori_loop(0, STEP_BLOCK * LANE_TILES // STEP_ROWS, some_rows, 0)


def step_shard(grad, table, widths, n_rows, factor, olds):
    units = STEP_BLOCK * LANE_TILES
    block_spec = pl.BlockSpec((units, LANES), lambda b, t, f: (b, 0))
    flat_shape = jax.ShapeDtypeStruct((n_rows * LANE_TILES, LANES), jnp.float32)
    made = pl.pallas_call(
        partial(step_kernel, widths),
        grid_spec=pltpu.PrefetchScalarGridSpec(
            num_scalar_prefetch=2,
            grid=(n_rows // STEP_BLOCK,),
            in_specs=[pl.BlockSpec(memory_space=pl.ANY)] + [block_spec] * 4,
            out_specs=[block_spec] * 4,
            scratch_shapes=[
                pltpu.VMEM((n_rows, D), jnp.float32),
                pltpu.VMEM((units, LANES), jnp.float32),
                pltpu.SemaphoreType.DMA,
            ],
        ),
        out_shape=[flat_shape] * 4,
        compiler_params=pltpu.CompilerParams(vmem_limit_bytes=50 * 1024 * 1024),
    )(table, factor, grad, *[old.reshape(-1, LANES) for old in olds])
    return [value.reshape(-1) for value in made]


def head_span(head):
    width = D // HEADS
    start = head * width // LANES * LANES
    stop = -(-(head + 1) * width // LANES) * LANES
    lane = start + lax.broadcasted_iota(jnp.int32, (1, stop - start), 1)
    ones = (lane >= head * width) & (lane < (head + 1) * width)
    return slice(start, stop), ones.astype(jnp.float32).astype(jnp.bfloat16)


def dot_rows(left, right):
    return lax.dot_general(left, right, (((1,), (1,)), ((), ())), preferred_element_type=jnp.float32)


def dot_down(left, right):
    return lax.dot_general(left, right, (((0,), (0,)), ((), ())), preferred_element_type=jnp.float32)


def live_keys(mode, live, n_queries, n_keys):
    key = lax.broadcasted_iota(jnp.int32, (n_queries, n_keys), 1)
    if mode == "cross":
        return key < live[0]
    if mode == "all":
        return None
    query = lax.broadcasted_iota(jnp.int32, (n_queries, n_keys), 0)
    return query // mode == key // mode


def head_scores(queries, keys, valid):
    scores = dot_rows(queries, keys) * (D // HEADS) ** (-0.5)
    return scores if valid is None else jnp.where(valid, scores, MASKED_SCORE)


def heads_kernel(mode, live, queries, keys, values, out, log_total, total):
    n_queries, n_keys = queries.shape[0], keys.shape[0]
    valid = live_keys(mode, live, n_queries, n_keys)
    lane = lax.broadcasted_iota(jnp.int32, (1, LANES), 1)
    total[...] = jnp.zeros_like(total)
    log_total[...] = jnp.zeros_like(log_total)
    for head in range(HEADS):
        span, ones = head_span(head)
        scores = head_scores(queries[:, span], keys[:, span] * ones, valid)
        summit = jnp.max(scores, -1, keepdims=True)
        powers = jnp.exp(scores - summit)
        sums = jnp.sum(powers, -1, keepdims=True)
        probs = (powers / sums).astype(jnp.bfloat16)
        total[:, span] += jnp.dot(
            probs, values[:, span] * ones, preferred_element_type=jnp.float32
        )
        log_total[...] += jnp.where(lane == head, summit + jnp.log(sums), 0.0)
    out[...] = total[...].astype(jnp.bfloat16)


def heads_back_kernel(
    mode, live, queries, keys, values, log_total, grad_out, grad_q, grad_k, grad_v, sum_q, sum_k, sum_v
):
    n_queries, n_keys = queries.shape[0], keys.shape[0]
    valid = live_keys(mode, live, n_queries, n_keys)
    scale = (D // HEADS) ** (-0.5)
    block, last = pl.program_id(0), pl.num_programs(0) - 1
    sum_q[...] = jnp.zeros_like(sum_q)

    @pl.when((block == 0) | (mode != "cross"))
    def _():
        sum_k[...] = jnp.zeros_like(sum_k)
        sum_v[...] = jnp.zeros_like(sum_v)

    for head in range(HEADS):
        span, ones = head_span(head)
        some_keys = keys[:, span] * ones
        scores = head_scores(queries[:, span], some_keys, valid)
        probs = jnp.exp(scores - log_total[:, head : head + 1])
        grad_probs = dot_rows(grad_out[:, span], values[:, span] * ones)
        row = jnp.sum(probs * grad_probs, -1, keepdims=True)
        grad_scores = (probs * (grad_probs - row)).astype(jnp.bfloat16)
        sum_q[:, span] += jnp.dot(grad_scores, some_keys, preferred_element_type=jnp.float32)
        sum_k[:, span] += dot_down(grad_scores, queries[:, span] * ones)
        sum_v[:, span] += dot_down(probs.astype(jnp.bfloat16), grad_out[:, span] * ones)
    grad_q[...] = (sum_q[...] * scale).astype(grad_q.dtype)

    @pl.when((block == last) | (mode != "cross"))
    def _():
        grad_k[...] = (sum_k[...] * scale).astype(grad_k.dtype)
        grad_v[...] = sum_v[...].astype(grad_v.dtype)


HEAD_ROWS = 256


def heads_specs(mode, keys):
    own = pl.BlockSpec((HEAD_ROWS, D), lambda b: (b, 0))
    side = pl.BlockSpec((HEAD_ROWS, LANES), lambda b: (b, 0))
    shared = pl.BlockSpec(keys.shape, lambda b: (0, 0)) if mode == "cross" else own
    return own, side, shared


def heads_forward(mode, queries, keys, values, live):
    own, side, shared = heads_specs(mode, keys)
    n_keys = keys.shape[0] if mode == "cross" else HEAD_ROWS
    return pl.pallas_call(
        partial(heads_kernel, mode),
        grid=(queries.shape[0] // HEAD_ROWS,),
        in_specs=[pl.BlockSpec(memory_space=pltpu.SMEM), own, shared, shared],
        out_specs=[own, side],
        out_shape=[
            jax.ShapeDtypeStruct(queries.shape, jnp.bfloat16),
            jax.ShapeDtypeStruct((queries.shape[0], LANES), jnp.float32),
        ],
        scratch_shapes=[pltpu.VMEM((HEAD_ROWS, D), jnp.float32)],
        compiler_params=pltpu.CompilerParams(vmem_limit_bytes=32 * 1024 * 1024),
    )(live, queries, keys, values)


def heads_backward(mode, queries, keys, values, live, log_total, grad_out):
    own, side, shared = heads_specs(mode, keys)
    n_keys = keys.shape[0] if mode == "cross" else HEAD_ROWS
    kind = jnp.float32 if mode == "cross" else jnp.bfloat16
    return pl.pallas_call(
        partial(heads_back_kernel, mode),
        grid=(queries.shape[0] // HEAD_ROWS,),
        in_specs=[pl.BlockSpec(memory_space=pltpu.SMEM), own, shared, shared, side, own],
        out_specs=[own, shared, shared],
        out_shape=[
            jax.ShapeDtypeStruct(queries.shape, jnp.bfloat16),
            jax.ShapeDtypeStruct(keys.shape, kind),
            jax.ShapeDtypeStruct(keys.shape, kind),
        ],
        scratch_shapes=[
            pltpu.VMEM((HEAD_ROWS, D), jnp.float32),
            pltpu.VMEM((n_keys, D), jnp.float32),
            pltpu.VMEM((n_keys, D), jnp.float32),
        ],
        compiler_params=pltpu.CompilerParams(vmem_limit_bytes=40 * 1024 * 1024),
    )(live, queries, keys, values, log_total, grad_out)


ROW_TIME_ONE = PATCH_VALUES
ROW_TIME_TWO = ROW_TIME_ONE + TFREQ
ROW_BLOCK = ROW_TIME_TWO + D
ROW_CAP_ONE = ROW_BLOCK + 6 * D
ROW_CAP_TWO = ROW_CAP_ONE + CAPW
ROW_FINAL = ROW_CAP_TWO + D
ROW_NULL = ROW_FINAL + PATCH_VALUES
EMB_UNITS = 16158720 // LANES // N_OWN
EMB_FIRST = [EMB_UNITS * c // LANE_TILES for c in range(N_OWN)]
EMB_SHIFT = [EMB_UNITS * c % LANE_TILES for c in range(N_OWN)]


def two_parts(product, value):
    both = product(jnp.concatenate(halves(value), 0))
    return both[: value.shape[0]] + both[value.shape[0] :]


def grad_two_parts(left, value):
    return weight_grad(jnp.concatenate([left, left], 0), jnp.concatenate(halves(value), 0))


def shards_block(
    latents,
    noise,
    timesteps,
    captions,
    cap_lengths,
    null_flags,
    sample_weight,
    embed_w,
    attend_w,
    dense_w,
    vector_w,
    embed_m,
    attend_m,
    dense_m,
    vector_m,
    embed_v,
    attend_v,
    dense_v,
    vector_v,
    embed_e,
    attend_e,
    dense_e,
    vector_e,
):
    clip_dev, frame_dev, patches = (latents.shape[0], latents.shape[1], latents.shape[2])
    n_frame = lax.axis_size("frame")
    n_clip = lax.axis_size("clip")
    local_pos = patches // n_frame
    tokens = frame_dev * patches
    frame_id = lax.axis_index("frame")
    clip_id = lax.axis_index("clip")
    x_id, core_id = frame_id // CORES, frame_id % CORES
    z_id, y_id = clip_id // Y_SIZE, clip_id % Y_SIZE

    emb_first = jnp.asarray(EMB_FIRST, jnp.int32)[clip_id]
    emb_shift = jnp.asarray(EMB_SHIFT, jnp.int32)[clip_id]
    emb_rows = flat_to_rows(embed_w.reshape(-1, LANES), EMB_PAD, emb_shift, jnp.bfloat16)
    dense_cast = cast_shard(
        dense_w, jnp.asarray(cast_table(DENSE_SEGS, CAST_BLOCK))[clip_id], (1, 4), DENSE_ROWS
    )
    cap_owners = range(4, N_OWN)
    cap_plan = (
        [(EMB_PAD * len(cap_owners), D)],
        [(0, EMB_PAD * k, 0, owner, 0, EMB_PAD) for k, owner in enumerate(cap_owners)],
    )
    own_clip = jnp.arange(n_clip) == clip_id
    facts = jnp.stack([timesteps.astype(jnp.float32)[0], sample_weight[0], null_flags.astype(jnp.float32)[0]])
    facts = jnp.broadcast_to(jnp.pad(facts, (0, LANES - 3))[None], (8, LANES))
    cap_weights, fc_in, fc_out, facts = spread_shards(
        [emb_rows, dense_cast],
        [(cap_owners,) + cap_plan + (False,), (range(N_OWN),) + matrix_plan(DENSE, DENSE_SEGS) + (True,)],
        2,
        given=[(facts, "gather")],
    )
    facts = facts[:, 0, :3]
    last = N_OWN - 1
    cap_last = cap_weights[EMB_PAD * (len(cap_owners) - 1) :]
    null_end = 16158720 - ROW_NULL * D
    null_first, final_first = ROW_NULL - EMB_FIRST[last], ROW_FINAL - EMB_FIRST[last]
    null_caption = (
        cap_last[null_first : null_first - (-null_end // D)]
        .reshape(-1)[:null_end]
        .reshape(L_CAP, CAPW)
    )
    final_w = cap_last[final_first : final_first + PATCH_VALUES].reshape(D, PATCH_VALUES)
    two_first = ROW_CAP_TWO - EMB_FIRST[last]

    def to_cap_rows(value):
        padded = jnp.pad(value, ((0, 0), (EMB_PAD, EMB_PAD)))
        starts = [EMB_FIRST[owner] - ROW_CAP_ONE + EMB_PAD for owner in cap_owners]
        return jnp.concatenate([padded[:, start : start + EMB_PAD] for start in starts], 1)

    def from_cap_rows(value):
        total = 0.0
        for k, owner in enumerate(cap_owners):
            start = EMB_FIRST[owner] - ROW_CAP_ONE
            low, high = max(0, -start), min(EMB_PAD, CAPW - start)
            part = value[:, EMB_PAD * k + low : EMB_PAD * k + high]
            total = total + jnp.pad(part, ((0, 0), (start + low, CAPW - start - high)))
        return total

    (
        patch_b,
        time_b1,
        time_b2,
        block_b,
        cap_b1,
        cap_b2,
        space_bq,
        space_bv,
        space_bo,
        time_bq,
        time_bv,
        time_bo,
        cross_bq,
        cross_bv,
        cross_bo,
        fc_in_b,
        fc_out_b,
        final_b,
        table,
        final_table,
    ) = split_flat(vector_w, vector_shapes())

    all_steps, all_null = facts[:, 0], facts[:, 2] == 1.0
    angle = (all_steps / 1000.0 + 0.008) / 1.008 * (math.pi / 2)
    signal = jnp.cos(angle) ** 2
    ratio = signal / (1.0 - signal)
    all_weights = facts[:, 1] * jnp.minimum(ratio, SNR_LIMIT) / ratio
    weight_total = jnp.sum(all_weights)
    signal = lax.dynamic_slice_in_dim(signal, clip_id, 1, 0)
    loss_weight = lax.dynamic_slice_in_dim(all_weights, clip_id, 1, 0)

    freq_in = sincos(all_steps, TFREQ).astype(jnp.bfloat16)
    at_start = clip_id == 0
    time_one = emb_rows[ROW_TIME_ONE:ROW_TIME_TWO]
    time_two = emb_rows[ROW_TIME_TWO:ROW_BLOCK]
    pre_one = matmul_low(freq_in, time_one) + time_b1
    act_one = jax.nn.silu(pre_one).astype(jnp.bfloat16)
    time_embed = matmul_low(act_one, time_two) + time_b2
    early = jnp.concatenate(
        [pre_one, time_embed, emb_rows[:ROW_TIME_ONE].astype(jnp.float32)], 0
    )
    is_null = null_flags == 1
    cap_in = jnp.where(is_null[:, None, None], null_caption[None], captions)
    cap_pre = (matmul_low(to_cap_rows(cap_in[0]), cap_weights) + cap_b1)[None]
    cap_act = gelu_tanh(cap_pre).astype(jnp.bfloat16)
    act_rows = jnp.pad(cap_act[0], ((0, 0), (two_first, EMB_PAD - two_first - D)))
    cap_rows = (matmul_low(act_rows, cap_last) + cap_b2).astype(jnp.bfloat16)[None]
    live_len = jnp.where(is_null, L_CAP, cap_lengths)
    cap_wide = jnp.concatenate([cap_in[0], cap_act[0]], -1)
    cap_wide = jnp.pad(cap_wide, ((0, 0), (EMB_PAD, EMB_PAD)))
    wanted = []
    for owner in range(n_clip):
        start = EMB_FIRST[owner] - ROW_CAP_ONE + EMB_PAD
        if start + EMB_PAD <= EMB_PAD:
            wanted.append(jnp.zeros((L_CAP, EMB_PAD // 4), jnp.bfloat16))
        else:
            wanted.append(
                lax.dynamic_slice_in_dim(cap_wide, start + frame_id * (EMB_PAD // 4), EMB_PAD // 4, 1)
            )
    attend_cast = cast_shard(
        attend_w, jnp.asarray(cast_table(ATTEND_SEGS, CAST_BLOCK))[clip_id], (1, 2, 3), ATTEND_ROWS
    )
    space_qkv, space_out, time_qkv, time_out, cross_q, cross_kv, cross_out, early, cap_left = spread_shards(
        [attend_cast],
        [(range(N_OWN),) + matrix_plan(ATTEND, ATTEND_SEGS) + (True,)],
        1,
        given=[(early, "first"), (jnp.pad(jnp.stack(wanted), ((0, 0), (0, 128 - L_CAP), (0, 0))), "swap")],
    )
    early = early[0]
    cap_left = cap_left[:, :L_CAP].reshape(n_clip * L_CAP, EMB_PAD // 4)
    pre_one, time_embed = early[:n_clip], early[n_clip : 2 * n_clip]
    patch_w = early[2 * n_clip :].astype(jnp.bfloat16)
    act_one = jax.nn.silu(pre_one).astype(jnp.bfloat16)
    silu_time = jax.nn.silu(time_embed).astype(jnp.bfloat16)
    local_row = emb_first + jnp.arange(EMB_PAD, dtype=jnp.int32)
    block_row = local_row - ROW_BLOCK
    in_block = (block_row >= 0) & (block_row < 6 * D)
    block_part = jnp.where(in_block, block_row % 6, -1)
    block_line = jnp.where(in_block, block_row // 6, -1)
    chooser = jnp.arange(D, dtype=jnp.int32)[:, None] == block_line[None]
    silu_rows = matmul_low(silu_time, chooser.astype(jnp.bfloat16)).astype(jnp.bfloat16)
    part_mask = jnp.arange(6, dtype=jnp.int32)[:, None] == block_part[None]
    block_left = jnp.where(part_mask[None], silu_rows[:, None], 0).reshape(n_clip * 6, EMB_PAD)
    block_out = sum_clips(matmul_low(block_left, emb_rows)).reshape(n_clip, 6, D)
    all_mods = table[None] + (block_out + block_b.reshape(6, D))
    mods = lax.dynamic_slice_in_dim(all_mods, clip_id, 1, 0)
    my_embed = lax.dynamic_slice_in_dim(time_embed, clip_id, 1, 0)

    keep_part = jnp.sqrt(signal)[:, None, None, None]
    fade_part = jnp.sqrt(1.0 - signal)[:, None, None, None]
    noisy = (keep_part * latents + fade_part * noise).astype(jnp.bfloat16)
    frame_ids = frame_id * frame_dev + jnp.arange(frame_dev)
    patch_ids = jnp.arange(patches)
    place = jnp.concatenate(
        [sincos(patch_ids // PGRID, D // 2), sincos(patch_ids % PGRID, D // 2)], -1
    )[None, None]
    hidden_zero = matmul_low(noisy, patch_w) + patch_b + place + sincos(frame_ids, D)[None, :, None]

    def mod_row(number):
        return mods[:, number][:, None, None, :]

    def flat2(value):
        return value.reshape(-1, value.shape[-1])

    space_in = modulate(hidden_zero, mod_row(0), mod_row(1)).astype(jnp.bfloat16)
    live = live_len.astype(jnp.int32)
    space_q, space_k, space_v = split_qkv(matmul_low(flat2(space_in), space_qkv), space_bq, space_bv)
    space_o, space_lse = heads_forward("all", space_q, space_k, space_v, live)
    space_flat = space_o.reshape(clip_dev, frame_dev, patches, D)
    space_res = matmul_low(space_flat, space_out) + space_bo
    hidden_one = hidden_zero + mod_row(2) * space_res
    time_in = lax.all_to_all(
        hidden_one.astype(jnp.bfloat16), "frame", split_axis=2, concat_axis=1, tiled=True
    )
    time_in = jnp.swapaxes(time_in, 1, 2)
    frames = time_in.shape[2]
    time_q, time_k, time_v = split_qkv(matmul_low(flat2(time_in), time_qkv), time_bq, time_bv)
    time_o, time_lse = heads_forward(frames, time_q, time_k, time_v, live)
    time_back = jnp.swapaxes(time_o.reshape(clip_dev, local_pos, frames, D), 1, 2)
    time_flat = lax.all_to_all(time_back, "frame", split_axis=1, concat_axis=2, tiled=True)
    time_res = matmul_low(time_flat, time_out) + time_bo
    hidden_two = hidden_one + mod_row(2) * time_res
    cross_in = hidden_two.astype(jnp.bfloat16)
    cross_query = (matmul_low(flat2(cross_in), cross_q) + cross_bq).astype(jnp.bfloat16)
    cross_merged = matmul_low(jnp.pad(cap_rows[0], ((0, -L_CAP % 16), (0, 0))), cross_kv)
    cross_k = cross_merged[..., :D].astype(jnp.bfloat16)
    cross_v = (cross_merged[..., D:] + cross_bv).astype(jnp.bfloat16)
    cross_o, cross_lse = heads_forward("cross", cross_query, cross_k, cross_v, live)
    cross_flat = cross_o.reshape(clip_dev, frame_dev, patches, D)
    hidden_three = hidden_two + matmul_low(cross_flat, cross_out) + cross_bo
    dense_in = modulate(hidden_three, mod_row(3), mod_row(4)).astype(jnp.bfloat16)
    dense_pre = matmul_low(dense_in, fc_in) + fc_in_b
    dense_act = gelu_tanh(dense_pre).astype(jnp.bfloat16)
    dense_res = matmul_low(dense_act, fc_out) + fc_out_b
    hidden_four = hidden_three + mod_row(5) * dense_res
    final_mod = final_table[None] + my_embed[:, None, :]
    final_shift = final_mod[:, 0][:, None, None, :]
    final_scale = final_mod[:, 1][:, None, None, :]
    final_in = modulate(hidden_four, final_shift, final_scale).astype(jnp.bfloat16)
    predicted = matmul_low(final_in, final_w) + final_b
    miss = predicted - noise
    clip_error = jnp.sum(jnp.mean(miss * miss, -1), (1, 2))
    local_loss = jnp.sum(loss_weight * clip_error)

    inputs = {}
    for label, value in (
        ("space_qkv", space_in),
        ("space_out", space_flat),
        ("time_qkv", time_in),
        ("time_out", time_flat),
        ("cross_q", cross_in),
        ("cross_out", cross_flat),
        ("fc_in", dense_in),
    ):
        segments = DENSE_SEGS if label == "fc_in" else ATTEND_SEGS
        inputs[label] = pick_columns(both_cores(flat2(value)), half_rows(segments, label), core_id)
    act_both = both_cores(flat2(dense_act))
    half = half_rows([[("square", 0, D, 1)]], "square")
    for block in range(MLP // D):
        inputs["fc_out", block] = pick_columns(act_both[:, block * D : (block + 1) * D], half, core_id)

    def core_grad(left, outs):
        return [weight_grad(left, both_cores(flat2(out))) for out in outs]

    def columns(value):
        return [value[..., j * D : (j + 1) * D] for j in range(value.shape[-1] // D)]

    grad_pred = (
        2.0 / miss.shape[-1] * (loss_weight / weight_total)[:, None, None, None] * miss
    ).astype(jnp.bfloat16)
    g_final_w = weight_grad(final_in, grad_pred)
    g_final_b = bias_grad(grad_pred)
    unused, pullback = jax.vjp(modulate, hidden_four, final_shift, final_scale)
    grad_hidden, grad_fshift, grad_fscale = pullback(back_low(grad_pred, final_w))
    grad_fmod = jnp.concatenate([grad_fshift.reshape(1, D), grad_fscale.reshape(1, D)], 0)
    grad_dense = (grad_hidden * mod_row(5)).astype(jnp.bfloat16)
    grad_gate_b = jnp.sum(grad_hidden * dense_res, (1, 2))
    grads = {}
    dense_both = both_cores(flat2(grad_dense))
    g_fc_out = [weight_grad(inputs["fc_out", block], dense_both) for block in range(MLP // D)]
    grads["fc_out"] = [jnp.concatenate(g_fc_out, 0)]
    g_fc_out_b = bias_grad(grad_dense)
    unused, pullback = jax.vjp(gelu_tanh, dense_pre)
    grad_pre = pullback(back_low(grad_dense, fc_out))[0].astype(jnp.bfloat16)
    grads["fc_in"] = core_grad(inputs["fc_in"], columns(grad_pre))
    g_fc_in_b = bias_grad(grad_pre)
    unused, pullback = jax.vjp(modulate, hidden_three, mod_row(3), mod_row(4))
    grad_input, grad_shift_b, grad_scale_b = pullback(back_low(grad_pre, fc_in))
    grad_hidden = grad_hidden + grad_input
    grad_cross = grad_hidden.astype(jnp.bfloat16)
    grads["cross_out"] = core_grad(inputs["cross_out"], [grad_cross])
    g_cross_bo = bias_grad(grad_cross)
    grad_cross_o = back_low(flat2(grad_cross), cross_out).astype(jnp.bfloat16)
    grad_cq, grad_ck, grad_cv = heads_backward(
        "cross", cross_query, cross_k, cross_v, live, cross_lse, grad_cross_o
    )
    grad_cq = grad_cq.reshape(clip_dev, frame_dev, patches, D)
    grads["cross_q"] = core_grad(inputs["cross_q"], [grad_cq])
    g_cross_bq = bias_grad(grad_cq)
    grad_hidden = grad_hidden + back_low(grad_cq, cross_q)
    grad_cv = grad_cv[:L_CAP]
    grad_ckv = jnp.concatenate([grad_ck[:L_CAP], grad_cv], -1)
    g_cross_bv = bias_grad(grad_cv)
    grad_ckv = grad_ckv + shift(grad_ckv, SWAP_CORE)
    cap_half = pick_columns(cap_rows[0], half_rows(ATTEND_SEGS, "cross_kv"), core_id)
    grads["cross_kv"] = [grad_two_parts(cap_half, part) for part in columns(grad_ckv)]
    grad_ckv = grad_ckv + shift(grad_ckv, SWAP_X)
    grad_cap_rows = two_parts(lambda part: back_low(part, cross_kv), grad_ckv)

    grad_time = (grad_hidden * mod_row(2)).astype(jnp.bfloat16)
    grads["time_out"] = core_grad(inputs["time_out"], [grad_time])
    g_time_bo = bias_grad(grad_time)
    grad_time_o = lax.all_to_all(
        back_low(grad_time, time_out).astype(jnp.bfloat16),
        "frame",
        split_axis=2,
        concat_axis=1,
        tiled=True,
    )
    grad_time_o = flat2(jnp.swapaxes(grad_time_o, 1, 2))
    grad_tqkv = [
        piece.reshape(clip_dev, local_pos, frames, D)
        for piece in heads_backward(frames, time_q, time_k, time_v, live, time_lse, grad_time_o)
    ]
    grads["time_qkv"] = core_grad(inputs["time_qkv"], grad_tqkv)
    g_time_bq = bias_grad(grad_tqkv[0])
    g_time_bv = bias_grad(grad_tqkv[2])
    grad_tqkv = lax.all_to_all(
        jnp.swapaxes(jnp.concatenate(grad_tqkv, -1), 1, 2), "frame", split_axis=1, concat_axis=2, tiled=True
    )
    grad_gate_a = jnp.sum(grad_hidden * time_res, (1, 2))
    grad_hidden = grad_hidden + back_low(grad_tqkv, time_qkv)
    grad_gate_a = grad_gate_a + jnp.sum(grad_hidden * space_res, (1, 2))
    grad_space = (grad_hidden * mod_row(2)).astype(jnp.bfloat16)
    grads["space_out"] = core_grad(inputs["space_out"], [grad_space])
    g_space_bo = bias_grad(grad_space)
    grad_space_o = back_low(flat2(grad_space), space_out).astype(jnp.bfloat16)
    grad_sqkv = [
        piece.reshape(clip_dev, frame_dev, patches, D)
        for piece in heads_backward("all", space_q, space_k, space_v, live, space_lse, grad_space_o)
    ]
    grads["space_qkv"] = core_grad(inputs["space_qkv"], grad_sqkv)
    g_space_bq = bias_grad(grad_sqkv[0])
    g_space_bv = bias_grad(grad_sqkv[2])
    grad_sqkv = jnp.concatenate(grad_sqkv, -1)
    unused, pullback = jax.vjp(modulate, hidden_zero, mod_row(0), mod_row(1))
    grad_input, grad_shift_a, grad_scale_a = pullback(back_low(grad_sqkv, space_qkv))
    grad_hidden = grad_hidden + grad_input
    g_patch_w = weight_split(noisy, grad_hidden)
    g_patch_b = bias_grad(grad_hidden)
    grad_mods = jnp.concatenate(
        [
            grad_shift_a.reshape(clip_dev, D),
            grad_scale_a.reshape(clip_dev, D),
            grad_gate_a,
            grad_shift_b.reshape(clip_dev, D),
            grad_scale_b.reshape(clip_dev, D),
            grad_gate_b,
            grad_fmod,
        ],
        0,
    )

    unused, pullback = jax.vjp(gelu_tanh, cap_pre[0])
    grad_cap_act = two_parts(lambda part: back_low(part, cap_last), grad_cap_rows)
    grad_cap_pre = pullback(grad_cap_act[:, two_first : two_first + D])[0]
    cap_right = lax.all_gather(
        jnp.stack([grad_cap_pre, grad_cap_rows]), "clip", axis=1, tiled=True
    )
    null_sum = jnp.sum(jnp.where(all_null[:, None, None], cap_right[0].reshape(n_clip, L_CAP, D), 0.0), 0)
    g_cap_b1 = bias_grad(grad_cap_pre)
    g_cap_b2 = bias_grad(grad_cap_rows)

    once = frame_id == 0
    gathered_mods = jnp.where(own_clip[:, None, None], grad_mods[None], 0.0)
    zero_d = jnp.zeros((D,), jnp.float32)
    ends = jnp.concatenate([g_final_b, local_loss.reshape(1)])
    vector_rows = [
        g_patch_b,
        jnp.where(once, g_cap_b1, 0.0),
        jnp.where(once, g_cap_b2, 0.0),
        g_space_bq,
        g_space_bv,
        g_space_bo,
        g_time_bq,
        g_time_bv,
        g_time_bo,
        g_cross_bq,
        g_cross_bv,
        g_cross_bo,
        g_fc_in_b.reshape(-1, D),
        g_fc_out_b,
        jnp.pad(ends, (0, D - ends.shape[0])),
    ]
    small = [gathered_mods.reshape(-1, D), g_patch_w, g_final_w.reshape(PATCH_VALUES, D)]
    small = small + [value.reshape(-1, D) for value in vector_rows]
    spare = -sum(value.shape[0] for value in small) % 8
    small = jnp.concatenate(small + [jnp.zeros((spare, D), jnp.float32)] * (spare > 0), 0)
    dense_grad, small = collect_shard(
        jnp.stack([owner_chunk(grads, DENSE_SEGS, owner) for owner in range(N_OWN)]),
        144,
        3,
        small=small,
    )
    dense_grad = dense_grad.reshape(DENSE_ROWS, D)
    at = 8 * n_clip
    gathered_mods = small[:at].reshape(n_clip, 8, D)
    g_patch_w = small[at : at + PATCH_VALUES]
    g_final_w = small[at + PATCH_VALUES : at + 2 * PATCH_VALUES]
    rest = small[at + 2 * PATCH_VALUES :]
    n_whole = 12 + MLP // D + 1
    loss_sum = rest[n_whole, PATCH_VALUES]
    vector_grad = jnp.concatenate([rest[:n_whole].reshape(-1), rest[n_whole, :PATCH_VALUES]])

    grad_zero = gathered_mods[:, :6]
    grad_final = gathered_mods[:, 6:]
    zero_rows = grad_zero.reshape(n_clip * 6, D)
    back_rows = two_parts(lambda part: back_low(part, emb_rows), zero_rows)
    back_rows = jnp.sum(jnp.where(part_mask[None], back_rows.reshape(n_clip, 6, EMB_PAD), 0.0), 1)
    grad_silu = lax.dot_general(
        back_rows,
        chooser.astype(jnp.float32),
        (((1,), (1,)), ((), ())),
        precision=lax.Precision.HIGHEST,
        preferred_element_type=jnp.float32,
    )
    grad_silu = sum_clips(grad_silu)
    unused, pullback = jax.vjp(jax.nn.silu, time_embed)
    grad_embed = grad_final[:, 0] + grad_final[:, 1] + pullback(grad_silu)[0]
    grad_act = two_parts(lambda part: back_low(part, time_two), grad_embed)
    grad_act = sum_clips(jnp.where(at_start, grad_act, 0.0))
    unused, pullback = jax.vjp(jax.nn.silu, pre_one)
    grad_one = pullback(grad_act)[0]
    g_table = jnp.sum(grad_zero, 0)
    vector_sum = flatten_all(
        [
            vector_grad[:D],
            jnp.sum(grad_one, 0),
            jnp.sum(grad_embed, 0),
            g_table,
            vector_grad[D:],
            g_table,
            jnp.sum(grad_final, 0),
        ]
    )

    per = EMB_PAD // 4
    quarter_row = emb_first + frame_id * per + jnp.arange(per, dtype=jnp.int32)
    time_left = jnp.concatenate(
        [
            jnp.pad(freq_in, ((0, 0), (ROW_TIME_ONE, EMB_PAD - ROW_TIME_TWO))),
            jnp.pad(act_one, ((0, 0), (ROW_TIME_TWO, EMB_PAD - ROW_BLOCK))),
        ],
        0,
    )
    time_left = jnp.where(at_start, time_left, jnp.zeros_like(time_left))
    small_left = lax.dynamic_slice_in_dim(
        jnp.concatenate([time_left, block_left], 0), frame_id * per, per, 1
    )
    small_right = jnp.concatenate([grad_one, grad_embed, zero_rows], 0)
    first_kind = (quarter_row < ROW_CAP_TWO)[None]
    no_left = jnp.zeros_like(cap_left)
    g_null = from_cap_rows(two_parts(lambda part: back_low(part, cap_weights), null_sum))
    n_null = -(-null_end // D)
    n_known = -(-(2 * PATCH_VALUES + n_null) // 16) * 16
    null_rows = jnp.pad(g_null.reshape(-1), (0, (n_known - 2 * PATCH_VALUES) * D - null_end))
    known = jnp.concatenate([g_patch_w, g_final_w, null_rows.reshape(-1, D)], 0)
    known_row = np.concatenate(
        [np.arange(PATCH_VALUES), ROW_FINAL + np.arange(n_known - PATCH_VALUES)]
    ).astype(np.int32)
    known_left = (jnp.asarray(known_row)[:, None] == quarter_row[None]).astype(jnp.bfloat16)
    emb_left = jnp.concatenate(
        [
            small_left,
            jnp.where(first_kind, cap_left, no_left),
            jnp.where(first_kind, no_left, cap_left),
            known_left,
        ],
        0,
    )
    emb_right = jnp.concatenate([small_right, cap_right[0], cap_right[1], known], 0)
    emb_grad = weight_split(emb_left, emb_right)
    unit = (
        LANE_TILES * (frame_id * per + jnp.arange(per, dtype=jnp.int32))[:, None]
        + jnp.arange(D, dtype=jnp.int32)[None] // LANES
        - emb_shift
    )
    emb_grad = jnp.where((unit >= 0) & (unit < EMB_UNITS), emb_grad, 0.0)

    attend_grad, emb_whole = collect_shard(
        jnp.stack([owner_chunk(grads, ATTEND_SEGS, owner) for owner in range(N_OWN)]),
        176,
        4,
        part=emb_grad,
    )
    attend_grad = attend_grad.reshape(ATTEND_ROWS, D)
    local_square = sum(jnp.sum(value * value) for value in (dense_grad, attend_grad, emb_whole))
    vector_square = jnp.sum(vector_sum * vector_sum)
    grad_norm = jnp.sqrt(sum_clips(local_square.reshape(1))[0] + vector_square)
    factor = jnp.minimum(1.0, CLIP_LIMIT / (grad_norm + NORM_FLOOR))
    scale = factor.reshape(1)
    dense_r = step_shard(
        dense_grad,
        jnp.asarray(step_table(DENSE_SEGS, STEP_BLOCK, DENSE_ROWS))[clip_id],
        (1, 4),
        DENSE_ROWS,
        scale,
        (dense_w, dense_m, dense_v, dense_e),
    )
    attend_r = step_shard(
        attend_grad,
        jnp.asarray(step_table(ATTEND_SEGS, STEP_BLOCK, ATTEND_ROWS))[clip_id],
        (1, 2, 3),
        ATTEND_ROWS,
        scale,
        (attend_w, attend_m, attend_v, attend_e),
    )
    emb_flat = rows_to_flat(emb_whole.reshape(EMB_PAD, D))
    emb_owned = lax.dynamic_slice_in_dim(emb_flat, emb_shift, EMB_UNITS, 0).reshape(-1)
    embed_r = adam_step(embed_w, emb_owned, embed_m, embed_v, embed_e, factor)
    vector_r = adam_step(vector_w, vector_sum, vector_m, vector_v, vector_e, factor)
    return (
        loss_sum,
        weight_total,
        grad_norm,
        embed_r[0],
        attend_r[0],
        dense_r[0],
        vector_r[0],
        embed_r[1],
        attend_r[1],
        dense_r[1],
        vector_r[1],
        embed_r[2],
        attend_r[2],
        dense_r[2],
        vector_r[2],
        embed_r[3],
        attend_r[3],
        dense_r[3],
        vector_r[3],
    )


def pick_plan(mesh):
    if mesh.shape["frame"] == X_SIZE * CORES and mesh.shape["clip"] == N_OWN:
        return shards_block
    return shards


def solution(mesh):
    in_specs = (
        P("clip", "frame", None, None),
        P("clip", "frame", None, None),
        P("clip"),
        P("clip", None, None),
        P("clip"),
        P("clip"),
        P("clip"),
        P("clip"),
        P("clip"),
        P("clip"),
        P(),
        P("clip"),
        P("clip"),
        P("clip"),
        P(),
        P("clip"),
        P("clip"),
        P("clip"),
        P(),
        P("clip"),
        P("clip"),
        P("clip"),
        P(),
    )
    out_specs = (
        P(),
        P(),
        P(),
        P("clip"),
        P("clip"),
        P("clip"),
        P(),
        P("clip"),
        P("clip"),
        P("clip"),
        P(),
        P("clip"),
        P("clip"),
        P("clip"),
        P(),
        P("clip"),
        P("clip"),
        P("clip"),
        P(),
    )
    return jax.shard_map(pick_plan(mesh), mesh=mesh, in_specs=in_specs, out_specs=out_specs, check_vma=False)
```

```python
import math
from functools import partial

import jax
import jax.numpy as jnp
import numpy as np
from jax import lax
from jax.experimental import pallas as pl
from jax.experimental.pallas import tpu as pltpu
from jax.sharding import PartitionSpec as P

D = 1152
HEADS = 16
MLP = 4608
CAPW = 4096
L_CAP = 120
TFREQ = 256
PATCH_VALUES = 16
PGRID = 16
STEP = 10


NORM_FLOOR = 1e-06
CLIP_LIMIT = 1.0
SNR_LIMIT = 5.0
BETA_FIRST = 0.5
BETA_SECOND = 0.5
LEARN_RATE = 0.02
WEIGHT_DECAY = 0.01
ADAM_FLOOR = 1e-08
AVERAGE_KEEP = 0.9999
MASKED_SCORE = -1e30


def embed_shapes():
    return [
        (PATCH_VALUES, D),
        (TFREQ, D),
        (D, D),
        (D, 6 * D),
        (CAPW, D),
        (D, D),
        (D, PATCH_VALUES),
        (L_CAP, CAPW),
    ]


def attend_shapes():
    return [(D, 3 * D), (D, D), (D, 3 * D), (D, D), (D, D), (D, 2 * D), (D, D)]


def dense_shapes():
    return [(D, MLP), (MLP, D)]


def vector_shapes():
    return [(D,)] * 3 + [(6 * D,)] + [(D,)] * 11 + [(MLP,), (D,), (PATCH_VALUES,), (6, D), (2, D)]


def split_flat(flat, shapes):
    pieces = []
    offset = 0
    for extent in shapes:
        length = math.prod(extent)
        pieces.append(flat[offset : offset + length].reshape(extent))
        offset += length
    return pieces


def flatten_all(pieces):
    return jnp.concatenate([piece.reshape(-1) for piece in pieces])


def reduce_group(grad):
    n_clip = lax.axis_size("clip")
    n_frame = lax.axis_size("frame")
    reorder = grad.reshape(n_clip, n_frame, -1).swapaxes(0, 1).reshape(-1)
    share = lax.psum_scatter(reorder, ("frame", "clip"), scatter_dimension=0, tiled=True)
    return lax.all_gather(share, "frame", axis=0, tiled=True)


def sincos(places, width):
    half = width // 2
    omega = jnp.exp(-math.log(10000.0) * jnp.arange(half, dtype=jnp.float32) / half)
    angle = places.astype(jnp.float32)[..., None] * omega
    return jnp.concatenate([jnp.sin(angle), jnp.cos(angle)], -1)


def modulate(hidden, shift, scale):
    center = hidden - jnp.mean(hidden, -1, keepdims=True)
    normed = center * lax.rsqrt(jnp.mean(center * center, -1, keepdims=True) + NORM_FLOOR)
    return normed * (1.0 + scale) + shift


def gelu_tanh(value):
    return jax.nn.gelu(value, approximate=True)


def matmul_low(left, right):
    return lax.dot_general(
        left, right, (((left.ndim - 1,), (0,)), ((), ())), preferred_element_type=jnp.float32
    )


def halves(value):
    upper = lax.optimization_barrier(value.astype(jnp.bfloat16))
    return (upper, (value - upper.astype(jnp.float32)).astype(jnp.bfloat16))


def back_low(grads, weight):
    return lax.dot_general(
        grads, weight, (((grads.ndim - 1,), (1,)), ((), ())), preferred_element_type=jnp.float32
    )


def back_split(grads, weight):
    upper, lower = halves(grads)
    return back_low(upper, weight) + back_low(lower, weight)


def weight_grad(inputs, grads):
    left = inputs.reshape(-1, inputs.shape[-1])
    right = grads.reshape(-1, grads.shape[-1])
    return lax.dot_general(
        left, right, (((0,), (0,)), ((), ())), preferred_element_type=jnp.float32
    )


def weight_split(inputs, grads):
    upper, lower = halves(grads)
    return weight_grad(inputs, upper) + weight_grad(inputs, lower)


def bias_grad(grads):
    return jnp.sum(grads.astype(jnp.float32).reshape(-1, grads.shape[-1]), 0)


def heads_of(tensor, batch):
    return tensor.reshape(batch, -1, HEADS, tensor.shape[-1] // HEADS)


def split_qkv(merged, bias_q, bias_v):
    width = merged.shape[-1] // 3
    return (
        (merged[..., :width] + bias_q).astype(jnp.bfloat16),
        merged[..., width : 2 * width].astype(jnp.bfloat16),
        (merged[..., 2 * width :] + bias_v).astype(jnp.bfloat16),
    )


def attend_scores(queries, key_rows, mask):
    scores = jnp.einsum("bqhe,bkhe->bhqk", queries, key_rows, preferred_element_type=jnp.float32)
    scores = scores * queries.shape[-1] ** (-0.5)
    if mask is not None:
        scores = jnp.where(mask[:, None, None, :], scores, MASKED_SCORE)
    return scores


def attend_forward(queries, key_rows, values, mask):
    scores = attend_scores(queries, key_rows, mask)
    summit = jnp.max(scores, -1, keepdims=True)
    powers = jnp.exp(scores - summit)
    totals = jnp.sum(powers, -1, keepdims=True)
    probs = (powers / totals).astype(jnp.bfloat16)
    output = jnp.einsum("bhqk,bkhe->bqhe", probs, values, preferred_element_type=jnp.float32)
    return (output.astype(jnp.bfloat16), summit + jnp.log(totals))


def attend_backward(queries, key_rows, values, mask, log_total, grad_out):
    scale = queries.shape[-1] ** (-0.5)
    probs = jnp.exp(attend_scores(queries, key_rows, mask) - log_total)
    grad_probs = jnp.einsum("bqhe,bkhe->bhqk", grad_out, values, preferred_element_type=jnp.float32)
    grad_scores = (probs * (grad_probs - jnp.sum(probs * grad_probs, -1, keepdims=True))).astype(
        jnp.bfloat16
    )
    grad_query = (
        jnp.einsum("bhqk,bkhe->bqhe", grad_scores, key_rows, preferred_element_type=jnp.float32)
        * scale
    )
    grad_keys = (
        jnp.einsum("bhqk,bqhe->bkhe", grad_scores, queries, preferred_element_type=jnp.float32)
        * scale
    )
    grad_values = jnp.einsum(
        "bhqk,bqhe->bkhe", probs.astype(jnp.bfloat16), grad_out, preferred_element_type=jnp.float32
    )
    return (grad_query, grad_keys, grad_values)


def unpack_all(gathered):
    return (
        split_flat(gathered[0], embed_shapes()),
        split_flat(gathered[1], attend_shapes()),
        split_flat(gathered[2], dense_shapes()),
    )


def adam_step(master, grad, first, second, average, factor):
    keep = min(AVERAGE_KEEP, (1.0 + STEP) / (10.0 + STEP))
    grad = grad * factor
    first = BETA_FIRST * first + (1.0 - BETA_FIRST) * grad
    second = BETA_SECOND * second + (1.0 - BETA_SECOND) * grad * grad
    moved = (
        first
        / (1.0 - BETA_FIRST**STEP)
        / (jnp.sqrt(second / (1.0 - BETA_SECOND**STEP)) + ADAM_FLOOR)
    )
    master = master - LEARN_RATE * (moved + WEIGHT_DECAY * master)
    return (master, first, second, keep * average + (1.0 - keep) * master)


def shards(
    latents,
    noise,
    timesteps,
    captions,
    cap_lengths,
    null_flags,
    sample_weight,
    embed_w,
    attend_w,
    dense_w,
    vector_w,
    embed_m,
    attend_m,
    dense_m,
    vector_m,
    embed_v,
    attend_v,
    dense_v,
    vector_v,
    embed_e,
    attend_e,
    dense_e,
    vector_e,
):
    clip_dev, frame_dev, patches = (latents.shape[0], latents.shape[1], latents.shape[2])
    n_frame = lax.axis_size("frame")
    n_clip = lax.axis_size("clip")
    local_pos = patches // n_frame
    gathered = (
        lax.all_gather(embed_w.astype(jnp.bfloat16), "clip", axis=0, tiled=True),
        lax.all_gather(attend_w.astype(jnp.bfloat16), "clip", axis=0, tiled=True),
        lax.all_gather(dense_w.astype(jnp.bfloat16), "clip", axis=0, tiled=True),
    )
    embeds, attends, denses = unpack_all(gathered)
    patch_w, time_one, time_two, block_w, cap_one, cap_two, final_w, null_caption = embeds
    space_qkv, space_out, time_qkv, time_out, cross_q, cross_kv, cross_out = attends
    fc_in, fc_out = denses
    (
        patch_b,
        time_b1,
        time_b2,
        block_b,
        cap_b1,
        cap_b2,
        space_bq,
        space_bv,
        space_bo,
        time_bq,
        time_bv,
        time_bo,
        cross_bq,
        cross_bv,
        cross_bo,
        fc_in_b,
        fc_out_b,
        final_b,
        table,
        final_table,
    ) = split_flat(vector_w, vector_shapes())
    angle = (timesteps.astype(jnp.float32) / 1000.0 + 0.008) / 1.008 * (math.pi / 2)
    signal = jnp.cos(angle) ** 2
    ratio = signal / (1.0 - signal)
    loss_weight = sample_weight * jnp.minimum(ratio, SNR_LIMIT) / ratio
    weight_total = lax.psum(jnp.sum(loss_weight), "clip")
    keep_part = jnp.sqrt(signal)[:, None, None, None]
    fade_part = jnp.sqrt(1.0 - signal)[:, None, None, None]
    noisy = (keep_part * latents + fade_part * noise).astype(jnp.bfloat16)
    frame_ids = lax.axis_index("frame") * frame_dev + jnp.arange(frame_dev)
    patch_ids = jnp.arange(patches)
    place = jnp.concatenate(
        [sincos(patch_ids // PGRID, D // 2), sincos(patch_ids % PGRID, D // 2)], -1
    )[None, None]
    hidden_zero = matmul_low(noisy, patch_w) + patch_b + place + sincos(frame_ids, D)[None, :, None]
    freq_in = sincos(timesteps, TFREQ).astype(jnp.bfloat16)
    pre_one = matmul_low(freq_in, time_one) + time_b1
    act_one = jax.nn.silu(pre_one).astype(jnp.bfloat16)
    time_embed = matmul_low(act_one, time_two) + time_b2
    silu_time = jax.nn.silu(time_embed).astype(jnp.bfloat16)
    mods = table[None] + (matmul_low(silu_time, block_w) + block_b).reshape(clip_dev, 6, D)

    def mod_row(number):
        return mods[:, number][:, None, None, :]

    is_null = null_flags == 1
    cap_in = jnp.where(is_null[:, None, None], null_caption[None], captions)
    cap_pre = matmul_low(cap_in, cap_one) + cap_b1
    cap_act = gelu_tanh(cap_pre).astype(jnp.bfloat16)
    cap_rows = (matmul_low(cap_act, cap_two) + cap_b2).astype(jnp.bfloat16)
    live_len = jnp.where(is_null, L_CAP, cap_lengths)
    key_mask = jnp.arange(L_CAP)[None, :] < live_len[:, None]
    space_in = modulate(hidden_zero, mod_row(0), mod_row(1)).astype(jnp.bfloat16)
    space_q, space_k, space_v = (
        heads_of(piece, clip_dev * frame_dev)
        for piece in split_qkv(matmul_low(space_in, space_qkv), space_bq, space_bv)
    )
    space_o, space_lse = attend_forward(space_q, space_k, space_v, None)
    space_flat = space_o.reshape(clip_dev, frame_dev, patches, D)
    space_res = matmul_low(space_flat, space_out) + space_bo
    hidden_one = hidden_zero + mod_row(2) * space_res
    time_in = lax.all_to_all(
        hidden_one.astype(jnp.bfloat16), "frame", split_axis=2, concat_axis=1, tiled=True
    )
    time_in = jnp.swapaxes(time_in, 1, 2)
    frames = time_in.shape[2]
    time_q, time_k, time_v = (
        heads_of(piece, clip_dev * local_pos)
        for piece in split_qkv(matmul_low(time_in, time_qkv), time_bq, time_bv)
    )
    time_o, time_lse = attend_forward(time_q, time_k, time_v, None)
    time_back = jnp.swapaxes(time_o.reshape(clip_dev, local_pos, frames, D), 1, 2)
    time_flat = lax.all_to_all(time_back, "frame", split_axis=1, concat_axis=2, tiled=True)
    time_res = matmul_low(time_flat, time_out) + time_bo
    hidden_two = hidden_one + mod_row(2) * time_res
    cross_in = hidden_two.astype(jnp.bfloat16)
    cross_query = heads_of(
        (matmul_low(cross_in, cross_q) + cross_bq).astype(jnp.bfloat16), clip_dev
    )
    cross_merged = matmul_low(cap_rows, cross_kv)
    cross_k = heads_of(cross_merged[..., :D].astype(jnp.bfloat16), clip_dev)
    cross_v = heads_of((cross_merged[..., D:] + cross_bv).astype(jnp.bfloat16), clip_dev)
    cross_o, cross_lse = attend_forward(cross_query, cross_k, cross_v, key_mask)
    cross_flat = cross_o.reshape(clip_dev, frame_dev, patches, D)
    hidden_three = hidden_two + matmul_low(cross_flat, cross_out) + cross_bo
    dense_in = modulate(hidden_three, mod_row(3), mod_row(4)).astype(jnp.bfloat16)
    dense_pre = matmul_low(dense_in, fc_in) + fc_in_b
    dense_act = gelu_tanh(dense_pre).astype(jnp.bfloat16)
    dense_res = matmul_low(dense_act, fc_out) + fc_out_b
    hidden_four = hidden_three + mod_row(5) * dense_res
    final_mod = final_table[None] + time_embed[:, None, :]
    final_shift = final_mod[:, 0][:, None, None, :]
    final_scale = final_mod[:, 1][:, None, None, :]
    final_in = modulate(hidden_four, final_shift, final_scale).astype(jnp.bfloat16)
    predicted = matmul_low(final_in, final_w) + final_b
    miss = predicted - noise
    clip_error = jnp.sum(jnp.mean(miss * miss, -1), (1, 2))
    local_loss = jnp.sum(loss_weight * clip_error)
    grad_pred = (
        2.0 / miss.shape[-1] * (loss_weight / weight_total)[:, None, None, None] * miss
    ).astype(jnp.bfloat16)
    g_final_w = weight_grad(final_in, grad_pred)
    g_final_b = bias_grad(grad_pred)
    unused, pullback = jax.vjp(modulate, hidden_four, final_shift, final_scale)
    grad_hidden, grad_fshift, grad_fscale = pullback(back_low(grad_pred, final_w))
    grad_fmod = jnp.stack([grad_fshift.reshape(clip_dev, D), grad_fscale.reshape(clip_dev, D)], 1)
    g_final_table = jnp.sum(grad_fmod, 0)
    grad_time_embed = grad_fmod[:, 0] + grad_fmod[:, 1]
    grad_dense = (grad_hidden * mod_row(5)).astype(jnp.bfloat16)
    grad_gate_b = jnp.sum(grad_hidden * dense_res, (1, 2))
    g_fc_out = weight_grad(dense_act, grad_dense)
    g_fc_out_b = bias_grad(grad_dense)
    unused, pullback = jax.vjp(gelu_tanh, dense_pre)
    grad_pre = pullback(back_low(grad_dense, fc_out))[0].astype(jnp.bfloat16)
    g_fc_in = weight_grad(dense_in, grad_pre)
    g_fc_in_b = bias_grad(grad_pre)
    dense_owned = reduce_group(flatten_all([g_fc_in, g_fc_out]))
    unused, pullback = jax.vjp(modulate, hidden_three, mod_row(3), mod_row(4))
    grad_input, grad_shift_b, grad_scale_b = pullback(back_low(grad_pre, fc_in))
    grad_hidden = grad_hidden + grad_input
    grad_cross = grad_hidden.astype(jnp.bfloat16)
    g_cross_out = weight_grad(cross_flat, grad_cross)
    g_cross_bo = bias_grad(grad_cross)
    grad_cross_o = heads_of(back_low(grad_cross, cross_out).astype(jnp.bfloat16), clip_dev)
    grad_cq, grad_ck, grad_cv = attend_backward(
        cross_query, cross_k, cross_v, key_mask, cross_lse, grad_cross_o
    )
    grad_cq = grad_cq.astype(jnp.bfloat16).reshape(clip_dev, frame_dev, patches, D)
    g_cross_q = weight_grad(cross_in, grad_cq)
    g_cross_bq = bias_grad(grad_cq)
    grad_hidden = grad_hidden + back_low(grad_cq, cross_q)
    grad_cv = grad_cv.reshape(clip_dev, L_CAP, D)
    grad_ckv = jnp.concatenate([grad_ck.reshape(clip_dev, L_CAP, D), grad_cv], -1)
    g_cross_kv = weight_split(cap_rows, grad_ckv)
    g_cross_bv = bias_grad(grad_cv)
    grad_cap_rows = back_split(grad_ckv, cross_kv)
    grad_time = (grad_hidden * mod_row(2)).astype(jnp.bfloat16)
    g_time_out = weight_grad(time_flat, grad_time)
    g_time_bo = bias_grad(grad_time)
    grad_time_o = lax.all_to_all(
        back_low(grad_time, time_out).astype(jnp.bfloat16),
        "frame",
        split_axis=2,
        concat_axis=1,
        tiled=True,
    )
    grad_time_o = heads_of(jnp.swapaxes(grad_time_o, 1, 2), clip_dev * local_pos)
    grad_tq, grad_tk, grad_tv = attend_backward(time_q, time_k, time_v, None, time_lse, grad_time_o)
    grad_tqkv = jnp.concatenate(
        [
            piece.astype(jnp.bfloat16).reshape(clip_dev, local_pos, frames, D)
            for piece in (grad_tq, grad_tk, grad_tv)
        ],
        -1,
    )
    g_time_qkv = weight_grad(time_in, grad_tqkv)
    g_time_bq = bias_grad(grad_tqkv[..., :D])
    g_time_bv = bias_grad(grad_tqkv[..., 2 * D :])
    grad_tqkv = lax.all_to_all(
        jnp.swapaxes(grad_tqkv, 1, 2), "frame", split_axis=1, concat_axis=2, tiled=True
    )
    grad_gate_a = jnp.sum(grad_hidden * time_res, (1, 2))
    grad_hidden = grad_hidden + back_low(grad_tqkv, time_qkv)
    grad_gate_a = grad_gate_a + jnp.sum(grad_hidden * space_res, (1, 2))
    grad_space = (grad_hidden * mod_row(2)).astype(jnp.bfloat16)
    g_space_out = weight_grad(space_flat, grad_space)
    g_space_bo = bias_grad(grad_space)
    grad_space_o = heads_of(
        back_low(grad_space, space_out).astype(jnp.bfloat16), clip_dev * frame_dev
    )
    grad_sq, grad_sk, grad_sv = attend_backward(
        space_q, space_k, space_v, None, space_lse, grad_space_o
    )
    grad_sqkv = jnp.concatenate(
        [
            piece.astype(jnp.bfloat16).reshape(clip_dev, frame_dev, patches, D)
            for piece in (grad_sq, grad_sk, grad_sv)
        ],
        -1,
    )
    g_space_qkv = weight_grad(space_in, grad_sqkv)
    g_space_bq = bias_grad(grad_sqkv[..., :D])
    g_space_bv = bias_grad(grad_sqkv[..., 2 * D :])
    attend_owned = reduce_group(
        flatten_all(
            [g_space_qkv, g_space_out, g_time_qkv, g_time_out, g_cross_q, g_cross_kv, g_cross_out]
        )
    )
    unused, pullback = jax.vjp(modulate, hidden_zero, mod_row(0), mod_row(1))
    grad_input, grad_shift_a, grad_scale_a = pullback(back_low(grad_sqkv, space_qkv))
    grad_hidden = grad_hidden + grad_input
    g_patch_w = weight_split(noisy, grad_hidden)
    g_patch_b = bias_grad(grad_hidden)
    grad_mods = jnp.stack(
        [
            grad_shift_a.reshape(clip_dev, D),
            grad_scale_a.reshape(clip_dev, D),
            grad_gate_a,
            grad_shift_b.reshape(clip_dev, D),
            grad_scale_b.reshape(clip_dev, D),
            grad_gate_b,
        ],
        1,
    )
    g_table = jnp.sum(grad_mods, 0)
    grad_zero = grad_mods.reshape(clip_dev, 6 * D)
    g_block_b = jnp.sum(grad_zero, 0)
    g_block_w = weight_split(silu_time, grad_zero)
    unused, pullback = jax.vjp(jax.nn.silu, time_embed)
    grad_time_embed = grad_time_embed + pullback(back_split(grad_zero, block_w))[0]
    g_time_b2 = jnp.sum(grad_time_embed, 0)
    g_time_two = weight_split(act_one, grad_time_embed)
    unused, pullback = jax.vjp(jax.nn.silu, pre_one)
    grad_pre_one = pullback(back_split(grad_time_embed, time_two))[0]
    g_time_b1 = jnp.sum(grad_pre_one, 0)
    g_time_one = weight_split(freq_in, grad_pre_one)
    g_cap_b2 = bias_grad(grad_cap_rows)
    g_cap_two = weight_split(cap_act, grad_cap_rows)
    unused, pullback = jax.vjp(gelu_tanh, cap_pre)
    grad_cap_pre = pullback(back_split(grad_cap_rows, cap_two))[0]
    g_cap_b1 = bias_grad(grad_cap_pre)
    g_cap_one = weight_split(cap_in, grad_cap_pre)
    grad_cap_in = back_split(grad_cap_pre, cap_one)
    g_null = jnp.sum(jnp.where(is_null[:, None, None], grad_cap_in, 0.0), 0)
    embed_owned = reduce_group(
        flatten_all(
            [g_patch_w, g_time_one, g_time_two, g_block_w, g_cap_one, g_cap_two, g_final_w, g_null]
        )
    )
    vector_grad = flatten_all(
        [
            g_patch_b,
            g_time_b1,
            g_time_b2,
            g_block_b,
            g_cap_b1,
            g_cap_b2,
            g_space_bq,
            g_space_bv,
            g_space_bo,
            g_time_bq,
            g_time_bv,
            g_time_bo,
            g_cross_bq,
            g_cross_bv,
            g_cross_bo,
            g_fc_in_b,
            g_fc_out_b,
            g_final_b,
            g_table,
            g_final_table,
        ]
    )
    vector_sum, loss_sum = lax.psum((vector_grad, local_loss), ("frame", "clip"))
    owned = (embed_owned, attend_owned, dense_owned)
    local_square = (
        sum((jnp.sum(shard_piece * shard_piece) for shard_piece in owned))
        + jnp.sum(vector_sum * vector_sum) / n_clip
    )
    grad_norm = jnp.sqrt(lax.psum(local_square, "clip"))
    factor = jnp.minimum(1.0, CLIP_LIMIT / (grad_norm + NORM_FLOOR))
    embed_r = adam_step(embed_w, owned[0], embed_m, embed_v, embed_e, factor)
    attend_r = adam_step(attend_w, owned[1], attend_m, attend_v, attend_e, factor)
    dense_r = adam_step(dense_w, owned[2], dense_m, dense_v, dense_e, factor)
    vector_r = adam_step(vector_w, vector_sum, vector_m, vector_v, vector_e, factor)
    return (
        loss_sum,
        weight_total,
        grad_norm,
        embed_r[0],
        attend_r[0],
        dense_r[0],
        vector_r[0],
        embed_r[1],
        attend_r[1],
        dense_r[1],
        vector_r[1],
        embed_r[2],
        attend_r[2],
        dense_r[2],
        vector_r[2],
        embed_r[3],
        attend_r[3],
        dense_r[3],
        vector_r[3],
    )


AXES = ("frame", "clip")
LANES = 128
LANE_TILES = D // LANES
EMB_PAD = 1856


X_SIZE, CORES, Z_SIZE, Y_SIZE = 2, 2, 4, 2
N_OWN = Z_SIZE * Y_SIZE
RING = [(0, 0), (1, 0), (2, 0), (3, 0), (3, 1), (2, 1), (1, 1), (0, 1)]
RING_CLIP = [z * Y_SIZE + y for z, y in RING]
CLIP_RING = [RING_CLIP.index(c) for c in range(N_OWN)]


def pairs(move):
    out = []
    for x in range(X_SIZE):
        for core in range(CORES):
            for z in range(Z_SIZE):
                for y in range(Y_SIZE):
                    to = move(x, core, z, y)
                    if to is not None:
                        rank = lambda a, b, c, d: (a * CORES + b) * N_OWN + c * Y_SIZE + d
                        out.append((rank(x, core, z, y), rank(*to)))
    return out


SWAP_X = pairs(lambda x, c, z, y: (1 - x, c, z, y))
SWAP_CORE = pairs(lambda x, c, z, y: (x, 1 - c, z, y))
SWAP_Y = pairs(lambda x, c, z, y: (x, c, z, 1 - y))
SWAP_Z1 = pairs(lambda x, c, z, y: (x, c, z ^ 1, y))
SWAP_Z2 = pairs(lambda x, c, z, y: (x, c, z ^ 2, y))


def shift(value, perm):
    return lax.ppermute(value, AXES, perm)


def sum_clips(value):
    for perm in (SWAP_Y, SWAP_Z1, SWAP_Z2):
        value = value + shift(value, perm)
    return value


def sum_frames(value):
    for perm in (SWAP_CORE, SWAP_X):
        value = value + shift(value, perm)
    return value


def shard_segments(matrices, n_rows):
    spans, offset = [], 0
    for name, rows, wide in matrices:
        spans.append((name, offset, rows, wide))
        offset += rows * wide
    out = []
    for owner in range(N_OWN):
        low, high = owner * n_rows, (owner + 1) * n_rows
        mine = []
        for name, start, rows, wide in spans:
            begin, end = max(low, start), min(high, start + rows * wide)
            if begin < end:
                mine.append((name, (begin - start) // wide, (end - begin) // wide, wide))
        out.append(mine)
    return out


ATTEND = [
    ("space_qkv", D, 3),
    ("space_out", D, 1),
    ("time_qkv", D, 3),
    ("time_out", D, 1),
    ("cross_q", D, 1),
    ("cross_kv", D, 2),
    ("cross_out", D, 1),
]
DENSE = [("fc_in", D, 4), ("fc_out", MLP, 1)]
ATTEND_ROWS = 13824 // N_OWN
DENSE_ROWS = 9216 // N_OWN
ATTEND_SEGS = shard_segments(ATTEND, ATTEND_ROWS)
DENSE_SEGS = shard_segments(DENSE, DENSE_ROWS)


def cast_table(segments, block):
    out = []
    for mine in segments:
        rows, offset = [], 0
        for name, first, count, wide in mine:
            for start in range(0, count * wide, block):
                rows.append((wide, offset + start // wide, count))
            offset += count * wide
        out.append(rows)
    return np.array(out, np.int32)


def step_table(segments, block, n_rows):
    out = []
    for mine in segments:
        rows, offset = [], 0
        for name, first, count, wide in mine:
            half = count // 2
            for start in range(0, count * wide, block):
                core, inner = divmod(start // wide, half)
                rows.append((wide, core * (n_rows // 2) + offset + inner, half))
            offset += half * wide
        out.append(rows)
    return np.array(out, np.int32)


CAST_BLOCK = 576
STEP_BLOCK = 288


def cast_kernel(widths, table, flat, out):
    block = pl.program_id(0)
    for wide in widths:
        count = CAST_BLOCK // wide

        @pl.when(table[block, 0] == wide)
        def _():
            for slab in range(wide):
                row = pl.multiple_of(table[block, 1] + slab * table[block, 2], 16)
                for tile in range(LANE_TILES):
                    piece = flat[pl.ds(LANE_TILES * slab + tile, count, stride=LANE_TILES * wide), :]
                    out[pl.ds(row, count), tile * LANES : (tile + 1) * LANES] = piece.astype(jnp.bfloat16)


def cast_shard(flat, table, widths, n_rows):
    units = CAST_BLOCK * LANE_TILES
    return pl.pallas_call(
        partial(cast_kernel, widths),
        grid_spec=pltpu.PrefetchScalarGridSpec(
            num_scalar_prefetch=1,
            grid=(n_rows // CAST_BLOCK,),
            in_specs=[pl.BlockSpec((units, LANES), lambda b, t: (b, 0))],
            out_specs=pl.BlockSpec((n_rows, D), lambda b, t: (0, 0)),
        ),
        out_shape=jax.ShapeDtypeStruct((n_rows, D), jnp.bfloat16),
        compiler_params=pltpu.CompilerParams(vmem_limit_bytes=40 * 1024 * 1024),
    )(table, flat.reshape(-1, LANES))


ROWS_AHEAD = 16


def rows_kernel(shift_ref, flat, out, held, sem):
    units, count = flat.shape[0], out.shape[0]
    block = pl.program_id(0)

    @pl.when(block == 0)
    def _():
        end = (ROWS_AHEAD + units) // 8 * 8
        held[pl.ds(0, ROWS_AHEAD), :] = jnp.zeros((ROWS_AHEAD, LANES), jnp.float32)
        held[pl.ds(end, held.shape[0] - end), :] = jnp.zeros((held.shape[0] - end, LANES), jnp.float32)
        copy = pltpu.make_async_copy(flat, held.at[pl.ds(ROWS_AHEAD, units)], sem)
        copy.start()
        copy.wait()

    begin = ROWS_AHEAD + block * (count * LANE_TILES) - shift_ref[0]
    for tile in range(LANE_TILES):
        piece = held[pl.ds(begin + tile, count, stride=LANE_TILES), :]
        out[:, tile * LANES : (tile + 1) * LANES] = piece.astype(out.dtype)


def flat_to_rows(flat, rows, shift, dtype):
    block = rows // 4
    return pl.pallas_call(
        rows_kernel,
        grid_spec=pltpu.PrefetchScalarGridSpec(
            num_scalar_prefetch=1,
            grid=(4,),
            in_specs=[pl.BlockSpec(memory_space=pl.ANY)],
            out_specs=pl.BlockSpec((block, D), lambda b, t: (b, 0)),
            scratch_shapes=[
                pltpu.VMEM((ROWS_AHEAD + rows * LANE_TILES + 8, LANES), jnp.float32),
                pltpu.SemaphoreType.DMA,
            ],
        ),
        out_shape=jax.ShapeDtypeStruct((rows, D), dtype),
        compiler_params=pltpu.CompilerParams(vmem_limit_bytes=32 * 1024 * 1024),
    )(shift.reshape(1), flat)


def flat_kernel(rows, out):
    count = rows.shape[0]
    for tile in range(LANE_TILES):
        out[pl.ds(tile, count, stride=LANE_TILES), :] = rows[:, tile * LANES : (tile + 1) * LANES]


def rows_to_flat(rows):
    block = rows.shape[0] // 4
    return pl.pallas_call(
        flat_kernel,
        grid=(4,),
        in_specs=[pl.BlockSpec((block, D), lambda b: (b, 0))],
        out_specs=pl.BlockSpec((block * LANE_TILES, LANES), lambda b: (b, 0)),
        out_shape=jax.ShapeDtypeStruct((rows.shape[0] * LANE_TILES, LANES), rows.dtype),
        compiler_params=pltpu.CompilerParams(vmem_limit_bytes=32 * 1024 * 1024),
    )(rows)


def ring_place(clip):
    return jnp.where(clip % 2 == 0, clip // 2, N_OWN - 1 - clip // 2)


def clip_at(place):
    return jnp.where(place < N_OWN // 2, 2 * place, 2 * N_OWN - 1 - 2 * place)


def partners(frame, clip):
    place = ring_place(clip)
    x, core = frame // CORES, frame % CORES
    return (
        {"clip": clip_at((place + 1) % N_OWN)},
        {"clip": clip_at((place + N_OWN - 1) % N_OWN)},
        {"frame": (1 - x) * CORES + core},
        {"frame": x * CORES + 1 - core},
    )


def greet(devices):
    barrier = pltpu.get_barrier_semaphore()
    for device in devices:
        pl.semaphore_signal(barrier, inc=1, device_id=device, device_id_type=pl.DeviceIdType.MESH)
    pl.semaphore_wait(barrier, len(devices))


def spread_kernel(groups, modes, *refs):
    n, m = len(groups), len(modes)
    counts = [len(shapes) for keep, shapes, stores, common in groups]
    refs = list(refs)
    take = lambda number: [refs.pop(0) for _ in range(number)]
    owns, given, outs, given_outs = take(n), take(m), take(sum(counts)), take(m)
    helds, sources, landings = take(n), take(m), take(m)
    load_sem, send_sem, recv_sem, out_sem, peer_sem, peer_send, peer_recv = refs
    frame, clip = lax.axis_index("frame"), lax.axis_index("clip")
    x, core = frame // CORES, frame % CORES
    place = ring_place(clip)
    right, left, over_x, other = partners(frame, clip)
    half = N_OWN // 2
    owners = [clip_at((place + N_OWN - k) % N_OWN) for k in range(half + 1)]
    owners += [clip_at((place + k) % N_OWN) for k in range(1, half)]
    flip_x = (1 - x) * CORES + core
    mine = [core, frame, flip_x]
    theirs = [1 - core, x * CORES + 1 - core, (1 - x) * CORES + 1 - core]
    landing = mine + theirs

    def block_of(group, kinds, kind):
        return kinds[kind] + (2 if groups[group][3] and kind % 3 else 0)

    def held_at(group, slot):
        return helds[group].at[owners[slot] - min(groups[group][0])]

    def where_kept(group, slot, action):
        keep = groups[group][0]
        if len(keep) == N_OWN:
            action()
        else:
            pl.when(owners[slot] >= min(keep))(action)

    def load(group):
        return pltpu.make_async_copy(owns[group], held_at(group, 0), load_sem.at[group])

    def copy_of(group, slot, block, device, to_slot, kind):
        return pltpu.make_async_remote_copy(
            src_ref=held_at(group, slot).at[block],
            dst_ref=held_at(group, slot).at[block],
            send_sem=send_sem.at[group, to_slot, kind],
            recv_sem=recv_sem.at[group, to_slot, kind],
            device_id=device,
            device_id_type=pl.DeviceIdType.MESH,
        )

    sent = []

    def send(group, slot, from_kind, device, to_slot, kind):
        if from_kind == 0 and not groups[group][3]:
            return
        args = (group, slot, block_of(group, mine, from_kind), device, to_slot, kind)
        where_kept(group, slot, lambda: copy_of(*args).start())
        sent.append(args)

    def arrive(group, slot, kind):
        if kind % 3 == 0 and not groups[group][3]:
            return
        block = block_of(group, landing, kind)
        where_kept(group, slot, lambda: copy_of(group, slot, block, other, slot, kind).wait_recv())

    def onward(group, slot, kind):
        if slot < half:
            send(group, slot, kind, right, slot + 1, kind)
        if slot == 0:
            send(group, slot, kind, left, half + 1, kind)
        elif half < slot < N_OWN - 1:
            send(group, slot, kind, left, slot + 1, kind)

    def peer_load(item):
        return pltpu.make_async_copy(given[item], sources[item], peer_sem.at[item, 0])

    def peer_own(item):
        source = sources[item].at[clip] if modes[item] == "swap" else sources[item]
        return pltpu.make_async_copy(source, landings[item].at[clip], peer_sem.at[item, 1])

    def peer_copy(item, k):
        to = (clip + k) % N_OWN
        return pltpu.make_async_remote_copy(
            src_ref=sources[item].at[to] if modes[item] == "swap" else sources[item],
            dst_ref=landings[item].at[clip],
            send_sem=peer_send.at[item, k - 1],
            recv_sem=peer_recv.at[item, k - 1],
            device_id={"clip": to},
            device_id_type=pl.DeviceIdType.MESH,
        )

    def peers(item, arriving, action):
        for k in range(1, N_OWN):
            if modes[item] != "first":
                action(k)
            else:
                pl.when(clip == (k if arriving else 0))(lambda: action(k))

    for group in range(n):
        where_kept(group, 0, lambda: load(group).start())
    for item in range(m):
        peer_load(item).start()
    everyone = tuple({"clip": (clip + k) % N_OWN} for k in range(1, N_OWN)) if m else ()
    greet((right, left, over_x, other) + everyone)
    for group in range(n):
        where_kept(group, 0, lambda: load(group).wait())
        onward(group, 0, 1)
        onward(group, 0, 0)
    for item in range(m):
        peer_load(item).wait()
        peer_own(item).start()
        peers(item, False, lambda k: peer_copy(item, k).start())
    waiting = []
    for step in range(1, half + 1):
        slots = [step] + ([half + step] if step < half else [])
        pairs_now = [(group, slot) for group in range(n) for slot in slots]
        for group, slot in pairs_now:
            arrive(group, slot, 1)
            onward(group, slot, 1)
            send(group, slot, 1, over_x, slot, 2)
            send(group, slot, 1, other, slot, 4)
            arrive(group, slot, 0)
            onward(group, slot, 0)
            send(group, slot, 0, other, slot, 3)
        for group, slot in waiting:
            arrive(group, slot, 2)
            send(group, slot, 2, other, slot, 5)
        waiting = pairs_now
    for group, slot in waiting:
        arrive(group, slot, 2)
        send(group, slot, 2, other, slot, 5)
    for group in range(n):
        for slot in range(1, N_OWN):
            for kind in (3, 4, 5):
                arrive(group, slot, kind)
    done, base = [], 0
    for group, (keep, shapes, stores, common) in enumerate(groups):
        held = helds[group]
        rows = held.shape[2]
        for out, row, column, owner, first, count in stores:
            while count > 0:
                part, inner = divmod(first, rows)
                some = min(count, rows - inner)
                copy = pltpu.make_async_copy(
                    held.at[owner - min(keep), part, pl.ds(inner, some)],
                    outs[base + out].at[pl.ds(row, some), pl.ds(column, D)],
                    out_sem.at[len(done)],
                )
                copy.start()
                done.append(copy)
                first, row, count = first + some, row + some, count - some
        base += counts[group]
    for item in range(m):
        peer_own(item).wait()
        peers(item, True, lambda k: peer_copy(item, k).wait_recv())
        copy = pltpu.make_async_copy(landings[item], given_outs[item], peer_sem.at[item, 2])
        copy.start()
        done.append(copy)
    for item in range(m):
        peers(item, False, lambda k: peer_copy(item, k).wait_send())
    for args in sent:
        where_kept(args[0], args[1], lambda: copy_of(*args).wait_send())
    for copy in done:
        copy.wait()


def spread_shards(owns, groups, collective, given=()):
    spec = pl.BlockSpec(memory_space=pl.ANY)
    shapes = [shape for keep, some, stores, common in groups for shape in some]
    n_stores = sum(6 * len(stores) for keep, some, stores, common in groups)
    blocks = [6 if group[3] else 4 for group in groups]
    modes = [mode for value, mode in given]
    values = [value for value, mode in given]
    landed = [
        value.shape if mode == "swap" else (N_OWN,) + value.shape for value, mode in given
    ]
    many = max(len(given), 1)
    return pl.pallas_call(
        partial(spread_kernel, groups, modes),
        in_specs=[spec] * (len(owns) + len(given)),
        out_specs=[spec] * (len(shapes) + len(given)),
        out_shape=[jax.ShapeDtypeStruct(shape, jnp.bfloat16) for shape in shapes]
        + [jax.ShapeDtypeStruct(shape, value.dtype) for shape, value in zip(landed, values)],
        scratch_shapes=[
            pltpu.VMEM((len(group[0]), count, own.shape[0] // count, D), jnp.bfloat16)
            for own, group, count in zip(owns, groups, blocks)
        ]
        + [pltpu.VMEM(value.shape, value.dtype) for value in values]
        + [pltpu.VMEM(shape, value.dtype) for shape, value in zip(landed, values)]
        + [
            pltpu.SemaphoreType.DMA((len(owns),)),
            pltpu.SemaphoreType.DMA((len(owns), N_OWN, 6)),
            pltpu.SemaphoreType.DMA((len(owns), N_OWN, 6)),
            pltpu.SemaphoreType.DMA((n_stores,)),
            pltpu.SemaphoreType.DMA((many, 3)),
            pltpu.SemaphoreType.DMA((many, N_OWN - 1)),
            pltpu.SemaphoreType.DMA((many, N_OWN - 1)),
        ],
        compiler_params=pltpu.CompilerParams(
            collective_id=collective, has_side_effects=True, vmem_limit_bytes=50 * 1024 * 1024
        ),
        cost_estimate=pl.CostEstimate(
            flops=0, bytes_accessed=200 * 1000 * 1000, transcendentals=0
        ),
    )(*[own.reshape(count, own.shape[0] // count, D) for own, count in zip(owns, blocks)], *values)


LAG = 5


def collect_kernel(first, last, chunks, small, part, out, small_out, part_out, scratch):
    bufs, extra, locals_, finals, result = scratch[:2], scratch[2], scratch[3:5], scratch[5:7], scratch[7]
    ring_send, ring_recv, x_send, x_recv, end_send, end_recv, load_sem, own_sem = scratch[8:16]
    if small is not None:
        sums, arrived, small_send, small_recv = scratch[16:]
    if part is not None:
        frames, part_send, part_recv = scratch[16:]
    frame, clip = lax.axis_index("frame"), lax.axis_index("clip")
    x, core = frame // CORES, frame % CORES
    place = ring_place(clip)
    right, left, over_x, other = partners(frame, clip)
    swaps = [
        other,
        over_x,
        {"clip": clip + 1 - 2 * (clip % 2)},
        {"clip": clip + 2 - 4 * (clip // 2 % 2)},
        {"clip": clip + 4 - 8 * (clip // 4)},
    ]
    greet((right, left) + (tuple(swaps) if small is not None else (over_x, other)))
    f, l = first // 2, last // 2
    toward = (right, left)

    def owner(way, step):
        moved = N_OWN - 1 - step if way == 0 else 1 + step
        return clip_at((place + moved) % N_OWN)

    def f_rows(side, way):
        return pl.ds(pl.multiple_of(side * first + way * f, 8), f)

    def l_rows(way):
        return pl.ds(2 * first + way * l, l)

    def remote(src, dst, send_sem, recv_sem, device):
        return pltpu.make_async_remote_copy(
            src_ref=src,
            dst_ref=dst,
            send_sem=send_sem,
            recv_sem=recv_sem,
            device_id=device,
            device_id_type=pl.DeviceIdType.MESH,
        )

    def x_copy(way, step):
        return remote(
            chunks.at[owner(way, step), f_rows(1 - x, way)],
            extra.at[way, step],
            x_send.at[way, step],
            x_recv.at[way, step],
            over_x,
        )

    def load(kind, way, step):
        to = bufs[kind].at[way, 0] if step == 0 else locals_[kind].at[way, step % 2]
        rows = l_rows(way) if kind == 0 else f_rows(x, way)
        return pltpu.make_async_copy(
            chunks.at[owner(way, step), rows], to, load_sem.at[kind, way, step % 2]
        )

    def ring_copy(kind, way, step):
        return remote(
            bufs[kind].at[way, step],
            bufs[kind].at[way, step + 1],
            ring_send.at[kind, way, step],
            ring_recv.at[kind, way, step],
            toward[way],
        )

    def final_copy(kind, way):
        return remote(
            bufs[kind].at[way, N_OWN - 1],
            finals[kind].at[way],
            end_send.at[kind, way],
            end_recv.at[kind, way],
            over_x,
        )

    def small_copy(stage):
        return remote(
            sums.at[stage], arrived.at[stage], small_send.at[stage], small_recv.at[stage], swaps[stage]
        )

    flip_x = (1 - x) * CORES + core

    def part_copy(number, block=None):
        block = (frame, frame, flip_x)[number] if block is None else block
        return remote(
            frames.at[block],
            frames.at[block],
            part_send.at[number],
            part_recv.at[number],
            (over_x, other, other)[number],
        )

    def over_rows(start, count, work):
        def body(number, carry):
            work(pl.multiple_of(start + number * 8, 8))
            return carry

        lax.fori_loop(0, count // 8, body, 0)

    def small_load():
        return pltpu.make_async_copy(small, sums.at[0], own_sem.at[7])

    def part_load():
        return pltpu.make_async_copy(part, frames.at[frame], own_sem.at[7])

    for kind in range(2):
        for way in range(2):
            load(kind, way, 0).start()
    for way in range(2):
        x_copy(way, 0).start()
    if small is not None:
        small_load().start()
    if part is not None:
        part_load().start()

    def ring_step(kind, way, step):
        load(kind, way, step).wait()
        if step + 1 < N_OWN:
            load(kind, way, step + 1).start()
        if kind == 1:
            x_copy(way, step).wait_recv()
        if step > 0:
            ring_copy(kind, way, step - 1).wait_recv()
        buf, local = bufs[kind], locals_[kind]

        def add(row):
            at = pl.ds(row, 8)
            total = buf[way, step, at]
            if kind == 1:
                total = total + extra[way, step, at]
            if step > 0:
                total = total + local[way, step % 2, at]
            buf[way, step, at] = total

        if kind == 1 or step > 0:
            over_rows(0, f if kind == 1 else l, add)
        if step + 1 < N_OWN:
            ring_copy(kind, way, step).start()
        else:
            final_copy(kind, way).start()

    def own_half(kind):
        return pl.ds(2 * first, last) if kind == 0 else pl.ds(0, 2 * first)

    def core_swap(kind, to):
        return remote(
            result.at[own_half(kind)],
            out.at[to, own_half(kind)],
            own_sem.at[kind],
            own_sem.at[2 + kind],
            other,
        )

    def own_store(kind):
        return pltpu.make_async_copy(
            result.at[own_half(kind)], out.at[core, own_half(kind)], own_sem.at[4 + kind]
        )

    def finish(kind):
        for way in range(2):
            final_copy(kind, way).wait_recv()
            buf, final = bufs[kind], finals[kind]

            def put(row):
                at = pl.ds(row, 8)
                if kind == 0:
                    to = pl.multiple_of(2 * first + way * l + row, 8)
                    result[pl.ds(to, 8)] = buf[way, N_OWN - 1, at] + final[way, at]
                else:
                    to = pl.multiple_of(x * first + way * f + row, 8)
                    back = pl.multiple_of((1 - x) * first + way * f + row, 8)
                    result[pl.ds(to, 8)] = buf[way, N_OWN - 1, at]
                    result[pl.ds(back, 8)] = final[way, at]

            over_rows(0, l if kind == 0 else f, put)
        core_swap(kind, core).start()
        own_store(kind).start()

    for tick in range(N_OWN + LAG):
        if small is not None and tick < len(swaps) + 1:
            if tick == 0:
                small_load().wait()
            else:
                small_copy(tick - 1).wait_recv()

                def add_small(row):
                    at = pl.ds(row, 8)
                    sums[tick, at] = sums[tick - 1, at] + arrived[tick - 1, at]

                over_rows(0, small.shape[0], add_small)
            if tick < len(swaps):
                small_copy(tick).start()
        if 0 < tick < N_OWN:
            for way in range(2):
                x_copy(way, tick).start()
        if part is not None and tick == N_OWN - 1:
            part_load().wait()
            part_copy(0).start()
            part_copy(1).start()
        for way in range(2):
            if tick < N_OWN:
                ring_step(0, way, tick)
            if tick >= LAG:
                ring_step(1, way, tick - LAG)
    if small is not None:
        small_store = pltpu.make_async_copy(sums.at[len(swaps)], small_out, own_sem.at[6])
        small_store.start()
    finish(0)
    if part is not None:
        part_copy(0, flip_x).wait_recv()
        part_copy(2).start()
    finish(1)
    if part is not None:
        part_copy(1, x * CORES + 1 - core).wait_recv()
        part_copy(2, (1 - x) * CORES + 1 - core).wait_recv()
        part_store = pltpu.make_async_copy(frames, part_out, own_sem.at[6])
        part_store.start()
        part_store.wait()
        for number in range(3):
            part_copy(number).wait_send()
    if small is not None:
        small_store.wait()
        for stage in range(len(swaps)):
            small_copy(stage).wait_send()
    for way in range(2):
        for step in range(N_OWN):
            x_copy(way, step).wait_send()
    for kind in range(2):
        for way in range(2):
            for step in range(N_OWN - 1):
                ring_copy(kind, way, step).wait_send()
            final_copy(kind, way).wait_send()
        core_swap(kind, 1 - core).wait_recv()
        core_swap(kind, core).wait_send()
        own_store(kind).wait()


def collect_shard(chunks, first, collective, small=None, part=None):
    rows = chunks.shape[1]
    last = rows - 2 * first
    spec = pl.BlockSpec(memory_space=pl.ANY)
    out_shape = [jax.ShapeDtypeStruct((2, rows, D), jnp.float32)]
    beside = small if part is None else part
    if part is None:
        out_shape.append(jax.ShapeDtypeStruct(small.shape, jnp.float32))
        more = [
            pltpu.VMEM((6,) + small.shape, jnp.float32),
            pltpu.VMEM((5,) + small.shape, jnp.float32),
            pltpu.SemaphoreType.DMA((5,)),
            pltpu.SemaphoreType.DMA((5,)),
        ]
    else:
        out_shape.append(jax.ShapeDtypeStruct((4,) + part.shape, jnp.float32))
        more = [
            pltpu.VMEM((4,) + part.shape, jnp.float32),
            pltpu.SemaphoreType.DMA((3,)),
            pltpu.SemaphoreType.DMA((3,)),
        ]

    def kernel(chunks, beside, out, beside_out, *scratch):
        if part is None:
            collect_kernel(first, last, chunks, beside, None, out, beside_out, None, scratch)
        else:
            collect_kernel(first, last, chunks, None, beside, out, None, beside_out, scratch)

    return pl.pallas_call(
        kernel,
        in_specs=[spec] * 2,
        out_specs=[spec] * 2,
        out_shape=out_shape,
        scratch_shapes=[
            pltpu.VMEM((2, N_OWN, last // 2, D), jnp.float32),
            pltpu.VMEM((2, N_OWN, first // 2, D), jnp.float32),
            pltpu.VMEM((2, N_OWN, first // 2, D), jnp.float32),
            pltpu.VMEM((2, 2, last // 2, D), jnp.float32),
            pltpu.VMEM((2, 2, first // 2, D), jnp.float32),
            pltpu.VMEM((2, last // 2, D), jnp.float32),
            pltpu.VMEM((2, first // 2, D), jnp.float32),
            pltpu.VMEM((rows, D), jnp.float32),
            pltpu.SemaphoreType.DMA((2, 2, N_OWN)),
            pltpu.SemaphoreType.DMA((2, 2, N_OWN)),
            pltpu.SemaphoreType.DMA((2, N_OWN)),
            pltpu.SemaphoreType.DMA((2, N_OWN)),
            pltpu.SemaphoreType.DMA((2, 2)),
            pltpu.SemaphoreType.DMA((2, 2)),
            pltpu.SemaphoreType.DMA((2, 2, 2)),
            pltpu.SemaphoreType.DMA((8,)),
        ]
        + more,
        compiler_params=pltpu.CompilerParams(
            collective_id=collective, has_side_effects=True, vmem_limit_bytes=58 * 1024 * 1024
        ),
        cost_estimate=pl.CostEstimate(
            flops=0, bytes_accessed=800 * 1000 * 1000, transcendentals=0
        ),
    )(chunks, beside)


def matrix_plan(matrices, segments):
    shapes = [(rows, wide * D) for name, rows, wide in matrices]
    names = [name for name, rows, wide in matrices]
    stores = []
    for owner in range(N_OWN):
        offset = 0
        for name, first, count, wide in segments[owner]:
            for j in range(wide):
                stores.append((names.index(name), first, j * D, owner, offset, count))
                offset += count
    return shapes, stores


GRAD_COLUMNS = 384


def grad_plan(matrices, segments, lefts, rights):
    squares = {}
    for owner in range(N_OWN):
        row = 0
        for name, first, count, wide in segments[owner]:
            for j in range(wide):
                block, inner = divmod(first, D)
                piece = (inner, count // 2, owner, row)
                squares.setdefault((name, block, j), []).append(piece)
                row += count // 2
    plan = []
    for name, rows, wide in matrices:
        for block in range(rows // D):
            for j in range(wide):
                right, column = rights[name][j]
                plan.append((lefts[name], block * D, right, column, squares[name, block, j]))
    return plan


def grad_kernel(plan, parts, n_left, core_ref, *refs):
    n_in = sum(parts)
    ins, out = refs[:n_in], refs[n_in]
    left_buf, right_buf, made, left_sem, right_sem, out_sem = refs[n_in + 1 :]
    core = core_ref[0]
    place = [sum(parts[:k]) for k in range(len(parts))]

    def left_copies(square, slot):
        left, row = square[:2]
        return [
            pltpu.make_async_copy(
                ins[place[left] + part].at[pl.ds(row, D)],
                left_buf.at[slot, part, :, pl.ds(0, ins[place[left]].shape[1])],
                left_sem.at[slot, part],
            )
            for part in range(parts[left])
        ]

    def right_copies(square, slot):
        right, column = n_left + square[2], square[3]
        return [
            pltpu.make_async_copy(
                ins[place[right] + part].at[:, pl.ds(column, D)],
                right_buf.at[slot, part, pl.ds(0, ins[place[right]].shape[0])],
                right_sem.at[slot, part],
            )
            for part in range(parts[right])
        ]

    def out_copies(number):
        row, copies = 0, []
        for k, (first, count, owner, to) in enumerate(plan[number][4]):
            copies.append(
                pltpu.make_async_copy(
                    made.at[number % 2, pl.ds(row, count)],
                    out.at[owner, pl.ds(to, count)],
                    out_sem.at[number % 2, k],
                )
            )
            row += count
        return copies

    slots = []
    for number, square in enumerate(plan):
        if number == 0:
            slots.append((0, True, 0, True))
            continue
        left, _, right, _ = slots[-1]
        new_left = square[:2] != plan[number - 1][:2]
        new_right = square[2:4] != plan[number - 1][2:4]
        slots.append((left ^ new_left, new_left, right ^ new_right, new_right))

    def operands(number):
        left, new_left, right, new_right = slots[number]
        copies = left_copies(plan[number], left) if new_left else []
        return copies + (right_copies(plan[number], right) if new_right else [])

    for copy in operands(0):
        copy.start()
    for number, square in enumerate(plan):
        for copy in operands(number):
            copy.wait()
        if number + 1 < len(plan):
            for copy in operands(number + 1):
                copy.start()
        if number >= 2:
            for copy in out_copies(number - 2):
                copy.wait()
        left, _, right, _ = slots[number]
        depth = ins[place[square[0]]].shape[1]

        def some_columns(step, carry):
            columns = pl.ds(pl.multiple_of(step * GRAD_COLUMNS, LANES), GRAD_COLUMNS)
            row = 0
            for first, count, owner, to in square[4]:
                rows = pl.ds(pl.multiple_of(first + core * count, 16), count)
                total = 0.0
                for part in range(parts[square[0]]):
                    total = total + jnp.dot(
                        left_buf[left, part, rows, :depth],
                        right_buf[right, part, :depth, columns],
                        preferred_element_type=jnp.float32,
                    )
                made[number % 2, row : row + count, columns] = total
                row += count
            return carry

        lax.fori_loop(0, D // GRAD_COLUMNS, some_columns, 0)
        for copy in out_copies(number):
            copy.start()
    for number in range(max(len(plan) - 2, 0), len(plan)):
        for copy in out_copies(number):
            copy.wait()


def core_chunks(plan, core, lefts, rights, n_rows):
    operands = list(lefts) + list(rights)
    parts = [len(arrays) for arrays in operands]
    tokens = max(arrays[0].shape[1] for arrays in lefts)
    spec = pl.BlockSpec(memory_space=pl.ANY)
    return pl.pallas_call(
        partial(grad_kernel, plan, parts, len(lefts)),
        in_specs=[pl.BlockSpec(memory_space=pltpu.SMEM)] + [spec] * sum(parts),
        out_specs=spec,
        out_shape=jax.ShapeDtypeStruct((N_OWN, n_rows // 2, D), jnp.float32),
        scratch_shapes=[
            pltpu.VMEM((2, 2, D, tokens), jnp.bfloat16),
            pltpu.VMEM((2, 2, tokens, D), jnp.bfloat16),
            pltpu.VMEM((2, D // 2, D), jnp.float32),
            pltpu.SemaphoreType.DMA((2, 2)),
            pltpu.SemaphoreType.DMA((2, 2)),
            pltpu.SemaphoreType.DMA((2, N_OWN)),
        ],
        compiler_params=pltpu.CompilerParams(vmem_limit_bytes=36 * 1024 * 1024),
    )(core.astype(jnp.int32).reshape(1), *[array for arrays in operands for array in arrays])


def step_values(master, grad, first, second, average):
    keep = min(AVERAGE_KEEP, (1.0 + STEP) / (10.0 + STEP))
    first = BETA_FIRST * first + (1.0 - BETA_FIRST) * grad
    second = BETA_SECOND * second + (1.0 - BETA_SECOND) * grad * grad
    moved = (
        first
        / (1.0 - BETA_FIRST**STEP)
        / (jnp.sqrt(second / (1.0 - BETA_SECOND**STEP)) + ADAM_FLOOR)
    )
    master = master - LEARN_RATE * (moved + WEIGHT_DECAY * master)
    return (master, first, second, keep * average + (1.0 - keep) * master)


STEP_ROWS = 144


def step_kernel(widths, table, factor, grad, *refs):
    olds, news, (shard, flat, sem) = refs[:4], refs[4:8], refs[8:]
    block = pl.program_id(0)

    @pl.when(block == 0)
    def _():
        copy = pltpu.make_async_copy(grad, shard, sem)
        copy.start()
        copy.wait()

    for wide in widths:
        count = STEP_BLOCK // wide

        @pl.when(table[block, 0] == wide)
        def _():
            for slab in range(wide):
                row = pl.multiple_of(table[block, 1] + slab * table[block, 2], 8)
                for tile in range(LANE_TILES):
                    flat[pl.ds(LANE_TILES * slab + tile, count, stride=LANE_TILES * wide), :] = shard[
                        pl.ds(row, count), tile * LANES : (tile + 1) * LANES
                    ]

    scale = factor[0]

    def some_rows(number, carry):
        at = pl.ds(pl.multiple_of(number * STEP_ROWS, 8), STEP_ROWS)
        old = [ref[at, :] for ref in olds]
        made = step_values(old[0], flat[at, :] * scale, old[1], old[2], old[3])
        for ref, value in zip(news, made):
            ref[at, :] = value
        return carry

    lax.fori_loop(0, STEP_BLOCK * LANE_TILES // STEP_ROWS, some_rows, 0)


def step_shard(grad, table, widths, n_rows, factor, olds):
    units = STEP_BLOCK * LANE_TILES
    block_spec = pl.BlockSpec((units, LANES), lambda b, t, f: (b, 0))
    flat_shape = jax.ShapeDtypeStruct((n_rows * LANE_TILES, LANES), jnp.float32)
    made = pl.pallas_call(
        partial(step_kernel, widths),
        grid_spec=pltpu.PrefetchScalarGridSpec(
            num_scalar_prefetch=2,
            grid=(n_rows // STEP_BLOCK,),
            in_specs=[pl.BlockSpec(memory_space=pl.ANY)] + [block_spec] * 4,
            out_specs=[block_spec] * 4,
            scratch_shapes=[
                pltpu.VMEM((n_rows, D), jnp.float32),
                pltpu.VMEM((units, LANES), jnp.float32),
                pltpu.SemaphoreType.DMA,
            ],
        ),
        out_shape=[flat_shape] * 4,
        compiler_params=pltpu.CompilerParams(vmem_limit_bytes=50 * 1024 * 1024),
    )(table, factor, grad, *[old.reshape(-1, LANES) for old in olds])
    return [value.reshape(-1) for value in made]


def head_span(head):
    width = D // HEADS
    start = head * width // LANES * LANES
    stop = -(-(head + 1) * width // LANES) * LANES
    lane = start + lax.broadcasted_iota(jnp.int32, (1, stop - start), 1)
    ones = (lane >= head * width) & (lane < (head + 1) * width)
    return slice(start, stop), ones.astype(jnp.float32).astype(jnp.bfloat16)


def dot_rows(left, right):
    return lax.dot_general(left, right, (((1,), (1,)), ((), ())), preferred_element_type=jnp.float32)


def dot_down(left, right):
    return lax.dot_general(left, right, (((0,), (0,)), ((), ())), preferred_element_type=jnp.float32)


def live_keys(mode, live, n_queries, n_keys):
    key = lax.broadcasted_iota(jnp.int32, (n_queries, n_keys), 1)
    if mode == "cross":
        return key < live[0]
    if mode == "all":
        return None
    query = lax.broadcasted_iota(jnp.int32, (n_queries, n_keys), 0)
    return query // mode == key // mode


def head_scores(queries, keys, valid):
    scores = dot_rows(queries, keys) * (D // HEADS) ** (-0.5)
    return scores if valid is None else jnp.where(valid, scores, MASKED_SCORE)


def heads_kernel(mode, live, queries, keys, values, out, log_total, total):
    n_queries, n_keys = queries.shape[0], keys.shape[0]
    valid = live_keys(mode, live, n_queries, n_keys)
    lane = lax.broadcasted_iota(jnp.int32, (1, LANES), 1)
    total[...] = jnp.zeros_like(total)
    log_total[...] = jnp.zeros_like(log_total)
    for head in range(HEADS):
        span, ones = head_span(head)
        scores = head_scores(queries[:, span], keys[:, span] * ones, valid)
        summit = jnp.max(scores, -1, keepdims=True)
        powers = jnp.exp(scores - summit)
        sums = jnp.sum(powers, -1, keepdims=True)
        probs = (powers / sums).astype(jnp.bfloat16)
        total[:, span] += jnp.dot(
            probs, values[:, span] * ones, preferred_element_type=jnp.float32
        )
        log_total[...] += jnp.where(lane == head, summit + jnp.log(sums), 0.0)
    out[...] = total[...].astype(jnp.bfloat16)


def heads_back_kernel(
    mode, live, queries, keys, values, log_total, grad_out, grad_q, grad_k, grad_v, sum_q, sum_k, sum_v
):
    n_queries, n_keys = queries.shape[0], keys.shape[0]
    valid = live_keys(mode, live, n_queries, n_keys)
    scale = (D // HEADS) ** (-0.5)
    block, last = pl.program_id(0), pl.num_programs(0) - 1
    sum_q[...] = jnp.zeros_like(sum_q)

    @pl.when((block == 0) | (mode != "cross"))
    def _():
        sum_k[...] = jnp.zeros_like(sum_k)
        sum_v[...] = jnp.zeros_like(sum_v)

    for head in range(HEADS):
        span, ones = head_span(head)
        some_keys = keys[:, span] * ones
        scores = head_scores(queries[:, span], some_keys, valid)
        probs = jnp.exp(scores - log_total[:, head : head + 1])
        grad_probs = dot_rows(grad_out[:, span], values[:, span] * ones)
        row = jnp.sum(probs * grad_probs, -1, keepdims=True)
        grad_scores = (probs * (grad_probs - row)).astype(jnp.bfloat16)
        sum_q[:, span] += jnp.dot(grad_scores, some_keys, preferred_element_type=jnp.float32)
        sum_k[:, span] += dot_down(grad_scores, queries[:, span] * ones)
        sum_v[:, span] += dot_down(probs.astype(jnp.bfloat16), grad_out[:, span] * ones)
    grad_q[...] = (sum_q[...] * scale).astype(grad_q.dtype)

    @pl.when((block == last) | (mode != "cross"))
    def _():
        grad_k[...] = (sum_k[...] * scale).astype(grad_k.dtype)
        grad_v[...] = sum_v[...].astype(grad_v.dtype)


HEAD_ROWS = 256


def heads_specs(mode, keys):
    own = pl.BlockSpec((HEAD_ROWS, D), lambda b: (b, 0))
    side = pl.BlockSpec((HEAD_ROWS, LANES), lambda b: (b, 0))
    shared = pl.BlockSpec(keys.shape, lambda b: (0, 0)) if mode == "cross" else own
    return own, side, shared


def heads_forward(mode, queries, keys, values, live):
    own, side, shared = heads_specs(mode, keys)
    n_keys = keys.shape[0] if mode == "cross" else HEAD_ROWS
    return pl.pallas_call(
        partial(heads_kernel, mode),
        grid=(queries.shape[0] // HEAD_ROWS,),
        in_specs=[pl.BlockSpec(memory_space=pltpu.SMEM), own, shared, shared],
        out_specs=[own, side],
        out_shape=[
            jax.ShapeDtypeStruct(queries.shape, jnp.bfloat16),
            jax.ShapeDtypeStruct((queries.shape[0], LANES), jnp.float32),
        ],
        scratch_shapes=[pltpu.VMEM((HEAD_ROWS, D), jnp.float32)],
        compiler_params=pltpu.CompilerParams(vmem_limit_bytes=32 * 1024 * 1024),
    )(live, queries, keys, values)


def heads_backward(mode, queries, keys, values, live, log_total, grad_out):
    own, side, shared = heads_specs(mode, keys)
    n_keys = keys.shape[0] if mode == "cross" else HEAD_ROWS
    kind = jnp.float32 if mode == "cross" else jnp.bfloat16
    return pl.pallas_call(
        partial(heads_back_kernel, mode),
        grid=(queries.shape[0] // HEAD_ROWS,),
        in_specs=[pl.BlockSpec(memory_space=pltpu.SMEM), own, shared, shared, side, own],
        out_specs=[own, shared, shared],
        out_shape=[
            jax.ShapeDtypeStruct(queries.shape, jnp.bfloat16),
            jax.ShapeDtypeStruct(keys.shape, kind),
            jax.ShapeDtypeStruct(keys.shape, kind),
        ],
        scratch_shapes=[
            pltpu.VMEM((HEAD_ROWS, D), jnp.float32),
            pltpu.VMEM((n_keys, D), jnp.float32),
            pltpu.VMEM((n_keys, D), jnp.float32),
        ],
        compiler_params=pltpu.CompilerParams(vmem_limit_bytes=40 * 1024 * 1024),
    )(live, queries, keys, values, log_total, grad_out)


ROW_TIME_ONE = PATCH_VALUES
ROW_TIME_TWO = ROW_TIME_ONE + TFREQ
ROW_BLOCK = ROW_TIME_TWO + D
ROW_CAP_ONE = ROW_BLOCK + 6 * D
ROW_CAP_TWO = ROW_CAP_ONE + CAPW
ROW_FINAL = ROW_CAP_TWO + D
ROW_NULL = ROW_FINAL + PATCH_VALUES
EMB_UNITS = 16158720 // LANES // N_OWN
EMB_FIRST = [EMB_UNITS * c // LANE_TILES for c in range(N_OWN)]
EMB_SHIFT = [EMB_UNITS * c % LANE_TILES for c in range(N_OWN)]


def two_parts(product, value):
    both = product(jnp.concatenate(halves(value), 0))
    return both[: value.shape[0]] + both[value.shape[0] :]


def shards_block(
    latents,
    noise,
    timesteps,
    captions,
    cap_lengths,
    null_flags,
    sample_weight,
    embed_w,
    attend_w,
    dense_w,
    vector_w,
    embed_m,
    attend_m,
    dense_m,
    vector_m,
    embed_v,
    attend_v,
    dense_v,
    vector_v,
    embed_e,
    attend_e,
    dense_e,
    vector_e,
):
    clip_dev, frame_dev, patches = (latents.shape[0], latents.shape[1], latents.shape[2])
    n_frame = lax.axis_size("frame")
    n_clip = lax.axis_size("clip")
    local_pos = patches // n_frame
    tokens = frame_dev * patches
    frame_id = lax.axis_index("frame")
    clip_id = lax.axis_index("clip")
    x_id, core_id = frame_id // CORES, frame_id % CORES
    z_id, y_id = clip_id // Y_SIZE, clip_id % Y_SIZE

    emb_first = jnp.asarray(EMB_FIRST, jnp.int32)[clip_id]
    emb_shift = jnp.asarray(EMB_SHIFT, jnp.int32)[clip_id]
    emb_rows = flat_to_rows(embed_w.reshape(-1, LANES), EMB_PAD, emb_shift, jnp.bfloat16)
    dense_cast = cast_shard(
        dense_w, jnp.asarray(cast_table(DENSE_SEGS, CAST_BLOCK))[clip_id], (1, 4), DENSE_ROWS
    )
    cap_owners = range(4, N_OWN)
    cap_plan = (
        [(EMB_PAD * len(cap_owners), D)],
        [(0, EMB_PAD * k, 0, owner, 0, EMB_PAD) for k, owner in enumerate(cap_owners)],
    )
    own_clip = jnp.arange(n_clip) == clip_id
    facts = jnp.stack([timesteps.astype(jnp.float32)[0], sample_weight[0], null_flags.astype(jnp.float32)[0]])
    facts = jnp.broadcast_to(jnp.pad(facts, (0, LANES - 3))[None], (8, LANES))
    cap_weights, fc_in, fc_out, facts = spread_shards(
        [emb_rows, dense_cast],
        [(cap_owners,) + cap_plan + (False,), (range(N_OWN),) + matrix_plan(DENSE, DENSE_SEGS) + (True,)],
        2,
        given=[(facts, "gather")],
    )
    facts = facts[:, 0, :3]
    last = N_OWN - 1
    cap_last = cap_weights[EMB_PAD * (len(cap_owners) - 1) :]
    null_end = 16158720 - ROW_NULL * D
    null_first, final_first = ROW_NULL - EMB_FIRST[last], ROW_FINAL - EMB_FIRST[last]
    null_caption = (
        cap_last[null_first : null_first - (-null_end // D)]
        .reshape(-1)[:null_end]
        .reshape(L_CAP, CAPW)
    )
    final_w = cap_last[final_first : final_first + PATCH_VALUES].reshape(D, PATCH_VALUES)
    two_first = ROW_CAP_TWO - EMB_FIRST[last]

    def to_cap_rows(value):
        padded = jnp.pad(value, ((0, 0), (EMB_PAD, EMB_PAD)))
        starts = [EMB_FIRST[owner] - ROW_CAP_ONE + EMB_PAD for owner in cap_owners]
        return jnp.concatenate([padded[:, start : start + EMB_PAD] for start in starts], 1)

    def from_cap_rows(value):
        total = 0.0
        for k, owner in enumerate(cap_owners):
            start = EMB_FIRST[owner] - ROW_CAP_ONE
            low, high = max(0, -start), min(EMB_PAD, CAPW - start)
            part = value[:, EMB_PAD * k + low : EMB_PAD * k + high]
            total = total + jnp.pad(part, ((0, 0), (start + low, CAPW - start - high)))
        return total

    (
        patch_b,
        time_b1,
        time_b2,
        block_b,
        cap_b1,
        cap_b2,
        space_bq,
        space_bv,
        space_bo,
        time_bq,
        time_bv,
        time_bo,
        cross_bq,
        cross_bv,
        cross_bo,
        fc_in_b,
        fc_out_b,
        final_b,
        table,
        final_table,
    ) = split_flat(vector_w, vector_shapes())

    all_steps, all_null = facts[:, 0], facts[:, 2] == 1.0
    angle = (all_steps / 1000.0 + 0.008) / 1.008 * (math.pi / 2)
    signal = jnp.cos(angle) ** 2
    ratio = signal / (1.0 - signal)
    all_weights = facts[:, 1] * jnp.minimum(ratio, SNR_LIMIT) / ratio
    weight_total = jnp.sum(all_weights)
    signal = lax.dynamic_slice_in_dim(signal, clip_id, 1, 0)
    loss_weight = lax.dynamic_slice_in_dim(all_weights, clip_id, 1, 0)

    freq_in = sincos(all_steps, TFREQ).astype(jnp.bfloat16)
    at_start = clip_id == 0
    time_one = emb_rows[ROW_TIME_ONE:ROW_TIME_TWO]
    time_two = emb_rows[ROW_TIME_TWO:ROW_BLOCK]
    pre_one = matmul_low(freq_in, time_one) + time_b1
    act_one = jax.nn.silu(pre_one).astype(jnp.bfloat16)
    time_embed = matmul_low(act_one, time_two) + time_b2
    early = jnp.concatenate(
        [pre_one, time_embed, emb_rows[:ROW_TIME_ONE].astype(jnp.float32)], 0
    )
    is_null = null_flags == 1
    cap_in = jnp.where(is_null[:, None, None], null_caption[None], captions)
    cap_pre = (matmul_low(to_cap_rows(cap_in[0]), cap_weights) + cap_b1)[None]
    cap_act = gelu_tanh(cap_pre).astype(jnp.bfloat16)
    act_rows = jnp.pad(cap_act[0], ((0, 0), (two_first, EMB_PAD - two_first - D)))
    cap_rows = (matmul_low(act_rows, cap_last) + cap_b2).astype(jnp.bfloat16)[None]
    live_len = jnp.where(is_null, L_CAP, cap_lengths)
    cap_wide = jnp.concatenate([cap_in[0], cap_act[0]], -1)
    cap_wide = jnp.pad(cap_wide, ((0, 0), (EMB_PAD, EMB_PAD)))
    wanted = []
    for owner in range(n_clip):
        start = EMB_FIRST[owner] - ROW_CAP_ONE + EMB_PAD
        if start + EMB_PAD <= EMB_PAD:
            wanted.append(jnp.zeros((L_CAP, EMB_PAD // 4), jnp.bfloat16))
        else:
            wanted.append(
                lax.dynamic_slice_in_dim(cap_wide, start + frame_id * (EMB_PAD // 4), EMB_PAD // 4, 1)
            )
    attend_cast = cast_shard(
        attend_w, jnp.asarray(cast_table(ATTEND_SEGS, CAST_BLOCK))[clip_id], (1, 2, 3), ATTEND_ROWS
    )
    space_qkv, space_out, time_qkv, time_out, cross_q, cross_kv, cross_out, early, cap_left = spread_shards(
        [attend_cast],
        [(range(N_OWN),) + matrix_plan(ATTEND, ATTEND_SEGS) + (True,)],
        1,
        given=[(early, "first"), (jnp.pad(jnp.stack(wanted), ((0, 0), (0, 128 - L_CAP), (0, 0))), "swap")],
    )
    early = early[0]
    cap_left = cap_left[:, :L_CAP].reshape(n_clip * L_CAP, EMB_PAD // 4)
    pre_one, time_embed = early[:n_clip], early[n_clip : 2 * n_clip]
    patch_w = early[2 * n_clip :].astype(jnp.bfloat16)
    act_one = jax.nn.silu(pre_one).astype(jnp.bfloat16)
    silu_time = jax.nn.silu(time_embed).astype(jnp.bfloat16)
    local_row = emb_first + jnp.arange(EMB_PAD, dtype=jnp.int32)
    block_row = local_row - ROW_BLOCK
    in_block = (block_row >= 0) & (block_row < 6 * D)
    block_part = jnp.where(in_block, block_row % 6, -1)
    block_line = jnp.where(in_block, block_row // 6, -1)
    chooser = jnp.arange(D, dtype=jnp.int32)[:, None] == block_line[None]
    silu_rows = matmul_low(silu_time, chooser.astype(jnp.bfloat16)).astype(jnp.bfloat16)
    part_mask = jnp.arange(6, dtype=jnp.int32)[:, None] == block_part[None]
    block_left = jnp.where(part_mask[None], silu_rows[:, None], 0).reshape(n_clip * 6, EMB_PAD)
    block_out = sum_clips(matmul_low(block_left, emb_rows)).reshape(n_clip, 6, D)
    all_mods = table[None] + (block_out + block_b.reshape(6, D))
    mods = lax.dynamic_slice_in_dim(all_mods, clip_id, 1, 0)
    my_embed = lax.dynamic_slice_in_dim(time_embed, clip_id, 1, 0)

    keep_part = jnp.sqrt(signal)[:, None, None, None]
    fade_part = jnp.sqrt(1.0 - signal)[:, None, None, None]
    noisy = (keep_part * latents + fade_part * noise).astype(jnp.bfloat16)
    frame_ids = frame_id * frame_dev + jnp.arange(frame_dev)
    patch_ids = jnp.arange(patches)
    place = jnp.concatenate(
        [sincos(patch_ids // PGRID, D // 2), sincos(patch_ids % PGRID, D // 2)], -1
    )[None, None]
    hidden_zero = matmul_low(noisy, patch_w) + patch_b + place + sincos(frame_ids, D)[None, :, None]

    def mod_row(number):
        return mods[:, number][:, None, None, :]

    def flat2(value):
        return value.reshape(-1, value.shape[-1])

    space_in = modulate(hidden_zero, mod_row(0), mod_row(1)).astype(jnp.bfloat16)
    live = live_len.astype(jnp.int32)
    space_q, space_k, space_v = split_qkv(matmul_low(flat2(space_in), space_qkv), space_bq, space_bv)
    space_o, space_lse = heads_forward("all", space_q, space_k, space_v, live)
    space_flat = space_o.reshape(clip_dev, frame_dev, patches, D)
    space_res = matmul_low(space_flat, space_out) + space_bo
    hidden_one = hidden_zero + mod_row(2) * space_res
    time_in = lax.all_to_all(
        hidden_one.astype(jnp.bfloat16), "frame", split_axis=2, concat_axis=1, tiled=True
    )
    time_in = jnp.swapaxes(time_in, 1, 2)
    frames = time_in.shape[2]
    time_q, time_k, time_v = split_qkv(matmul_low(flat2(time_in), time_qkv), time_bq, time_bv)
    time_o, time_lse = heads_forward(frames, time_q, time_k, time_v, live)
    time_back = jnp.swapaxes(time_o.reshape(clip_dev, local_pos, frames, D), 1, 2)
    time_flat = lax.all_to_all(time_back, "frame", split_axis=1, concat_axis=2, tiled=True)
    time_res = matmul_low(time_flat, time_out) + time_bo
    hidden_two = hidden_one + mod_row(2) * time_res
    cross_in = hidden_two.astype(jnp.bfloat16)
    cross_query = (matmul_low(flat2(cross_in), cross_q) + cross_bq).astype(jnp.bfloat16)
    cross_merged = matmul_low(jnp.pad(cap_rows[0], ((0, -L_CAP % 16), (0, 0))), cross_kv)
    cross_k = cross_merged[..., :D].astype(jnp.bfloat16)
    cross_v = (cross_merged[..., D:] + cross_bv).astype(jnp.bfloat16)
    cross_o, cross_lse = heads_forward("cross", cross_query, cross_k, cross_v, live)
    cross_flat = cross_o.reshape(clip_dev, frame_dev, patches, D)
    hidden_three = hidden_two + matmul_low(cross_flat, cross_out) + cross_bo
    dense_in = modulate(hidden_three, mod_row(3), mod_row(4)).astype(jnp.bfloat16)
    dense_pre = matmul_low(dense_in, fc_in) + fc_in_b
    dense_act = gelu_tanh(dense_pre).astype(jnp.bfloat16)
    dense_res = matmul_low(dense_act, fc_out) + fc_out_b
    hidden_four = hidden_three + mod_row(5) * dense_res
    final_mod = final_table[None] + my_embed[:, None, :]
    final_shift = final_mod[:, 0][:, None, None, :]
    final_scale = final_mod[:, 1][:, None, None, :]
    final_in = modulate(hidden_four, final_shift, final_scale).astype(jnp.bfloat16)
    predicted = matmul_low(final_in, final_w) + final_b
    miss = predicted - noise
    clip_error = jnp.sum(jnp.mean(miss * miss, -1), (1, 2))
    local_loss = jnp.sum(loss_weight * clip_error)

    def two_cores(value):
        return [value, shift(value, SWAP_CORE)]

    lefts = {
        label: two_cores(flat2(value).T)
        for label, value in (
            ("space_qkv", space_in),
            ("space_out", space_flat),
            ("time_qkv", time_in),
            ("time_out", time_flat),
            ("cross_q", cross_in),
            ("cross_out", cross_flat),
            ("fc_in", dense_in),
            ("fc_out", dense_act),
        )
    }

    def chunks_of(matrices, segments, rights, n_rows):
        arrays, where = [], {}
        for label, blocks in rights.items():
            where[label] = []
            for value, column in blocks:
                known = [k for k, other in enumerate(arrays) if other is value]
                if not known:
                    arrays.append(value)
                where[label].append((known[0] if known else len(arrays) - 1, column))
        order = {label: number for number, (label, rows, wide) in enumerate(matrices)}
        plan = grad_plan(matrices, segments, order, where)
        return core_chunks(plan, core_id, [lefts[label] for label in order], arrays, n_rows)

    grad_pred = (
        2.0 / miss.shape[-1] * (loss_weight / weight_total)[:, None, None, None] * miss
    ).astype(jnp.bfloat16)
    g_final_w = weight_grad(final_in, grad_pred)
    g_final_b = bias_grad(grad_pred)
    unused, pullback = jax.vjp(modulate, hidden_four, final_shift, final_scale)
    grad_hidden, grad_fshift, grad_fscale = pullback(back_low(grad_pred, final_w))
    grad_fmod = jnp.concatenate([grad_fshift.reshape(1, D), grad_fscale.reshape(1, D)], 0)
    grad_dense = (grad_hidden * mod_row(5)).astype(jnp.bfloat16)
    grad_gate_b = jnp.sum(grad_hidden * dense_res, (1, 2))
    dense_both = two_cores(flat2(grad_dense))
    g_fc_out_b = bias_grad(grad_dense)
    unused, pullback = jax.vjp(gelu_tanh, dense_pre)
    grad_pre = pullback(back_low(grad_dense, fc_out))[0].astype(jnp.bfloat16)
    pre_both = two_cores(flat2(grad_pre))
    dense_chunks = chunks_of(
        DENSE,
        DENSE_SEGS,
        {"fc_in": [(pre_both, j * D) for j in range(MLP // D)], "fc_out": [(dense_both, 0)]},
        DENSE_ROWS,
    )
    rights = {}
    g_fc_in_b = bias_grad(grad_pre)
    unused, pullback = jax.vjp(modulate, hidden_three, mod_row(3), mod_row(4))
    grad_input, grad_shift_b, grad_scale_b = pullback(back_low(grad_pre, fc_in))
    grad_hidden = grad_hidden + grad_input
    grad_cross = grad_hidden.astype(jnp.bfloat16)
    rights["cross_out"] = [(two_cores(flat2(grad_cross)), 0)]
    g_cross_bo = bias_grad(grad_cross)
    grad_cross_o = back_low(flat2(grad_cross), cross_out).astype(jnp.bfloat16)
    grad_cq, grad_ck, grad_cv = heads_backward(
        "cross", cross_query, cross_k, cross_v, live, cross_lse, grad_cross_o
    )
    grad_cq = grad_cq.reshape(clip_dev, frame_dev, patches, D)
    rights["cross_q"] = [(two_cores(flat2(grad_cq)), 0)]
    g_cross_bq = bias_grad(grad_cq)
    grad_hidden = grad_hidden + back_low(grad_cq, cross_q)
    grad_cv = grad_cv[:L_CAP]
    grad_ckv = jnp.concatenate([grad_ck[:L_CAP], grad_cv], -1)
    g_cross_bv = bias_grad(grad_cv)
    grad_ckv = grad_ckv + shift(grad_ckv, SWAP_CORE)
    pad_rows = lambda value: jnp.pad(value, ((0, -L_CAP % LANES), (0, 0)))
    cap_twice = pad_rows(cap_rows[0]).T
    lefts["cross_kv"] = [jnp.concatenate([cap_twice, cap_twice], 1)]
    ckv_parts = [jnp.concatenate([pad_rows(part) for part in halves(grad_ckv)], 0)]
    rights["cross_kv"] = [(ckv_parts, 0), (ckv_parts, D)]
    grad_ckv = grad_ckv + shift(grad_ckv, SWAP_X)
    grad_cap_rows = two_parts(lambda part: back_low(part, cross_kv), grad_ckv)

    grad_time = (grad_hidden * mod_row(2)).astype(jnp.bfloat16)
    rights["time_out"] = [(two_cores(flat2(grad_time)), 0)]
    g_time_bo = bias_grad(grad_time)
    grad_time_o = lax.all_to_all(
        back_low(grad_time, time_out).astype(jnp.bfloat16),
        "frame",
        split_axis=2,
        concat_axis=1,
        tiled=True,
    )
    grad_time_o = flat2(jnp.swapaxes(grad_time_o, 1, 2))
    grad_tqkv = [
        piece.reshape(clip_dev, local_pos, frames, D)
        for piece in heads_backward(frames, time_q, time_k, time_v, live, time_lse, grad_time_o)
    ]
    rights["time_qkv"] = [(two_cores(flat2(part)), 0) for part in grad_tqkv]
    g_time_bq = bias_grad(grad_tqkv[0])
    g_time_bv = bias_grad(grad_tqkv[2])
    grad_tqkv = lax.all_to_all(
        jnp.swapaxes(jnp.concatenate(grad_tqkv, -1), 1, 2), "frame", split_axis=1, concat_axis=2, tiled=True
    )
    grad_gate_a = jnp.sum(grad_hidden * time_res, (1, 2))
    grad_hidden = grad_hidden + back_low(grad_tqkv, time_qkv)
    grad_gate_a = grad_gate_a + jnp.sum(grad_hidden * space_res, (1, 2))
    grad_space = (grad_hidden * mod_row(2)).astype(jnp.bfloat16)
    rights["space_out"] = [(two_cores(flat2(grad_space)), 0)]
    g_space_bo = bias_grad(grad_space)
    grad_space_o = back_low(flat2(grad_space), space_out).astype(jnp.bfloat16)
    grad_sqkv = [
        piece.reshape(clip_dev, frame_dev, patches, D)
        for piece in heads_backward("all", space_q, space_k, space_v, live, space_lse, grad_space_o)
    ]
    rights["space_qkv"] = [(two_cores(flat2(part)), 0) for part in grad_sqkv]
    attend_chunks = chunks_of(ATTEND, ATTEND_SEGS, rights, ATTEND_ROWS)
    g_space_bq = bias_grad(grad_sqkv[0])
    g_space_bv = bias_grad(grad_sqkv[2])
    grad_sqkv = jnp.concatenate(grad_sqkv, -1)
    unused, pullback = jax.vjp(modulate, hidden_zero, mod_row(0), mod_row(1))
    grad_input, grad_shift_a, grad_scale_a = pullback(back_low(grad_sqkv, space_qkv))
    grad_hidden = grad_hidden + grad_input
    g_patch_w = weight_split(noisy, grad_hidden)
    g_patch_b = bias_grad(grad_hidden)
    grad_mods = jnp.concatenate(
        [
            grad_shift_a.reshape(clip_dev, D),
            grad_scale_a.reshape(clip_dev, D),
            grad_gate_a,
            grad_shift_b.reshape(clip_dev, D),
            grad_scale_b.reshape(clip_dev, D),
            grad_gate_b,
            grad_fmod,
        ],
        0,
    )

    unused, pullback = jax.vjp(gelu_tanh, cap_pre[0])
    grad_cap_act = two_parts(lambda part: back_low(part, cap_last), grad_cap_rows)
    grad_cap_pre = pullback(grad_cap_act[:, two_first : two_first + D])[0]
    cap_right = lax.all_gather(
        jnp.stack([grad_cap_pre, grad_cap_rows]), "clip", axis=1, tiled=True
    )
    null_sum = jnp.sum(jnp.where(all_null[:, None, None], cap_right[0].reshape(n_clip, L_CAP, D), 0.0), 0)
    g_cap_b1 = bias_grad(grad_cap_pre)
    g_cap_b2 = bias_grad(grad_cap_rows)

    once = frame_id == 0
    gathered_mods = jnp.where(own_clip[:, None, None], grad_mods[None], 0.0)
    ends = jnp.concatenate([g_final_b, local_loss.reshape(1)])
    vector_rows = [
        g_patch_b,
        jnp.where(once, g_cap_b1, 0.0),
        jnp.where(once, g_cap_b2, 0.0),
        g_space_bq,
        g_space_bv,
        g_space_bo,
        g_time_bq,
        g_time_bv,
        g_time_bo,
        g_cross_bq,
        g_cross_bv,
        g_cross_bo,
        g_fc_in_b.reshape(-1, D),
        g_fc_out_b,
        jnp.pad(ends, (0, D - ends.shape[0])),
    ]
    small = [gathered_mods.reshape(-1, D), g_patch_w, g_final_w.reshape(PATCH_VALUES, D)]
    small = small + [value.reshape(-1, D) for value in vector_rows]
    spare = -sum(value.shape[0] for value in small) % 8
    small = jnp.concatenate(small + [jnp.zeros((spare, D), jnp.float32)] * (spare > 0), 0)
    dense_grad, small = collect_shard(
        dense_chunks,
        144,
        3,
        small=small,
    )
    dense_grad = dense_grad.reshape(DENSE_ROWS, D)
    at = 8 * n_clip
    gathered_mods = small[:at].reshape(n_clip, 8, D)
    g_patch_w = small[at : at + PATCH_VALUES]
    g_final_w = small[at + PATCH_VALUES : at + 2 * PATCH_VALUES]
    rest = small[at + 2 * PATCH_VALUES :]
    n_whole = 12 + MLP // D + 1
    loss_sum = rest[n_whole, PATCH_VALUES]
    vector_grad = jnp.concatenate([rest[:n_whole].reshape(-1), rest[n_whole, :PATCH_VALUES]])

    grad_zero = gathered_mods[:, :6]
    grad_final = gathered_mods[:, 6:]
    zero_rows = grad_zero.reshape(n_clip * 6, D)
    back_rows = two_parts(lambda part: back_low(part, emb_rows), zero_rows)
    back_rows = jnp.sum(jnp.where(part_mask[None], back_rows.reshape(n_clip, 6, EMB_PAD), 0.0), 1)
    grad_silu = lax.dot_general(
        back_rows,
        chooser.astype(jnp.float32),
        (((1,), (1,)), ((), ())),
        precision=lax.Precision.HIGHEST,
        preferred_element_type=jnp.float32,
    )
    grad_silu = sum_clips(grad_silu)
    unused, pullback = jax.vjp(jax.nn.silu, time_embed)
    grad_embed = grad_final[:, 0] + grad_final[:, 1] + pullback(grad_silu)[0]
    grad_act = two_parts(lambda part: back_low(part, time_two), grad_embed)
    grad_act = sum_clips(jnp.where(at_start, grad_act, 0.0))
    unused, pullback = jax.vjp(jax.nn.silu, pre_one)
    grad_one = pullback(grad_act)[0]
    g_table = jnp.sum(grad_zero, 0)
    vector_sum = flatten_all(
        [
            vector_grad[:D],
            jnp.sum(grad_one, 0),
            jnp.sum(grad_embed, 0),
            g_table,
            vector_grad[D:],
            g_table,
            jnp.sum(grad_final, 0),
        ]
    )

    per = EMB_PAD // 4
    quarter_row = emb_first + frame_id * per + jnp.arange(per, dtype=jnp.int32)
    time_left = jnp.concatenate(
        [
            jnp.pad(freq_in, ((0, 0), (ROW_TIME_ONE, EMB_PAD - ROW_TIME_TWO))),
            jnp.pad(act_one, ((0, 0), (ROW_TIME_TWO, EMB_PAD - ROW_BLOCK))),
        ],
        0,
    )
    time_left = jnp.where(at_start, time_left, jnp.zeros_like(time_left))
    small_left = lax.dynamic_slice_in_dim(
        jnp.concatenate([time_left, block_left], 0), frame_id * per, per, 1
    )
    small_right = jnp.concatenate([grad_one, grad_embed, zero_rows], 0)
    first_kind = (quarter_row < ROW_CAP_TWO)[None]
    no_left = jnp.zeros_like(cap_left)
    g_null = from_cap_rows(two_parts(lambda part: back_low(part, cap_weights), null_sum))
    n_null = -(-null_end // D)
    n_known = -(-(2 * PATCH_VALUES + n_null) // 16) * 16
    null_rows = jnp.pad(g_null.reshape(-1), (0, (n_known - 2 * PATCH_VALUES) * D - null_end))
    known = jnp.concatenate([g_patch_w, g_final_w, null_rows.reshape(-1, D)], 0)
    known_row = np.concatenate(
        [np.arange(PATCH_VALUES), ROW_FINAL + np.arange(n_known - PATCH_VALUES)]
    ).astype(np.int32)
    known_left = (jnp.asarray(known_row)[:, None] == quarter_row[None]).astype(jnp.bfloat16)
    emb_left = jnp.concatenate(
        [
            small_left,
            jnp.where(first_kind, cap_left, no_left),
            jnp.where(first_kind, no_left, cap_left),
            known_left,
        ],
        0,
    )
    emb_right = jnp.concatenate([small_right, cap_right[0], cap_right[1], known], 0)
    emb_grad = weight_split(emb_left, emb_right)
    unit = (
        LANE_TILES * (frame_id * per + jnp.arange(per, dtype=jnp.int32))[:, None]
        + jnp.arange(D, dtype=jnp.int32)[None] // LANES
        - emb_shift
    )
    emb_grad = jnp.where((unit >= 0) & (unit < EMB_UNITS), emb_grad, 0.0)

    attend_grad, emb_whole = collect_shard(
        attend_chunks,
        176,
        4,
        part=emb_grad,
    )
    attend_grad = attend_grad.reshape(ATTEND_ROWS, D)
    local_square = sum(jnp.sum(value * value) for value in (dense_grad, attend_grad, emb_whole))
    vector_square = jnp.sum(vector_sum * vector_sum)
    grad_norm = jnp.sqrt(sum_clips(local_square.reshape(1))[0] + vector_square)
    factor = jnp.minimum(1.0, CLIP_LIMIT / (grad_norm + NORM_FLOOR))
    scale = factor.reshape(1)
    dense_r = step_shard(
        dense_grad,
        jnp.asarray(step_table(DENSE_SEGS, STEP_BLOCK, DENSE_ROWS))[clip_id],
        (1, 4),
        DENSE_ROWS,
        scale,
        (dense_w, dense_m, dense_v, dense_e),
    )
    attend_r = step_shard(
        attend_grad,
        jnp.asarray(step_table(ATTEND_SEGS, STEP_BLOCK, ATTEND_ROWS))[clip_id],
        (1, 2, 3),
        ATTEND_ROWS,
        scale,
        (attend_w, attend_m, attend_v, attend_e),
    )
    emb_flat = rows_to_flat(emb_whole.reshape(EMB_PAD, D))
    emb_owned = lax.dynamic_slice_in_dim(emb_flat, emb_shift, EMB_UNITS, 0).reshape(-1)
    embed_r = adam_step(embed_w, emb_owned, embed_m, embed_v, embed_e, factor)
    vector_r = adam_step(vector_w, vector_sum, vector_m, vector_v, vector_e, factor)
    return (
        loss_sum,
        weight_total,
        grad_norm,
        embed_r[0],
        attend_r[0],
        dense_r[0],
        vector_r[0],
        embed_r[1],
        attend_r[1],
        dense_r[1],
        vector_r[1],
        embed_r[2],
        attend_r[2],
        dense_r[2],
        vector_r[2],
        embed_r[3],
        attend_r[3],
        dense_r[3],
        vector_r[3],
    )


def pick_plan(mesh):
    if mesh.shape["frame"] == X_SIZE * CORES and mesh.shape["clip"] == N_OWN:
        return shards_block
    return shards


def solution(mesh):
    in_specs = (
        P("clip", "frame", None, None),
        P("clip", "frame", None, None),
        P("clip"),
        P("clip", None, None),
        P("clip"),
        P("clip"),
        P("clip"),
        P("clip"),
        P("clip"),
        P("clip"),
        P(),
        P("clip"),
        P("clip"),
        P("clip"),
        P(),
        P("clip"),
        P("clip"),
        P("clip"),
        P(),
        P("clip"),
        P("clip"),
        P("clip"),
        P(),
    )
    out_specs = (
        P(),
        P(),
        P(),
        P("clip"),
        P("clip"),
        P("clip"),
        P(),
        P("clip"),
        P("clip"),
        P("clip"),
        P(),
        P("clip"),
        P("clip"),
        P("clip"),
        P(),
        P("clip"),
        P("clip"),
        P("clip"),
        P(),
    )
    return jax.shard_map(pick_plan(mesh), mesh=mesh, in_specs=in_specs, out_specs=out_specs, check_vma=False)
```

```python
import math
from functools import partial

import jax
import jax.numpy as jnp
import numpy as np
from jax import lax
from jax.experimental import pallas as pl
from jax.experimental.pallas import tpu as pltpu
from jax.sharding import PartitionSpec as P

D = 1152
HEADS = 16
MLP = 4608
CAPW = 4096
L_CAP = 120
TFREQ = 256
PATCH_VALUES = 16
PGRID = 16
STEP = 10


NORM_FLOOR = 1e-06
CLIP_LIMIT = 1.0
SNR_LIMIT = 5.0
BETA_FIRST = 0.5
BETA_SECOND = 0.5
LEARN_RATE = 0.02
WEIGHT_DECAY = 0.01
ADAM_FLOOR = 1e-08
AVERAGE_KEEP = 0.9999
MASKED_SCORE = -1e30


def embed_shapes():
    return [
        (PATCH_VALUES, D),
        (TFREQ, D),
        (D, D),
        (D, 6 * D),
        (CAPW, D),
        (D, D),
        (D, PATCH_VALUES),
        (L_CAP, CAPW),
    ]


def attend_shapes():
    return [(D, 3 * D), (D, D), (D, 3 * D), (D, D), (D, D), (D, 2 * D), (D, D)]


def dense_shapes():
    return [(D, MLP), (MLP, D)]


def vector_shapes():
    return [(D,)] * 3 + [(6 * D,)] + [(D,)] * 11 + [(MLP,), (D,), (PATCH_VALUES,), (6, D), (2, D)]


def split_flat(flat, shapes):
    pieces = []
    offset = 0
    for extent in shapes:
        length = math.prod(extent)
        pieces.append(flat[offset : offset + length].reshape(extent))
        offset += length
    return pieces


def flatten_all(pieces):
    return jnp.concatenate([piece.reshape(-1) for piece in pieces])


def reduce_group(grad):
    n_clip = lax.axis_size("clip")
    n_frame = lax.axis_size("frame")
    reorder = grad.reshape(n_clip, n_frame, -1).swapaxes(0, 1).reshape(-1)
    share = lax.psum_scatter(reorder, ("frame", "clip"), scatter_dimension=0, tiled=True)
    return lax.all_gather(share, "frame", axis=0, tiled=True)


def sincos(places, width):
    half = width // 2
    omega = jnp.exp(-math.log(10000.0) * jnp.arange(half, dtype=jnp.float32) / half)
    angle = places.astype(jnp.float32)[..., None] * omega
    return jnp.concatenate([jnp.sin(angle), jnp.cos(angle)], -1)


def modulate(hidden, shift, scale):
    center = hidden - jnp.mean(hidden, -1, keepdims=True)
    normed = center * lax.rsqrt(jnp.mean(center * center, -1, keepdims=True) + NORM_FLOOR)
    return normed * (1.0 + scale) + shift


def gelu_tanh(value):
    return jax.nn.gelu(value, approximate=True)


def matmul_low(left, right):
    return lax.dot_general(
        left, right, (((left.ndim - 1,), (0,)), ((), ())), preferred_element_type=jnp.float32
    )


def halves(value):
    upper = lax.optimization_barrier(value.astype(jnp.bfloat16))
    return (upper, (value - upper.astype(jnp.float32)).astype(jnp.bfloat16))


def back_low(grads, weight):
    return lax.dot_general(
        grads, weight, (((grads.ndim - 1,), (1,)), ((), ())), preferred_element_type=jnp.float32
    )


def back_split(grads, weight):
    upper, lower = halves(grads)
    return back_low(upper, weight) + back_low(lower, weight)


def weight_grad(inputs, grads):
    left = inputs.reshape(-1, inputs.shape[-1])
    right = grads.reshape(-1, grads.shape[-1])
    return lax.dot_general(
        left, right, (((0,), (0,)), ((), ())), preferred_element_type=jnp.float32
    )


def weight_split(inputs, grads):
    upper, lower = halves(grads)
    return weight_grad(inputs, upper) + weight_grad(inputs, lower)


def bias_grad(grads):
    return jnp.sum(grads.astype(jnp.float32).reshape(-1, grads.shape[-1]), 0)


def heads_of(tensor, batch):
    return tensor.reshape(batch, -1, HEADS, tensor.shape[-1] // HEADS)


def split_qkv(merged, bias_q, bias_v):
    width = merged.shape[-1] // 3
    return (
        (merged[..., :width] + bias_q).astype(jnp.bfloat16),
        merged[..., width : 2 * width].astype(jnp.bfloat16),
        (merged[..., 2 * width :] + bias_v).astype(jnp.bfloat16),
    )


def attend_scores(queries, key_rows, mask):
    scores = jnp.einsum("bqhe,bkhe->bhqk", queries, key_rows, preferred_element_type=jnp.float32)
    scores = scores * queries.shape[-1] ** (-0.5)
    if mask is not None:
        scores = jnp.where(mask[:, None, None, :], scores, MASKED_SCORE)
    return scores


def attend_forward(queries, key_rows, values, mask):
    scores = attend_scores(queries, key_rows, mask)
    summit = jnp.max(scores, -1, keepdims=True)
    powers = jnp.exp(scores - summit)
    totals = jnp.sum(powers, -1, keepdims=True)
    probs = (powers / totals).astype(jnp.bfloat16)
    output = jnp.einsum("bhqk,bkhe->bqhe", probs, values, preferred_element_type=jnp.float32)
    return (output.astype(jnp.bfloat16), summit + jnp.log(totals))


def attend_backward(queries, key_rows, values, mask, log_total, grad_out):
    scale = queries.shape[-1] ** (-0.5)
    probs = jnp.exp(attend_scores(queries, key_rows, mask) - log_total)
    grad_probs = jnp.einsum("bqhe,bkhe->bhqk", grad_out, values, preferred_element_type=jnp.float32)
    grad_scores = (probs * (grad_probs - jnp.sum(probs * grad_probs, -1, keepdims=True))).astype(
        jnp.bfloat16
    )
    grad_query = (
        jnp.einsum("bhqk,bkhe->bqhe", grad_scores, key_rows, preferred_element_type=jnp.float32)
        * scale
    )
    grad_keys = (
        jnp.einsum("bhqk,bqhe->bkhe", grad_scores, queries, preferred_element_type=jnp.float32)
        * scale
    )
    grad_values = jnp.einsum(
        "bhqk,bqhe->bkhe", probs.astype(jnp.bfloat16), grad_out, preferred_element_type=jnp.float32
    )
    return (grad_query, grad_keys, grad_values)


def unpack_all(gathered):
    return (
        split_flat(gathered[0], embed_shapes()),
        split_flat(gathered[1], attend_shapes()),
        split_flat(gathered[2], dense_shapes()),
    )


def adam_step(master, grad, first, second, average, factor):
    keep = min(AVERAGE_KEEP, (1.0 + STEP) / (10.0 + STEP))
    grad = grad * factor
    first = BETA_FIRST * first + (1.0 - BETA_FIRST) * grad
    second = BETA_SECOND * second + (1.0 - BETA_SECOND) * grad * grad
    moved = (
        first
        / (1.0 - BETA_FIRST**STEP)
        / (jnp.sqrt(second / (1.0 - BETA_SECOND**STEP)) + ADAM_FLOOR)
    )
    master = master - LEARN_RATE * (moved + WEIGHT_DECAY * master)
    return (master, first, second, keep * average + (1.0 - keep) * master)


def shards(
    latents,
    noise,
    timesteps,
    captions,
    cap_lengths,
    null_flags,
    sample_weight,
    embed_w,
    attend_w,
    dense_w,
    vector_w,
    embed_m,
    attend_m,
    dense_m,
    vector_m,
    embed_v,
    attend_v,
    dense_v,
    vector_v,
    embed_e,
    attend_e,
    dense_e,
    vector_e,
):
    clip_dev, frame_dev, patches = (latents.shape[0], latents.shape[1], latents.shape[2])
    n_frame = lax.axis_size("frame")
    n_clip = lax.axis_size("clip")
    local_pos = patches // n_frame
    gathered = (
        lax.all_gather(embed_w.astype(jnp.bfloat16), "clip", axis=0, tiled=True),
        lax.all_gather(attend_w.astype(jnp.bfloat16), "clip", axis=0, tiled=True),
        lax.all_gather(dense_w.astype(jnp.bfloat16), "clip", axis=0, tiled=True),
    )
    embeds, attends, denses = unpack_all(gathered)
    patch_w, time_one, time_two, block_w, cap_one, cap_two, final_w, null_caption = embeds
    space_qkv, space_out, time_qkv, time_out, cross_q, cross_kv, cross_out = attends
    fc_in, fc_out = denses
    (
        patch_b,
        time_b1,
        time_b2,
        block_b,
        cap_b1,
        cap_b2,
        space_bq,
        space_bv,
        space_bo,
        time_bq,
        time_bv,
        time_bo,
        cross_bq,
        cross_bv,
        cross_bo,
        fc_in_b,
        fc_out_b,
        final_b,
        table,
        final_table,
    ) = split_flat(vector_w, vector_shapes())
    angle = (timesteps.astype(jnp.float32) / 1000.0 + 0.008) / 1.008 * (math.pi / 2)
    signal = jnp.cos(angle) ** 2
    ratio = signal / (1.0 - signal)
    loss_weight = sample_weight * jnp.minimum(ratio, SNR_LIMIT) / ratio
    weight_total = lax.psum(jnp.sum(loss_weight), "clip")
    keep_part = jnp.sqrt(signal)[:, None, None, None]
    fade_part = jnp.sqrt(1.0 - signal)[:, None, None, None]
    noisy = (keep_part * latents + fade_part * noise).astype(jnp.bfloat16)
    frame_ids = lax.axis_index("frame") * frame_dev + jnp.arange(frame_dev)
    patch_ids = jnp.arange(patches)
    place = jnp.concatenate(
        [sincos(patch_ids // PGRID, D // 2), sincos(patch_ids % PGRID, D // 2)], -1
    )[None, None]
    hidden_zero = matmul_low(noisy, patch_w) + patch_b + place + sincos(frame_ids, D)[None, :, None]
    freq_in = sincos(timesteps, TFREQ).astype(jnp.bfloat16)
    pre_one = matmul_low(freq_in, time_one) + time_b1
    act_one = jax.nn.silu(pre_one).astype(jnp.bfloat16)
    time_embed = matmul_low(act_one, time_two) + time_b2
    silu_time = jax.nn.silu(time_embed).astype(jnp.bfloat16)
    mods = table[None] + (matmul_low(silu_time, block_w) + block_b).reshape(clip_dev, 6, D)

    def mod_row(number):
        return mods[:, number][:, None, None, :]

    is_null = null_flags == 1
    cap_in = jnp.where(is_null[:, None, None], null_caption[None], captions)
    cap_pre = matmul_low(cap_in, cap_one) + cap_b1
    cap_act = gelu_tanh(cap_pre).astype(jnp.bfloat16)
    cap_rows = (matmul_low(cap_act, cap_two) + cap_b2).astype(jnp.bfloat16)
    live_len = jnp.where(is_null, L_CAP, cap_lengths)
    key_mask = jnp.arange(L_CAP)[None, :] < live_len[:, None]
    space_in = modulate(hidden_zero, mod_row(0), mod_row(1)).astype(jnp.bfloat16)
    space_q, space_k, space_v = (
        heads_of(piece, clip_dev * frame_dev)
        for piece in split_qkv(matmul_low(space_in, space_qkv), space_bq, space_bv)
    )
    space_o, space_lse = attend_forward(space_q, space_k, space_v, None)
    space_flat = space_o.reshape(clip_dev, frame_dev, patches, D)
    space_res = matmul_low(space_flat, space_out) + space_bo
    hidden_one = hidden_zero + mod_row(2) * space_res
    time_in = lax.all_to_all(
        hidden_one.astype(jnp.bfloat16), "frame", split_axis=2, concat_axis=1, tiled=True
    )
    time_in = jnp.swapaxes(time_in, 1, 2)
    frames = time_in.shape[2]
    time_q, time_k, time_v = (
        heads_of(piece, clip_dev * local_pos)
        for piece in split_qkv(matmul_low(time_in, time_qkv), time_bq, time_bv)
    )
    time_o, time_lse = attend_forward(time_q, time_k, time_v, None)
    time_back = jnp.swapaxes(time_o.reshape(clip_dev, local_pos, frames, D), 1, 2)
    time_flat = lax.all_to_all(time_back, "frame", split_axis=1, concat_axis=2, tiled=True)
    time_res = matmul_low(time_flat, time_out) + time_bo
    hidden_two = hidden_one + mod_row(2) * time_res
    cross_in = hidden_two.astype(jnp.bfloat16)
    cross_query = heads_of(
        (matmul_low(cross_in, cross_q) + cross_bq).astype(jnp.bfloat16), clip_dev
    )
    cross_merged = matmul_low(cap_rows, cross_kv)
    cross_k = heads_of(cross_merged[..., :D].astype(jnp.bfloat16), clip_dev)
    cross_v = heads_of((cross_merged[..., D:] + cross_bv).astype(jnp.bfloat16), clip_dev)
    cross_o, cross_lse = attend_forward(cross_query, cross_k, cross_v, key_mask)
    cross_flat = cross_o.reshape(clip_dev, frame_dev, patches, D)
    hidden_three = hidden_two + matmul_low(cross_flat, cross_out) + cross_bo
    dense_in = modulate(hidden_three, mod_row(3), mod_row(4)).astype(jnp.bfloat16)
    dense_pre = matmul_low(dense_in, fc_in) + fc_in_b
    dense_act = gelu_tanh(dense_pre).astype(jnp.bfloat16)
    dense_res = matmul_low(dense_act, fc_out) + fc_out_b
    hidden_four = hidden_three + mod_row(5) * dense_res
    final_mod = final_table[None] + time_embed[:, None, :]
    final_shift = final_mod[:, 0][:, None, None, :]
    final_scale = final_mod[:, 1][:, None, None, :]
    final_in = modulate(hidden_four, final_shift, final_scale).astype(jnp.bfloat16)
    predicted = matmul_low(final_in, final_w) + final_b
    miss = predicted - noise
    clip_error = jnp.sum(jnp.mean(miss * miss, -1), (1, 2))
    local_loss = jnp.sum(loss_weight * clip_error)
    grad_pred = (
        2.0 / miss.shape[-1] * (loss_weight / weight_total)[:, None, None, None] * miss
    ).astype(jnp.bfloat16)
    g_final_w = weight_grad(final_in, grad_pred)
    g_final_b = bias_grad(grad_pred)
    unused, pullback = jax.vjp(modulate, hidden_four, final_shift, final_scale)
    grad_hidden, grad_fshift, grad_fscale = pullback(back_low(grad_pred, final_w))
    grad_fmod = jnp.stack([grad_fshift.reshape(clip_dev, D), grad_fscale.reshape(clip_dev, D)], 1)
    g_final_table = jnp.sum(grad_fmod, 0)
    grad_time_embed = grad_fmod[:, 0] + grad_fmod[:, 1]
    grad_dense = (grad_hidden * mod_row(5)).astype(jnp.bfloat16)
    grad_gate_b = jnp.sum(grad_hidden * dense_res, (1, 2))
    g_fc_out = weight_grad(dense_act, grad_dense)
    g_fc_out_b = bias_grad(grad_dense)
    unused, pullback = jax.vjp(gelu_tanh, dense_pre)
    grad_pre = pullback(back_low(grad_dense, fc_out))[0].astype(jnp.bfloat16)
    g_fc_in = weight_grad(dense_in, grad_pre)
    g_fc_in_b = bias_grad(grad_pre)
    dense_owned = reduce_group(flatten_all([g_fc_in, g_fc_out]))
    unused, pullback = jax.vjp(modulate, hidden_three, mod_row(3), mod_row(4))
    grad_input, grad_shift_b, grad_scale_b = pullback(back_low(grad_pre, fc_in))
    grad_hidden = grad_hidden + grad_input
    grad_cross = grad_hidden.astype(jnp.bfloat16)
    g_cross_out = weight_grad(cross_flat, grad_cross)
    g_cross_bo = bias_grad(grad_cross)
    grad_cross_o = heads_of(back_low(grad_cross, cross_out).astype(jnp.bfloat16), clip_dev)
    grad_cq, grad_ck, grad_cv = attend_backward(
        cross_query, cross_k, cross_v, key_mask, cross_lse, grad_cross_o
    )
    grad_cq = grad_cq.astype(jnp.bfloat16).reshape(clip_dev, frame_dev, patches, D)
    g_cross_q = weight_grad(cross_in, grad_cq)
    g_cross_bq = bias_grad(grad_cq)
    grad_hidden = grad_hidden + back_low(grad_cq, cross_q)
    grad_cv = grad_cv.reshape(clip_dev, L_CAP, D)
    grad_ckv = jnp.concatenate([grad_ck.reshape(clip_dev, L_CAP, D), grad_cv], -1)
    g_cross_kv = weight_split(cap_rows, grad_ckv)
    g_cross_bv = bias_grad(grad_cv)
    grad_cap_rows = back_split(grad_ckv, cross_kv)
    grad_time = (grad_hidden * mod_row(2)).astype(jnp.bfloat16)
    g_time_out = weight_grad(time_flat, grad_time)
    g_time_bo = bias_grad(grad_time)
    grad_time_o = lax.all_to_all(
        back_low(grad_time, time_out).astype(jnp.bfloat16),
        "frame",
        split_axis=2,
        concat_axis=1,
        tiled=True,
    )
    grad_time_o = heads_of(jnp.swapaxes(grad_time_o, 1, 2), clip_dev * local_pos)
    grad_tq, grad_tk, grad_tv = attend_backward(time_q, time_k, time_v, None, time_lse, grad_time_o)
    grad_tqkv = jnp.concatenate(
        [
            piece.astype(jnp.bfloat16).reshape(clip_dev, local_pos, frames, D)
            for piece in (grad_tq, grad_tk, grad_tv)
        ],
        -1,
    )
    g_time_qkv = weight_grad(time_in, grad_tqkv)
    g_time_bq = bias_grad(grad_tqkv[..., :D])
    g_time_bv = bias_grad(grad_tqkv[..., 2 * D :])
    grad_tqkv = lax.all_to_all(
        jnp.swapaxes(grad_tqkv, 1, 2), "frame", split_axis=1, concat_axis=2, tiled=True
    )
    grad_gate_a = jnp.sum(grad_hidden * time_res, (1, 2))
    grad_hidden = grad_hidden + back_low(grad_tqkv, time_qkv)
    grad_gate_a = grad_gate_a + jnp.sum(grad_hidden * space_res, (1, 2))
    grad_space = (grad_hidden * mod_row(2)).astype(jnp.bfloat16)
    g_space_out = weight_grad(space_flat, grad_space)
    g_space_bo = bias_grad(grad_space)
    grad_space_o = heads_of(
        back_low(grad_space, space_out).astype(jnp.bfloat16), clip_dev * frame_dev
    )
    grad_sq, grad_sk, grad_sv = attend_backward(
        space_q, space_k, space_v, None, space_lse, grad_space_o
    )
    grad_sqkv = jnp.concatenate(
        [
            piece.astype(jnp.bfloat16).reshape(clip_dev, frame_dev, patches, D)
            for piece in (grad_sq, grad_sk, grad_sv)
        ],
        -1,
    )
    g_space_qkv = weight_grad(space_in, grad_sqkv)
    g_space_bq = bias_grad(grad_sqkv[..., :D])
    g_space_bv = bias_grad(grad_sqkv[..., 2 * D :])
    attend_owned = reduce_group(
        flatten_all(
            [g_space_qkv, g_space_out, g_time_qkv, g_time_out, g_cross_q, g_cross_kv, g_cross_out]
        )
    )
    unused, pullback = jax.vjp(modulate, hidden_zero, mod_row(0), mod_row(1))
    grad_input, grad_shift_a, grad_scale_a = pullback(back_low(grad_sqkv, space_qkv))
    grad_hidden = grad_hidden + grad_input
    g_patch_w = weight_split(noisy, grad_hidden)
    g_patch_b = bias_grad(grad_hidden)
    grad_mods = jnp.stack(
        [
            grad_shift_a.reshape(clip_dev, D),
            grad_scale_a.reshape(clip_dev, D),
            grad_gate_a,
            grad_shift_b.reshape(clip_dev, D),
            grad_scale_b.reshape(clip_dev, D),
            grad_gate_b,
        ],
        1,
    )
    g_table = jnp.sum(grad_mods, 0)
    grad_zero = grad_mods.reshape(clip_dev, 6 * D)
    g_block_b = jnp.sum(grad_zero, 0)
    g_block_w = weight_split(silu_time, grad_zero)
    unused, pullback = jax.vjp(jax.nn.silu, time_embed)
    grad_time_embed = grad_time_embed + pullback(back_split(grad_zero, block_w))[0]
    g_time_b2 = jnp.sum(grad_time_embed, 0)
    g_time_two = weight_split(act_one, grad_time_embed)
    unused, pullback = jax.vjp(jax.nn.silu, pre_one)
    grad_pre_one = pullback(back_split(grad_time_embed, time_two))[0]
    g_time_b1 = jnp.sum(grad_pre_one, 0)
    g_time_one = weight_split(freq_in, grad_pre_one)
    g_cap_b2 = bias_grad(grad_cap_rows)
    g_cap_two = weight_split(cap_act, grad_cap_rows)
    unused, pullback = jax.vjp(gelu_tanh, cap_pre)
    grad_cap_pre = pullback(back_split(grad_cap_rows, cap_two))[0]
    g_cap_b1 = bias_grad(grad_cap_pre)
    g_cap_one = weight_split(cap_in, grad_cap_pre)
    grad_cap_in = back_split(grad_cap_pre, cap_one)
    g_null = jnp.sum(jnp.where(is_null[:, None, None], grad_cap_in, 0.0), 0)
    embed_owned = reduce_group(
        flatten_all(
            [g_patch_w, g_time_one, g_time_two, g_block_w, g_cap_one, g_cap_two, g_final_w, g_null]
        )
    )
    vector_grad = flatten_all(
        [
            g_patch_b,
            g_time_b1,
            g_time_b2,
            g_block_b,
            g_cap_b1,
            g_cap_b2,
            g_space_bq,
            g_space_bv,
            g_space_bo,
            g_time_bq,
            g_time_bv,
            g_time_bo,
            g_cross_bq,
            g_cross_bv,
            g_cross_bo,
            g_fc_in_b,
            g_fc_out_b,
            g_final_b,
            g_table,
            g_final_table,
        ]
    )
    vector_sum, loss_sum = lax.psum((vector_grad, local_loss), ("frame", "clip"))
    owned = (embed_owned, attend_owned, dense_owned)
    local_square = (
        sum((jnp.sum(shard_piece * shard_piece) for shard_piece in owned))
        + jnp.sum(vector_sum * vector_sum) / n_clip
    )
    grad_norm = jnp.sqrt(lax.psum(local_square, "clip"))
    factor = jnp.minimum(1.0, CLIP_LIMIT / (grad_norm + NORM_FLOOR))
    embed_r = adam_step(embed_w, owned[0], embed_m, embed_v, embed_e, factor)
    attend_r = adam_step(attend_w, owned[1], attend_m, attend_v, attend_e, factor)
    dense_r = adam_step(dense_w, owned[2], dense_m, dense_v, dense_e, factor)
    vector_r = adam_step(vector_w, vector_sum, vector_m, vector_v, vector_e, factor)
    return (
        loss_sum,
        weight_total,
        grad_norm,
        embed_r[0],
        attend_r[0],
        dense_r[0],
        vector_r[0],
        embed_r[1],
        attend_r[1],
        dense_r[1],
        vector_r[1],
        embed_r[2],
        attend_r[2],
        dense_r[2],
        vector_r[2],
        embed_r[3],
        attend_r[3],
        dense_r[3],
        vector_r[3],
    )


AXES = ("frame", "clip")
LANES = 128
LANE_TILES = D // LANES
EMB_PAD = 1824


X_SIZE, CORES, Z_SIZE, Y_SIZE = 2, 2, 4, 2
N_OWN = Z_SIZE * Y_SIZE
RING = [(0, 0), (1, 0), (2, 0), (3, 0), (3, 1), (2, 1), (1, 1), (0, 1)]
RING_CLIP = [z * Y_SIZE + y for z, y in RING]
CLIP_RING = [RING_CLIP.index(c) for c in range(N_OWN)]


def pairs(move):
    out = []
    for x in range(X_SIZE):
        for core in range(CORES):
            for z in range(Z_SIZE):
                for y in range(Y_SIZE):
                    to = move(x, core, z, y)
                    if to is not None:
                        rank = lambda a, b, c, d: (a * CORES + b) * N_OWN + c * Y_SIZE + d
                        out.append((rank(x, core, z, y), rank(*to)))
    return out


SWAP_X = pairs(lambda x, c, z, y: (1 - x, c, z, y))
SWAP_CORE = pairs(lambda x, c, z, y: (x, 1 - c, z, y))
SWAP_Y = pairs(lambda x, c, z, y: (x, c, z, 1 - y))
SWAP_Z1 = pairs(lambda x, c, z, y: (x, c, z ^ 1, y))
SWAP_Z2 = pairs(lambda x, c, z, y: (x, c, z ^ 2, y))


def shift(value, perm):
    return lax.ppermute(value, AXES, perm)


def sum_clips(value):
    for perm in (SWAP_Y, SWAP_Z1, SWAP_Z2):
        value = value + shift(value, perm)
    return value


def sum_frames(value):
    for perm in (SWAP_CORE, SWAP_X):
        value = value + shift(value, perm)
    return value


def shard_segments(matrices, n_rows):
    spans, offset = [], 0
    for name, rows, wide in matrices:
        spans.append((name, offset, rows, wide))
        offset += rows * wide
    out = []
    for owner in range(N_OWN):
        low, high = owner * n_rows, (owner + 1) * n_rows
        mine = []
        for name, start, rows, wide in spans:
            begin, end = max(low, start), min(high, start + rows * wide)
            if begin < end:
                mine.append((name, (begin - start) // wide, (end - begin) // wide, wide))
        out.append(mine)
    return out


ATTEND = [
    ("space_qkv", D, 3),
    ("space_out", D, 1),
    ("time_qkv", D, 3),
    ("time_out", D, 1),
    ("cross_q", D, 1),
    ("cross_kv", D, 2),
    ("cross_out", D, 1),
]
DENSE = [("fc_in", D, 4), ("fc_out", MLP, 1)]
ATTEND_ROWS = 13824 // N_OWN
DENSE_ROWS = 9216 // N_OWN
ATTEND_SEGS = shard_segments(ATTEND, ATTEND_ROWS)
DENSE_SEGS = shard_segments(DENSE, DENSE_ROWS)


def cast_table(segments, block):
    out = []
    for mine in segments:
        rows, offset = [], 0
        for name, first, count, wide in mine:
            for start in range(0, count * wide, block):
                rows.append((wide, offset + start // wide, count))
            offset += count * wide
        out.append(rows)
    return np.array(out, np.int32)


def step_table(segments, block, n_rows):
    out = []
    for mine in segments:
        rows, offset = [], 0
        for name, first, count, wide in mine:
            half = count // 2
            for start in range(0, count * wide, block):
                core, inner = divmod(start // wide, half)
                rows.append((wide, core * (n_rows // 2) + offset + inner, half))
            offset += half * wide
        out.append(rows)
    return np.array(out, np.int32)


CAST_BLOCK = 576
STEP_BLOCK = 288


def cast_kernel(widths, table, flat, out):
    block = pl.program_id(0)
    for wide in widths:
        count = CAST_BLOCK // wide

        @pl.when(table[block, 0] == wide)
        def _():
            for slab in range(wide):
                row = pl.multiple_of(table[block, 1] + slab * table[block, 2], 16)
                for tile in range(LANE_TILES):
                    piece = flat[pl.ds(LANE_TILES * slab + tile, count, stride=LANE_TILES * wide), :]
                    out[pl.ds(row, count), tile * LANES : (tile + 1) * LANES] = piece.astype(jnp.bfloat16)


def cast_shard(flat, table, widths, n_rows):
    units = CAST_BLOCK * LANE_TILES
    return pl.pallas_call(
        partial(cast_kernel, widths),
        grid_spec=pltpu.PrefetchScalarGridSpec(
            num_scalar_prefetch=1,
            grid=(n_rows // CAST_BLOCK,),
            in_specs=[pl.BlockSpec((units, LANES), lambda b, t: (b, 0))],
            out_specs=pl.BlockSpec((n_rows, D), lambda b, t: (0, 0)),
        ),
        out_shape=jax.ShapeDtypeStruct((n_rows, D), jnp.bfloat16),
        compiler_params=pltpu.CompilerParams(vmem_limit_bytes=40 * 1024 * 1024),
    )(table, flat.reshape(-1, LANES))


ROWS_AHEAD = 16


def rows_kernel(shift_ref, flat, out, held, sem):
    units, count = flat.shape[0], out.shape[0]
    block = pl.program_id(0)

    @pl.when(block == 0)
    def _():
        end = (ROWS_AHEAD + units) // 8 * 8
        held[pl.ds(0, ROWS_AHEAD), :] = jnp.zeros((ROWS_AHEAD, LANES), jnp.float32)
        held[pl.ds(end, held.shape[0] - end), :] = jnp.zeros((held.shape[0] - end, LANES), jnp.float32)
        copy = pltpu.make_async_copy(flat, held.at[pl.ds(ROWS_AHEAD, units)], sem)
        copy.start()
        copy.wait()

    begin = ROWS_AHEAD + block * (count * LANE_TILES) - shift_ref[0]
    for tile in range(LANE_TILES):
        piece = held[pl.ds(begin + tile, count, stride=LANE_TILES), :]
        out[:, tile * LANES : (tile + 1) * LANES] = piece.astype(out.dtype)


def flat_to_rows(flat, rows, shift, dtype):
    block = rows // 6
    return pl.pallas_call(
        rows_kernel,
        grid_spec=pltpu.PrefetchScalarGridSpec(
            num_scalar_prefetch=1,
            grid=(6,),
            in_specs=[pl.BlockSpec(memory_space=pl.ANY)],
            out_specs=pl.BlockSpec((block, D), lambda b, t: (b, 0)),
            scratch_shapes=[
                pltpu.VMEM((ROWS_AHEAD + rows * LANE_TILES + 8, LANES), jnp.float32),
                pltpu.SemaphoreType.DMA,
            ],
        ),
        out_shape=jax.ShapeDtypeStruct((rows, D), dtype),
        compiler_params=pltpu.CompilerParams(vmem_limit_bytes=32 * 1024 * 1024),
    )(shift.reshape(1), flat)


def flat_kernel(rows, out):
    count = rows.shape[0]
    for tile in range(LANE_TILES):
        out[pl.ds(tile, count, stride=LANE_TILES), :] = rows[:, tile * LANES : (tile + 1) * LANES]


def rows_to_flat(rows):
    block = rows.shape[0] // 6
    return pl.pallas_call(
        flat_kernel,
        grid=(6,),
        in_specs=[pl.BlockSpec((block, D), lambda b: (b, 0))],
        out_specs=pl.BlockSpec((block * LANE_TILES, LANES), lambda b: (b, 0)),
        out_shape=jax.ShapeDtypeStruct((rows.shape[0] * LANE_TILES, LANES), rows.dtype),
        compiler_params=pltpu.CompilerParams(vmem_limit_bytes=32 * 1024 * 1024),
    )(rows)


def ring_place(clip):
    return jnp.where(clip % 2 == 0, clip // 2, N_OWN - 1 - clip // 2)


def clip_at(place):
    return jnp.where(place < N_OWN // 2, 2 * place, 2 * N_OWN - 1 - 2 * place)


def partners(frame, clip):
    place = ring_place(clip)
    x, core = frame // CORES, frame % CORES
    return (
        {"clip": clip_at((place + 1) % N_OWN)},
        {"clip": clip_at((place + N_OWN - 1) % N_OWN)},
        {"frame": (1 - x) * CORES + core},
        {"frame": x * CORES + 1 - core},
    )


def greet(devices):
    barrier = pltpu.get_barrier_semaphore()
    for device in devices:
        pl.semaphore_signal(barrier, inc=1, device_id=device, device_id_type=pl.DeviceIdType.MESH)
    pl.semaphore_wait(barrier, len(devices))


def spread_kernel(groups, modes, *refs):
    n, m = len(groups), len(modes)
    counts = [len(shapes) for keep, shapes, stores, common in groups]
    refs = list(refs)
    take = lambda number: [refs.pop(0) for _ in range(number)]
    owns, given, outs, given_outs = take(n), take(m), take(sum(counts)), take(m)
    helds, sources, landings = take(n), take(m), take(m)
    load_sem, send_sem, recv_sem, out_sem, peer_sem, peer_send, peer_recv = refs
    frame, clip = lax.axis_index("frame"), lax.axis_index("clip")
    x, core = frame // CORES, frame % CORES
    place = ring_place(clip)
    right, left, over_x, other = partners(frame, clip)
    half = N_OWN // 2
    owners = [clip_at((place + N_OWN - k) % N_OWN) for k in range(half + 1)]
    owners += [clip_at((place + k) % N_OWN) for k in range(1, half)]
    flip_x = (1 - x) * CORES + core
    mine = [core, frame, flip_x]
    theirs = [1 - core, x * CORES + 1 - core, (1 - x) * CORES + 1 - core]
    landing = mine + theirs

    def block_of(group, kinds, kind):
        return kinds[kind] + (2 if groups[group][3] and kind % 3 else 0)

    z, y = clip // Y_SIZE, clip % Y_SIZE
    below, above = {"clip": clip - Y_SIZE}, {"clip": clip + Y_SIZE}
    across = {"clip": clip + 1 - 2 * y}
    rings = [group for group in range(n) if len(groups[group][0]) == N_OWN]
    falls = [group for group in range(n) if group not in rings]
    first_z = Z_SIZE - 2

    def held_at(group, slot):
        if group in rings:
            return helds[group].at[owners[slot]]
        return helds[group].at[slot % 2 * Y_SIZE + (y if slot < 2 else 1 - y)]

    def is_own(slot):
        return z == first_z + slot

    def load(group):
        to = held_at(group, 0) if group in rings else helds[group].at[(z - first_z) * Y_SIZE + y]
        return pltpu.make_async_copy(owns[group], to, load_sem.at[group])

    def loading(group, action):
        if group in rings:
            action(load(group))
        else:
            pl.when(z >= first_z)(lambda: action(load(group)))

    def copy_of(group, slot, block, device, to_slot, kind, sender=None):
        row, column = (to_slot, kind) if sender is None else sender
        return pltpu.make_async_remote_copy(
            src_ref=held_at(group, slot).at[block],
            dst_ref=held_at(group, slot).at[block],
            send_sem=send_sem.at[group, row, column],
            recv_sem=recv_sem.at[group, to_slot, kind],
            device_id=device,
            device_id_type=pl.DeviceIdType.MESH,
        )

    sent = []

    def send(group, slot, from_kind, device, to_slot, kind):
        if from_kind == 0 and not groups[group][3]:
            return
        args = (group, slot, block_of(group, mine, from_kind), device, to_slot, kind)
        copy_of(*args).start()
        sent.append(args)

    def arrive(group, slot, kind):
        if kind % 3 == 0 and not groups[group][3]:
            return
        block = block_of(group, landing, kind)
        copy_of(group, slot, block, other, slot, kind).wait_recv()

    def onward(group, slot, kind):
        if slot < half:
            send(group, slot, kind, right, slot + 1, kind)
        if slot == 0:
            send(group, slot, kind, left, half + 1, kind)
        elif half < slot < N_OWN - 1:
            send(group, slot, kind, left, slot + 1, kind)

    def peer_load(item):
        return pltpu.make_async_copy(given[item], sources[item], peer_sem.at[item, 0])

    def peer_own(item):
        source = sources[item].at[clip] if modes[item] == "swap" else sources[item]
        return pltpu.make_async_copy(source, landings[item].at[clip], peer_sem.at[item, 1])

    def peer_copy(item, k):
        to = (clip + k) % N_OWN
        return pltpu.make_async_remote_copy(
            src_ref=sources[item].at[to] if modes[item] == "swap" else sources[item],
            dst_ref=landings[item].at[clip],
            send_sem=peer_send.at[item, k - 1],
            recv_sem=peer_recv.at[item, k - 1],
            device_id={"clip": to},
            device_id_type=pl.DeviceIdType.MESH,
        )

    def peers(item, arriving, action):
        for k in range(1, N_OWN):
            if modes[item] != "first":
                action(k)
            else:
                pl.when(clip == (k if arriving else 0))(lambda: action(k))

    fallen = []

    def run(chosen, action):
        action() if chosen is None else pl.when(chosen)(action)

    def fall(group, slot, kind, device, to_slot, to_kind, sender, chosen):
        args = (group, slot, block_of(group, mine, kind), device, to_slot, to_kind, sender)
        run(chosen, lambda: copy_of(*args).start())
        fallen.append((args, chosen))

    def fall_on(group, slot, kind, chosen):
        going_down = (z >= 1) & (z <= first_z + slot) & chosen
        fall(group, slot, kind, below, slot, kind, (slot, kind), going_down)
        if slot == 0:
            fall(group, slot, kind, above, slot, kind, (4, 3 + kind), is_own(slot) & chosen)
        fall(group, slot, kind, across, slot + 2, kind, (4 + slot, kind), chosen)

    def fall_beside(group, slot, kind, chosen):
        if kind == 1:
            fall(group, slot, 1, over_x, slot, 2, (slot, 2), chosen)
        fall(group, slot, kind, other, slot, 3 + kind, (slot, 3 + kind), chosen)

    def fall_arrive(group, slot, kind, chosen):
        run(chosen, lambda: arrive(group, slot, kind))

    def not_own(slot):
        return None if slot >= 2 else z != first_z + slot

    def fall_start():
        for group in falls:
            for slot in (1, 0):
                for kind in (1, 0):
                    fall_on(group, slot, kind, is_own(slot))

    def fall_phase(phase):
        turns = {
            1: [(0, (z > 0) & not_own(0))],
            2: [(0, z == 0), (1, (z > 0) & not_own(1))],
            3: [(1, z == 0), (2, None)],
            4: [(3, None)],
        }[phase]
        for group in falls:
            for slot, chosen in turns:
                for kind in (1, 0):
                    fall_arrive(group, slot, kind, chosen)
                    if slot < 2:
                        fall_on(group, slot, kind, chosen)
                    fall_beside(group, slot, kind, chosen)
            if phase == half:
                for slot in range(4):
                    fall_arrive(group, slot, 2, not_own(slot))
                    fall_beside(group, slot, 2, not_own(slot))

    for group in range(n):
        loading(group, lambda copy: copy.start())
    for item in range(m):
        peer_load(item).start()
    everyone = tuple({"clip": (clip + k) % N_OWN} for k in range(1, N_OWN)) if m else ()
    greet((right, left, over_x, other) + everyone + ((across,) if falls else ()))
    for group in range(n):
        loading(group, lambda copy: copy.wait())
    fall_start()
    for group in rings:
        onward(group, 0, 1)
        onward(group, 0, 0)
    for item in range(m):
        peer_load(item).wait()
        peer_own(item).start()
        peers(item, False, lambda k: peer_copy(item, k).start())
    waiting = []
    for step in range(1, half + 1):
        slots = [step] + ([half + step] if step < half else [])
        pairs_now = [(group, slot) for group in rings for slot in slots]
        for group, slot in pairs_now:
            arrive(group, slot, 1)
            onward(group, slot, 1)
            send(group, slot, 1, over_x, slot, 2)
            send(group, slot, 1, other, slot, 4)
            arrive(group, slot, 0)
            onward(group, slot, 0)
            send(group, slot, 0, other, slot, 3)
        for group, slot in waiting:
            arrive(group, slot, 2)
            send(group, slot, 2, other, slot, 5)
        fall_phase(step)
        waiting = pairs_now
    for group, slot in waiting:
        arrive(group, slot, 2)
        send(group, slot, 2, other, slot, 5)
    for group in rings:
        for slot in range(1, N_OWN):
            for kind in (3, 4, 5):
                arrive(group, slot, kind)
    for group in falls:
        for slot in range(4):
            for kind in (3, 4, 5):
                fall_arrive(group, slot, kind, not_own(slot))
    done, base = [], 0
    for group, (keep, shapes, stores, common) in enumerate(groups):
        held = helds[group]
        rows = held.shape[2]
        for out, row, column, owner, first, count in stores:
            while count > 0:
                part, inner = divmod(first, rows)
                some = min(count, rows - inner)
                copy = pltpu.make_async_copy(
                    held.at[owner - min(keep), part, pl.ds(inner, some)],
                    outs[base + out].at[pl.ds(row, some), pl.ds(column, D)],
                    out_sem.at[len(done)],
                )
                copy.start()
                done.append(copy)
                first, row, count = first + some, row + some, count - some
        base += counts[group]
    for item in range(m):
        peer_own(item).wait()
        peers(item, True, lambda k: peer_copy(item, k).wait_recv())
        copy = pltpu.make_async_copy(landings[item], given_outs[item], peer_sem.at[item, 2])
        copy.start()
        done.append(copy)
    for item in range(m):
        peers(item, False, lambda k: peer_copy(item, k).wait_send())
    for args in sent:
        copy_of(*args).wait_send()
    for args, chosen in fallen:
        run(chosen, lambda: copy_of(*args).wait_send())
    for copy in done:
        copy.wait()


def spread_shards(owns, groups, collective, given=()):
    spec = pl.BlockSpec(memory_space=pl.ANY)
    shapes = [shape for keep, some, stores, common in groups for shape in some]
    n_stores = sum(6 * len(stores) for keep, some, stores, common in groups)
    blocks = [6 if group[3] else 4 for group in groups]
    modes = [mode for value, mode in given]
    values = [value for value, mode in given]
    landed = [
        value.shape if mode == "swap" else (N_OWN,) + value.shape for value, mode in given
    ]
    many = max(len(given), 1)
    return pl.pallas_call(
        partial(spread_kernel, groups, modes),
        in_specs=[spec] * (len(owns) + len(given)),
        out_specs=[spec] * (len(shapes) + len(given)),
        out_shape=[jax.ShapeDtypeStruct(shape, jnp.bfloat16) for shape in shapes]
        + [jax.ShapeDtypeStruct(shape, value.dtype) for shape, value in zip(landed, values)],
        scratch_shapes=[
            pltpu.VMEM((len(group[0]), count, own.shape[0] // count, D), jnp.bfloat16)
            for own, group, count in zip(owns, groups, blocks)
        ]
        + [pltpu.VMEM(value.shape, value.dtype) for value in values]
        + [pltpu.VMEM(shape, value.dtype) for shape, value in zip(landed, values)]
        + [
            pltpu.SemaphoreType.DMA((len(owns),)),
            pltpu.SemaphoreType.DMA((len(owns), N_OWN, 6)),
            pltpu.SemaphoreType.DMA((len(owns), N_OWN, 6)),
            pltpu.SemaphoreType.DMA((n_stores,)),
            pltpu.SemaphoreType.DMA((many, 3)),
            pltpu.SemaphoreType.DMA((many, N_OWN - 1)),
            pltpu.SemaphoreType.DMA((many, N_OWN - 1)),
        ],
        compiler_params=pltpu.CompilerParams(
            collective_id=collective, has_side_effects=True, vmem_limit_bytes=50 * 1024 * 1024
        ),
        cost_estimate=pl.CostEstimate(
            flops=0, bytes_accessed=200 * 1000 * 1000, transcendentals=0
        ),
    )(*[own.reshape(count, own.shape[0] // count, D) for own, count in zip(owns, blocks)], *values)


LAG = 5


def collect_kernel(first, last, chunks, small, part, out, small_out, part_out, scratch):
    bufs, extra, locals_, finals, result = scratch[:2], scratch[2], scratch[3:5], scratch[5:7], scratch[7]
    ring_send, ring_recv, x_send, x_recv, end_send, end_recv, load_sem, own_sem = scratch[8:16]
    if small is not None:
        sums, arrived, small_send, small_recv = scratch[16:]
    if part is not None:
        frames, part_send, part_recv = scratch[16:]
    frame, clip = lax.axis_index("frame"), lax.axis_index("clip")
    x, core = frame // CORES, frame % CORES
    place = ring_place(clip)
    right, left, over_x, other = partners(frame, clip)
    swaps = [
        other,
        over_x,
        {"clip": clip + 1 - 2 * (clip % 2)},
        {"clip": clip + 2 - 4 * (clip // 2 % 2)},
        {"clip": clip + 4 - 8 * (clip // 4)},
    ]
    greet((right, left) + (tuple(swaps) if small is not None else (over_x, other)))
    f, l = first // 2, last // 2
    toward = (right, left)

    def owner(way, step):
        moved = N_OWN - 1 - step if way == 0 else 1 + step
        return clip_at((place + moved) % N_OWN)

    def f_rows(side, way):
        return pl.ds(pl.multiple_of(side * first + way * f, 8), f)

    def l_rows(way):
        return pl.ds(2 * first + way * l, l)

    def remote(src, dst, send_sem, recv_sem, device):
        return pltpu.make_async_remote_copy(
            src_ref=src,
            dst_ref=dst,
            send_sem=send_sem,
            recv_sem=recv_sem,
            device_id=device,
            device_id_type=pl.DeviceIdType.MESH,
        )

    def x_copy(way, step):
        return remote(
            chunks.at[owner(way, step), f_rows(1 - x, way)],
            extra.at[way, step],
            x_send.at[way, step],
            x_recv.at[way, step],
            over_x,
        )

    def load(kind, way, step):
        to = bufs[kind].at[way, 0] if step == 0 else locals_[kind].at[way, step % 2]
        rows = l_rows(way) if kind == 0 else f_rows(x, way)
        return pltpu.make_async_copy(
            chunks.at[owner(way, step), rows], to, load_sem.at[kind, way, step % 2]
        )

    def ring_copy(kind, way, step):
        return remote(
            bufs[kind].at[way, step],
            bufs[kind].at[way, step + 1],
            ring_send.at[kind, way, step],
            ring_recv.at[kind, way, step],
            toward[way],
        )

    def final_copy(kind, way):
        return remote(
            bufs[kind].at[way, N_OWN - 1],
            finals[kind].at[way],
            end_send.at[kind, way],
            end_recv.at[kind, way],
            over_x,
        )

    def small_copy(stage):
        return remote(
            sums.at[stage], arrived.at[stage], small_send.at[stage], small_recv.at[stage], swaps[stage]
        )

    flip_x = (1 - x) * CORES + core

    def part_copy(number, block=None):
        block = (frame, frame, flip_x)[number] if block is None else block
        return remote(
            frames.at[block],
            frames.at[block],
            part_send.at[number],
            part_recv.at[number],
            (over_x, other, other)[number],
        )

    def over_rows(start, count, work):
        def body(number, carry):
            work(pl.multiple_of(start + number * 8, 8))
            return carry

        lax.fori_loop(0, count // 8, body, 0)

    def small_load():
        return pltpu.make_async_copy(small, sums.at[0], own_sem.at[7])

    def part_load():
        return pltpu.make_async_copy(part, frames.at[frame], own_sem.at[7])

    for kind in range(2):
        for way in range(2):
            load(kind, way, 0).start()
    for way in range(2):
        x_copy(way, 0).start()
    if small is not None:
        small_load().start()
    if part is not None:
        part_load().start()

    def ring_step(kind, way, step):
        load(kind, way, step).wait()
        if step + 1 < N_OWN:
            load(kind, way, step + 1).start()
        if kind == 1:
            x_copy(way, step).wait_recv()
        if step > 0:
            ring_copy(kind, way, step - 1).wait_recv()
        buf, local = bufs[kind], locals_[kind]

        def add(row):
            at = pl.ds(row, 8)
            total = buf[way, step, at]
            if kind == 1:
                total = total + extra[way, step, at]
            if step > 0:
                total = total + local[way, step % 2, at]
            buf[way, step, at] = total

        if kind == 1 or step > 0:
            over_rows(0, f if kind == 1 else l, add)
        if step + 1 < N_OWN:
            ring_copy(kind, way, step).start()
        else:
            final_copy(kind, way).start()

    def own_half(kind):
        return pl.ds(2 * first, last) if kind == 0 else pl.ds(0, 2 * first)

    def core_swap(kind, to):
        return remote(
            result.at[own_half(kind)],
            out.at[to, own_half(kind)],
            own_sem.at[kind],
            own_sem.at[2 + kind],
            other,
        )

    def own_store(kind):
        return pltpu.make_async_copy(
            result.at[own_half(kind)], out.at[core, own_half(kind)], own_sem.at[4 + kind]
        )

    def finish(kind):
        for way in range(2):
            final_copy(kind, way).wait_recv()
            buf, final = bufs[kind], finals[kind]

            def put(row):
                at = pl.ds(row, 8)
                if kind == 0:
                    to = pl.multiple_of(2 * first + way * l + row, 8)
                    result[pl.ds(to, 8)] = buf[way, N_OWN - 1, at] + final[way, at]
                else:
                    to = pl.multiple_of(x * first + way * f + row, 8)
                    back = pl.multiple_of((1 - x) * first + way * f + row, 8)
                    result[pl.ds(to, 8)] = buf[way, N_OWN - 1, at]
                    result[pl.ds(back, 8)] = final[way, at]

            over_rows(0, l if kind == 0 else f, put)
        core_swap(kind, core).start()
        own_store(kind).start()

    for tick in range(N_OWN + LAG):
        if small is not None and tick < len(swaps) + 1:
            if tick == 0:
                small_load().wait()
            else:
                small_copy(tick - 1).wait_recv()

                def add_small(row):
                    at = pl.ds(row, 8)
                    sums[tick, at] = sums[tick - 1, at] + arrived[tick - 1, at]

                over_rows(0, small.shape[0], add_small)
            if tick < len(swaps):
                small_copy(tick).start()
        if 0 < tick < N_OWN:
            for way in range(2):
                x_copy(way, tick).start()
        if part is not None and tick == N_OWN - 1:
            part_load().wait()
            part_copy(0).start()
            part_copy(1).start()
        for way in range(2):
            if tick < N_OWN:
                ring_step(0, way, tick)
            if tick >= LAG:
                ring_step(1, way, tick - LAG)
    if small is not None:
        small_store = pltpu.make_async_copy(sums.at[len(swaps)], small_out, own_sem.at[6])
        small_store.start()
    finish(0)
    if part is not None:
        part_copy(0, flip_x).wait_recv()
        part_copy(2).start()
    finish(1)
    if part is not None:
        part_copy(1, x * CORES + 1 - core).wait_recv()
        part_copy(2, (1 - x) * CORES + 1 - core).wait_recv()
        part_store = pltpu.make_async_copy(frames, part_out, own_sem.at[6])
        part_store.start()
        part_store.wait()
        for number in range(3):
            part_copy(number).wait_send()
    if small is not None:
        small_store.wait()
        for stage in range(len(swaps)):
            small_copy(stage).wait_send()
    for way in range(2):
        for step in range(N_OWN):
            x_copy(way, step).wait_send()
    for kind in range(2):
        for way in range(2):
            for step in range(N_OWN - 1):
                ring_copy(kind, way, step).wait_send()
            final_copy(kind, way).wait_send()
        core_swap(kind, 1 - core).wait_recv()
        core_swap(kind, core).wait_send()
        own_store(kind).wait()


def collect_shard(chunks, first, collective, small=None, part=None):
    rows = chunks.shape[1]
    last = rows - 2 * first
    spec = pl.BlockSpec(memory_space=pl.ANY)
    out_shape = [jax.ShapeDtypeStruct((2, rows, D), jnp.float32)]
    beside = small if part is None else part
    if part is None:
        out_shape.append(jax.ShapeDtypeStruct(small.shape, jnp.float32))
        more = [
            pltpu.VMEM((6,) + small.shape, jnp.float32),
            pltpu.VMEM((5,) + small.shape, jnp.float32),
            pltpu.SemaphoreType.DMA((5,)),
            pltpu.SemaphoreType.DMA((5,)),
        ]
    else:
        out_shape.append(jax.ShapeDtypeStruct((4,) + part.shape, jnp.float32))
        more = [
            pltpu.VMEM((4,) + part.shape, jnp.float32),
            pltpu.SemaphoreType.DMA((3,)),
            pltpu.SemaphoreType.DMA((3,)),
        ]

    def kernel(chunks, beside, out, beside_out, *scratch):
        if part is None:
            collect_kernel(first, last, chunks, beside, None, out, beside_out, None, scratch)
        else:
            collect_kernel(first, last, chunks, None, beside, out, None, beside_out, scratch)

    return pl.pallas_call(
        kernel,
        in_specs=[spec] * 2,
        out_specs=[spec] * 2,
        out_shape=out_shape,
        scratch_shapes=[
            pltpu.VMEM((2, N_OWN, last // 2, D), jnp.float32),
            pltpu.VMEM((2, N_OWN, first // 2, D), jnp.float32),
            pltpu.VMEM((2, N_OWN, first // 2, D), jnp.float32),
            pltpu.VMEM((2, 2, last // 2, D), jnp.float32),
            pltpu.VMEM((2, 2, first // 2, D), jnp.float32),
            pltpu.VMEM((2, last // 2, D), jnp.float32),
            pltpu.VMEM((2, first // 2, D), jnp.float32),
            pltpu.VMEM((rows, D), jnp.float32),
            pltpu.SemaphoreType.DMA((2, 2, N_OWN)),
            pltpu.SemaphoreType.DMA((2, 2, N_OWN)),
            pltpu.SemaphoreType.DMA((2, N_OWN)),
            pltpu.SemaphoreType.DMA((2, N_OWN)),
            pltpu.SemaphoreType.DMA((2, 2)),
            pltpu.SemaphoreType.DMA((2, 2)),
            pltpu.SemaphoreType.DMA((2, 2, 2)),
            pltpu.SemaphoreType.DMA((8,)),
        ]
        + more,
        compiler_params=pltpu.CompilerParams(
            collective_id=collective, has_side_effects=True, vmem_limit_bytes=58 * 1024 * 1024
        ),
        cost_estimate=pl.CostEstimate(
            flops=0, bytes_accessed=800 * 1000 * 1000, transcendentals=0
        ),
    )(chunks, beside)


def matrix_plan(matrices, segments):
    shapes = [(rows, wide * D) for name, rows, wide in matrices]
    names = [name for name, rows, wide in matrices]
    stores = []
    for owner in range(N_OWN):
        offset = 0
        for name, first, count, wide in segments[owner]:
            for j in range(wide):
                stores.append((names.index(name), first, j * D, owner, offset, count))
                offset += count
    return shapes, stores


GRAD_COLUMNS = 384


def grad_plan(matrices, segments, lefts, rights):
    squares = {}
    for owner in range(N_OWN):
        row = 0
        for name, first, count, wide in segments[owner]:
            for j in range(wide):
                block, inner = divmod(first, D)
                piece = (inner, count // 2, owner, row)
                squares.setdefault((name, block, j), []).append(piece)
                row += count // 2
    plan = []
    for name, rows, wide in matrices:
        for block in range(rows // D):
            for j in range(wide):
                right, column = rights[name][j]
                plan.append((lefts[name], block * D, right, column, squares[name, block, j]))
    return plan


def grad_kernel(plan, parts, n_left, core_ref, *refs):
    n_in = sum(parts)
    ins, out = refs[:n_in], refs[n_in]
    left_buf, right_buf, made, left_sem, right_sem, out_sem = refs[n_in + 1 :]
    core = core_ref[0]
    place = [sum(parts[:k]) for k in range(len(parts))]

    def left_copies(square, slot):
        left, row = square[:2]
        return [
            pltpu.make_async_copy(
                ins[place[left] + part].at[pl.ds(row, D)],
                left_buf.at[slot, part, :, pl.ds(0, ins[place[left]].shape[1])],
                left_sem.at[slot, part],
            )
            for part in range(parts[left])
        ]

    def right_copies(square, slot):
        right, column = n_left + square[2], square[3]
        return [
            pltpu.make_async_copy(
                ins[place[right] + part].at[:, pl.ds(column, D)],
                right_buf.at[slot, part, pl.ds(0, ins[place[right]].shape[0])],
                right_sem.at[slot, part],
            )
            for part in range(parts[right])
        ]

    def out_copies(number):
        row, copies = 0, []
        for k, (first, count, owner, to) in enumerate(plan[number][4]):
            copies.append(
                pltpu.make_async_copy(
                    made.at[number % 2, pl.ds(row, count)],
                    out.at[owner, pl.ds(to, count)],
                    out_sem.at[number % 2, k],
                )
            )
            row += count
        return copies

    slots = []
    for number, square in enumerate(plan):
        if number == 0:
            slots.append((0, True, 0, True))
            continue
        left, _, right, _ = slots[-1]
        new_left = square[:2] != plan[number - 1][:2]
        new_right = square[2:4] != plan[number - 1][2:4]
        slots.append((left ^ new_left, new_left, right ^ new_right, new_right))

    def operands(number):
        left, new_left, right, new_right = slots[number]
        copies = left_copies(plan[number], left) if new_left else []
        return copies + (right_copies(plan[number], right) if new_right else [])

    for copy in operands(0):
        copy.start()
    for number, square in enumerate(plan):
        for copy in operands(number):
            copy.wait()
        if number + 1 < len(plan):
            for copy in operands(number + 1):
                copy.start()
        if number >= 2:
            for copy in out_copies(number - 2):
                copy.wait()
        left, _, right, _ = slots[number]
        depth = ins[place[square[0]]].shape[1]

        def some_columns(step, carry):
            columns = pl.ds(pl.multiple_of(step * GRAD_COLUMNS, LANES), GRAD_COLUMNS)
            row = 0
            for first, count, owner, to in square[4]:
                rows = pl.ds(pl.multiple_of(first + core * count, 16), count)
                total = 0.0
                for part in range(parts[square[0]]):
                    total = total + jnp.dot(
                        left_buf[left, part, rows, :depth],
                        right_buf[right, part, :depth, columns],
                        preferred_element_type=jnp.float32,
                    )
                made[number % 2, row : row + count, columns] = total
                row += count
            return carry

        lax.fori_loop(0, D // GRAD_COLUMNS, some_columns, 0)
        for copy in out_copies(number):
            copy.start()
    for number in range(max(len(plan) - 2, 0), len(plan)):
        for copy in out_copies(number):
            copy.wait()


def core_chunks(plan, core, lefts, rights, n_rows):
    operands = list(lefts) + list(rights)
    parts = [len(arrays) for arrays in operands]
    tokens = max(arrays[0].shape[1] for arrays in lefts)
    spec = pl.BlockSpec(memory_space=pl.ANY)
    return pl.pallas_call(
        partial(grad_kernel, plan, parts, len(lefts)),
        in_specs=[pl.BlockSpec(memory_space=pltpu.SMEM)] + [spec] * sum(parts),
        out_specs=spec,
        out_shape=jax.ShapeDtypeStruct((N_OWN, n_rows // 2, D), jnp.float32),
        scratch_shapes=[
            pltpu.VMEM((2, 2, D, tokens), jnp.bfloat16),
            pltpu.VMEM((2, 2, tokens, D), jnp.bfloat16),
            pltpu.VMEM((2, D // 2, D), jnp.float32),
            pltpu.SemaphoreType.DMA((2, 2)),
            pltpu.SemaphoreType.DMA((2, 2)),
            pltpu.SemaphoreType.DMA((2, N_OWN)),
        ],
        compiler_params=pltpu.CompilerParams(vmem_limit_bytes=36 * 1024 * 1024),
    )(core.astype(jnp.int32).reshape(1), *[array for arrays in operands for array in arrays])


def step_values(master, grad, first, second, average):
    keep = min(AVERAGE_KEEP, (1.0 + STEP) / (10.0 + STEP))
    first = BETA_FIRST * first + (1.0 - BETA_FIRST) * grad
    second = BETA_SECOND * second + (1.0 - BETA_SECOND) * grad * grad
    moved = (
        first
        / (1.0 - BETA_FIRST**STEP)
        / (jnp.sqrt(second / (1.0 - BETA_SECOND**STEP)) + ADAM_FLOOR)
    )
    master = master - LEARN_RATE * (moved + WEIGHT_DECAY * master)
    return (master, first, second, keep * average + (1.0 - keep) * master)


STEP_ROWS = 144


def step_kernel(widths, table, factor, grad, *refs):
    olds, news, (shard, flat, sem) = refs[:4], refs[4:8], refs[8:]
    block = pl.program_id(0)

    @pl.when(block == 0)
    def _():
        copy = pltpu.make_async_copy(grad, shard, sem)
        copy.start()
        copy.wait()

    for wide in widths:
        count = STEP_BLOCK // wide

        @pl.when(table[block, 0] == wide)
        def _():
            for slab in range(wide):
                row = pl.multiple_of(table[block, 1] + slab * table[block, 2], 8)
                for tile in range(LANE_TILES):
                    flat[pl.ds(LANE_TILES * slab + tile, count, stride=LANE_TILES * wide), :] = shard[
                        pl.ds(row, count), tile * LANES : (tile + 1) * LANES
                    ]

    scale = factor[0]

    def some_rows(number, carry):
        at = pl.ds(pl.multiple_of(number * STEP_ROWS, 8), STEP_ROWS)
        old = [ref[at, :] for ref in olds]
        made = step_values(old[0], flat[at, :] * scale, old[1], old[2], old[3])
        for ref, value in zip(news, made):
            ref[at, :] = value
        return carry

    lax.fori_loop(0, STEP_BLOCK * LANE_TILES // STEP_ROWS, some_rows, 0)


def step_shard(grad, table, widths, n_rows, factor, olds):
    units = STEP_BLOCK * LANE_TILES
    block_spec = pl.BlockSpec((units, LANES), lambda b, t, f: (b, 0))
    flat_shape = jax.ShapeDtypeStruct((n_rows * LANE_TILES, LANES), jnp.float32)
    made = pl.pallas_call(
        partial(step_kernel, widths),
        grid_spec=pltpu.PrefetchScalarGridSpec(
            num_scalar_prefetch=2,
            grid=(n_rows // STEP_BLOCK,),
            in_specs=[pl.BlockSpec(memory_space=pl.ANY)] + [block_spec] * 4,
            out_specs=[block_spec] * 4,
            scratch_shapes=[
                pltpu.VMEM((n_rows, D), jnp.float32),
                pltpu.VMEM((units, LANES), jnp.float32),
                pltpu.SemaphoreType.DMA,
            ],
        ),
        out_shape=[flat_shape] * 4,
        compiler_params=pltpu.CompilerParams(vmem_limit_bytes=50 * 1024 * 1024),
    )(table, factor, grad, *[old.reshape(-1, LANES) for old in olds])
    return [value.reshape(-1) for value in made]


def head_span(head):
    width = D // HEADS
    start = head * width // LANES * LANES
    stop = -(-(head + 1) * width // LANES) * LANES
    lane = start + lax.broadcasted_iota(jnp.int32, (1, stop - start), 1)
    ones = (lane >= head * width) & (lane < (head + 1) * width)
    return slice(start, stop), ones.astype(jnp.float32).astype(jnp.bfloat16)


def dot_rows(left, right):
    return lax.dot_general(left, right, (((1,), (1,)), ((), ())), preferred_element_type=jnp.float32)


def dot_down(left, right):
    return lax.dot_general(left, right, (((0,), (0,)), ((), ())), preferred_element_type=jnp.float32)


def live_keys(mode, live, n_queries, n_keys):
    key = lax.broadcasted_iota(jnp.int32, (n_queries, n_keys), 1)
    if mode == "cross":
        return key < live[0]
    if mode == "all":
        return None
    query = lax.broadcasted_iota(jnp.int32, (n_queries, n_keys), 0)
    return query // mode == key // mode


def head_scores(queries, keys, valid):
    scores = dot_rows(queries, keys) * (D // HEADS) ** (-0.5)
    return scores if valid is None else jnp.where(valid, scores, MASKED_SCORE)


def heads_kernel(mode, live, queries, keys, values, out, log_total, total):
    n_queries, n_keys = queries.shape[0], keys.shape[0]
    valid = live_keys(mode, live, n_queries, n_keys)
    lane = lax.broadcasted_iota(jnp.int32, (1, LANES), 1)
    total[...] = jnp.zeros_like(total)
    log_total[...] = jnp.zeros_like(log_total)
    for head in range(HEADS):
        span, ones = head_span(head)
        scores = head_scores(queries[:, span], keys[:, span] * ones, valid)
        summit = jnp.max(scores, -1, keepdims=True)
        powers = jnp.exp(scores - summit)
        sums = jnp.sum(powers, -1, keepdims=True)
        probs = (powers / sums).astype(jnp.bfloat16)
        total[:, span] += jnp.dot(
            probs, values[:, span] * ones, preferred_element_type=jnp.float32
        )
        log_total[...] += jnp.where(lane == head, summit + jnp.log(sums), 0.0)
    out[...] = total[...].astype(jnp.bfloat16)


def heads_back_kernel(
    mode, live, queries, keys, values, log_total, grad_out, grad_q, grad_k, grad_v, sum_q, sum_k, sum_v
):
    n_queries, n_keys = queries.shape[0], keys.shape[0]
    valid = live_keys(mode, live, n_queries, n_keys)
    scale = (D // HEADS) ** (-0.5)
    block, last = pl.program_id(0), pl.num_programs(0) - 1
    sum_q[...] = jnp.zeros_like(sum_q)

    @pl.when((block == 0) | (mode != "cross"))
    def _():
        sum_k[...] = jnp.zeros_like(sum_k)
        sum_v[...] = jnp.zeros_like(sum_v)

    for head in range(HEADS):
        span, ones = head_span(head)
        some_keys = keys[:, span] * ones
        scores = head_scores(queries[:, span], some_keys, valid)
        probs = jnp.exp(scores - log_total[:, head : head + 1])
        grad_probs = dot_rows(grad_out[:, span], values[:, span] * ones)
        row = jnp.sum(probs * grad_probs, -1, keepdims=True)
        grad_scores = (probs * (grad_probs - row)).astype(jnp.bfloat16)
        sum_q[:, span] += jnp.dot(grad_scores, some_keys, preferred_element_type=jnp.float32)
        sum_k[:, span] += dot_down(grad_scores, queries[:, span] * ones)
        sum_v[:, span] += dot_down(probs.astype(jnp.bfloat16), grad_out[:, span] * ones)
    grad_q[...] = (sum_q[...] * scale).astype(grad_q.dtype)

    @pl.when((block == last) | (mode != "cross"))
    def _():
        grad_k[...] = (sum_k[...] * scale).astype(grad_k.dtype)
        grad_v[...] = sum_v[...].astype(grad_v.dtype)


HEAD_ROWS = 256


def heads_specs(mode, keys):
    own = pl.BlockSpec((HEAD_ROWS, D), lambda b: (b, 0))
    side = pl.BlockSpec((HEAD_ROWS, LANES), lambda b: (b, 0))
    shared = pl.BlockSpec(keys.shape, lambda b: (0, 0)) if mode == "cross" else own
    return own, side, shared


def heads_forward(mode, queries, keys, values, live):
    own, side, shared = heads_specs(mode, keys)
    n_keys = keys.shape[0] if mode == "cross" else HEAD_ROWS
    return pl.pallas_call(
        partial(heads_kernel, mode),
        grid=(queries.shape[0] // HEAD_ROWS,),
        in_specs=[pl.BlockSpec(memory_space=pltpu.SMEM), own, shared, shared],
        out_specs=[own, side],
        out_shape=[
            jax.ShapeDtypeStruct(queries.shape, jnp.bfloat16),
            jax.ShapeDtypeStruct((queries.shape[0], LANES), jnp.float32),
        ],
        scratch_shapes=[pltpu.VMEM((HEAD_ROWS, D), jnp.float32)],
        compiler_params=pltpu.CompilerParams(vmem_limit_bytes=32 * 1024 * 1024),
    )(live, queries, keys, values)


def heads_backward(mode, queries, keys, values, live, log_total, grad_out):
    own, side, shared = heads_specs(mode, keys)
    n_keys = keys.shape[0] if mode == "cross" else HEAD_ROWS
    kind = jnp.float32 if mode == "cross" else jnp.bfloat16
    return pl.pallas_call(
        partial(heads_back_kernel, mode),
        grid=(queries.shape[0] // HEAD_ROWS,),
        in_specs=[pl.BlockSpec(memory_space=pltpu.SMEM), own, shared, shared, side, own],
        out_specs=[own, shared, shared],
        out_shape=[
            jax.ShapeDtypeStruct(queries.shape, jnp.bfloat16),
            jax.ShapeDtypeStruct(keys.shape, kind),
            jax.ShapeDtypeStruct(keys.shape, kind),
        ],
        scratch_shapes=[
            pltpu.VMEM((HEAD_ROWS, D), jnp.float32),
            pltpu.VMEM((n_keys, D), jnp.float32),
            pltpu.VMEM((n_keys, D), jnp.float32),
        ],
        compiler_params=pltpu.CompilerParams(vmem_limit_bytes=40 * 1024 * 1024),
    )(live, queries, keys, values, log_total, grad_out)


ROW_TIME_ONE = PATCH_VALUES
ROW_TIME_TWO = ROW_TIME_ONE + TFREQ
ROW_BLOCK = ROW_TIME_TWO + D
ROW_CAP_ONE = ROW_BLOCK + 6 * D
ROW_CAP_TWO = ROW_CAP_ONE + CAPW
ROW_FINAL = ROW_CAP_TWO + D
ROW_NULL = ROW_FINAL + PATCH_VALUES
EMB_UNITS = 16158720 // LANES // N_OWN
EMB_FIRST = [EMB_UNITS * c // LANE_TILES for c in range(N_OWN)]
EMB_SHIFT = [EMB_UNITS * c % LANE_TILES for c in range(N_OWN)]


def two_parts(product, value):
    both = product(jnp.concatenate(halves(value), 0))
    return both[: value.shape[0]] + both[value.shape[0] :]


def shards_block(
    latents,
    noise,
    timesteps,
    captions,
    cap_lengths,
    null_flags,
    sample_weight,
    embed_w,
    attend_w,
    dense_w,
    vector_w,
    embed_m,
    attend_m,
    dense_m,
    vector_m,
    embed_v,
    attend_v,
    dense_v,
    vector_v,
    embed_e,
    attend_e,
    dense_e,
    vector_e,
):
    clip_dev, frame_dev, patches = (latents.shape[0], latents.shape[1], latents.shape[2])
    n_frame = lax.axis_size("frame")
    n_clip = lax.axis_size("clip")
    local_pos = patches // n_frame
    tokens = frame_dev * patches
    frame_id = lax.axis_index("frame")
    clip_id = lax.axis_index("clip")
    x_id, core_id = frame_id // CORES, frame_id % CORES
    z_id, y_id = clip_id // Y_SIZE, clip_id % Y_SIZE

    emb_first = jnp.asarray(EMB_FIRST, jnp.int32)[clip_id]
    emb_shift = jnp.asarray(EMB_SHIFT, jnp.int32)[clip_id]
    emb_rows = flat_to_rows(embed_w.reshape(-1, LANES), EMB_PAD, emb_shift, jnp.bfloat16)
    dense_cast = cast_shard(
        dense_w, jnp.asarray(cast_table(DENSE_SEGS, CAST_BLOCK))[clip_id], (1, 4), DENSE_ROWS
    )
    cap_owners = range(4, N_OWN)
    cap_plan = (
        [(EMB_PAD * len(cap_owners), D)],
        [(0, EMB_PAD * k, 0, owner, 0, EMB_PAD) for k, owner in enumerate(cap_owners)],
    )
    own_clip = jnp.arange(n_clip) == clip_id
    facts = jnp.stack([timesteps.astype(jnp.float32)[0], sample_weight[0], null_flags.astype(jnp.float32)[0]])
    facts = jnp.broadcast_to(jnp.pad(facts, (0, LANES - 3))[None], (8, LANES))
    cap_weights, fc_in, fc_out, facts = spread_shards(
        [emb_rows, dense_cast],
        [(cap_owners,) + cap_plan + (True,), (range(N_OWN),) + matrix_plan(DENSE, DENSE_SEGS) + (True,)],
        2,
        given=[(facts, "gather")],
    )
    facts = facts[:, 0, :3]
    last = N_OWN - 1
    cap_last = cap_weights[EMB_PAD * (len(cap_owners) - 1) :]
    null_end = 16158720 - ROW_NULL * D
    null_first, final_first = ROW_NULL - EMB_FIRST[last], ROW_FINAL - EMB_FIRST[last]
    null_caption = (
        cap_last[null_first : null_first - (-null_end // D)]
        .reshape(-1)[:null_end]
        .reshape(L_CAP, CAPW)
    )
    final_w = cap_last[final_first : final_first + PATCH_VALUES].reshape(D, PATCH_VALUES)
    two_first = ROW_CAP_TWO - EMB_FIRST[last]

    def to_cap_rows(value):
        padded = jnp.pad(value, ((0, 0), (EMB_PAD, EMB_PAD)))
        starts = [EMB_FIRST[owner] - ROW_CAP_ONE + EMB_PAD for owner in cap_owners]
        return jnp.concatenate([padded[:, start : start + EMB_PAD] for start in starts], 1)

    def from_cap_rows(value):
        total = 0.0
        for k, owner in enumerate(cap_owners):
            start = EMB_FIRST[owner] - ROW_CAP_ONE
            low, high = max(0, -start), min(EMB_PAD, CAPW - start)
            part = value[:, EMB_PAD * k + low : EMB_PAD * k + high]
            total = total + jnp.pad(part, ((0, 0), (start + low, CAPW - start - high)))
        return total

    (
        patch_b,
        time_b1,
        time_b2,
        block_b,
        cap_b1,
        cap_b2,
        space_bq,
        space_bv,
        space_bo,
        time_bq,
        time_bv,
        time_bo,
        cross_bq,
        cross_bv,
        cross_bo,
        fc_in_b,
        fc_out_b,
        final_b,
        table,
        final_table,
    ) = split_flat(vector_w, vector_shapes())

    all_steps, all_null = facts[:, 0], facts[:, 2] == 1.0
    angle = (all_steps / 1000.0 + 0.008) / 1.008 * (math.pi / 2)
    signal = jnp.cos(angle) ** 2
    ratio = signal / (1.0 - signal)
    all_weights = facts[:, 1] * jnp.minimum(ratio, SNR_LIMIT) / ratio
    weight_total = jnp.sum(all_weights)
    signal = lax.dynamic_slice_in_dim(signal, clip_id, 1, 0)
    loss_weight = lax.dynamic_slice_in_dim(all_weights, clip_id, 1, 0)

    freq_in = sincos(all_steps, TFREQ).astype(jnp.bfloat16)
    at_start = clip_id == 0
    time_one = emb_rows[ROW_TIME_ONE:ROW_TIME_TWO]
    time_two = emb_rows[ROW_TIME_TWO:ROW_BLOCK]
    pre_one = matmul_low(freq_in, time_one) + time_b1
    act_one = jax.nn.silu(pre_one).astype(jnp.bfloat16)
    time_embed = matmul_low(act_one, time_two) + time_b2
    early = jnp.concatenate(
        [pre_one, time_embed, emb_rows[:ROW_TIME_ONE].astype(jnp.float32)], 0
    )
    is_null = null_flags == 1
    cap_in = jnp.where(is_null[:, None, None], null_caption[None], captions)
    cap_pre = (matmul_low(to_cap_rows(cap_in[0]), cap_weights) + cap_b1)[None]
    cap_act = gelu_tanh(cap_pre).astype(jnp.bfloat16)
    act_rows = jnp.pad(cap_act[0], ((0, 0), (two_first, EMB_PAD - two_first - D)))
    cap_rows = (matmul_low(act_rows, cap_last) + cap_b2).astype(jnp.bfloat16)[None]
    live_len = jnp.where(is_null, L_CAP, cap_lengths)
    cap_wide = jnp.concatenate([cap_in[0], cap_act[0]], -1)
    cap_wide = jnp.pad(cap_wide, ((0, 0), (EMB_PAD, EMB_PAD)))
    wanted = []
    for owner in range(n_clip):
        start = EMB_FIRST[owner] - ROW_CAP_ONE + EMB_PAD
        if start + EMB_PAD <= EMB_PAD:
            wanted.append(jnp.zeros((L_CAP, EMB_PAD // 4), jnp.bfloat16))
        else:
            wanted.append(
                lax.dynamic_slice_in_dim(cap_wide, start + frame_id * (EMB_PAD // 4), EMB_PAD // 4, 1)
            )
    attend_cast = cast_shard(
        attend_w, jnp.asarray(cast_table(ATTEND_SEGS, CAST_BLOCK))[clip_id], (1, 2, 3), ATTEND_ROWS
    )
    space_qkv, space_out, time_qkv, time_out, cross_q, cross_kv, cross_out, early, cap_left = spread_shards(
        [attend_cast],
        [(range(N_OWN),) + matrix_plan(ATTEND, ATTEND_SEGS) + (True,)],
        1,
        given=[(early, "first"), (jnp.pad(jnp.stack(wanted), ((0, 0), (0, 128 - L_CAP), (0, 0))), "swap")],
    )
    early = early[0]
    cap_left = cap_left[:, :L_CAP].reshape(n_clip * L_CAP, EMB_PAD // 4)
    pre_one, time_embed = early[:n_clip], early[n_clip : 2 * n_clip]
    patch_w = early[2 * n_clip :].astype(jnp.bfloat16)
    act_one = jax.nn.silu(pre_one).astype(jnp.bfloat16)
    silu_time = jax.nn.silu(time_embed).astype(jnp.bfloat16)
    local_row = emb_first + jnp.arange(EMB_PAD, dtype=jnp.int32)
    block_row = local_row - ROW_BLOCK
    in_block = (block_row >= 0) & (block_row < 6 * D)
    block_part = jnp.where(in_block, block_row % 6, -1)
    block_line = jnp.where(in_block, block_row // 6, -1)
    chooser = jnp.arange(D, dtype=jnp.int32)[:, None] == block_line[None]
    silu_rows = matmul_low(silu_time, chooser.astype(jnp.bfloat16)).astype(jnp.bfloat16)
    part_mask = jnp.arange(6, dtype=jnp.int32)[:, None] == block_part[None]
    block_left = jnp.where(part_mask[None], silu_rows[:, None], 0).reshape(n_clip * 6, EMB_PAD)
    block_out = sum_clips(matmul_low(block_left, emb_rows)).reshape(n_clip, 6, D)
    all_mods = table[None] + (block_out + block_b.reshape(6, D))
    mods = lax.dynamic_slice_in_dim(all_mods, clip_id, 1, 0)
    my_embed = lax.dynamic_slice_in_dim(time_embed, clip_id, 1, 0)

    keep_part = jnp.sqrt(signal)[:, None, None, None]
    fade_part = jnp.sqrt(1.0 - signal)[:, None, None, None]
    noisy = (keep_part * latents + fade_part * noise).astype(jnp.bfloat16)
    frame_ids = frame_id * frame_dev + jnp.arange(frame_dev)
    patch_ids = jnp.arange(patches)
    place = jnp.concatenate(
        [sincos(patch_ids // PGRID, D // 2), sincos(patch_ids % PGRID, D // 2)], -1
    )[None, None]
    hidden_zero = matmul_low(noisy, patch_w) + patch_b + place + sincos(frame_ids, D)[None, :, None]

    def mod_row(number):
        return mods[:, number][:, None, None, :]

    def flat2(value):
        return value.reshape(-1, value.shape[-1])

    space_in = modulate(hidden_zero, mod_row(0), mod_row(1)).astype(jnp.bfloat16)
    live = live_len.astype(jnp.int32)
    space_q, space_k, space_v = split_qkv(matmul_low(flat2(space_in), space_qkv), space_bq, space_bv)
    space_o, space_lse = heads_forward("all", space_q, space_k, space_v, live)
    space_flat = space_o.reshape(clip_dev, frame_dev, patches, D)
    space_res = matmul_low(space_flat, space_out) + space_bo
    hidden_one = hidden_zero + mod_row(2) * space_res
    time_in = lax.all_to_all(
        hidden_one.astype(jnp.bfloat16), "frame", split_axis=2, concat_axis=1, tiled=True
    )
    time_in = jnp.swapaxes(time_in, 1, 2)
    frames = time_in.shape[2]
    time_q, time_k, time_v = split_qkv(matmul_low(flat2(time_in), time_qkv), time_bq, time_bv)
    time_o, time_lse = heads_forward(frames, time_q, time_k, time_v, live)
    time_back = jnp.swapaxes(time_o.reshape(clip_dev, local_pos, frames, D), 1, 2)
    time_flat = lax.all_to_all(time_back, "frame", split_axis=1, concat_axis=2, tiled=True)
    time_res = matmul_low(time_flat, time_out) + time_bo
    hidden_two = hidden_one + mod_row(2) * time_res
    cross_in = hidden_two.astype(jnp.bfloat16)
    cross_query = (matmul_low(flat2(cross_in), cross_q) + cross_bq).astype(jnp.bfloat16)
    cross_merged = matmul_low(jnp.pad(cap_rows[0], ((0, -L_CAP % 16), (0, 0))), cross_kv)
    cross_k = cross_merged[..., :D].astype(jnp.bfloat16)
    cross_v = (cross_merged[..., D:] + cross_bv).astype(jnp.bfloat16)
    cross_o, cross_lse = heads_forward("cross", cross_query, cross_k, cross_v, live)
    cross_flat = cross_o.reshape(clip_dev, frame_dev, patches, D)
    hidden_three = hidden_two + matmul_low(cross_flat, cross_out) + cross_bo
    dense_in = modulate(hidden_three, mod_row(3), mod_row(4)).astype(jnp.bfloat16)
    dense_pre = matmul_low(dense_in, fc_in) + fc_in_b
    dense_act = gelu_tanh(dense_pre).astype(jnp.bfloat16)
    dense_res = matmul_low(dense_act, fc_out) + fc_out_b
    hidden_four = hidden_three + mod_row(5) * dense_res
    final_mod = final_table[None] + my_embed[:, None, :]
    final_shift = final_mod[:, 0][:, None, None, :]
    final_scale = final_mod[:, 1][:, None, None, :]
    final_in = modulate(hidden_four, final_shift, final_scale).astype(jnp.bfloat16)
    predicted = matmul_low(final_in, final_w) + final_b
    miss = predicted - noise
    clip_error = jnp.sum(jnp.mean(miss * miss, -1), (1, 2))
    local_loss = jnp.sum(loss_weight * clip_error)

    def two_cores(value):
        return [value, shift(value, SWAP_CORE)]

    lefts = {
        label: two_cores(flat2(value).T)
        for label, value in (
            ("space_qkv", space_in),
            ("space_out", space_flat),
            ("time_qkv", time_in),
            ("time_out", time_flat),
            ("cross_q", cross_in),
            ("cross_out", cross_flat),
            ("fc_in", dense_in),
            ("fc_out", dense_act),
        )
    }

    def chunks_of(matrices, segments, rights, n_rows):
        arrays, where = [], {}
        for label, blocks in rights.items():
            where[label] = []
            for value, column in blocks:
                known = [k for k, other in enumerate(arrays) if other is value]
                if not known:
                    arrays.append(value)
                where[label].append((known[0] if known else len(arrays) - 1, column))
        order = {label: number for number, (label, rows, wide) in enumerate(matrices)}
        plan = grad_plan(matrices, segments, order, where)
        return core_chunks(plan, core_id, [lefts[label] for label in order], arrays, n_rows)

    grad_pred = (
        2.0 / miss.shape[-1] * (loss_weight / weight_total)[:, None, None, None] * miss
    ).astype(jnp.bfloat16)
    g_final_w = weight_grad(final_in, grad_pred)
    g_final_b = bias_grad(grad_pred)
    unused, pullback = jax.vjp(modulate, hidden_four, final_shift, final_scale)
    grad_hidden, grad_fshift, grad_fscale = pullback(back_low(grad_pred, final_w))
    grad_fmod = jnp.concatenate([grad_fshift.reshape(1, D), grad_fscale.reshape(1, D)], 0)
    grad_dense = (grad_hidden * mod_row(5)).astype(jnp.bfloat16)
    grad_gate_b = jnp.sum(grad_hidden * dense_res, (1, 2))
    dense_both = two_cores(flat2(grad_dense))
    g_fc_out_b = bias_grad(grad_dense)
    unused, pullback = jax.vjp(gelu_tanh, dense_pre)
    grad_pre = pullback(back_low(grad_dense, fc_out))[0].astype(jnp.bfloat16)
    pre_both = two_cores(flat2(grad_pre))
    dense_chunks = chunks_of(
        DENSE,
        DENSE_SEGS,
        {"fc_in": [(pre_both, j * D) for j in range(MLP // D)], "fc_out": [(dense_both, 0)]},
        DENSE_ROWS,
    )
    rights = {}
    g_fc_in_b = bias_grad(grad_pre)
    unused, pullback = jax.vjp(modulate, hidden_three, mod_row(3), mod_row(4))
    grad_input, grad_shift_b, grad_scale_b = pullback(back_low(grad_pre, fc_in))
    grad_hidden = grad_hidden + grad_input
    grad_cross = grad_hidden.astype(jnp.bfloat16)
    rights["cross_out"] = [(two_cores(flat2(grad_cross)), 0)]
    g_cross_bo = bias_grad(grad_cross)
    grad_cross_o = back_low(flat2(grad_cross), cross_out).astype(jnp.bfloat16)
    grad_cq, grad_ck, grad_cv = heads_backward(
        "cross", cross_query, cross_k, cross_v, live, cross_lse, grad_cross_o
    )
    grad_cq = grad_cq.reshape(clip_dev, frame_dev, patches, D)
    rights["cross_q"] = [(two_cores(flat2(grad_cq)), 0)]
    g_cross_bq = bias_grad(grad_cq)
    grad_hidden = grad_hidden + back_low(grad_cq, cross_q)
    grad_cv = grad_cv[:L_CAP]
    grad_ckv = jnp.concatenate([grad_ck[:L_CAP], grad_cv], -1)
    g_cross_bv = bias_grad(grad_cv)
    grad_ckv = grad_ckv + shift(grad_ckv, SWAP_CORE)
    pad_rows = lambda value: jnp.pad(value, ((0, -L_CAP % LANES), (0, 0)))
    cap_twice = pad_rows(cap_rows[0]).T
    lefts["cross_kv"] = [jnp.concatenate([cap_twice, cap_twice], 1)]
    ckv_parts = [jnp.concatenate([pad_rows(part) for part in halves(grad_ckv)], 0)]
    rights["cross_kv"] = [(ckv_parts, 0), (ckv_parts, D)]
    grad_ckv = grad_ckv + shift(grad_ckv, SWAP_X)
    grad_cap_rows = two_parts(lambda part: back_low(part, cross_kv), grad_ckv)

    grad_time = (grad_hidden * mod_row(2)).astype(jnp.bfloat16)
    rights["time_out"] = [(two_cores(flat2(grad_time)), 0)]
    g_time_bo = bias_grad(grad_time)
    grad_time_o = lax.all_to_all(
        back_low(grad_time, time_out).astype(jnp.bfloat16),
        "frame",
        split_axis=2,
        concat_axis=1,
        tiled=True,
    )
    grad_time_o = flat2(jnp.swapaxes(grad_time_o, 1, 2))
    grad_tqkv = [
        piece.reshape(clip_dev, local_pos, frames, D)
        for piece in heads_backward(frames, time_q, time_k, time_v, live, time_lse, grad_time_o)
    ]
    rights["time_qkv"] = [(two_cores(flat2(part)), 0) for part in grad_tqkv]
    g_time_bq = bias_grad(grad_tqkv[0])
    g_time_bv = bias_grad(grad_tqkv[2])
    grad_tqkv = lax.all_to_all(
        jnp.swapaxes(jnp.concatenate(grad_tqkv, -1), 1, 2), "frame", split_axis=1, concat_axis=2, tiled=True
    )
    grad_gate_a = jnp.sum(grad_hidden * time_res, (1, 2))
    grad_hidden = grad_hidden + back_low(grad_tqkv, time_qkv)
    grad_gate_a = grad_gate_a + jnp.sum(grad_hidden * space_res, (1, 2))
    grad_space = (grad_hidden * mod_row(2)).astype(jnp.bfloat16)
    rights["space_out"] = [(two_cores(flat2(grad_space)), 0)]
    g_space_bo = bias_grad(grad_space)
    grad_space_o = back_low(flat2(grad_space), space_out).astype(jnp.bfloat16)
    grad_sqkv = [
        piece.reshape(clip_dev, frame_dev, patches, D)
        for piece in heads_backward("all", space_q, space_k, space_v, live, space_lse, grad_space_o)
    ]
    rights["space_qkv"] = [(two_cores(flat2(part)), 0) for part in grad_sqkv]
    attend_chunks = chunks_of(ATTEND, ATTEND_SEGS, rights, ATTEND_ROWS)
    g_space_bq = bias_grad(grad_sqkv[0])
    g_space_bv = bias_grad(grad_sqkv[2])
    grad_sqkv = jnp.concatenate(grad_sqkv, -1)
    unused, pullback = jax.vjp(modulate, hidden_zero, mod_row(0), mod_row(1))
    grad_input, grad_shift_a, grad_scale_a = pullback(back_low(grad_sqkv, space_qkv))
    grad_hidden = grad_hidden + grad_input
    g_patch_w = weight_split(noisy, grad_hidden)
    g_patch_b = bias_grad(grad_hidden)
    grad_mods = jnp.concatenate(
        [
            grad_shift_a.reshape(clip_dev, D),
            grad_scale_a.reshape(clip_dev, D),
            grad_gate_a,
            grad_shift_b.reshape(clip_dev, D),
            grad_scale_b.reshape(clip_dev, D),
            grad_gate_b,
            grad_fmod,
        ],
        0,
    )

    unused, pullback = jax.vjp(gelu_tanh, cap_pre[0])
    grad_cap_act = two_parts(lambda part: back_low(part, cap_last), grad_cap_rows)
    grad_cap_pre = pullback(grad_cap_act[:, two_first : two_first + D])[0]
    cap_right = lax.all_gather(
        jnp.stack([grad_cap_pre, grad_cap_rows]), "clip", axis=1, tiled=True
    )
    null_sum = jnp.sum(jnp.where(all_null[:, None, None], cap_right[0].reshape(n_clip, L_CAP, D), 0.0), 0)
    g_cap_b1 = bias_grad(grad_cap_pre)
    g_cap_b2 = bias_grad(grad_cap_rows)

    once = frame_id == 0
    gathered_mods = jnp.where(own_clip[:, None, None], grad_mods[None], 0.0)
    ends = jnp.concatenate([g_final_b, local_loss.reshape(1)])
    vector_rows = [
        g_patch_b,
        jnp.where(once, g_cap_b1, 0.0),
        jnp.where(once, g_cap_b2, 0.0),
        g_space_bq,
        g_space_bv,
        g_space_bo,
        g_time_bq,
        g_time_bv,
        g_time_bo,
        g_cross_bq,
        g_cross_bv,
        g_cross_bo,
        g_fc_in_b.reshape(-1, D),
        g_fc_out_b,
        jnp.pad(ends, (0, D - ends.shape[0])),
    ]
    small = [gathered_mods.reshape(-1, D), g_patch_w, g_final_w.reshape(PATCH_VALUES, D)]
    small = small + [value.reshape(-1, D) for value in vector_rows]
    spare = -sum(value.shape[0] for value in small) % 8
    small = jnp.concatenate(small + [jnp.zeros((spare, D), jnp.float32)] * (spare > 0), 0)
    dense_grad, small = collect_shard(
        dense_chunks,
        160,
        3,
        small=small,
    )
    dense_grad = dense_grad.reshape(DENSE_ROWS, D)
    at = 8 * n_clip
    gathered_mods = small[:at].reshape(n_clip, 8, D)
    g_patch_w = small[at : at + PATCH_VALUES]
    g_final_w = small[at + PATCH_VALUES : at + 2 * PATCH_VALUES]
    rest = small[at + 2 * PATCH_VALUES :]
    n_whole = 12 + MLP // D + 1
    loss_sum = rest[n_whole, PATCH_VALUES]
    vector_grad = jnp.concatenate([rest[:n_whole].reshape(-1), rest[n_whole, :PATCH_VALUES]])

    grad_zero = gathered_mods[:, :6]
    grad_final = gathered_mods[:, 6:]
    zero_rows = grad_zero.reshape(n_clip * 6, D)
    back_rows = two_parts(lambda part: back_low(part, emb_rows), zero_rows)
    back_rows = jnp.sum(jnp.where(part_mask[None], back_rows.reshape(n_clip, 6, EMB_PAD), 0.0), 1)
    grad_silu = lax.dot_general(
        back_rows,
        chooser.astype(jnp.float32),
        (((1,), (1,)), ((), ())),
        precision=lax.Precision.HIGHEST,
        preferred_element_type=jnp.float32,
    )
    grad_silu = sum_clips(grad_silu)
    unused, pullback = jax.vjp(jax.nn.silu, time_embed)
    grad_embed = grad_final[:, 0] + grad_final[:, 1] + pullback(grad_silu)[0]
    grad_act = two_parts(lambda part: back_low(part, time_two), grad_embed)
    grad_act = sum_clips(jnp.where(at_start, grad_act, 0.0))
    unused, pullback = jax.vjp(jax.nn.silu, pre_one)
    grad_one = pullback(grad_act)[0]
    g_table = jnp.sum(grad_zero, 0)
    vector_sum = flatten_all(
        [
            vector_grad[:D],
            jnp.sum(grad_one, 0),
            jnp.sum(grad_embed, 0),
            g_table,
            vector_grad[D:],
            g_table,
            jnp.sum(grad_final, 0),
        ]
    )

    per = EMB_PAD // 4
    quarter_row = emb_first + frame_id * per + jnp.arange(per, dtype=jnp.int32)
    time_left = jnp.concatenate(
        [
            jnp.pad(freq_in, ((0, 0), (ROW_TIME_ONE, EMB_PAD - ROW_TIME_TWO))),
            jnp.pad(act_one, ((0, 0), (ROW_TIME_TWO, EMB_PAD - ROW_BLOCK))),
        ],
        0,
    )
    time_left = jnp.where(at_start, time_left, jnp.zeros_like(time_left))
    small_left = lax.dynamic_slice_in_dim(
        jnp.concatenate([time_left, block_left], 0), frame_id * per, per, 1
    )
    small_right = jnp.concatenate([grad_one, grad_embed, zero_rows], 0)
    first_kind = (quarter_row < ROW_CAP_TWO)[None]
    no_left = jnp.zeros_like(cap_left)
    g_null = from_cap_rows(two_parts(lambda part: back_low(part, cap_weights), null_sum))
    n_null = -(-null_end // D)
    n_known = -(-(2 * PATCH_VALUES + n_null) // 16) * 16
    null_rows = jnp.pad(g_null.reshape(-1), (0, (n_known - 2 * PATCH_VALUES) * D - null_end))
    known = jnp.concatenate([g_patch_w, g_final_w, null_rows.reshape(-1, D)], 0)
    known_row = np.concatenate(
        [np.arange(PATCH_VALUES), ROW_FINAL + np.arange(n_known - PATCH_VALUES)]
    ).astype(np.int32)
    known_left = (jnp.asarray(known_row)[:, None] == quarter_row[None]).astype(jnp.bfloat16)
    emb_left = jnp.concatenate(
        [
            small_left,
            jnp.where(first_kind, cap_left, no_left),
            jnp.where(first_kind, no_left, cap_left),
            known_left,
        ],
        0,
    )
    emb_right = jnp.concatenate([small_right, cap_right[0], cap_right[1], known], 0)
    emb_grad = weight_split(emb_left, emb_right)
    unit = (
        LANE_TILES * (frame_id * per + jnp.arange(per, dtype=jnp.int32))[:, None]
        + jnp.arange(D, dtype=jnp.int32)[None] // LANES
        - emb_shift
    )
    emb_grad = jnp.where((unit >= 0) & (unit < EMB_UNITS), emb_grad, 0.0)

    attend_grad, emb_whole = collect_shard(
        attend_chunks,
        208,
        4,
        part=emb_grad,
    )
    attend_grad = attend_grad.reshape(ATTEND_ROWS, D)
    local_square = sum(jnp.sum(value * value) for value in (dense_grad, attend_grad, emb_whole))
    vector_square = jnp.sum(vector_sum * vector_sum)
    grad_norm = jnp.sqrt(sum_clips(local_square.reshape(1))[0] + vector_square)
    factor = jnp.minimum(1.0, CLIP_LIMIT / (grad_norm + NORM_FLOOR))
    scale = factor.reshape(1)
    dense_r = step_shard(
        dense_grad,
        jnp.asarray(step_table(DENSE_SEGS, STEP_BLOCK, DENSE_ROWS))[clip_id],
        (1, 4),
        DENSE_ROWS,
        scale,
        (dense_w, dense_m, dense_v, dense_e),
    )
    attend_r = step_shard(
        attend_grad,
        jnp.asarray(step_table(ATTEND_SEGS, STEP_BLOCK, ATTEND_ROWS))[clip_id],
        (1, 2, 3),
        ATTEND_ROWS,
        scale,
        (attend_w, attend_m, attend_v, attend_e),
    )
    emb_flat = rows_to_flat(emb_whole.reshape(EMB_PAD, D))
    emb_owned = lax.dynamic_slice_in_dim(emb_flat, emb_shift, EMB_UNITS, 0).reshape(-1)
    embed_r = adam_step(embed_w, emb_owned, embed_m, embed_v, embed_e, factor)
    vector_r = adam_step(vector_w, vector_sum, vector_m, vector_v, vector_e, factor)
    return (
        loss_sum,
        weight_total,
        grad_norm,
        embed_r[0],
        attend_r[0],
        dense_r[0],
        vector_r[0],
        embed_r[1],
        attend_r[1],
        dense_r[1],
        vector_r[1],
        embed_r[2],
        attend_r[2],
        dense_r[2],
        vector_r[2],
        embed_r[3],
        attend_r[3],
        dense_r[3],
        vector_r[3],
    )


def pick_plan(mesh):
    if mesh.shape["frame"] == X_SIZE * CORES and mesh.shape["clip"] == N_OWN:
        return shards_block
    return shards


def solution(mesh):
    in_specs = (
        P("clip", "frame", None, None),
        P("clip", "frame", None, None),
        P("clip"),
        P("clip", None, None),
        P("clip"),
        P("clip"),
        P("clip"),
        P("clip"),
        P("clip"),
        P("clip"),
        P(),
        P("clip"),
        P("clip"),
        P("clip"),
        P(),
        P("clip"),
        P("clip"),
        P("clip"),
        P(),
        P("clip"),
        P("clip"),
        P("clip"),
        P(),
    )
    out_specs = (
        P(),
        P(),
        P(),
        P("clip"),
        P("clip"),
        P("clip"),
        P(),
        P("clip"),
        P("clip"),
        P("clip"),
        P(),
        P("clip"),
        P("clip"),
        P("clip"),
        P(),
        P("clip"),
        P("clip"),
        P("clip"),
        P(),
    )
    return jax.shard_map(pick_plan(mesh), mesh=mesh, in_specs=in_specs, out_specs=out_specs, check_vma=False)
```

```python
import math
from functools import partial

import jax
import jax.numpy as jnp
import numpy as np
from jax import lax
from jax.experimental import pallas as pl
from jax.experimental.pallas import tpu as pltpu
from jax.sharding import PartitionSpec as P

D = 1152
HEADS = 16
MLP = 4608
CAPW = 4096
L_CAP = 120
TFREQ = 256
PATCH_VALUES = 16
PGRID = 16
STEP = 10


NORM_FLOOR = 1e-06
CLIP_LIMIT = 1.0
SNR_LIMIT = 5.0
BETA_FIRST = 0.5
BETA_SECOND = 0.5
LEARN_RATE = 0.02
WEIGHT_DECAY = 0.01
ADAM_FLOOR = 1e-08
AVERAGE_KEEP = 0.9999
MASKED_SCORE = -1e30


def embed_shapes():
    return [
        (PATCH_VALUES, D),
        (TFREQ, D),
        (D, D),
        (D, 6 * D),
        (CAPW, D),
        (D, D),
        (D, PATCH_VALUES),
        (L_CAP, CAPW),
    ]


def attend_shapes():
    return [(D, 3 * D), (D, D), (D, 3 * D), (D, D), (D, D), (D, 2 * D), (D, D)]


def dense_shapes():
    return [(D, MLP), (MLP, D)]


def vector_shapes():
    return [(D,)] * 3 + [(6 * D,)] + [(D,)] * 11 + [(MLP,), (D,), (PATCH_VALUES,), (6, D), (2, D)]


def split_flat(flat, shapes):
    pieces = []
    offset = 0
    for extent in shapes:
        length = math.prod(extent)
        pieces.append(flat[offset : offset + length].reshape(extent))
        offset += length
    return pieces


def flatten_all(pieces):
    return jnp.concatenate([piece.reshape(-1) for piece in pieces])


def reduce_group(grad):
    n_clip = lax.axis_size("clip")
    n_frame = lax.axis_size("frame")
    reorder = grad.reshape(n_clip, n_frame, -1).swapaxes(0, 1).reshape(-1)
    share = lax.psum_scatter(reorder, ("frame", "clip"), scatter_dimension=0, tiled=True)
    return lax.all_gather(share, "frame", axis=0, tiled=True)


def sincos(places, width):
    half = width // 2
    omega = jnp.exp(-math.log(10000.0) * jnp.arange(half, dtype=jnp.float32) / half)
    angle = places.astype(jnp.float32)[..., None] * omega
    return jnp.concatenate([jnp.sin(angle), jnp.cos(angle)], -1)


def modulate(hidden, shift, scale):
    center = hidden - jnp.mean(hidden, -1, keepdims=True)
    normed = center * lax.rsqrt(jnp.mean(center * center, -1, keepdims=True) + NORM_FLOOR)
    return normed * (1.0 + scale) + shift


def gelu_tanh(value):
    return jax.nn.gelu(value, approximate=True)


def matmul_low(left, right):
    return lax.dot_general(
        left, right, (((left.ndim - 1,), (0,)), ((), ())), preferred_element_type=jnp.float32
    )


def halves(value):
    upper = lax.optimization_barrier(value.astype(jnp.bfloat16))
    return (upper, (value - upper.astype(jnp.float32)).astype(jnp.bfloat16))


def back_low(grads, weight):
    return lax.dot_general(
        grads, weight, (((grads.ndim - 1,), (1,)), ((), ())), preferred_element_type=jnp.float32
    )


def back_split(grads, weight):
    upper, lower = halves(grads)
    return back_low(upper, weight) + back_low(lower, weight)


def weight_grad(inputs, grads):
    left = inputs.reshape(-1, inputs.shape[-1])
    right = grads.reshape(-1, grads.shape[-1])
    return lax.dot_general(
        left, right, (((0,), (0,)), ((), ())), preferred_element_type=jnp.float32
    )


def weight_split(inputs, grads):
    upper, lower = halves(grads)
    return weight_grad(inputs, upper) + weight_grad(inputs, lower)


def bias_grad(grads):
    return jnp.sum(grads.astype(jnp.float32).reshape(-1, grads.shape[-1]), 0)


def heads_of(tensor, batch):
    return tensor.reshape(batch, -1, HEADS, tensor.shape[-1] // HEADS)


def split_qkv(merged, bias_q, bias_v):
    width = merged.shape[-1] // 3
    return (
        (merged[..., :width] + bias_q).astype(jnp.bfloat16),
        merged[..., width : 2 * width].astype(jnp.bfloat16),
        (merged[..., 2 * width :] + bias_v).astype(jnp.bfloat16),
    )


def attend_scores(queries, key_rows, mask):
    scores = jnp.einsum("bqhe,bkhe->bhqk", queries, key_rows, preferred_element_type=jnp.float32)
    scores = scores * queries.shape[-1] ** (-0.5)
    if mask is not None:
        scores = jnp.where(mask[:, None, None, :], scores, MASKED_SCORE)
    return scores


def attend_forward(queries, key_rows, values, mask):
    scores = attend_scores(queries, key_rows, mask)
    summit = jnp.max(scores, -1, keepdims=True)
    powers = jnp.exp(scores - summit)
    totals = jnp.sum(powers, -1, keepdims=True)
    probs = (powers / totals).astype(jnp.bfloat16)
    output = jnp.einsum("bhqk,bkhe->bqhe", probs, values, preferred_element_type=jnp.float32)
    return (output.astype(jnp.bfloat16), summit + jnp.log(totals))


def attend_backward(queries, key_rows, values, mask, log_total, grad_out):
    scale = queries.shape[-1] ** (-0.5)
    probs = jnp.exp(attend_scores(queries, key_rows, mask) - log_total)
    grad_probs = jnp.einsum("bqhe,bkhe->bhqk", grad_out, values, preferred_element_type=jnp.float32)
    grad_scores = (probs * (grad_probs - jnp.sum(probs * grad_probs, -1, keepdims=True))).astype(
        jnp.bfloat16
    )
    grad_query = (
        jnp.einsum("bhqk,bkhe->bqhe", grad_scores, key_rows, preferred_element_type=jnp.float32)
        * scale
    )
    grad_keys = (
        jnp.einsum("bhqk,bqhe->bkhe", grad_scores, queries, preferred_element_type=jnp.float32)
        * scale
    )
    grad_values = jnp.einsum(
        "bhqk,bqhe->bkhe", probs.astype(jnp.bfloat16), grad_out, preferred_element_type=jnp.float32
    )
    return (grad_query, grad_keys, grad_values)


def unpack_all(gathered):
    return (
        split_flat(gathered[0], embed_shapes()),
        split_flat(gathered[1], attend_shapes()),
        split_flat(gathered[2], dense_shapes()),
    )


def adam_step(master, grad, first, second, average, factor):
    keep = min(AVERAGE_KEEP, (1.0 + STEP) / (10.0 + STEP))
    grad = grad * factor
    first = BETA_FIRST * first + (1.0 - BETA_FIRST) * grad
    second = BETA_SECOND * second + (1.0 - BETA_SECOND) * grad * grad
    moved = (
        first
        / (1.0 - BETA_FIRST**STEP)
        / (jnp.sqrt(second / (1.0 - BETA_SECOND**STEP)) + ADAM_FLOOR)
    )
    master = master - LEARN_RATE * (moved + WEIGHT_DECAY * master)
    return (master, first, second, keep * average + (1.0 - keep) * master)


def shards(
    latents,
    noise,
    timesteps,
    captions,
    cap_lengths,
    null_flags,
    sample_weight,
    embed_w,
    attend_w,
    dense_w,
    vector_w,
    embed_m,
    attend_m,
    dense_m,
    vector_m,
    embed_v,
    attend_v,
    dense_v,
    vector_v,
    embed_e,
    attend_e,
    dense_e,
    vector_e,
):
    clip_dev, frame_dev, patches = (latents.shape[0], latents.shape[1], latents.shape[2])
    n_frame = lax.axis_size("frame")
    n_clip = lax.axis_size("clip")
    local_pos = patches // n_frame
    gathered = (
        lax.all_gather(embed_w.astype(jnp.bfloat16), "clip", axis=0, tiled=True),
        lax.all_gather(attend_w.astype(jnp.bfloat16), "clip", axis=0, tiled=True),
        lax.all_gather(dense_w.astype(jnp.bfloat16), "clip", axis=0, tiled=True),
    )
    embeds, attends, denses = unpack_all(gathered)
    patch_w, time_one, time_two, block_w, cap_one, cap_two, final_w, null_caption = embeds
    space_qkv, space_out, time_qkv, time_out, cross_q, cross_kv, cross_out = attends
    fc_in, fc_out = denses
    (
        patch_b,
        time_b1,
        time_b2,
        block_b,
        cap_b1,
        cap_b2,
        space_bq,
        space_bv,
        space_bo,
        time_bq,
        time_bv,
        time_bo,
        cross_bq,
        cross_bv,
        cross_bo,
        fc_in_b,
        fc_out_b,
        final_b,
        table,
        final_table,
    ) = split_flat(vector_w, vector_shapes())
    angle = (timesteps.astype(jnp.float32) / 1000.0 + 0.008) / 1.008 * (math.pi / 2)
    signal = jnp.cos(angle) ** 2
    ratio = signal / (1.0 - signal)
    loss_weight = sample_weight * jnp.minimum(ratio, SNR_LIMIT) / ratio
    weight_total = lax.psum(jnp.sum(loss_weight), "clip")
    keep_part = jnp.sqrt(signal)[:, None, None, None]
    fade_part = jnp.sqrt(1.0 - signal)[:, None, None, None]
    noisy = (keep_part * latents + fade_part * noise).astype(jnp.bfloat16)
    frame_ids = lax.axis_index("frame") * frame_dev + jnp.arange(frame_dev)
    patch_ids = jnp.arange(patches)
    place = jnp.concatenate(
        [sincos(patch_ids // PGRID, D // 2), sincos(patch_ids % PGRID, D // 2)], -1
    )[None, None]
    hidden_zero = matmul_low(noisy, patch_w) + patch_b + place + sincos(frame_ids, D)[None, :, None]
    freq_in = sincos(timesteps, TFREQ).astype(jnp.bfloat16)
    pre_one = matmul_low(freq_in, time_one) + time_b1
    act_one = jax.nn.silu(pre_one).astype(jnp.bfloat16)
    time_embed = matmul_low(act_one, time_two) + time_b2
    silu_time = jax.nn.silu(time_embed).astype(jnp.bfloat16)
    mods = table[None] + (matmul_low(silu_time, block_w) + block_b).reshape(clip_dev, 6, D)

    def mod_row(number):
        return mods[:, number][:, None, None, :]

    is_null = null_flags == 1
    cap_in = jnp.where(is_null[:, None, None], null_caption[None], captions)
    cap_pre = matmul_low(cap_in, cap_one) + cap_b1
    cap_act = gelu_tanh(cap_pre).astype(jnp.bfloat16)
    cap_rows = (matmul_low(cap_act, cap_two) + cap_b2).astype(jnp.bfloat16)
    live_len = jnp.where(is_null, L_CAP, cap_lengths)
    key_mask = jnp.arange(L_CAP)[None, :] < live_len[:, None]
    space_in = modulate(hidden_zero, mod_row(0), mod_row(1)).astype(jnp.bfloat16)
    space_q, space_k, space_v = (
        heads_of(piece, clip_dev * frame_dev)
        for piece in split_qkv(matmul_low(space_in, space_qkv), space_bq, space_bv)
    )
    space_o, space_lse = attend_forward(space_q, space_k, space_v, None)
    space_flat = space_o.reshape(clip_dev, frame_dev, patches, D)
    space_res = matmul_low(space_flat, space_out) + space_bo
    hidden_one = hidden_zero + mod_row(2) * space_res
    time_in = lax.all_to_all(
        hidden_one.astype(jnp.bfloat16), "frame", split_axis=2, concat_axis=1, tiled=True
    )
    time_in = jnp.swapaxes(time_in, 1, 2)
    frames = time_in.shape[2]
    time_q, time_k, time_v = (
        heads_of(piece, clip_dev * local_pos)
        for piece in split_qkv(matmul_low(time_in, time_qkv), time_bq, time_bv)
    )
    time_o, time_lse = attend_forward(time_q, time_k, time_v, None)
    time_back = jnp.swapaxes(time_o.reshape(clip_dev, local_pos, frames, D), 1, 2)
    time_flat = lax.all_to_all(time_back, "frame", split_axis=1, concat_axis=2, tiled=True)
    time_res = matmul_low(time_flat, time_out) + time_bo
    hidden_two = hidden_one + mod_row(2) * time_res
    cross_in = hidden_two.astype(jnp.bfloat16)
    cross_query = heads_of(
        (matmul_low(cross_in, cross_q) + cross_bq).astype(jnp.bfloat16), clip_dev
    )
    cross_merged = matmul_low(cap_rows, cross_kv)
    cross_k = heads_of(cross_merged[..., :D].astype(jnp.bfloat16), clip_dev)
    cross_v = heads_of((cross_merged[..., D:] + cross_bv).astype(jnp.bfloat16), clip_dev)
    cross_o, cross_lse = attend_forward(cross_query, cross_k, cross_v, key_mask)
    cross_flat = cross_o.reshape(clip_dev, frame_dev, patches, D)
    hidden_three = hidden_two + matmul_low(cross_flat, cross_out) + cross_bo
    dense_in = modulate(hidden_three, mod_row(3), mod_row(4)).astype(jnp.bfloat16)
    dense_pre = matmul_low(dense_in, fc_in) + fc_in_b
    dense_act = gelu_tanh(dense_pre).astype(jnp.bfloat16)
    dense_res = matmul_low(dense_act, fc_out) + fc_out_b
    hidden_four = hidden_three + mod_row(5) * dense_res
    final_mod = final_table[None] + time_embed[:, None, :]
    final_shift = final_mod[:, 0][:, None, None, :]
    final_scale = final_mod[:, 1][:, None, None, :]
    final_in = modulate(hidden_four, final_shift, final_scale).astype(jnp.bfloat16)
    predicted = matmul_low(final_in, final_w) + final_b
    miss = predicted - noise
    clip_error = jnp.sum(jnp.mean(miss * miss, -1), (1, 2))
    local_loss = jnp.sum(loss_weight * clip_error)
    grad_pred = (
        2.0 / miss.shape[-1] * (loss_weight / weight_total)[:, None, None, None] * miss
    ).astype(jnp.bfloat16)
    g_final_w = weight_grad(final_in, grad_pred)
    g_final_b = bias_grad(grad_pred)
    unused, pullback = jax.vjp(modulate, hidden_four, final_shift, final_scale)
    grad_hidden, grad_fshift, grad_fscale = pullback(back_low(grad_pred, final_w))
    grad_fmod = jnp.stack([grad_fshift.reshape(clip_dev, D), grad_fscale.reshape(clip_dev, D)], 1)
    g_final_table = jnp.sum(grad_fmod, 0)
    grad_time_embed = grad_fmod[:, 0] + grad_fmod[:, 1]
    grad_dense = (grad_hidden * mod_row(5)).astype(jnp.bfloat16)
    grad_gate_b = jnp.sum(grad_hidden * dense_res, (1, 2))
    g_fc_out = weight_grad(dense_act, grad_dense)
    g_fc_out_b = bias_grad(grad_dense)
    unused, pullback = jax.vjp(gelu_tanh, dense_pre)
    grad_pre = pullback(back_low(grad_dense, fc_out))[0].astype(jnp.bfloat16)
    g_fc_in = weight_grad(dense_in, grad_pre)
    g_fc_in_b = bias_grad(grad_pre)
    dense_owned = reduce_group(flatten_all([g_fc_in, g_fc_out]))
    unused, pullback = jax.vjp(modulate, hidden_three, mod_row(3), mod_row(4))
    grad_input, grad_shift_b, grad_scale_b = pullback(back_low(grad_pre, fc_in))
    grad_hidden = grad_hidden + grad_input
    grad_cross = grad_hidden.astype(jnp.bfloat16)
    g_cross_out = weight_grad(cross_flat, grad_cross)
    g_cross_bo = bias_grad(grad_cross)
    grad_cross_o = heads_of(back_low(grad_cross, cross_out).astype(jnp.bfloat16), clip_dev)
    grad_cq, grad_ck, grad_cv = attend_backward(
        cross_query, cross_k, cross_v, key_mask, cross_lse, grad_cross_o
    )
    grad_cq = grad_cq.astype(jnp.bfloat16).reshape(clip_dev, frame_dev, patches, D)
    g_cross_q = weight_grad(cross_in, grad_cq)
    g_cross_bq = bias_grad(grad_cq)
    grad_hidden = grad_hidden + back_low(grad_cq, cross_q)
    grad_cv = grad_cv.reshape(clip_dev, L_CAP, D)
    grad_ckv = jnp.concatenate([grad_ck.reshape(clip_dev, L_CAP, D), grad_cv], -1)
    g_cross_kv = weight_split(cap_rows, grad_ckv)
    g_cross_bv = bias_grad(grad_cv)
    grad_cap_rows = back_split(grad_ckv, cross_kv)
    grad_time = (grad_hidden * mod_row(2)).astype(jnp.bfloat16)
    g_time_out = weight_grad(time_flat, grad_time)
    g_time_bo = bias_grad(grad_time)
    grad_time_o = lax.all_to_all(
        back_low(grad_time, time_out).astype(jnp.bfloat16),
        "frame",
        split_axis=2,
        concat_axis=1,
        tiled=True,
    )
    grad_time_o = heads_of(jnp.swapaxes(grad_time_o, 1, 2), clip_dev * local_pos)
    grad_tq, grad_tk, grad_tv = attend_backward(time_q, time_k, time_v, None, time_lse, grad_time_o)
    grad_tqkv = jnp.concatenate(
        [
            piece.astype(jnp.bfloat16).reshape(clip_dev, local_pos, frames, D)
            for piece in (grad_tq, grad_tk, grad_tv)
        ],
        -1,
    )
    g_time_qkv = weight_grad(time_in, grad_tqkv)
    g_time_bq = bias_grad(grad_tqkv[..., :D])
    g_time_bv = bias_grad(grad_tqkv[..., 2 * D :])
    grad_tqkv = lax.all_to_all(
        jnp.swapaxes(grad_tqkv, 1, 2), "frame", split_axis=1, concat_axis=2, tiled=True
    )
    grad_gate_a = jnp.sum(grad_hidden * time_res, (1, 2))
    grad_hidden = grad_hidden + back_low(grad_tqkv, time_qkv)
    grad_gate_a = grad_gate_a + jnp.sum(grad_hidden * space_res, (1, 2))
    grad_space = (grad_hidden * mod_row(2)).astype(jnp.bfloat16)
    g_space_out = weight_grad(space_flat, grad_space)
    g_space_bo = bias_grad(grad_space)
    grad_space_o = heads_of(
        back_low(grad_space, space_out).astype(jnp.bfloat16), clip_dev * frame_dev
    )
    grad_sq, grad_sk, grad_sv = attend_backward(
        space_q, space_k, space_v, None, space_lse, grad_space_o
    )
    grad_sqkv = jnp.concatenate(
        [
            piece.astype(jnp.bfloat16).reshape(clip_dev, frame_dev, patches, D)
            for piece in (grad_sq, grad_sk, grad_sv)
        ],
        -1,
    )
    g_space_qkv = weight_grad(space_in, grad_sqkv)
    g_space_bq = bias_grad(grad_sqkv[..., :D])
    g_space_bv = bias_grad(grad_sqkv[..., 2 * D :])
    attend_owned = reduce_group(
        flatten_all(
            [g_space_qkv, g_space_out, g_time_qkv, g_time_out, g_cross_q, g_cross_kv, g_cross_out]
        )
    )
    unused, pullback = jax.vjp(modulate, hidden_zero, mod_row(0), mod_row(1))
    grad_input, grad_shift_a, grad_scale_a = pullback(back_low(grad_sqkv, space_qkv))
    grad_hidden = grad_hidden + grad_input
    g_patch_w = weight_split(noisy, grad_hidden)
    g_patch_b = bias_grad(grad_hidden)
    grad_mods = jnp.stack(
        [
            grad_shift_a.reshape(clip_dev, D),
            grad_scale_a.reshape(clip_dev, D),
            grad_gate_a,
            grad_shift_b.reshape(clip_dev, D),
            grad_scale_b.reshape(clip_dev, D),
            grad_gate_b,
        ],
        1,
    )
    g_table = jnp.sum(grad_mods, 0)
    grad_zero = grad_mods.reshape(clip_dev, 6 * D)
    g_block_b = jnp.sum(grad_zero, 0)
    g_block_w = weight_split(silu_time, grad_zero)
    unused, pullback = jax.vjp(jax.nn.silu, time_embed)
    grad_time_embed = grad_time_embed + pullback(back_split(grad_zero, block_w))[0]
    g_time_b2 = jnp.sum(grad_time_embed, 0)
    g_time_two = weight_split(act_one, grad_time_embed)
    unused, pullback = jax.vjp(jax.nn.silu, pre_one)
    grad_pre_one = pullback(back_split(grad_time_embed, time_two))[0]
    g_time_b1 = jnp.sum(grad_pre_one, 0)
    g_time_one = weight_split(freq_in, grad_pre_one)
    g_cap_b2 = bias_grad(grad_cap_rows)
    g_cap_two = weight_split(cap_act, grad_cap_rows)
    unused, pullback = jax.vjp(gelu_tanh, cap_pre)
    grad_cap_pre = pullback(back_split(grad_cap_rows, cap_two))[0]
    g_cap_b1 = bias_grad(grad_cap_pre)
    g_cap_one = weight_split(cap_in, grad_cap_pre)
    grad_cap_in = back_split(grad_cap_pre, cap_one)
    g_null = jnp.sum(jnp.where(is_null[:, None, None], grad_cap_in, 0.0), 0)
    embed_owned = reduce_group(
        flatten_all(
            [g_patch_w, g_time_one, g_time_two, g_block_w, g_cap_one, g_cap_two, g_final_w, g_null]
        )
    )
    vector_grad = flatten_all(
        [
            g_patch_b,
            g_time_b1,
            g_time_b2,
            g_block_b,
            g_cap_b1,
            g_cap_b2,
            g_space_bq,
            g_space_bv,
            g_space_bo,
            g_time_bq,
            g_time_bv,
            g_time_bo,
            g_cross_bq,
            g_cross_bv,
            g_cross_bo,
            g_fc_in_b,
            g_fc_out_b,
            g_final_b,
            g_table,
            g_final_table,
        ]
    )
    vector_sum, loss_sum = lax.psum((vector_grad, local_loss), ("frame", "clip"))
    owned = (embed_owned, attend_owned, dense_owned)
    local_square = (
        sum((jnp.sum(shard_piece * shard_piece) for shard_piece in owned))
        + jnp.sum(vector_sum * vector_sum) / n_clip
    )
    grad_norm = jnp.sqrt(lax.psum(local_square, "clip"))
    factor = jnp.minimum(1.0, CLIP_LIMIT / (grad_norm + NORM_FLOOR))
    embed_r = adam_step(embed_w, owned[0], embed_m, embed_v, embed_e, factor)
    attend_r = adam_step(attend_w, owned[1], attend_m, attend_v, attend_e, factor)
    dense_r = adam_step(dense_w, owned[2], dense_m, dense_v, dense_e, factor)
    vector_r = adam_step(vector_w, vector_sum, vector_m, vector_v, vector_e, factor)
    return (
        loss_sum,
        weight_total,
        grad_norm,
        embed_r[0],
        attend_r[0],
        dense_r[0],
        vector_r[0],
        embed_r[1],
        attend_r[1],
        dense_r[1],
        vector_r[1],
        embed_r[2],
        attend_r[2],
        dense_r[2],
        vector_r[2],
        embed_r[3],
        attend_r[3],
        dense_r[3],
        vector_r[3],
    )


AXES = ("frame", "clip")
LANES = 128
LANE_TILES = D // LANES
EMB_PAD = 1824


X_SIZE, CORES, Z_SIZE, Y_SIZE = 2, 2, 4, 2
N_OWN = Z_SIZE * Y_SIZE
RING = [(0, 0), (1, 0), (2, 0), (3, 0), (3, 1), (2, 1), (1, 1), (0, 1)]
RING_CLIP = [z * Y_SIZE + y for z, y in RING]
CLIP_RING = [RING_CLIP.index(c) for c in range(N_OWN)]


def pairs(move):
    out = []
    for x in range(X_SIZE):
        for core in range(CORES):
            for z in range(Z_SIZE):
                for y in range(Y_SIZE):
                    to = move(x, core, z, y)
                    if to is not None:
                        rank = lambda a, b, c, d: (a * CORES + b) * N_OWN + c * Y_SIZE + d
                        out.append((rank(x, core, z, y), rank(*to)))
    return out


SWAP_X = pairs(lambda x, c, z, y: (1 - x, c, z, y))
SWAP_CORE = pairs(lambda x, c, z, y: (x, 1 - c, z, y))
SWAP_Y = pairs(lambda x, c, z, y: (x, c, z, 1 - y))
SWAP_Z1 = pairs(lambda x, c, z, y: (x, c, z ^ 1, y))
SWAP_Z2 = pairs(lambda x, c, z, y: (x, c, z ^ 2, y))


def shift(value, perm):
    return lax.ppermute(value, AXES, perm)


def sum_clips(value):
    for perm in (SWAP_Y, SWAP_Z1, SWAP_Z2):
        value = value + shift(value, perm)
    return value


def sum_frames(value):
    for perm in (SWAP_CORE, SWAP_X):
        value = value + shift(value, perm)
    return value


def shard_segments(matrices, n_rows):
    spans, offset = [], 0
    for name, rows, wide in matrices:
        spans.append((name, offset, rows, wide))
        offset += rows * wide
    out = []
    for owner in range(N_OWN):
        low, high = owner * n_rows, (owner + 1) * n_rows
        mine = []
        for name, start, rows, wide in spans:
            begin, end = max(low, start), min(high, start + rows * wide)
            if begin < end:
                mine.append((name, (begin - start) // wide, (end - begin) // wide, wide))
        out.append(mine)
    return out


ATTEND = [
    ("space_qkv", D, 3),
    ("space_out", D, 1),
    ("time_qkv", D, 3),
    ("time_out", D, 1),
    ("cross_q", D, 1),
    ("cross_kv", D, 2),
    ("cross_out", D, 1),
]
DENSE = [("fc_in", D, 4), ("fc_out", MLP, 1)]
ATTEND_ROWS = 13824 // N_OWN
DENSE_ROWS = 9216 // N_OWN
ATTEND_SEGS = shard_segments(ATTEND, ATTEND_ROWS)
DENSE_SEGS = shard_segments(DENSE, DENSE_ROWS)


def cast_table(segments, block):
    out = []
    for mine in segments:
        rows, offset = [], 0
        for name, first, count, wide in mine:
            for start in range(0, count * wide, block):
                rows.append((wide, offset + start // wide, count))
            offset += count * wide
        out.append(rows)
    return np.array(out, np.int32)


def step_table(segments, block, n_rows):
    out = []
    for mine in segments:
        rows, offset = [], 0
        for name, first, count, wide in mine:
            half = count // 2
            for start in range(0, count * wide, block):
                core, inner = divmod(start // wide, half)
                rows.append((wide, core * (n_rows // 2) + offset + inner, half))
            offset += half * wide
        out.append(rows)
    return np.array(out, np.int32)


CAST_BLOCK = 576
STEP_BLOCK = 288


def cast_kernel(widths, table, flat, out):
    block = pl.program_id(0)
    for wide in widths:
        count = CAST_BLOCK // wide

        @pl.when(table[block, 0] == wide)
        def _():
            for slab in range(wide):
                row = pl.multiple_of(table[block, 1] + slab * table[block, 2], 16)
                for tile in range(LANE_TILES):
                    piece = flat[pl.ds(LANE_TILES * slab + tile, count, stride=LANE_TILES * wide), :]
                    out[pl.ds(row, count), tile * LANES : (tile + 1) * LANES] = piece.astype(jnp.bfloat16)


def cast_shard(flat, table, widths, n_rows):
    units = CAST_BLOCK * LANE_TILES
    return pl.pallas_call(
        partial(cast_kernel, widths),
        grid_spec=pltpu.PrefetchScalarGridSpec(
            num_scalar_prefetch=1,
            grid=(n_rows // CAST_BLOCK,),
            in_specs=[pl.BlockSpec((units, LANES), lambda b, t: (b, 0))],
            out_specs=pl.BlockSpec((n_rows, D), lambda b, t: (0, 0)),
        ),
        out_shape=jax.ShapeDtypeStruct((n_rows, D), jnp.bfloat16),
        compiler_params=pltpu.CompilerParams(vmem_limit_bytes=40 * 1024 * 1024),
    )(table, flat.reshape(-1, LANES))


ROWS_AHEAD = 16


def rows_kernel(shift_ref, flat, out, held, sem):
    units, count = flat.shape[0], out.shape[0]
    block = pl.program_id(0)

    @pl.when(block == 0)
    def _():
        end = (ROWS_AHEAD + units) // 8 * 8
        held[pl.ds(0, ROWS_AHEAD), :] = jnp.zeros((ROWS_AHEAD, LANES), jnp.float32)
        held[pl.ds(end, held.shape[0] - end), :] = jnp.zeros((held.shape[0] - end, LANES), jnp.float32)
        copy = pltpu.make_async_copy(flat, held.at[pl.ds(ROWS_AHEAD, units)], sem)
        copy.start()
        copy.wait()

    begin = ROWS_AHEAD + block * (count * LANE_TILES) - shift_ref[0]
    for tile in range(LANE_TILES):
        piece = held[pl.ds(begin + tile, count, stride=LANE_TILES), :]
        out[:, tile * LANES : (tile + 1) * LANES] = piece.astype(out.dtype)


def flat_to_rows(flat, rows, shift, dtype):
    block = rows // 6
    return pl.pallas_call(
        rows_kernel,
        grid_spec=pltpu.PrefetchScalarGridSpec(
            num_scalar_prefetch=1,
            grid=(6,),
            in_specs=[pl.BlockSpec(memory_space=pl.ANY)],
            out_specs=pl.BlockSpec((block, D), lambda b, t: (b, 0)),
            scratch_shapes=[
                pltpu.VMEM((ROWS_AHEAD + rows * LANE_TILES + 8, LANES), jnp.float32),
                pltpu.SemaphoreType.DMA,
            ],
        ),
        out_shape=jax.ShapeDtypeStruct((rows, D), dtype),
        compiler_params=pltpu.CompilerParams(vmem_limit_bytes=32 * 1024 * 1024),
    )(shift.reshape(1), flat)


def flat_kernel(rows, out):
    count = rows.shape[0]
    for tile in range(LANE_TILES):
        out[pl.ds(tile, count, stride=LANE_TILES), :] = rows[:, tile * LANES : (tile + 1) * LANES]


def rows_to_flat(rows):
    block = rows.shape[0] // 6
    return pl.pallas_call(
        flat_kernel,
        grid=(6,),
        in_specs=[pl.BlockSpec((block, D), lambda b: (b, 0))],
        out_specs=pl.BlockSpec((block * LANE_TILES, LANES), lambda b: (b, 0)),
        out_shape=jax.ShapeDtypeStruct((rows.shape[0] * LANE_TILES, LANES), rows.dtype),
        compiler_params=pltpu.CompilerParams(vmem_limit_bytes=32 * 1024 * 1024),
    )(rows)


def ring_place(clip):
    return jnp.where(clip % 2 == 0, clip // 2, N_OWN - 1 - clip // 2)


def clip_at(place):
    return jnp.where(place < N_OWN // 2, 2 * place, 2 * N_OWN - 1 - 2 * place)


def partners(frame, clip):
    place = ring_place(clip)
    x, core = frame // CORES, frame % CORES
    return (
        {"clip": clip_at((place + 1) % N_OWN)},
        {"clip": clip_at((place + N_OWN - 1) % N_OWN)},
        {"frame": (1 - x) * CORES + core},
        {"frame": x * CORES + 1 - core},
    )


def greet(devices):
    barrier = pltpu.get_barrier_semaphore()
    for device in devices:
        pl.semaphore_signal(barrier, inc=1, device_id=device, device_id_type=pl.DeviceIdType.MESH)
    pl.semaphore_wait(barrier, len(devices))


def spread_kernel(groups, modes, *refs):
    n, m = len(groups), len(modes)
    counts = [len(shapes) for keep, shapes, stores, common in groups]
    refs = list(refs)
    take = lambda number: [refs.pop(0) for _ in range(number)]
    owns, given, outs, given_outs = take(n), take(m), take(sum(counts)), take(m)
    helds, sources, landings = take(n), take(m), take(m)
    load_sem, send_sem, recv_sem, out_sem, peer_sem, peer_send, peer_recv = refs
    frame, clip = lax.axis_index("frame"), lax.axis_index("clip")
    x, core = frame // CORES, frame % CORES
    place = ring_place(clip)
    right, left, over_x, other = partners(frame, clip)
    half = N_OWN // 2
    owners = [clip_at((place + N_OWN - k) % N_OWN) for k in range(half + 1)]
    owners += [clip_at((place + k) % N_OWN) for k in range(1, half)]
    flip_x = (1 - x) * CORES + core
    mine = [core, frame, flip_x]
    theirs = [1 - core, x * CORES + 1 - core, (1 - x) * CORES + 1 - core]
    landing = mine + theirs

    def block_of(group, kinds, kind):
        return kinds[kind] + (2 if groups[group][3] and kind % 3 else 0)

    z, y = clip // Y_SIZE, clip % Y_SIZE
    below, above = {"clip": clip - Y_SIZE}, {"clip": clip + Y_SIZE}
    across = {"clip": clip + 1 - 2 * y}
    rings = [group for group in range(n) if len(groups[group][0]) == N_OWN]
    falls = [group for group in range(n) if group not in rings]
    first_z = Z_SIZE - 2

    def held_at(group, slot):
        if group in rings:
            return helds[group].at[owners[slot]]
        return helds[group].at[slot % 2 * Y_SIZE + (y if slot < 2 else 1 - y)]

    def is_own(slot):
        return z == first_z + slot

    def load(group):
        to = held_at(group, 0) if group in rings else helds[group].at[(z - first_z) * Y_SIZE + y]
        return pltpu.make_async_copy(owns[group], to, load_sem.at[group])

    def loading(group, action):
        if group in rings:
            action(load(group))
        else:
            pl.when(z >= first_z)(lambda: action(load(group)))

    def copy_of(group, slot, block, device, to_slot, kind, sender=None):
        row, column = (to_slot, kind) if sender is None else sender
        return pltpu.make_async_remote_copy(
            src_ref=held_at(group, slot).at[block],
            dst_ref=held_at(group, slot).at[block],
            send_sem=send_sem.at[group, row, column],
            recv_sem=recv_sem.at[group, to_slot, kind],
            device_id=device,
            device_id_type=pl.DeviceIdType.MESH,
        )

    sent = []

    def send(group, slot, from_kind, device, to_slot, kind):
        if from_kind == 0 and not groups[group][3]:
            return
        args = (group, slot, block_of(group, mine, from_kind), device, to_slot, kind)
        copy_of(*args).start()
        sent.append(args)

    def arrive(group, slot, kind):
        if kind % 3 == 0 and not groups[group][3]:
            return
        block = block_of(group, landing, kind)
        copy_of(group, slot, block, other, slot, kind).wait_recv()

    def onward(group, slot, kind):
        if slot < half:
            send(group, slot, kind, right, slot + 1, kind)
        if slot == 0:
            send(group, slot, kind, left, half + 1, kind)
        elif half < slot < N_OWN - 1:
            send(group, slot, kind, left, slot + 1, kind)

    def peer_load(item):
        return pltpu.make_async_copy(given[item], sources[item], peer_sem.at[item, 0])

    def peer_own(item):
        source = sources[item].at[clip] if modes[item] == "swap" else sources[item]
        return pltpu.make_async_copy(source, landings[item].at[clip], peer_sem.at[item, 1])

    def peer_copy(item, k):
        to = (clip + k) % N_OWN
        return pltpu.make_async_remote_copy(
            src_ref=sources[item].at[to] if modes[item] == "swap" else sources[item],
            dst_ref=landings[item].at[clip],
            send_sem=peer_send.at[item, k - 1],
            recv_sem=peer_recv.at[item, k - 1],
            device_id={"clip": to},
            device_id_type=pl.DeviceIdType.MESH,
        )

    def peers(item, arriving, action):
        for k in range(1, N_OWN):
            if modes[item] == "gather":
                action(k)
            elif modes[item] == "first":
                pl.when(clip == (k if arriving else 0))(lambda: action(k))
            else:
                to = clip if arriving else (clip + k) % N_OWN
                pl.when(to >= N_OWN // 2)(lambda: action(k))

    fallen = []

    def run(chosen, action):
        action() if chosen is None else pl.when(chosen)(action)

    def fall(group, slot, kind, device, to_slot, to_kind, sender, chosen):
        args = (group, slot, block_of(group, mine, kind), device, to_slot, to_kind, sender)
        run(chosen, lambda: copy_of(*args).start())
        fallen.append((args, chosen))

    def fall_on(group, slot, kind, chosen):
        going_down = (z >= 1) & (z <= first_z + slot) & chosen
        fall(group, slot, kind, below, slot, kind, (slot, kind), going_down)
        if slot == 0:
            fall(group, slot, kind, above, slot, kind, (4, 3 + kind), is_own(slot) & chosen)
        fall(group, slot, kind, across, slot + 2, kind, (4 + slot, kind), chosen)

    def fall_beside(group, slot, kind, chosen):
        if kind == 1:
            fall(group, slot, 1, over_x, slot, 2, (slot, 2), chosen)
        fall(group, slot, kind, other, slot, 3 + kind, (slot, 3 + kind), chosen)

    def fall_arrive(group, slot, kind, chosen):
        run(chosen, lambda: arrive(group, slot, kind))

    def not_own(slot):
        return None if slot >= 2 else z != first_z + slot

    def fall_start():
        for group in falls:
            for slot in (1, 0):
                for kind in (1, 0):
                    fall_on(group, slot, kind, is_own(slot))

    def fall_phase(phase):
        turns = {
            1: [(0, (z > 0) & not_own(0))],
            2: [(0, z == 0), (1, (z > 0) & not_own(1))],
            3: [(1, z == 0), (2, None)],
            4: [(3, None)],
        }[phase]
        for group in falls:
            for slot, chosen in turns:
                for kind in (1, 0):
                    fall_arrive(group, slot, kind, chosen)
                    if slot < 2:
                        fall_on(group, slot, kind, chosen)
                    fall_beside(group, slot, kind, chosen)
            if phase == half:
                for slot in range(4):
                    fall_arrive(group, slot, 2, not_own(slot))
                    fall_beside(group, slot, 2, not_own(slot))

    for group in range(n):
        loading(group, lambda copy: copy.start())
    for item in range(m):
        peer_load(item).start()
    everyone = tuple({"clip": (clip + k) % N_OWN} for k in range(1, N_OWN)) if m else ()
    greet((right, left, over_x, other) + everyone + ((across,) if falls else ()))
    for group in range(n):
        loading(group, lambda copy: copy.wait())
    fall_start()
    for group in rings:
        onward(group, 0, 1)
        onward(group, 0, 0)
    for item in range(m):
        peer_load(item).wait()
        peer_own(item).start()
        peers(item, False, lambda k: peer_copy(item, k).start())
    waiting = []
    for step in range(1, half + 1):
        slots = [step] + ([half + step] if step < half else [])
        pairs_now = [(group, slot) for group in rings for slot in slots]
        for group, slot in pairs_now:
            arrive(group, slot, 1)
            onward(group, slot, 1)
            send(group, slot, 1, over_x, slot, 2)
            send(group, slot, 1, other, slot, 4)
            arrive(group, slot, 0)
            onward(group, slot, 0)
            send(group, slot, 0, other, slot, 3)
        for group, slot in waiting:
            arrive(group, slot, 2)
            send(group, slot, 2, other, slot, 5)
        fall_phase(step)
        waiting = pairs_now
    for group, slot in waiting:
        arrive(group, slot, 2)
        send(group, slot, 2, other, slot, 5)
    for group in rings:
        for slot in range(1, N_OWN):
            for kind in (3, 4, 5):
                arrive(group, slot, kind)
    for group in falls:
        for slot in range(4):
            for kind in (3, 4, 5):
                fall_arrive(group, slot, kind, not_own(slot))
    done, base = [], 0
    for group, (keep, shapes, stores, common) in enumerate(groups):
        held = helds[group]
        rows = held.shape[2]
        for out, row, column, owner, first, count in stores:
            while count > 0:
                part, inner = divmod(first, rows)
                some = min(count, rows - inner)
                copy = pltpu.make_async_copy(
                    held.at[owner - min(keep), part, pl.ds(inner, some)],
                    outs[base + out].at[pl.ds(row, some), pl.ds(column, D)],
                    out_sem.at[len(done)],
                )
                copy.start()
                done.append(copy)
                first, row, count = first + some, row + some, count - some
        base += counts[group]
    for item in range(m):
        peer_own(item).wait()
        peers(item, True, lambda k: peer_copy(item, k).wait_recv())
        copy = pltpu.make_async_copy(landings[item], given_outs[item], peer_sem.at[item, 2])
        copy.start()
        done.append(copy)
    for item in range(m):
        peers(item, False, lambda k: peer_copy(item, k).wait_send())
    for args in sent:
        copy_of(*args).wait_send()
    for args, chosen in fallen:
        run(chosen, lambda: copy_of(*args).wait_send())
    for copy in done:
        copy.wait()


def spread_shards(owns, groups, collective, given=()):
    spec = pl.BlockSpec(memory_space=pl.ANY)
    shapes = [shape for keep, some, stores, common in groups for shape in some]
    n_stores = sum(6 * len(stores) for keep, some, stores, common in groups)
    blocks = [6 if group[3] else 4 for group in groups]
    modes = [mode for value, mode in given]
    values = [value for value, mode in given]
    landed = [
        value.shape if mode == "swap" else (N_OWN,) + value.shape for value, mode in given
    ]
    many = max(len(given), 1)
    return pl.pallas_call(
        partial(spread_kernel, groups, modes),
        in_specs=[spec] * (len(owns) + len(given)),
        out_specs=[spec] * (len(shapes) + len(given)),
        out_shape=[jax.ShapeDtypeStruct(shape, jnp.bfloat16) for shape in shapes]
        + [jax.ShapeDtypeStruct(shape, value.dtype) for shape, value in zip(landed, values)],
        scratch_shapes=[
            pltpu.VMEM((len(group[0]), count, own.shape[0] // count, D), jnp.bfloat16)
            for own, group, count in zip(owns, groups, blocks)
        ]
        + [pltpu.VMEM(value.shape, value.dtype) for value in values]
        + [pltpu.VMEM(shape, value.dtype) for shape, value in zip(landed, values)]
        + [
            pltpu.SemaphoreType.DMA((len(owns),)),
            pltpu.SemaphoreType.DMA((len(owns), N_OWN, 6)),
            pltpu.SemaphoreType.DMA((len(owns), N_OWN, 6)),
            pltpu.SemaphoreType.DMA((n_stores,)),
            pltpu.SemaphoreType.DMA((many, 3)),
            pltpu.SemaphoreType.DMA((many, N_OWN - 1)),
            pltpu.SemaphoreType.DMA((many, N_OWN - 1)),
        ],
        compiler_params=pltpu.CompilerParams(
            collective_id=collective, has_side_effects=True, vmem_limit_bytes=50 * 1024 * 1024
        ),
        cost_estimate=pl.CostEstimate(
            flops=0, bytes_accessed=200 * 1000 * 1000, transcendentals=0
        ),
    )(*[own.reshape(count, own.shape[0] // count, D) for own, count in zip(owns, blocks)], *values)


LAG = 5


def collect_kernel(first, last, chunks, small, part, out, small_out, part_out, scratch):
    bufs, extra, locals_, finals, result = scratch[:2], scratch[2], scratch[3:5], scratch[5:7], scratch[7]
    ring_send, ring_recv, x_send, x_recv, end_send, end_recv, load_sem, own_sem = scratch[8:16]
    if small is not None:
        sums, arrived, small_send, small_recv = scratch[16:]
    if part is not None:
        frames, part_send, part_recv = scratch[16:]
    frame, clip = lax.axis_index("frame"), lax.axis_index("clip")
    x, core = frame // CORES, frame % CORES
    place = ring_place(clip)
    right, left, over_x, other = partners(frame, clip)
    swaps = [
        other,
        over_x,
        {"clip": clip + 1 - 2 * (clip % 2)},
        {"clip": clip + 2 - 4 * (clip // 2 % 2)},
        {"clip": clip + 4 - 8 * (clip // 4)},
    ]
    greet((right, left) + (tuple(swaps) if small is not None else (over_x, other)))
    f, l = first // 2, last // 2
    toward = (right, left)

    def owner(way, step):
        moved = N_OWN - 1 - step if way == 0 else 1 + step
        return clip_at((place + moved) % N_OWN)

    def f_rows(side, way):
        return pl.ds(pl.multiple_of(side * first + way * f, 8), f)

    def l_rows(way):
        return pl.ds(2 * first + way * l, l)

    def remote(src, dst, send_sem, recv_sem, device):
        return pltpu.make_async_remote_copy(
            src_ref=src,
            dst_ref=dst,
            send_sem=send_sem,
            recv_sem=recv_sem,
            device_id=device,
            device_id_type=pl.DeviceIdType.MESH,
        )

    def x_copy(way, step):
        return remote(
            chunks.at[owner(way, step), f_rows(1 - x, way)],
            extra.at[way, step],
            x_send.at[way, step],
            x_recv.at[way, step],
            over_x,
        )

    def load(kind, way, step):
        to = bufs[kind].at[way, 0] if step == 0 else locals_[kind].at[way, step % 2]
        rows = l_rows(way) if kind == 0 else f_rows(x, way)
        return pltpu.make_async_copy(
            chunks.at[owner(way, step), rows], to, load_sem.at[kind, way, step % 2]
        )

    def ring_copy(kind, way, step):
        return remote(
            bufs[kind].at[way, step],
            bufs[kind].at[way, step + 1],
            ring_send.at[kind, way, step],
            ring_recv.at[kind, way, step],
            toward[way],
        )

    def final_copy(kind, way):
        return remote(
            bufs[kind].at[way, N_OWN - 1],
            finals[kind].at[way],
            end_send.at[kind, way],
            end_recv.at[kind, way],
            over_x,
        )

    def small_copy(stage):
        return remote(
            sums.at[stage], arrived.at[stage], small_send.at[stage], small_recv.at[stage], swaps[stage]
        )

    flip_x = (1 - x) * CORES + core

    def part_copy(number, block=None):
        block = (frame, frame, flip_x)[number] if block is None else block
        return remote(
            frames.at[block],
            frames.at[block],
            part_send.at[number],
            part_recv.at[number],
            (over_x, other, other)[number],
        )

    def over_rows(start, count, work):
        def body(number, carry):
            work(pl.multiple_of(start + number * 8, 8))
            return carry

        lax.fori_loop(0, count // 8, body, 0)

    def small_load():
        return pltpu.make_async_copy(small, sums.at[0], own_sem.at[7])

    def part_load():
        return pltpu.make_async_copy(part, frames.at[frame], own_sem.at[7])

    for kind in range(2):
        for way in range(2):
            load(kind, way, 0).start()
    for way in range(2):
        x_copy(way, 0).start()
    if small is not None:
        small_load().start()
    if part is not None:
        part_load().start()

    def ring_step(kind, way, step):
        load(kind, way, step).wait()
        if step + 1 < N_OWN:
            load(kind, way, step + 1).start()
        if kind == 1:
            x_copy(way, step).wait_recv()
        if step > 0:
            ring_copy(kind, way, step - 1).wait_recv()
        buf, local = bufs[kind], locals_[kind]

        def add(row):
            at = pl.ds(row, 8)
            total = buf[way, step, at]
            if kind == 1:
                total = total + extra[way, step, at]
            if step > 0:
                total = total + local[way, step % 2, at]
            buf[way, step, at] = total

        if kind == 1 or step > 0:
            over_rows(0, f if kind == 1 else l, add)
        if step + 1 < N_OWN:
            ring_copy(kind, way, step).start()
        else:
            final_copy(kind, way).start()

    def own_half(kind):
        return pl.ds(2 * first, last) if kind == 0 else pl.ds(0, 2 * first)

    def core_swap(kind, to):
        return remote(
            result.at[own_half(kind)],
            out.at[to, own_half(kind)],
            own_sem.at[kind],
            own_sem.at[2 + kind],
            other,
        )

    def own_store(kind):
        return pltpu.make_async_copy(
            result.at[own_half(kind)], out.at[core, own_half(kind)], own_sem.at[4 + kind]
        )

    def finish(kind):
        for way in range(2):
            final_copy(kind, way).wait_recv()
            buf, final = bufs[kind], finals[kind]

            def put(row):
                at = pl.ds(row, 8)
                if kind == 0:
                    to = pl.multiple_of(2 * first + way * l + row, 8)
                    result[pl.ds(to, 8)] = buf[way, N_OWN - 1, at] + final[way, at]
                else:
                    to = pl.multiple_of(x * first + way * f + row, 8)
                    back = pl.multiple_of((1 - x) * first + way * f + row, 8)
                    result[pl.ds(to, 8)] = buf[way, N_OWN - 1, at]
                    result[pl.ds(back, 8)] = final[way, at]

            over_rows(0, l if kind == 0 else f, put)
        core_swap(kind, core).start()
        own_store(kind).start()

    for tick in range(N_OWN + LAG):
        if small is not None and tick < len(swaps) + 1:
            if tick == 0:
                small_load().wait()
            else:
                small_copy(tick - 1).wait_recv()

                def add_small(row):
                    at = pl.ds(row, 8)
                    sums[tick, at] = sums[tick - 1, at] + arrived[tick - 1, at]

                over_rows(0, small.shape[0], add_small)
            if tick < len(swaps):
                small_copy(tick).start()
        if 0 < tick < N_OWN:
            for way in range(2):
                x_copy(way, tick).start()
        if part is not None and tick == N_OWN - 1:
            part_load().wait()
            part_copy(0).start()
            part_copy(1).start()
        for way in range(2):
            if tick < N_OWN:
                ring_step(0, way, tick)
            if tick >= LAG:
                ring_step(1, way, tick - LAG)
    if small is not None:
        small_store = pltpu.make_async_copy(sums.at[len(swaps)], small_out, own_sem.at[6])
        small_store.start()
    finish(0)
    if part is not None:
        part_copy(0, flip_x).wait_recv()
        part_copy(2).start()
    finish(1)
    if part is not None:
        part_copy(1, x * CORES + 1 - core).wait_recv()
        part_copy(2, (1 - x) * CORES + 1 - core).wait_recv()
        part_store = pltpu.make_async_copy(frames, part_out, own_sem.at[6])
        part_store.start()
        part_store.wait()
        for number in range(3):
            part_copy(number).wait_send()
    if small is not None:
        small_store.wait()
        for stage in range(len(swaps)):
            small_copy(stage).wait_send()
    for way in range(2):
        for step in range(N_OWN):
            x_copy(way, step).wait_send()
    for kind in range(2):
        for way in range(2):
            for step in range(N_OWN - 1):
                ring_copy(kind, way, step).wait_send()
            final_copy(kind, way).wait_send()
        core_swap(kind, 1 - core).wait_recv()
        core_swap(kind, core).wait_send()
        own_store(kind).wait()


def collect_shard(chunks, first, collective, small=None, part=None):
    rows = chunks.shape[1]
    last = rows - 2 * first
    spec = pl.BlockSpec(memory_space=pl.ANY)
    out_shape = [jax.ShapeDtypeStruct((2, rows, D), jnp.float32)]
    beside = small if part is None else part
    if part is None:
        out_shape.append(jax.ShapeDtypeStruct(small.shape, jnp.float32))
        more = [
            pltpu.VMEM((6,) + small.shape, jnp.float32),
            pltpu.VMEM((5,) + small.shape, jnp.float32),
            pltpu.SemaphoreType.DMA((5,)),
            pltpu.SemaphoreType.DMA((5,)),
        ]
    else:
        out_shape.append(jax.ShapeDtypeStruct((4,) + part.shape, jnp.float32))
        more = [
            pltpu.VMEM((4,) + part.shape, jnp.float32),
            pltpu.SemaphoreType.DMA((3,)),
            pltpu.SemaphoreType.DMA((3,)),
        ]

    def kernel(chunks, beside, out, beside_out, *scratch):
        if part is None:
            collect_kernel(first, last, chunks, beside, None, out, beside_out, None, scratch)
        else:
            collect_kernel(first, last, chunks, None, beside, out, None, beside_out, scratch)

    return pl.pallas_call(
        kernel,
        in_specs=[spec] * 2,
        out_specs=[spec] * 2,
        out_shape=out_shape,
        scratch_shapes=[
            pltpu.VMEM((2, N_OWN, last // 2, D), jnp.float32),
            pltpu.VMEM((2, N_OWN, first // 2, D), jnp.float32),
            pltpu.VMEM((2, N_OWN, first // 2, D), jnp.float32),
            pltpu.VMEM((2, 2, last // 2, D), jnp.float32),
            pltpu.VMEM((2, 2, first // 2, D), jnp.float32),
            pltpu.VMEM((2, last // 2, D), jnp.float32),
            pltpu.VMEM((2, first // 2, D), jnp.float32),
            pltpu.VMEM((rows, D), jnp.float32),
            pltpu.SemaphoreType.DMA((2, 2, N_OWN)),
            pltpu.SemaphoreType.DMA((2, 2, N_OWN)),
            pltpu.SemaphoreType.DMA((2, N_OWN)),
            pltpu.SemaphoreType.DMA((2, N_OWN)),
            pltpu.SemaphoreType.DMA((2, 2)),
            pltpu.SemaphoreType.DMA((2, 2)),
            pltpu.SemaphoreType.DMA((2, 2, 2)),
            pltpu.SemaphoreType.DMA((8,)),
        ]
        + more,
        compiler_params=pltpu.CompilerParams(
            collective_id=collective, has_side_effects=True, vmem_limit_bytes=58 * 1024 * 1024
        ),
        cost_estimate=pl.CostEstimate(
            flops=0, bytes_accessed=800 * 1000 * 1000, transcendentals=0
        ),
    )(chunks, beside)


def matrix_plan(matrices, segments):
    shapes = [(rows, wide * D) for name, rows, wide in matrices]
    names = [name for name, rows, wide in matrices]
    stores = []
    for owner in range(N_OWN):
        offset = 0
        for name, first, count, wide in segments[owner]:
            for j in range(wide):
                stores.append((names.index(name), first, j * D, owner, offset, count))
                offset += count
    return shapes, stores


GRAD_COLUMNS = 384


def grad_plan(matrices, segments, lefts, rights):
    squares = {}
    for owner in range(N_OWN):
        row = 0
        for name, first, count, wide in segments[owner]:
            for j in range(wide):
                block, inner = divmod(first, D)
                piece = (inner, count // 2, owner, row)
                squares.setdefault((name, block, j), []).append(piece)
                row += count // 2
    plan = []
    for name, rows, wide in matrices:
        for block in range(rows // D):
            for j in range(wide):
                right, column = rights[name][j]
                plan.append((lefts[name], block * D, right, column, squares[name, block, j]))
    return plan


def grad_kernel(plan, parts, n_left, core_ref, *refs):
    n_in = sum(parts)
    ins, out = refs[:n_in], refs[n_in]
    left_buf, right_buf, made, left_sem, right_sem, out_sem = refs[n_in + 1 :]
    core = core_ref[0]
    place = [sum(parts[:k]) for k in range(len(parts))]

    def left_copies(square, slot):
        left, row = square[:2]
        return [
            pltpu.make_async_copy(
                ins[place[left] + part].at[pl.ds(row, D)],
                left_buf.at[slot, part, :, pl.ds(0, ins[place[left]].shape[1])],
                left_sem.at[slot, part],
            )
            for part in range(parts[left])
        ]

    def right_copies(square, slot):
        right, column = n_left + square[2], square[3]
        return [
            pltpu.make_async_copy(
                ins[place[right] + part].at[:, pl.ds(column, D)],
                right_buf.at[slot, part, pl.ds(0, ins[place[right]].shape[0])],
                right_sem.at[slot, part],
            )
            for part in range(parts[right])
        ]

    def out_copies(number):
        row, copies = 0, []
        for k, (first, count, owner, to) in enumerate(plan[number][4]):
            copies.append(
                pltpu.make_async_copy(
                    made.at[number % 2, pl.ds(row, count)],
                    out.at[owner, pl.ds(to, count)],
                    out_sem.at[number % 2, k],
                )
            )
            row += count
        return copies

    slots = []
    for number, square in enumerate(plan):
        if number == 0:
            slots.append((0, True, 0, True))
            continue
        left, _, right, _ = slots[-1]
        new_left = square[:2] != plan[number - 1][:2]
        new_right = square[2:4] != plan[number - 1][2:4]
        slots.append((left ^ new_left, new_left, right ^ new_right, new_right))

    def operands(number):
        left, new_left, right, new_right = slots[number]
        copies = left_copies(plan[number], left) if new_left else []
        return copies + (right_copies(plan[number], right) if new_right else [])

    for copy in operands(0):
        copy.start()
    for number, square in enumerate(plan):
        for copy in operands(number):
            copy.wait()
        if number + 1 < len(plan):
            for copy in operands(number + 1):
                copy.start()
        if number >= 2:
            for copy in out_copies(number - 2):
                copy.wait()
        left, _, right, _ = slots[number]
        depth = ins[place[square[0]]].shape[1]

        def some_columns(step, carry):
            columns = pl.ds(pl.multiple_of(step * GRAD_COLUMNS, LANES), GRAD_COLUMNS)
            row = 0
            for first, count, owner, to in square[4]:
                rows = pl.ds(pl.multiple_of(first + core * count, 16), count)
                total = 0.0
                for part in range(parts[square[0]]):
                    total = total + jnp.dot(
                        left_buf[left, part, rows, :depth],
                        right_buf[right, part, :depth, columns],
                        preferred_element_type=jnp.float32,
                    )
                made[number % 2, row : row + count, columns] = total
                row += count
            return carry

        lax.fori_loop(0, D // GRAD_COLUMNS, some_columns, 0)
        for copy in out_copies(number):
            copy.start()
    for number in range(max(len(plan) - 2, 0), len(plan)):
        for copy in out_copies(number):
            copy.wait()


def core_chunks(plan, core, lefts, rights, n_rows):
    operands = list(lefts) + list(rights)
    parts = [len(arrays) for arrays in operands]
    tokens = max(arrays[0].shape[1] for arrays in lefts)
    spec = pl.BlockSpec(memory_space=pl.ANY)
    return pl.pallas_call(
        partial(grad_kernel, plan, parts, len(lefts)),
        in_specs=[pl.BlockSpec(memory_space=pltpu.SMEM)] + [spec] * sum(parts),
        out_specs=spec,
        out_shape=jax.ShapeDtypeStruct((N_OWN, n_rows // 2, D), jnp.float32),
        scratch_shapes=[
            pltpu.VMEM((2, 2, D, tokens), jnp.bfloat16),
            pltpu.VMEM((2, 2, tokens, D), jnp.bfloat16),
            pltpu.VMEM((2, D // 2, D), jnp.float32),
            pltpu.SemaphoreType.DMA((2, 2)),
            pltpu.SemaphoreType.DMA((2, 2)),
            pltpu.SemaphoreType.DMA((2, N_OWN)),
        ],
        compiler_params=pltpu.CompilerParams(vmem_limit_bytes=36 * 1024 * 1024),
    )(core.astype(jnp.int32).reshape(1), *[array for arrays in operands for array in arrays])


def step_values(master, grad, first, second, average):
    keep = min(AVERAGE_KEEP, (1.0 + STEP) / (10.0 + STEP))
    first = BETA_FIRST * first + (1.0 - BETA_FIRST) * grad
    second = BETA_SECOND * second + (1.0 - BETA_SECOND) * grad * grad
    moved = (
        first
        / (1.0 - BETA_FIRST**STEP)
        / (jnp.sqrt(second / (1.0 - BETA_SECOND**STEP)) + ADAM_FLOOR)
    )
    master = master - LEARN_RATE * (moved + WEIGHT_DECAY * master)
    return (master, first, second, keep * average + (1.0 - keep) * master)


STEP_ROWS = 144


def step_kernel(widths, table, factor, grad, *refs):
    olds, news, (shard, flat, sem) = refs[:4], refs[4:8], refs[8:]
    block = pl.program_id(0)

    @pl.when(block == 0)
    def _():
        copy = pltpu.make_async_copy(grad, shard, sem)
        copy.start()
        copy.wait()

    for wide in widths:
        count = STEP_BLOCK // wide

        @pl.when(table[block, 0] == wide)
        def _():
            for slab in range(wide):
                row = pl.multiple_of(table[block, 1] + slab * table[block, 2], 8)
                for tile in range(LANE_TILES):
                    flat[pl.ds(LANE_TILES * slab + tile, count, stride=LANE_TILES * wide), :] = shard[
                        pl.ds(row, count), tile * LANES : (tile + 1) * LANES
                    ]

    scale = factor[0]

    def some_rows(number, carry):
        at = pl.ds(pl.multiple_of(number * STEP_ROWS, 8), STEP_ROWS)
        old = [ref[at, :] for ref in olds]
        made = step_values(old[0], flat[at, :] * scale, old[1], old[2], old[3])
        for ref, value in zip(news, made):
            ref[at, :] = value
        return carry

    lax.fori_loop(0, STEP_BLOCK * LANE_TILES // STEP_ROWS, some_rows, 0)


def step_shard(grad, table, widths, n_rows, factor, olds):
    units = STEP_BLOCK * LANE_TILES
    block_spec = pl.BlockSpec((units, LANES), lambda b, t, f: (b, 0))
    flat_shape = jax.ShapeDtypeStruct((n_rows * LANE_TILES, LANES), jnp.float32)
    made = pl.pallas_call(
        partial(step_kernel, widths),
        grid_spec=pltpu.PrefetchScalarGridSpec(
            num_scalar_prefetch=2,
            grid=(n_rows // STEP_BLOCK,),
            in_specs=[pl.BlockSpec(memory_space=pl.ANY)] + [block_spec] * 4,
            out_specs=[block_spec] * 4,
            scratch_shapes=[
                pltpu.VMEM((n_rows, D), jnp.float32),
                pltpu.VMEM((units, LANES), jnp.float32),
                pltpu.SemaphoreType.DMA,
            ],
        ),
        out_shape=[flat_shape] * 4,
        compiler_params=pltpu.CompilerParams(vmem_limit_bytes=50 * 1024 * 1024),
    )(table, factor, grad, *[old.reshape(-1, LANES) for old in olds])
    return [value.reshape(-1) for value in made]


def head_span(head):
    width = D // HEADS
    start = head * width // LANES * LANES
    stop = -(-(head + 1) * width // LANES) * LANES
    lane = start + lax.broadcasted_iota(jnp.int32, (1, stop - start), 1)
    ones = (lane >= head * width) & (lane < (head + 1) * width)
    return slice(start, stop), ones.astype(jnp.float32).astype(jnp.bfloat16)


def dot_rows(left, right):
    return lax.dot_general(left, right, (((1,), (1,)), ((), ())), preferred_element_type=jnp.float32)


def dot_down(left, right):
    return lax.dot_general(left, right, (((0,), (0,)), ((), ())), preferred_element_type=jnp.float32)


def live_keys(mode, live, n_queries, n_keys):
    key = lax.broadcasted_iota(jnp.int32, (n_queries, n_keys), 1)
    if mode == "cross":
        return key < live[0]
    if mode == "all":
        return None
    query = lax.broadcasted_iota(jnp.int32, (n_queries, n_keys), 0)
    return query // mode == key // mode


def head_scores(queries, keys, valid):
    scores = dot_rows(queries, keys) * (D // HEADS) ** (-0.5)
    return scores if valid is None else jnp.where(valid, scores, MASKED_SCORE)


def heads_kernel(mode, live, queries, keys, values, out, log_total, total):
    n_queries, n_keys = queries.shape[0], keys.shape[0]
    valid = live_keys(mode, live, n_queries, n_keys)
    lane = lax.broadcasted_iota(jnp.int32, (1, LANES), 1)
    total[...] = jnp.zeros_like(total)
    log_total[...] = jnp.zeros_like(log_total)
    for head in range(HEADS):
        span, ones = head_span(head)
        scores = head_scores(queries[:, span], keys[:, span] * ones, valid)
        summit = jnp.max(scores, -1, keepdims=True)
        powers = jnp.exp(scores - summit)
        sums = jnp.sum(powers, -1, keepdims=True)
        probs = (powers / sums).astype(jnp.bfloat16)
        total[:, span] += jnp.dot(
            probs, values[:, span] * ones, preferred_element_type=jnp.float32
        )
        log_total[...] += jnp.where(lane == head, summit + jnp.log(sums), 0.0)
    out[...] = total[...].astype(jnp.bfloat16)


def heads_back_kernel(
    mode, live, queries, keys, values, log_total, grad_out, grad_q, grad_k, grad_v, sum_q, sum_k, sum_v
):
    n_queries, n_keys = queries.shape[0], keys.shape[0]
    valid = live_keys(mode, live, n_queries, n_keys)
    scale = (D // HEADS) ** (-0.5)
    block, last = pl.program_id(0), pl.num_programs(0) - 1
    sum_q[...] = jnp.zeros_like(sum_q)

    @pl.when((block == 0) | (mode != "cross"))
    def _():
        sum_k[...] = jnp.zeros_like(sum_k)
        sum_v[...] = jnp.zeros_like(sum_v)

    for head in range(HEADS):
        span, ones = head_span(head)
        some_keys = keys[:, span] * ones
        scores = head_scores(queries[:, span], some_keys, valid)
        probs = jnp.exp(scores - log_total[:, head : head + 1])
        grad_probs = dot_rows(grad_out[:, span], values[:, span] * ones)
        row = jnp.sum(probs * grad_probs, -1, keepdims=True)
        grad_scores = (probs * (grad_probs - row)).astype(jnp.bfloat16)
        sum_q[:, span] += jnp.dot(grad_scores, some_keys, preferred_element_type=jnp.float32)
        sum_k[:, span] += dot_down(grad_scores, queries[:, span] * ones)
        sum_v[:, span] += dot_down(probs.astype(jnp.bfloat16), grad_out[:, span] * ones)
    grad_q[...] = (sum_q[...] * scale).astype(grad_q.dtype)

    @pl.when((block == last) | (mode != "cross"))
    def _():
        grad_k[...] = (sum_k[...] * scale).astype(grad_k.dtype)
        grad_v[...] = sum_v[...].astype(grad_v.dtype)


HEAD_ROWS = 256


def heads_specs(mode, keys):
    own = pl.BlockSpec((HEAD_ROWS, D), lambda b: (b, 0))
    side = pl.BlockSpec((HEAD_ROWS, LANES), lambda b: (b, 0))
    shared = pl.BlockSpec(keys.shape, lambda b: (0, 0)) if mode == "cross" else own
    return own, side, shared


def heads_forward(mode, queries, keys, values, live):
    own, side, shared = heads_specs(mode, keys)
    n_keys = keys.shape[0] if mode == "cross" else HEAD_ROWS
    return pl.pallas_call(
        partial(heads_kernel, mode),
        grid=(queries.shape[0] // HEAD_ROWS,),
        in_specs=[pl.BlockSpec(memory_space=pltpu.SMEM), own, shared, shared],
        out_specs=[own, side],
        out_shape=[
            jax.ShapeDtypeStruct(queries.shape, jnp.bfloat16),
            jax.ShapeDtypeStruct((queries.shape[0], LANES), jnp.float32),
        ],
        scratch_shapes=[pltpu.VMEM((HEAD_ROWS, D), jnp.float32)],
        compiler_params=pltpu.CompilerParams(vmem_limit_bytes=32 * 1024 * 1024),
    )(live, queries, keys, values)


def heads_backward(mode, queries, keys, values, live, log_total, grad_out):
    own, side, shared = heads_specs(mode, keys)
    n_keys = keys.shape[0] if mode == "cross" else HEAD_ROWS
    kind = jnp.float32 if mode == "cross" else jnp.bfloat16
    return pl.pallas_call(
        partial(heads_back_kernel, mode),
        grid=(queries.shape[0] // HEAD_ROWS,),
        in_specs=[pl.BlockSpec(memory_space=pltpu.SMEM), own, shared, shared, side, own],
        out_specs=[own, shared, shared],
        out_shape=[
            jax.ShapeDtypeStruct(queries.shape, jnp.bfloat16),
            jax.ShapeDtypeStruct(keys.shape, kind),
            jax.ShapeDtypeStruct(keys.shape, kind),
        ],
        scratch_shapes=[
            pltpu.VMEM((HEAD_ROWS, D), jnp.float32),
            pltpu.VMEM((n_keys, D), jnp.float32),
            pltpu.VMEM((n_keys, D), jnp.float32),
        ],
        compiler_params=pltpu.CompilerParams(vmem_limit_bytes=40 * 1024 * 1024),
    )(live, queries, keys, values, log_total, grad_out)


ROW_TIME_ONE = PATCH_VALUES
ROW_TIME_TWO = ROW_TIME_ONE + TFREQ
ROW_BLOCK = ROW_TIME_TWO + D
ROW_CAP_ONE = ROW_BLOCK + 6 * D
ROW_CAP_TWO = ROW_CAP_ONE + CAPW
ROW_FINAL = ROW_CAP_TWO + D
ROW_NULL = ROW_FINAL + PATCH_VALUES
EMB_UNITS = 16158720 // LANES // N_OWN
EMB_FIRST = [EMB_UNITS * c // LANE_TILES for c in range(N_OWN)]
EMB_SHIFT = [EMB_UNITS * c % LANE_TILES for c in range(N_OWN)]


def two_parts(product, value):
    both = product(jnp.concatenate(halves(value), 0))
    return both[: value.shape[0]] + both[value.shape[0] :]


def shards_block(
    latents,
    noise,
    timesteps,
    captions,
    cap_lengths,
    null_flags,
    sample_weight,
    embed_w,
    attend_w,
    dense_w,
    vector_w,
    embed_m,
    attend_m,
    dense_m,
    vector_m,
    embed_v,
    attend_v,
    dense_v,
    vector_v,
    embed_e,
    attend_e,
    dense_e,
    vector_e,
):
    clip_dev, frame_dev, patches = (latents.shape[0], latents.shape[1], latents.shape[2])
    n_frame = lax.axis_size("frame")
    n_clip = lax.axis_size("clip")
    local_pos = patches // n_frame
    tokens = frame_dev * patches
    frame_id = lax.axis_index("frame")
    clip_id = lax.axis_index("clip")
    x_id, core_id = frame_id // CORES, frame_id % CORES
    z_id, y_id = clip_id // Y_SIZE, clip_id % Y_SIZE

    emb_first = jnp.asarray(EMB_FIRST, jnp.int32)[clip_id]
    emb_shift = jnp.asarray(EMB_SHIFT, jnp.int32)[clip_id]
    emb_rows = flat_to_rows(embed_w.reshape(-1, LANES), EMB_PAD, emb_shift, jnp.bfloat16)
    dense_cast = cast_shard(
        dense_w, jnp.asarray(cast_table(DENSE_SEGS, CAST_BLOCK))[clip_id], (1, 4), DENSE_ROWS
    )
    cap_owners = range(4, N_OWN)
    cap_plan = (
        [(EMB_PAD * len(cap_owners), D)],
        [(0, EMB_PAD * k, 0, owner, 0, EMB_PAD) for k, owner in enumerate(cap_owners)],
    )
    own_clip = jnp.arange(n_clip) == clip_id
    facts = jnp.stack([timesteps.astype(jnp.float32)[0], sample_weight[0], null_flags.astype(jnp.float32)[0]])
    facts = jnp.broadcast_to(jnp.pad(facts, (0, LANES - 3))[None], (8, LANES))
    cap_weights, fc_in, fc_out, facts = spread_shards(
        [emb_rows, dense_cast],
        [(cap_owners,) + cap_plan + (True,), (range(N_OWN),) + matrix_plan(DENSE, DENSE_SEGS) + (True,)],
        2,
        given=[(facts, "gather")],
    )
    facts = facts[:, 0, :3]
    last = N_OWN - 1
    cap_last = cap_weights[EMB_PAD * (len(cap_owners) - 1) :]
    null_end = 16158720 - ROW_NULL * D
    null_first, final_first = ROW_NULL - EMB_FIRST[last], ROW_FINAL - EMB_FIRST[last]
    null_caption = (
        cap_last[null_first : null_first - (-null_end // D)]
        .reshape(-1)[:null_end]
        .reshape(L_CAP, CAPW)
    )
    final_w = cap_last[final_first : final_first + PATCH_VALUES].reshape(D, PATCH_VALUES)
    two_first = ROW_CAP_TWO - EMB_FIRST[last]

    def to_cap_rows(value):
        padded = jnp.pad(value, ((0, 0), (EMB_PAD, EMB_PAD)))
        starts = [EMB_FIRST[owner] - ROW_CAP_ONE + EMB_PAD for owner in cap_owners]
        return jnp.concatenate([padded[:, start : start + EMB_PAD] for start in starts], 1)

    def from_cap_rows(value):
        total = 0.0
        for k, owner in enumerate(cap_owners):
            start = EMB_FIRST[owner] - ROW_CAP_ONE
            low, high = max(0, -start), min(EMB_PAD, CAPW - start)
            part = value[:, EMB_PAD * k + low : EMB_PAD * k + high]
            total = total + jnp.pad(part, ((0, 0), (start + low, CAPW - start - high)))
        return total

    (
        patch_b,
        time_b1,
        time_b2,
        block_b,
        cap_b1,
        cap_b2,
        space_bq,
        space_bv,
        space_bo,
        time_bq,
        time_bv,
        time_bo,
        cross_bq,
        cross_bv,
        cross_bo,
        fc_in_b,
        fc_out_b,
        final_b,
        table,
        final_table,
    ) = split_flat(vector_w, vector_shapes())

    all_steps, all_null = facts[:, 0], facts[:, 2] == 1.0
    angle = (all_steps / 1000.0 + 0.008) / 1.008 * (math.pi / 2)
    signal = jnp.cos(angle) ** 2
    ratio = signal / (1.0 - signal)
    all_weights = facts[:, 1] * jnp.minimum(ratio, SNR_LIMIT) / ratio
    weight_total = jnp.sum(all_weights)
    signal = lax.dynamic_slice_in_dim(signal, clip_id, 1, 0)
    loss_weight = lax.dynamic_slice_in_dim(all_weights, clip_id, 1, 0)

    freq_in = sincos(all_steps, TFREQ).astype(jnp.bfloat16)
    at_start = clip_id == 0
    time_one = emb_rows[ROW_TIME_ONE:ROW_TIME_TWO]
    time_two = emb_rows[ROW_TIME_TWO:ROW_BLOCK]
    pre_one = matmul_low(freq_in, time_one) + time_b1
    act_one = jax.nn.silu(pre_one).astype(jnp.bfloat16)
    time_embed = matmul_low(act_one, time_two) + time_b2
    early = jnp.concatenate(
        [pre_one, time_embed, emb_rows[:ROW_TIME_ONE].astype(jnp.float32)], 0
    )
    is_null = null_flags == 1
    cap_in = jnp.where(is_null[:, None, None], null_caption[None], captions)
    cap_pre = (matmul_low(to_cap_rows(cap_in[0]), cap_weights) + cap_b1)[None]
    cap_act = gelu_tanh(cap_pre).astype(jnp.bfloat16)
    act_rows = jnp.pad(cap_act[0], ((0, 0), (two_first, EMB_PAD - two_first - D)))
    cap_rows = (matmul_low(act_rows, cap_last) + cap_b2).astype(jnp.bfloat16)[None]
    live_len = jnp.where(is_null, L_CAP, cap_lengths)
    cap_wide = jnp.concatenate([cap_in[0], cap_act[0]], -1)
    cap_wide = jnp.pad(cap_wide, ((0, 0), (EMB_PAD, EMB_PAD)))
    wanted = []
    for owner in range(n_clip):
        start = EMB_FIRST[owner] - ROW_CAP_ONE + EMB_PAD
        if start + EMB_PAD <= EMB_PAD:
            wanted.append(jnp.zeros((L_CAP, EMB_PAD // 4), jnp.bfloat16))
        else:
            wanted.append(
                lax.dynamic_slice_in_dim(cap_wide, start + frame_id * (EMB_PAD // 4), EMB_PAD // 4, 1)
            )
    attend_cast = cast_shard(
        attend_w, jnp.asarray(cast_table(ATTEND_SEGS, CAST_BLOCK))[clip_id], (1, 2, 3), ATTEND_ROWS
    )
    space_qkv, space_out, time_qkv, time_out, cross_q, cross_kv, cross_out, early, cap_left = spread_shards(
        [attend_cast],
        [(range(N_OWN),) + matrix_plan(ATTEND, ATTEND_SEGS) + (True,)],
        1,
        given=[(early, "first"), (jnp.pad(jnp.stack(wanted), ((0, 0), (0, 128 - L_CAP), (0, 0))), "swap")],
    )
    early = early[0]
    cap_left = cap_left[:, :L_CAP].reshape(n_clip * L_CAP, EMB_PAD // 4)
    cap_left = jnp.where(clip_id >= cap_owners[0], cap_left, jnp.zeros_like(cap_left))
    pre_one, time_embed = early[:n_clip], early[n_clip : 2 * n_clip]
    patch_w = early[2 * n_clip :].astype(jnp.bfloat16)
    act_one = jax.nn.silu(pre_one).astype(jnp.bfloat16)
    silu_time = jax.nn.silu(time_embed).astype(jnp.bfloat16)
    local_row = emb_first + jnp.arange(EMB_PAD, dtype=jnp.int32)
    block_row = local_row - ROW_BLOCK
    in_block = (block_row >= 0) & (block_row < 6 * D)
    block_part = jnp.where(in_block, block_row % 6, -1)
    block_line = jnp.where(in_block, block_row // 6, -1)
    chooser = jnp.arange(D, dtype=jnp.int32)[:, None] == block_line[None]
    silu_rows = matmul_low(silu_time, chooser.astype(jnp.bfloat16)).astype(jnp.bfloat16)
    part_mask = jnp.arange(6, dtype=jnp.int32)[:, None] == block_part[None]
    block_left = jnp.where(part_mask[None], silu_rows[:, None], 0).reshape(n_clip * 6, EMB_PAD)
    block_out = sum_clips(matmul_low(block_left, emb_rows)).reshape(n_clip, 6, D)
    all_mods = table[None] + (block_out + block_b.reshape(6, D))
    mods = lax.dynamic_slice_in_dim(all_mods, clip_id, 1, 0)
    my_embed = lax.dynamic_slice_in_dim(time_embed, clip_id, 1, 0)

    keep_part = jnp.sqrt(signal)[:, None, None, None]
    fade_part = jnp.sqrt(1.0 - signal)[:, None, None, None]
    noisy = (keep_part * latents + fade_part * noise).astype(jnp.bfloat16)
    frame_ids = frame_id * frame_dev + jnp.arange(frame_dev)
    patch_ids = jnp.arange(patches)
    place = jnp.concatenate(
        [sincos(patch_ids // PGRID, D // 2), sincos(patch_ids % PGRID, D // 2)], -1
    )[None, None]
    hidden_zero = matmul_low(noisy, patch_w) + patch_b + place + sincos(frame_ids, D)[None, :, None]

    def mod_row(number):
        return mods[:, number][:, None, None, :]

    def flat2(value):
        return value.reshape(-1, value.shape[-1])

    space_in = modulate(hidden_zero, mod_row(0), mod_row(1)).astype(jnp.bfloat16)
    live = live_len.astype(jnp.int32)
    space_q, space_k, space_v = split_qkv(matmul_low(flat2(space_in), space_qkv), space_bq, space_bv)
    space_o, space_lse = heads_forward("all", space_q, space_k, space_v, live)
    space_flat = space_o.reshape(clip_dev, frame_dev, patches, D)
    space_res = matmul_low(space_flat, space_out) + space_bo
    hidden_one = hidden_zero + mod_row(2) * space_res
    time_in = lax.all_to_all(
        hidden_one.astype(jnp.bfloat16), "frame", split_axis=2, concat_axis=1, tiled=True
    )
    time_in = jnp.swapaxes(time_in, 1, 2)
    frames = time_in.shape[2]
    time_q, time_k, time_v = split_qkv(matmul_low(flat2(time_in), time_qkv), time_bq, time_bv)
    time_o, time_lse = heads_forward(frames, time_q, time_k, time_v, live)
    time_back = jnp.swapaxes(time_o.reshape(clip_dev, local_pos, frames, D), 1, 2)
    time_flat = lax.all_to_all(time_back, "frame", split_axis=1, concat_axis=2, tiled=True)
    time_res = matmul_low(time_flat, time_out) + time_bo
    hidden_two = hidden_one + mod_row(2) * time_res
    cross_in = hidden_two.astype(jnp.bfloat16)
    cross_query = (matmul_low(flat2(cross_in), cross_q) + cross_bq).astype(jnp.bfloat16)
    cross_merged = matmul_low(jnp.pad(cap_rows[0], ((0, -L_CAP % 16), (0, 0))), cross_kv)
    cross_k = cross_merged[..., :D].astype(jnp.bfloat16)
    cross_v = (cross_merged[..., D:] + cross_bv).astype(jnp.bfloat16)
    cross_o, cross_lse = heads_forward("cross", cross_query, cross_k, cross_v, live)
    cross_flat = cross_o.reshape(clip_dev, frame_dev, patches, D)
    hidden_three = hidden_two + matmul_low(cross_flat, cross_out) + cross_bo
    dense_in = modulate(hidden_three, mod_row(3), mod_row(4)).astype(jnp.bfloat16)
    dense_pre = matmul_low(dense_in, fc_in) + fc_in_b
    dense_act = gelu_tanh(dense_pre).astype(jnp.bfloat16)
    dense_res = matmul_low(dense_act, fc_out) + fc_out_b
    hidden_four = hidden_three + mod_row(5) * dense_res
    final_mod = final_table[None] + my_embed[:, None, :]
    final_shift = final_mod[:, 0][:, None, None, :]
    final_scale = final_mod[:, 1][:, None, None, :]
    final_in = modulate(hidden_four, final_shift, final_scale).astype(jnp.bfloat16)
    predicted = matmul_low(final_in, final_w) + final_b
    miss = predicted - noise
    clip_error = jnp.sum(jnp.mean(miss * miss, -1), (1, 2))
    local_loss = jnp.sum(loss_weight * clip_error)

    def two_cores(value):
        return [value, shift(value, SWAP_CORE)]

    lefts = {
        label: two_cores(flat2(value).T)
        for label, value in (
            ("space_qkv", space_in),
            ("space_out", space_flat),
            ("time_qkv", time_in),
            ("time_out", time_flat),
            ("cross_q", cross_in),
            ("cross_out", cross_flat),
            ("fc_in", dense_in),
            ("fc_out", dense_act),
        )
    }

    def chunks_of(matrices, segments, rights, n_rows):
        arrays, where = [], {}
        for label, blocks in rights.items():
            where[label] = []
            for value, column in blocks:
                known = [k for k, other in enumerate(arrays) if other is value]
                if not known:
                    arrays.append(value)
                where[label].append((known[0] if known else len(arrays) - 1, column))
        order = {label: number for number, (label, rows, wide) in enumerate(matrices)}
        plan = grad_plan(matrices, segments, order, where)
        return core_chunks(plan, core_id, [lefts[label] for label in order], arrays, n_rows)

    grad_pred = (
        2.0 / miss.shape[-1] * (loss_weight / weight_total)[:, None, None, None] * miss
    ).astype(jnp.bfloat16)
    g_final_w = weight_grad(final_in, grad_pred)
    g_final_b = bias_grad(grad_pred)
    unused, pullback = jax.vjp(modulate, hidden_four, final_shift, final_scale)
    grad_hidden, grad_fshift, grad_fscale = pullback(back_low(grad_pred, final_w))
    grad_fmod = jnp.concatenate([grad_fshift.reshape(1, D), grad_fscale.reshape(1, D)], 0)
    grad_dense = (grad_hidden * mod_row(5)).astype(jnp.bfloat16)
    grad_gate_b = jnp.sum(grad_hidden * dense_res, (1, 2))
    dense_both = two_cores(flat2(grad_dense))
    g_fc_out_b = bias_grad(grad_dense)
    unused, pullback = jax.vjp(gelu_tanh, dense_pre)
    grad_pre = pullback(back_low(grad_dense, fc_out))[0].astype(jnp.bfloat16)
    pre_both = two_cores(flat2(grad_pre))
    dense_chunks = chunks_of(
        DENSE,
        DENSE_SEGS,
        {"fc_in": [(pre_both, j * D) for j in range(MLP // D)], "fc_out": [(dense_both, 0)]},
        DENSE_ROWS,
    )
    rights = {}
    g_fc_in_b = bias_grad(grad_pre)
    unused, pullback = jax.vjp(modulate, hidden_three, mod_row(3), mod_row(4))
    grad_input, grad_shift_b, grad_scale_b = pullback(back_low(grad_pre, fc_in))
    grad_hidden = grad_hidden + grad_input
    grad_cross = grad_hidden.astype(jnp.bfloat16)
    rights["cross_out"] = [(two_cores(flat2(grad_cross)), 0)]
    g_cross_bo = bias_grad(grad_cross)
    grad_cross_o = back_low(flat2(grad_cross), cross_out).astype(jnp.bfloat16)
    grad_cq, grad_ck, grad_cv = heads_backward(
        "cross", cross_query, cross_k, cross_v, live, cross_lse, grad_cross_o
    )
    grad_cq = grad_cq.reshape(clip_dev, frame_dev, patches, D)
    rights["cross_q"] = [(two_cores(flat2(grad_cq)), 0)]
    g_cross_bq = bias_grad(grad_cq)
    grad_hidden = grad_hidden + back_low(grad_cq, cross_q)
    grad_cv = grad_cv[:L_CAP]
    grad_ckv = jnp.concatenate([grad_ck[:L_CAP], grad_cv], -1)
    g_cross_bv = bias_grad(grad_cv)
    grad_ckv = grad_ckv + shift(grad_ckv, SWAP_CORE)
    pad_rows = lambda value: jnp.pad(value, ((0, -L_CAP % LANES), (0, 0)))
    cap_twice = pad_rows(cap_rows[0]).T
    lefts["cross_kv"] = [jnp.concatenate([cap_twice, cap_twice], 1)]
    ckv_parts = [jnp.concatenate([pad_rows(part) for part in halves(grad_ckv)], 0)]
    rights["cross_kv"] = [(ckv_parts, 0), (ckv_parts, D)]
    grad_ckv = grad_ckv + shift(grad_ckv, SWAP_X)
    grad_cap_rows = two_parts(lambda part: back_low(part, cross_kv), grad_ckv)

    grad_time = (grad_hidden * mod_row(2)).astype(jnp.bfloat16)
    rights["time_out"] = [(two_cores(flat2(grad_time)), 0)]
    g_time_bo = bias_grad(grad_time)
    grad_time_o = lax.all_to_all(
        back_low(grad_time, time_out).astype(jnp.bfloat16),
        "frame",
        split_axis=2,
        concat_axis=1,
        tiled=True,
    )
    grad_time_o = flat2(jnp.swapaxes(grad_time_o, 1, 2))
    grad_tqkv = [
        piece.reshape(clip_dev, local_pos, frames, D)
        for piece in heads_backward(frames, time_q, time_k, time_v, live, time_lse, grad_time_o)
    ]
    rights["time_qkv"] = [(two_cores(flat2(part)), 0) for part in grad_tqkv]
    g_time_bq = bias_grad(grad_tqkv[0])
    g_time_bv = bias_grad(grad_tqkv[2])
    grad_tqkv = lax.all_to_all(
        jnp.swapaxes(jnp.concatenate(grad_tqkv, -1), 1, 2), "frame", split_axis=1, concat_axis=2, tiled=True
    )
    grad_gate_a = jnp.sum(grad_hidden * time_res, (1, 2))
    grad_hidden = grad_hidden + back_low(grad_tqkv, time_qkv)
    grad_gate_a = grad_gate_a + jnp.sum(grad_hidden * space_res, (1, 2))
    grad_space = (grad_hidden * mod_row(2)).astype(jnp.bfloat16)
    rights["space_out"] = [(two_cores(flat2(grad_space)), 0)]
    g_space_bo = bias_grad(grad_space)
    grad_space_o = back_low(flat2(grad_space), space_out).astype(jnp.bfloat16)
    grad_sqkv = [
        piece.reshape(clip_dev, frame_dev, patches, D)
        for piece in heads_backward("all", space_q, space_k, space_v, live, space_lse, grad_space_o)
    ]
    rights["space_qkv"] = [(two_cores(flat2(part)), 0) for part in grad_sqkv]
    attend_chunks = chunks_of(ATTEND, ATTEND_SEGS, rights, ATTEND_ROWS)
    g_space_bq = bias_grad(grad_sqkv[0])
    g_space_bv = bias_grad(grad_sqkv[2])
    grad_sqkv = jnp.concatenate(grad_sqkv, -1)
    unused, pullback = jax.vjp(modulate, hidden_zero, mod_row(0), mod_row(1))
    grad_input, grad_shift_a, grad_scale_a = pullback(back_low(grad_sqkv, space_qkv))
    grad_hidden = grad_hidden + grad_input
    g_patch_w = weight_split(noisy, grad_hidden)
    g_patch_b = bias_grad(grad_hidden)
    grad_mods = jnp.concatenate(
        [
            grad_shift_a.reshape(clip_dev, D),
            grad_scale_a.reshape(clip_dev, D),
            grad_gate_a,
            grad_shift_b.reshape(clip_dev, D),
            grad_scale_b.reshape(clip_dev, D),
            grad_gate_b,
            grad_fmod,
        ],
        0,
    )

    unused, pullback = jax.vjp(gelu_tanh, cap_pre[0])
    grad_cap_act = two_parts(lambda part: back_low(part, cap_last), grad_cap_rows)
    grad_cap_pre = pullback(grad_cap_act[:, two_first : two_first + D])[0]
    cap_right = lax.all_gather(
        jnp.stack([grad_cap_pre, grad_cap_rows]), "clip", axis=1, tiled=True
    )
    null_sum = jnp.sum(jnp.where(all_null[:, None, None], cap_right[0].reshape(n_clip, L_CAP, D), 0.0), 0)
    g_cap_b1 = bias_grad(grad_cap_pre)
    g_cap_b2 = bias_grad(grad_cap_rows)

    once = frame_id == 0
    gathered_mods = jnp.where(own_clip[:, None, None], grad_mods[None], 0.0)
    ends = jnp.concatenate([g_final_b, local_loss.reshape(1)])
    vector_rows = [
        g_patch_b,
        jnp.where(once, g_cap_b1, 0.0),
        jnp.where(once, g_cap_b2, 0.0),
        g_space_bq,
        g_space_bv,
        g_space_bo,
        g_time_bq,
        g_time_bv,
        g_time_bo,
        g_cross_bq,
        g_cross_bv,
        g_cross_bo,
        g_fc_in_b.reshape(-1, D),
        g_fc_out_b,
        jnp.pad(ends, (0, D - ends.shape[0])),
    ]
    small = [gathered_mods.reshape(-1, D), g_patch_w, g_final_w.reshape(PATCH_VALUES, D)]
    small = small + [value.reshape(-1, D) for value in vector_rows]
    spare = -sum(value.shape[0] for value in small) % 8
    small = jnp.concatenate(small + [jnp.zeros((spare, D), jnp.float32)] * (spare > 0), 0)
    dense_grad, small = collect_shard(
        dense_chunks,
        160,
        3,
        small=small,
    )
    dense_grad = dense_grad.reshape(DENSE_ROWS, D)
    at = 8 * n_clip
    gathered_mods = small[:at].reshape(n_clip, 8, D)
    g_patch_w = small[at : at + PATCH_VALUES]
    g_final_w = small[at + PATCH_VALUES : at + 2 * PATCH_VALUES]
    rest = small[at + 2 * PATCH_VALUES :]
    n_whole = 12 + MLP // D + 1
    loss_sum = rest[n_whole, PATCH_VALUES]
    vector_grad = jnp.concatenate([rest[:n_whole].reshape(-1), rest[n_whole, :PATCH_VALUES]])

    grad_zero = gathered_mods[:, :6]
    grad_final = gathered_mods[:, 6:]
    zero_rows = grad_zero.reshape(n_clip * 6, D)
    back_rows = two_parts(lambda part: back_low(part, emb_rows), zero_rows)
    back_rows = jnp.sum(jnp.where(part_mask[None], back_rows.reshape(n_clip, 6, EMB_PAD), 0.0), 1)
    grad_silu = lax.dot_general(
        back_rows,
        chooser.astype(jnp.float32),
        (((1,), (1,)), ((), ())),
        precision=lax.Precision.HIGHEST,
        preferred_element_type=jnp.float32,
    )
    grad_silu = sum_clips(grad_silu)
    unused, pullback = jax.vjp(jax.nn.silu, time_embed)
    grad_embed = grad_final[:, 0] + grad_final[:, 1] + pullback(grad_silu)[0]
    grad_act = two_parts(lambda part: back_low(part, time_two), grad_embed)
    grad_act = sum_clips(jnp.where(at_start, grad_act, 0.0))
    unused, pullback = jax.vjp(jax.nn.silu, pre_one)
    grad_one = pullback(grad_act)[0]
    g_table = jnp.sum(grad_zero, 0)
    vector_sum = flatten_all(
        [
            vector_grad[:D],
            jnp.sum(grad_one, 0),
            jnp.sum(grad_embed, 0),
            g_table,
            vector_grad[D:],
            g_table,
            jnp.sum(grad_final, 0),
        ]
    )

    per = EMB_PAD // 4
    quarter_row = emb_first + frame_id * per + jnp.arange(per, dtype=jnp.int32)
    time_left = jnp.concatenate(
        [
            jnp.pad(freq_in, ((0, 0), (ROW_TIME_ONE, EMB_PAD - ROW_TIME_TWO))),
            jnp.pad(act_one, ((0, 0), (ROW_TIME_TWO, EMB_PAD - ROW_BLOCK))),
        ],
        0,
    )
    time_left = jnp.where(at_start, time_left, jnp.zeros_like(time_left))
    small_left = lax.dynamic_slice_in_dim(
        jnp.concatenate([time_left, block_left], 0), frame_id * per, per, 1
    )
    small_right = jnp.concatenate([grad_one, grad_embed, zero_rows], 0)
    first_kind = (quarter_row < ROW_CAP_TWO)[None]
    no_left = jnp.zeros_like(cap_left)
    null_back = back_low(cap_weights, jnp.concatenate(halves(null_sum), 0))
    g_null = from_cap_rows((null_back[:, :L_CAP] + null_back[:, L_CAP:]).T)
    n_null = -(-null_end // D)
    n_known = -(-(2 * PATCH_VALUES + n_null) // 16) * 16
    null_rows = jnp.pad(g_null.reshape(-1), (0, (n_known - 2 * PATCH_VALUES) * D - null_end))
    known = jnp.concatenate([g_patch_w, g_final_w, null_rows.reshape(-1, D)], 0)
    known_row = np.concatenate(
        [np.arange(PATCH_VALUES), ROW_FINAL + np.arange(n_known - PATCH_VALUES)]
    ).astype(np.int32)
    known_left = (jnp.asarray(known_row)[:, None] == quarter_row[None]).astype(jnp.bfloat16)
    emb_left = jnp.concatenate(
        [
            small_left,
            jnp.where(first_kind, cap_left, no_left),
            jnp.where(first_kind, no_left, cap_left),
            known_left,
        ],
        0,
    )
    emb_right = jnp.concatenate([small_right, cap_right[0], cap_right[1], known], 0)
    emb_grad = weight_split(emb_left, emb_right)
    unit = (
        LANE_TILES * (frame_id * per + jnp.arange(per, dtype=jnp.int32))[:, None]
        + jnp.arange(D, dtype=jnp.int32)[None] // LANES
        - emb_shift
    )
    emb_grad = jnp.where((unit >= 0) & (unit < EMB_UNITS), emb_grad, 0.0)

    attend_grad, emb_whole = collect_shard(
        attend_chunks,
        208,
        4,
        part=emb_grad,
    )
    attend_grad = attend_grad.reshape(ATTEND_ROWS, D)
    local_square = sum(jnp.sum(value * value) for value in (dense_grad, attend_grad, emb_whole))
    vector_square = jnp.sum(vector_sum * vector_sum)
    grad_norm = jnp.sqrt(sum_clips(local_square.reshape(1))[0] + vector_square)
    factor = jnp.minimum(1.0, CLIP_LIMIT / (grad_norm + NORM_FLOOR))
    scale = factor.reshape(1)
    dense_r = step_shard(
        dense_grad,
        jnp.asarray(step_table(DENSE_SEGS, STEP_BLOCK, DENSE_ROWS))[clip_id],
        (1, 4),
        DENSE_ROWS,
        scale,
        (dense_w, dense_m, dense_v, dense_e),
    )
    attend_r = step_shard(
        attend_grad,
        jnp.asarray(step_table(ATTEND_SEGS, STEP_BLOCK, ATTEND_ROWS))[clip_id],
        (1, 2, 3),
        ATTEND_ROWS,
        scale,
        (attend_w, attend_m, attend_v, attend_e),
    )
    emb_flat = rows_to_flat(emb_whole.reshape(EMB_PAD, D))
    emb_owned = lax.dynamic_slice_in_dim(emb_flat, emb_shift, EMB_UNITS, 0).reshape(-1)
    embed_r = adam_step(embed_w, emb_owned, embed_m, embed_v, embed_e, factor)
    vector_r = adam_step(vector_w, vector_sum, vector_m, vector_v, vector_e, factor)
    return (
        loss_sum,
        weight_total,
        grad_norm,
        embed_r[0],
        attend_r[0],
        dense_r[0],
        vector_r[0],
        embed_r[1],
        attend_r[1],
        dense_r[1],
        vector_r[1],
        embed_r[2],
        attend_r[2],
        dense_r[2],
        vector_r[2],
        embed_r[3],
        attend_r[3],
        dense_r[3],
        vector_r[3],
    )


def pick_plan(mesh):
    if mesh.shape["frame"] == X_SIZE * CORES and mesh.shape["clip"] == N_OWN:
        return shards_block
    return shards


def solution(mesh):
    in_specs = (
        P("clip", "frame", None, None),
        P("clip", "frame", None, None),
        P("clip"),
        P("clip", None, None),
        P("clip"),
        P("clip"),
        P("clip"),
        P("clip"),
        P("clip"),
        P("clip"),
        P(),
        P("clip"),
        P("clip"),
        P("clip"),
        P(),
        P("clip"),
        P("clip"),
        P("clip"),
        P(),
        P("clip"),
        P("clip"),
        P("clip"),
        P(),
    )
    out_specs = (
        P(),
        P(),
        P(),
        P("clip"),
        P("clip"),
        P("clip"),
        P(),
        P("clip"),
        P("clip"),
        P("clip"),
        P(),
        P("clip"),
        P("clip"),
        P("clip"),
        P(),
        P("clip"),
        P("clip"),
        P("clip"),
        P(),
    )
    return jax.shard_map(pick_plan(mesh), mesh=mesh, in_specs=in_specs, out_specs=out_specs, check_vma=False)
```

```python
import math
from functools import partial

import jax
import jax.numpy as jnp
import numpy as np
from jax import lax
from jax.experimental import pallas as pl
from jax.experimental.pallas import tpu as pltpu
from jax.sharding import PartitionSpec as P

D = 1152
HEADS = 16
MLP = 4608
CAPW = 4096
L_CAP = 120
TFREQ = 256
PATCH_VALUES = 16
PGRID = 16
STEP = 10


NORM_FLOOR = 1e-06
CLIP_LIMIT = 1.0
SNR_LIMIT = 5.0
BETA_FIRST = 0.5
BETA_SECOND = 0.5
LEARN_RATE = 0.02
WEIGHT_DECAY = 0.01
ADAM_FLOOR = 1e-08
AVERAGE_KEEP = 0.9999
MASKED_SCORE = -1e30


def embed_shapes():
    return [
        (PATCH_VALUES, D),
        (TFREQ, D),
        (D, D),
        (D, 6 * D),
        (CAPW, D),
        (D, D),
        (D, PATCH_VALUES),
        (L_CAP, CAPW),
    ]


def attend_shapes():
    return [(D, 3 * D), (D, D), (D, 3 * D), (D, D), (D, D), (D, 2 * D), (D, D)]


def dense_shapes():
    return [(D, MLP), (MLP, D)]


def vector_shapes():
    return [(D,)] * 3 + [(6 * D,)] + [(D,)] * 11 + [(MLP,), (D,), (PATCH_VALUES,), (6, D), (2, D)]


def split_flat(flat, shapes):
    pieces = []
    offset = 0
    for extent in shapes:
        length = math.prod(extent)
        pieces.append(flat[offset : offset + length].reshape(extent))
        offset += length
    return pieces


def flatten_all(pieces):
    return jnp.concatenate([piece.reshape(-1) for piece in pieces])


def reduce_group(grad):
    n_clip = lax.axis_size("clip")
    n_frame = lax.axis_size("frame")
    reorder = grad.reshape(n_clip, n_frame, -1).swapaxes(0, 1).reshape(-1)
    share = lax.psum_scatter(reorder, ("frame", "clip"), scatter_dimension=0, tiled=True)
    return lax.all_gather(share, "frame", axis=0, tiled=True)


def sincos(places, width):
    half = width // 2
    omega = jnp.exp(-math.log(10000.0) * jnp.arange(half, dtype=jnp.float32) / half)
    angle = places.astype(jnp.float32)[..., None] * omega
    return jnp.concatenate([jnp.sin(angle), jnp.cos(angle)], -1)


def modulate(hidden, shift, scale):
    center = hidden - jnp.mean(hidden, -1, keepdims=True)
    normed = center * lax.rsqrt(jnp.mean(center * center, -1, keepdims=True) + NORM_FLOOR)
    return normed * (1.0 + scale) + shift


def gelu_tanh(value):
    return jax.nn.gelu(value, approximate=True)


def matmul_low(left, right):
    return lax.dot_general(
        left, right, (((left.ndim - 1,), (0,)), ((), ())), preferred_element_type=jnp.float32
    )


def halves(value):
    upper = lax.optimization_barrier(value.astype(jnp.bfloat16))
    return (upper, (value - upper.astype(jnp.float32)).astype(jnp.bfloat16))


def back_low(grads, weight):
    return lax.dot_general(
        grads, weight, (((grads.ndim - 1,), (1,)), ((), ())), preferred_element_type=jnp.float32
    )


def back_split(grads, weight):
    upper, lower = halves(grads)
    return back_low(upper, weight) + back_low(lower, weight)


def weight_grad(inputs, grads):
    left = inputs.reshape(-1, inputs.shape[-1])
    right = grads.reshape(-1, grads.shape[-1])
    return lax.dot_general(
        left, right, (((0,), (0,)), ((), ())), preferred_element_type=jnp.float32
    )


def weight_split(inputs, grads):
    upper, lower = halves(grads)
    return weight_grad(inputs, upper) + weight_grad(inputs, lower)


def bias_grad(grads):
    return jnp.sum(grads.astype(jnp.float32).reshape(-1, grads.shape[-1]), 0)


def heads_of(tensor, batch):
    return tensor.reshape(batch, -1, HEADS, tensor.shape[-1] // HEADS)


def split_qkv(merged, bias_q, bias_v):
    width = merged.shape[-1] // 3
    return (
        (merged[..., :width] + bias_q).astype(jnp.bfloat16),
        merged[..., width : 2 * width].astype(jnp.bfloat16),
        (merged[..., 2 * width :] + bias_v).astype(jnp.bfloat16),
    )


def attend_scores(queries, key_rows, mask):
    scores = jnp.einsum("bqhe,bkhe->bhqk", queries, key_rows, preferred_element_type=jnp.float32)
    scores = scores * queries.shape[-1] ** (-0.5)
    if mask is not None:
        scores = jnp.where(mask[:, None, None, :], scores, MASKED_SCORE)
    return scores


def attend_forward(queries, key_rows, values, mask):
    scores = attend_scores(queries, key_rows, mask)
    summit = jnp.max(scores, -1, keepdims=True)
    powers = jnp.exp(scores - summit)
    totals = jnp.sum(powers, -1, keepdims=True)
    probs = (powers / totals).astype(jnp.bfloat16)
    output = jnp.einsum("bhqk,bkhe->bqhe", probs, values, preferred_element_type=jnp.float32)
    return (output.astype(jnp.bfloat16), summit + jnp.log(totals))


def attend_backward(queries, key_rows, values, mask, log_total, grad_out):
    scale = queries.shape[-1] ** (-0.5)
    probs = jnp.exp(attend_scores(queries, key_rows, mask) - log_total)
    grad_probs = jnp.einsum("bqhe,bkhe->bhqk", grad_out, values, preferred_element_type=jnp.float32)
    grad_scores = (probs * (grad_probs - jnp.sum(probs * grad_probs, -1, keepdims=True))).astype(
        jnp.bfloat16
    )
    grad_query = (
        jnp.einsum("bhqk,bkhe->bqhe", grad_scores, key_rows, preferred_element_type=jnp.float32)
        * scale
    )
    grad_keys = (
        jnp.einsum("bhqk,bqhe->bkhe", grad_scores, queries, preferred_element_type=jnp.float32)
        * scale
    )
    grad_values = jnp.einsum(
        "bhqk,bqhe->bkhe", probs.astype(jnp.bfloat16), grad_out, preferred_element_type=jnp.float32
    )
    return (grad_query, grad_keys, grad_values)


def unpack_all(gathered):
    return (
        split_flat(gathered[0], embed_shapes()),
        split_flat(gathered[1], attend_shapes()),
        split_flat(gathered[2], dense_shapes()),
    )


def adam_step(master, grad, first, second, average, factor):
    keep = min(AVERAGE_KEEP, (1.0 + STEP) / (10.0 + STEP))
    grad = grad * factor
    first = BETA_FIRST * first + (1.0 - BETA_FIRST) * grad
    second = BETA_SECOND * second + (1.0 - BETA_SECOND) * grad * grad
    moved = (
        first
        / (1.0 - BETA_FIRST**STEP)
        / (jnp.sqrt(second / (1.0 - BETA_SECOND**STEP)) + ADAM_FLOOR)
    )
    master = master - LEARN_RATE * (moved + WEIGHT_DECAY * master)
    return (master, first, second, keep * average + (1.0 - keep) * master)


def shards(
    latents,
    noise,
    timesteps,
    captions,
    cap_lengths,
    null_flags,
    sample_weight,
    embed_w,
    attend_w,
    dense_w,
    vector_w,
    embed_m,
    attend_m,
    dense_m,
    vector_m,
    embed_v,
    attend_v,
    dense_v,
    vector_v,
    embed_e,
    attend_e,
    dense_e,
    vector_e,
):
    clip_dev, frame_dev, patches = (latents.shape[0], latents.shape[1], latents.shape[2])
    n_frame = lax.axis_size("frame")
    n_clip = lax.axis_size("clip")
    local_pos = patches // n_frame
    gathered = (
        lax.all_gather(embed_w.astype(jnp.bfloat16), "clip", axis=0, tiled=True),
        lax.all_gather(attend_w.astype(jnp.bfloat16), "clip", axis=0, tiled=True),
        lax.all_gather(dense_w.astype(jnp.bfloat16), "clip", axis=0, tiled=True),
    )
    embeds, attends, denses = unpack_all(gathered)
    patch_w, time_one, time_two, block_w, cap_one, cap_two, final_w, null_caption = embeds
    space_qkv, space_out, time_qkv, time_out, cross_q, cross_kv, cross_out = attends
    fc_in, fc_out = denses
    (
        patch_b,
        time_b1,
        time_b2,
        block_b,
        cap_b1,
        cap_b2,
        space_bq,
        space_bv,
        space_bo,
        time_bq,
        time_bv,
        time_bo,
        cross_bq,
        cross_bv,
        cross_bo,
        fc_in_b,
        fc_out_b,
        final_b,
        table,
        final_table,
    ) = split_flat(vector_w, vector_shapes())
    angle = (timesteps.astype(jnp.float32) / 1000.0 + 0.008) / 1.008 * (math.pi / 2)
    signal = jnp.cos(angle) ** 2
    ratio = signal / (1.0 - signal)
    loss_weight = sample_weight * jnp.minimum(ratio, SNR_LIMIT) / ratio
    weight_total = lax.psum(jnp.sum(loss_weight), "clip")
    keep_part = jnp.sqrt(signal)[:, None, None, None]
    fade_part = jnp.sqrt(1.0 - signal)[:, None, None, None]
    noisy = (keep_part * latents + fade_part * noise).astype(jnp.bfloat16)
    frame_ids = lax.axis_index("frame") * frame_dev + jnp.arange(frame_dev)
    patch_ids = jnp.arange(patches)
    place = jnp.concatenate(
        [sincos(patch_ids // PGRID, D // 2), sincos(patch_ids % PGRID, D // 2)], -1
    )[None, None]
    hidden_zero = matmul_low(noisy, patch_w) + patch_b + place + sincos(frame_ids, D)[None, :, None]
    freq_in = sincos(timesteps, TFREQ).astype(jnp.bfloat16)
    pre_one = matmul_low(freq_in, time_one) + time_b1
    act_one = jax.nn.silu(pre_one).astype(jnp.bfloat16)
    time_embed = matmul_low(act_one, time_two) + time_b2
    silu_time = jax.nn.silu(time_embed).astype(jnp.bfloat16)
    mods = table[None] + (matmul_low(silu_time, block_w) + block_b).reshape(clip_dev, 6, D)

    def mod_row(number):
        return mods[:, number][:, None, None, :]

    is_null = null_flags == 1
    cap_in = jnp.where(is_null[:, None, None], null_caption[None], captions)
    cap_pre = matmul_low(cap_in, cap_one) + cap_b1
    cap_act = gelu_tanh(cap_pre).astype(jnp.bfloat16)
    cap_rows = (matmul_low(cap_act, cap_two) + cap_b2).astype(jnp.bfloat16)
    live_len = jnp.where(is_null, L_CAP, cap_lengths)
    key_mask = jnp.arange(L_CAP)[None, :] < live_len[:, None]
    space_in = modulate(hidden_zero, mod_row(0), mod_row(1)).astype(jnp.bfloat16)
    space_q, space_k, space_v = (
        heads_of(piece, clip_dev * frame_dev)
        for piece in split_qkv(matmul_low(space_in, space_qkv), space_bq, space_bv)
    )
    space_o, space_lse = attend_forward(space_q, space_k, space_v, None)
    space_flat = space_o.reshape(clip_dev, frame_dev, patches, D)
    space_res = matmul_low(space_flat, space_out) + space_bo
    hidden_one = hidden_zero + mod_row(2) * space_res
    time_in = lax.all_to_all(
        hidden_one.astype(jnp.bfloat16), "frame", split_axis=2, concat_axis=1, tiled=True
    )
    time_in = jnp.swapaxes(time_in, 1, 2)
    frames = time_in.shape[2]
    time_q, time_k, time_v = (
        heads_of(piece, clip_dev * local_pos)
        for piece in split_qkv(matmul_low(time_in, time_qkv), time_bq, time_bv)
    )
    time_o, time_lse = attend_forward(time_q, time_k, time_v, None)
    time_back = jnp.swapaxes(time_o.reshape(clip_dev, local_pos, frames, D), 1, 2)
    time_flat = lax.all_to_all(time_back, "frame", split_axis=1, concat_axis=2, tiled=True)
    time_res = matmul_low(time_flat, time_out) + time_bo
    hidden_two = hidden_one + mod_row(2) * time_res
    cross_in = hidden_two.astype(jnp.bfloat16)
    cross_query = heads_of(
        (matmul_low(cross_in, cross_q) + cross_bq).astype(jnp.bfloat16), clip_dev
    )
    cross_merged = matmul_low(cap_rows, cross_kv)
    cross_k = heads_of(cross_merged[..., :D].astype(jnp.bfloat16), clip_dev)
    cross_v = heads_of((cross_merged[..., D:] + cross_bv).astype(jnp.bfloat16), clip_dev)
    cross_o, cross_lse = attend_forward(cross_query, cross_k, cross_v, key_mask)
    cross_flat = cross_o.reshape(clip_dev, frame_dev, patches, D)
    hidden_three = hidden_two + matmul_low(cross_flat, cross_out) + cross_bo
    dense_in = modulate(hidden_three, mod_row(3), mod_row(4)).astype(jnp.bfloat16)
    dense_pre = matmul_low(dense_in, fc_in) + fc_in_b
    dense_act = gelu_tanh(dense_pre).astype(jnp.bfloat16)
    dense_res = matmul_low(dense_act, fc_out) + fc_out_b
    hidden_four = hidden_three + mod_row(5) * dense_res
    final_mod = final_table[None] + time_embed[:, None, :]
    final_shift = final_mod[:, 0][:, None, None, :]
    final_scale = final_mod[:, 1][:, None, None, :]
    final_in = modulate(hidden_four, final_shift, final_scale).astype(jnp.bfloat16)
    predicted = matmul_low(final_in, final_w) + final_b
    miss = predicted - noise
    clip_error = jnp.sum(jnp.mean(miss * miss, -1), (1, 2))
    local_loss = jnp.sum(loss_weight * clip_error)
    grad_pred = (
        2.0 / miss.shape[-1] * (loss_weight / weight_total)[:, None, None, None] * miss
    ).astype(jnp.bfloat16)
    g_final_w = weight_grad(final_in, grad_pred)
    g_final_b = bias_grad(grad_pred)
    unused, pullback = jax.vjp(modulate, hidden_four, final_shift, final_scale)
    grad_hidden, grad_fshift, grad_fscale = pullback(back_low(grad_pred, final_w))
    grad_fmod = jnp.stack([grad_fshift.reshape(clip_dev, D), grad_fscale.reshape(clip_dev, D)], 1)
    g_final_table = jnp.sum(grad_fmod, 0)
    grad_time_embed = grad_fmod[:, 0] + grad_fmod[:, 1]
    grad_dense = (grad_hidden * mod_row(5)).astype(jnp.bfloat16)
    grad_gate_b = jnp.sum(grad_hidden * dense_res, (1, 2))
    g_fc_out = weight_grad(dense_act, grad_dense)
    g_fc_out_b = bias_grad(grad_dense)
    unused, pullback = jax.vjp(gelu_tanh, dense_pre)
    grad_pre = pullback(back_low(grad_dense, fc_out))[0].astype(jnp.bfloat16)
    g_fc_in = weight_grad(dense_in, grad_pre)
    g_fc_in_b = bias_grad(grad_pre)
    dense_owned = reduce_group(flatten_all([g_fc_in, g_fc_out]))
    unused, pullback = jax.vjp(modulate, hidden_three, mod_row(3), mod_row(4))
    grad_input, grad_shift_b, grad_scale_b = pullback(back_low(grad_pre, fc_in))
    grad_hidden = grad_hidden + grad_input
    grad_cross = grad_hidden.astype(jnp.bfloat16)
    g_cross_out = weight_grad(cross_flat, grad_cross)
    g_cross_bo = bias_grad(grad_cross)
    grad_cross_o = heads_of(back_low(grad_cross, cross_out).astype(jnp.bfloat16), clip_dev)
    grad_cq, grad_ck, grad_cv = attend_backward(
        cross_query, cross_k, cross_v, key_mask, cross_lse, grad_cross_o
    )
    grad_cq = grad_cq.astype(jnp.bfloat16).reshape(clip_dev, frame_dev, patches, D)
    g_cross_q = weight_grad(cross_in, grad_cq)
    g_cross_bq = bias_grad(grad_cq)
    grad_hidden = grad_hidden + back_low(grad_cq, cross_q)
    grad_cv = grad_cv.reshape(clip_dev, L_CAP, D)
    grad_ckv = jnp.concatenate([grad_ck.reshape(clip_dev, L_CAP, D), grad_cv], -1)
    g_cross_kv = weight_split(cap_rows, grad_ckv)
    g_cross_bv = bias_grad(grad_cv)
    grad_cap_rows = back_split(grad_ckv, cross_kv)
    grad_time = (grad_hidden * mod_row(2)).astype(jnp.bfloat16)
    g_time_out = weight_grad(time_flat, grad_time)
    g_time_bo = bias_grad(grad_time)
    grad_time_o = lax.all_to_all(
        back_low(grad_time, time_out).astype(jnp.bfloat16),
        "frame",
        split_axis=2,
        concat_axis=1,
        tiled=True,
    )
    grad_time_o = heads_of(jnp.swapaxes(grad_time_o, 1, 2), clip_dev * local_pos)
    grad_tq, grad_tk, grad_tv = attend_backward(time_q, time_k, time_v, None, time_lse, grad_time_o)
    grad_tqkv = jnp.concatenate(
        [
            piece.astype(jnp.bfloat16).reshape(clip_dev, local_pos, frames, D)
            for piece in (grad_tq, grad_tk, grad_tv)
        ],
        -1,
    )
    g_time_qkv = weight_grad(time_in, grad_tqkv)
    g_time_bq = bias_grad(grad_tqkv[..., :D])
    g_time_bv = bias_grad(grad_tqkv[..., 2 * D :])
    grad_tqkv = lax.all_to_all(
        jnp.swapaxes(grad_tqkv, 1, 2), "frame", split_axis=1, concat_axis=2, tiled=True
    )
    grad_gate_a = jnp.sum(grad_hidden * time_res, (1, 2))
    grad_hidden = grad_hidden + back_low(grad_tqkv, time_qkv)
    grad_gate_a = grad_gate_a + jnp.sum(grad_hidden * space_res, (1, 2))
    grad_space = (grad_hidden * mod_row(2)).astype(jnp.bfloat16)
    g_space_out = weight_grad(space_flat, grad_space)
    g_space_bo = bias_grad(grad_space)
    grad_space_o = heads_of(
        back_low(grad_space, space_out).astype(jnp.bfloat16), clip_dev * frame_dev
    )
    grad_sq, grad_sk, grad_sv = attend_backward(
        space_q, space_k, space_v, None, space_lse, grad_space_o
    )
    grad_sqkv = jnp.concatenate(
        [
            piece.astype(jnp.bfloat16).reshape(clip_dev, frame_dev, patches, D)
            for piece in (grad_sq, grad_sk, grad_sv)
        ],
        -1,
    )
    g_space_qkv = weight_grad(space_in, grad_sqkv)
    g_space_bq = bias_grad(grad_sqkv[..., :D])
    g_space_bv = bias_grad(grad_sqkv[..., 2 * D :])
    attend_owned = reduce_group(
        flatten_all(
            [g_space_qkv, g_space_out, g_time_qkv, g_time_out, g_cross_q, g_cross_kv, g_cross_out]
        )
    )
    unused, pullback = jax.vjp(modulate, hidden_zero, mod_row(0), mod_row(1))
    grad_input, grad_shift_a, grad_scale_a = pullback(back_low(grad_sqkv, space_qkv))
    grad_hidden = grad_hidden + grad_input
    g_patch_w = weight_split(noisy, grad_hidden)
    g_patch_b = bias_grad(grad_hidden)
    grad_mods = jnp.stack(
        [
            grad_shift_a.reshape(clip_dev, D),
            grad_scale_a.reshape(clip_dev, D),
            grad_gate_a,
            grad_shift_b.reshape(clip_dev, D),
            grad_scale_b.reshape(clip_dev, D),
            grad_gate_b,
        ],
        1,
    )
    g_table = jnp.sum(grad_mods, 0)
    grad_zero = grad_mods.reshape(clip_dev, 6 * D)
    g_block_b = jnp.sum(grad_zero, 0)
    g_block_w = weight_split(silu_time, grad_zero)
    unused, pullback = jax.vjp(jax.nn.silu, time_embed)
    grad_time_embed = grad_time_embed + pullback(back_split(grad_zero, block_w))[0]
    g_time_b2 = jnp.sum(grad_time_embed, 0)
    g_time_two = weight_split(act_one, grad_time_embed)
    unused, pullback = jax.vjp(jax.nn.silu, pre_one)
    grad_pre_one = pullback(back_split(grad_time_embed, time_two))[0]
    g_time_b1 = jnp.sum(grad_pre_one, 0)
    g_time_one = weight_split(freq_in, grad_pre_one)
    g_cap_b2 = bias_grad(grad_cap_rows)
    g_cap_two = weight_split(cap_act, grad_cap_rows)
    unused, pullback = jax.vjp(gelu_tanh, cap_pre)
    grad_cap_pre = pullback(back_split(grad_cap_rows, cap_two))[0]
    g_cap_b1 = bias_grad(grad_cap_pre)
    g_cap_one = weight_split(cap_in, grad_cap_pre)
    grad_cap_in = back_split(grad_cap_pre, cap_one)
    g_null = jnp.sum(jnp.where(is_null[:, None, None], grad_cap_in, 0.0), 0)
    embed_owned = reduce_group(
        flatten_all(
            [g_patch_w, g_time_one, g_time_two, g_block_w, g_cap_one, g_cap_two, g_final_w, g_null]
        )
    )
    vector_grad = flatten_all(
        [
            g_patch_b,
            g_time_b1,
            g_time_b2,
            g_block_b,
            g_cap_b1,
            g_cap_b2,
            g_space_bq,
            g_space_bv,
            g_space_bo,
            g_time_bq,
            g_time_bv,
            g_time_bo,
            g_cross_bq,
            g_cross_bv,
            g_cross_bo,
            g_fc_in_b,
            g_fc_out_b,
            g_final_b,
            g_table,
            g_final_table,
        ]
    )
    vector_sum, loss_sum = lax.psum((vector_grad, local_loss), ("frame", "clip"))
    owned = (embed_owned, attend_owned, dense_owned)
    local_square = (
        sum((jnp.sum(shard_piece * shard_piece) for shard_piece in owned))
        + jnp.sum(vector_sum * vector_sum) / n_clip
    )
    grad_norm = jnp.sqrt(lax.psum(local_square, "clip"))
    factor = jnp.minimum(1.0, CLIP_LIMIT / (grad_norm + NORM_FLOOR))
    embed_r = adam_step(embed_w, owned[0], embed_m, embed_v, embed_e, factor)
    attend_r = adam_step(attend_w, owned[1], attend_m, attend_v, attend_e, factor)
    dense_r = adam_step(dense_w, owned[2], dense_m, dense_v, dense_e, factor)
    vector_r = adam_step(vector_w, vector_sum, vector_m, vector_v, vector_e, factor)
    return (
        loss_sum,
        weight_total,
        grad_norm,
        embed_r[0],
        attend_r[0],
        dense_r[0],
        vector_r[0],
        embed_r[1],
        attend_r[1],
        dense_r[1],
        vector_r[1],
        embed_r[2],
        attend_r[2],
        dense_r[2],
        vector_r[2],
        embed_r[3],
        attend_r[3],
        dense_r[3],
        vector_r[3],
    )


AXES = ("frame", "clip")
LANES = 128
LANE_TILES = D // LANES
EMB_PAD = 1824


X_SIZE, CORES, Z_SIZE, Y_SIZE = 2, 2, 4, 2
N_OWN = Z_SIZE * Y_SIZE
RING = [(0, 0), (1, 0), (2, 0), (3, 0), (3, 1), (2, 1), (1, 1), (0, 1)]
RING_CLIP = [z * Y_SIZE + y for z, y in RING]
CLIP_RING = [RING_CLIP.index(c) for c in range(N_OWN)]


def pairs(move):
    out = []
    for x in range(X_SIZE):
        for core in range(CORES):
            for z in range(Z_SIZE):
                for y in range(Y_SIZE):
                    to = move(x, core, z, y)
                    if to is not None:
                        rank = lambda a, b, c, d: (a * CORES + b) * N_OWN + c * Y_SIZE + d
                        out.append((rank(x, core, z, y), rank(*to)))
    return out


SWAP_X = pairs(lambda x, c, z, y: (1 - x, c, z, y))
SWAP_CORE = pairs(lambda x, c, z, y: (x, 1 - c, z, y))
SWAP_Y = pairs(lambda x, c, z, y: (x, c, z, 1 - y))
SWAP_Z1 = pairs(lambda x, c, z, y: (x, c, z ^ 1, y))
SWAP_Z2 = pairs(lambda x, c, z, y: (x, c, z ^ 2, y))


def shift(value, perm):
    return lax.ppermute(value, AXES, perm)


def sum_clips(value):
    for perm in (SWAP_Y, SWAP_Z1, SWAP_Z2):
        value = value + shift(value, perm)
    return value


def sum_frames(value):
    for perm in (SWAP_CORE, SWAP_X):
        value = value + shift(value, perm)
    return value


def shard_segments(matrices, n_rows):
    spans, offset = [], 0
    for name, rows, wide in matrices:
        spans.append((name, offset, rows, wide))
        offset += rows * wide
    out = []
    for owner in range(N_OWN):
        low, high = owner * n_rows, (owner + 1) * n_rows
        mine = []
        for name, start, rows, wide in spans:
            begin, end = max(low, start), min(high, start + rows * wide)
            if begin < end:
                mine.append((name, (begin - start) // wide, (end - begin) // wide, wide))
        out.append(mine)
    return out


ATTEND = [
    ("space_qkv", D, 3),
    ("space_out", D, 1),
    ("time_qkv", D, 3),
    ("time_out", D, 1),
    ("cross_q", D, 1),
    ("cross_kv", D, 2),
    ("cross_out", D, 1),
]
DENSE = [("fc_in", D, 4), ("fc_out", MLP, 1)]
ATTEND_ROWS = 13824 // N_OWN
DENSE_ROWS = 9216 // N_OWN
ATTEND_SEGS = shard_segments(ATTEND, ATTEND_ROWS)
DENSE_SEGS = shard_segments(DENSE, DENSE_ROWS)


def cast_table(segments, block):
    out = []
    for mine in segments:
        rows, offset = [], 0
        for name, first, count, wide in mine:
            for start in range(0, count * wide, block):
                rows.append((wide, offset + start // wide, count))
            offset += count * wide
        out.append(rows)
    return np.array(out, np.int32)


def step_table(segments, block, n_rows):
    out = []
    for mine in segments:
        rows, offset = [], 0
        for name, first, count, wide in mine:
            half = count // 2
            for start in range(0, count * wide, block):
                core, inner = divmod(start // wide, half)
                rows.append((wide, core * (n_rows // 2) + offset + inner, half))
            offset += half * wide
        out.append(rows)
    return np.array(out, np.int32)


CAST_BLOCK = 576
STEP_BLOCK = 288


def cast_kernel(widths, table, flat, out):
    block = pl.program_id(0)
    for wide in widths:
        count = CAST_BLOCK // wide

        @pl.when(table[block, 0] == wide)
        def _():
            for slab in range(wide):
                row = pl.multiple_of(table[block, 1] + slab * table[block, 2], 16)
                for tile in range(LANE_TILES):
                    piece = flat[pl.ds(LANE_TILES * slab + tile, count, stride=LANE_TILES * wide), :]
                    out[pl.ds(row, count), tile * LANES : (tile + 1) * LANES] = piece.astype(jnp.bfloat16)


def cast_shard(flat, table, widths, n_rows):
    units = CAST_BLOCK * LANE_TILES
    return pl.pallas_call(
        partial(cast_kernel, widths),
        grid_spec=pltpu.PrefetchScalarGridSpec(
            num_scalar_prefetch=1,
            grid=(n_rows // CAST_BLOCK,),
            in_specs=[pl.BlockSpec((units, LANES), lambda b, t: (b, 0))],
            out_specs=pl.BlockSpec((n_rows, D), lambda b, t: (0, 0)),
        ),
        out_shape=jax.ShapeDtypeStruct((n_rows, D), jnp.bfloat16),
        compiler_params=pltpu.CompilerParams(vmem_limit_bytes=40 * 1024 * 1024),
    )(table, flat.reshape(-1, LANES))


ROWS_AHEAD = 16


def rows_kernel(shift_ref, flat, out, held, sem):
    units, count = flat.shape[0], out.shape[0]
    block = pl.program_id(0)

    @pl.when(block == 0)
    def _():
        end = (ROWS_AHEAD + units) // 8 * 8
        held[pl.ds(0, ROWS_AHEAD), :] = jnp.zeros((ROWS_AHEAD, LANES), jnp.float32)
        held[pl.ds(end, held.shape[0] - end), :] = jnp.zeros((held.shape[0] - end, LANES), jnp.float32)
        copy = pltpu.make_async_copy(flat, held.at[pl.ds(ROWS_AHEAD, units)], sem)
        copy.start()
        copy.wait()

    begin = ROWS_AHEAD + block * (count * LANE_TILES) - shift_ref[0]
    for tile in range(LANE_TILES):
        piece = held[pl.ds(begin + tile, count, stride=LANE_TILES), :]
        out[:, tile * LANES : (tile + 1) * LANES] = piece.astype(out.dtype)


def flat_to_rows(flat, rows, shift, dtype):
    block = rows // 6
    return pl.pallas_call(
        rows_kernel,
        grid_spec=pltpu.PrefetchScalarGridSpec(
            num_scalar_prefetch=1,
            grid=(6,),
            in_specs=[pl.BlockSpec(memory_space=pl.ANY)],
            out_specs=pl.BlockSpec((block, D), lambda b, t: (b, 0)),
            scratch_shapes=[
                pltpu.VMEM((ROWS_AHEAD + rows * LANE_TILES + 8, LANES), jnp.float32),
                pltpu.SemaphoreType.DMA,
            ],
        ),
        out_shape=jax.ShapeDtypeStruct((rows, D), dtype),
        compiler_params=pltpu.CompilerParams(vmem_limit_bytes=32 * 1024 * 1024),
    )(shift.reshape(1), flat)


def flat_kernel(rows, out):
    count = rows.shape[0]
    for tile in range(LANE_TILES):
        out[pl.ds(tile, count, stride=LANE_TILES), :] = rows[:, tile * LANES : (tile + 1) * LANES]


def rows_to_flat(rows):
    block = rows.shape[0] // 6
    return pl.pallas_call(
        flat_kernel,
        grid=(6,),
        in_specs=[pl.BlockSpec((block, D), lambda b: (b, 0))],
        out_specs=pl.BlockSpec((block * LANE_TILES, LANES), lambda b: (b, 0)),
        out_shape=jax.ShapeDtypeStruct((rows.shape[0] * LANE_TILES, LANES), rows.dtype),
        compiler_params=pltpu.CompilerParams(vmem_limit_bytes=32 * 1024 * 1024),
    )(rows)


def ring_place(clip):
    return jnp.where(clip % 2 == 0, clip // 2, N_OWN - 1 - clip // 2)


def clip_at(place):
    return jnp.where(place < N_OWN // 2, 2 * place, 2 * N_OWN - 1 - 2 * place)


def partners(frame, clip):
    place = ring_place(clip)
    x, core = frame // CORES, frame % CORES
    return (
        {"clip": clip_at((place + 1) % N_OWN)},
        {"clip": clip_at((place + N_OWN - 1) % N_OWN)},
        {"frame": (1 - x) * CORES + core},
        {"frame": x * CORES + 1 - core},
    )


def greet(devices):
    barrier = pltpu.get_barrier_semaphore()
    for device in devices:
        pl.semaphore_signal(barrier, inc=1, device_id=device, device_id_type=pl.DeviceIdType.MESH)
    pl.semaphore_wait(barrier, len(devices))


def spread_kernel(groups, modes, *refs):
    n, m = len(groups), len(modes)
    counts = [len(shapes) for keep, shapes, stores, common in groups]
    refs = list(refs)
    take = lambda number: [refs.pop(0) for _ in range(number)]
    owns, given, outs, given_outs = take(n), take(m), take(sum(counts)), take(m)
    helds, sources, landings = take(n), take(m), take(m)
    load_sem, send_sem, recv_sem, out_sem, peer_sem, peer_send, peer_recv = refs
    frame, clip = lax.axis_index("frame"), lax.axis_index("clip")
    x, core = frame // CORES, frame % CORES
    place = ring_place(clip)
    right, left, over_x, other = partners(frame, clip)
    half = N_OWN // 2
    owners = [clip_at((place + N_OWN - k) % N_OWN) for k in range(half + 1)]
    owners += [clip_at((place + k) % N_OWN) for k in range(1, half)]
    flip_x = (1 - x) * CORES + core
    mine = [core, frame, flip_x]
    theirs = [1 - core, x * CORES + 1 - core, (1 - x) * CORES + 1 - core]
    landing = mine + theirs

    def block_of(group, kinds, kind):
        return kinds[kind] + (2 if groups[group][3] and kind % 3 else 0)

    z, y = clip // Y_SIZE, clip % Y_SIZE
    below, above = {"clip": clip - Y_SIZE}, {"clip": clip + Y_SIZE}
    across = {"clip": clip + 1 - 2 * y}
    rings = [group for group in range(n) if len(groups[group][0]) == N_OWN]
    falls = [group for group in range(n) if group not in rings]
    first_z = Z_SIZE - 2

    def held_at(group, slot):
        if group in rings:
            return helds[group].at[owners[slot]]
        return helds[group].at[slot % 2 * Y_SIZE + (y if slot < 2 else 1 - y)]

    def is_own(slot):
        return z == first_z + slot

    def load(group):
        to = held_at(group, 0) if group in rings else helds[group].at[(z - first_z) * Y_SIZE + y]
        return pltpu.make_async_copy(owns[group], to, load_sem.at[group])

    def loading(group, action):
        if group in rings:
            action(load(group))
        else:
            pl.when(z >= first_z)(lambda: action(load(group)))

    def copy_of(group, slot, block, device, to_slot, kind, sender=None):
        row, column = (to_slot, kind) if sender is None else sender
        return pltpu.make_async_remote_copy(
            src_ref=held_at(group, slot).at[block],
            dst_ref=held_at(group, slot).at[block],
            send_sem=send_sem.at[group, row, column],
            recv_sem=recv_sem.at[group, to_slot, kind],
            device_id=device,
            device_id_type=pl.DeviceIdType.MESH,
        )

    sent = []

    def send(group, slot, from_kind, device, to_slot, kind):
        if from_kind == 0 and not groups[group][3]:
            return
        args = (group, slot, block_of(group, mine, from_kind), device, to_slot, kind)
        copy_of(*args).start()
        sent.append(args)

    def arrive(group, slot, kind):
        if kind % 3 == 0 and not groups[group][3]:
            return
        block = block_of(group, landing, kind)
        copy_of(group, slot, block, other, slot, kind).wait_recv()

    def onward(group, slot, kind):
        if slot < half:
            send(group, slot, kind, right, slot + 1, kind)
        if slot == 0:
            send(group, slot, kind, left, half + 1, kind)
        elif half < slot < N_OWN - 1:
            send(group, slot, kind, left, slot + 1, kind)

    def peer_load(item):
        return pltpu.make_async_copy(given[item], sources[item], peer_sem.at[item, 0])

    def peer_own(item):
        source = sources[item].at[clip] if modes[item] == "swap" else sources[item]
        return pltpu.make_async_copy(source, landings[item].at[clip], peer_sem.at[item, 1])

    def peer_copy(item, k):
        to = (clip + k) % N_OWN
        return pltpu.make_async_remote_copy(
            src_ref=sources[item].at[to] if modes[item] == "swap" else sources[item],
            dst_ref=landings[item].at[clip],
            send_sem=peer_send.at[item, k - 1],
            recv_sem=peer_recv.at[item, k - 1],
            device_id={"clip": to},
            device_id_type=pl.DeviceIdType.MESH,
        )

    def peers(item, arriving, action):
        for k in range(1, N_OWN):
            if modes[item] == "gather":
                action(k)
            elif modes[item] == "first":
                pl.when(clip == (k if arriving else 0))(lambda: action(k))
            else:
                to = clip if arriving else (clip + k) % N_OWN
                pl.when(to >= N_OWN // 2)(lambda: action(k))

    fallen = []

    def run(chosen, action):
        action() if chosen is None else pl.when(chosen)(action)

    def fall(group, slot, kind, device, to_slot, to_kind, sender, chosen):
        args = (group, slot, block_of(group, mine, kind), device, to_slot, to_kind, sender)
        run(chosen, lambda: copy_of(*args).start())
        fallen.append((args, chosen))

    def fall_on(group, slot, kind, chosen):
        going_down = (z >= 1) & (z <= first_z + slot) & chosen
        fall(group, slot, kind, below, slot, kind, (slot, kind), going_down)
        if slot == 0:
            fall(group, slot, kind, above, slot, kind, (4, 3 + kind), is_own(slot) & chosen)
        fall(group, slot, kind, across, slot + 2, kind, (4 + slot, kind), chosen)

    def fall_beside(group, slot, kind, chosen):
        if kind == 1:
            fall(group, slot, 1, over_x, slot, 2, (slot, 2), chosen)
        fall(group, slot, kind, other, slot, 3 + kind, (slot, 3 + kind), chosen)

    def fall_arrive(group, slot, kind, chosen):
        run(chosen, lambda: arrive(group, slot, kind))

    def not_own(slot):
        return None if slot >= 2 else z != first_z + slot

    def fall_start():
        for group in falls:
            for slot in (1, 0):
                for kind in (1, 0):
                    fall_on(group, slot, kind, is_own(slot))

    def fall_phase(phase):
        turns = {
            1: [(0, (z > 0) & not_own(0))],
            2: [(0, z == 0), (1, (z > 0) & not_own(1))],
            3: [(1, z == 0), (2, None)],
            4: [(3, None)],
        }[phase]
        for group in falls:
            for slot, chosen in turns:
                for kind in (1, 0):
                    fall_arrive(group, slot, kind, chosen)
                    if slot < 2:
                        fall_on(group, slot, kind, chosen)
                    fall_beside(group, slot, kind, chosen)
            if phase == half:
                for slot in range(4):
                    fall_arrive(group, slot, 2, not_own(slot))
                    fall_beside(group, slot, 2, not_own(slot))

    for group in range(n):
        loading(group, lambda copy: copy.start())
    for item in range(m):
        peer_load(item).start()
    everyone = tuple({"clip": (clip + k) % N_OWN} for k in range(1, N_OWN)) if m else ()
    greet((right, left, over_x, other) + everyone + ((across,) if falls else ()))
    for group in range(n):
        loading(group, lambda copy: copy.wait())
    fall_start()
    for group in rings:
        onward(group, 0, 1)
        onward(group, 0, 0)
    for item in range(m):
        peer_load(item).wait()
        peer_own(item).start()
        peers(item, False, lambda k: peer_copy(item, k).start())
    waiting = []
    for step in range(1, half + 1):
        slots = [step] + ([half + step] if step < half else [])
        pairs_now = [(group, slot) for group in rings for slot in slots]
        for group, slot in pairs_now:
            arrive(group, slot, 1)
            onward(group, slot, 1)
            send(group, slot, 1, over_x, slot, 2)
            send(group, slot, 1, other, slot, 4)
            arrive(group, slot, 0)
            onward(group, slot, 0)
            send(group, slot, 0, other, slot, 3)
        for group, slot in waiting:
            arrive(group, slot, 2)
            send(group, slot, 2, other, slot, 5)
        fall_phase(step)
        waiting = pairs_now
    for group, slot in waiting:
        arrive(group, slot, 2)
        send(group, slot, 2, other, slot, 5)
    for group in rings:
        for slot in range(1, N_OWN):
            for kind in (3, 4, 5):
                arrive(group, slot, kind)
    for group in falls:
        for slot in range(4):
            for kind in (3, 4, 5):
                fall_arrive(group, slot, kind, not_own(slot))
    done, base = [], 0
    for group, (keep, shapes, stores, common) in enumerate(groups):
        held = helds[group]
        rows = held.shape[2]
        for out, row, column, owner, first, count in stores:
            while count > 0:
                part, inner = divmod(first, rows)
                some = min(count, rows - inner)
                copy = pltpu.make_async_copy(
                    held.at[owner - min(keep), part, pl.ds(inner, some)],
                    outs[base + out].at[pl.ds(row, some), pl.ds(column, D)],
                    out_sem.at[len(done)],
                )
                copy.start()
                done.append(copy)
                first, row, count = first + some, row + some, count - some
        base += counts[group]
    for item in range(m):
        peer_own(item).wait()
        peers(item, True, lambda k: peer_copy(item, k).wait_recv())
        copy = pltpu.make_async_copy(landings[item], given_outs[item], peer_sem.at[item, 2])
        copy.start()
        done.append(copy)
    for item in range(m):
        peers(item, False, lambda k: peer_copy(item, k).wait_send())
    for args in sent:
        copy_of(*args).wait_send()
    for args, chosen in fallen:
        run(chosen, lambda: copy_of(*args).wait_send())
    for copy in done:
        copy.wait()


def spread_shards(owns, groups, collective, given=()):
    spec = pl.BlockSpec(memory_space=pl.ANY)
    shapes = [shape for keep, some, stores, common in groups for shape in some]
    n_stores = sum(6 * len(stores) for keep, some, stores, common in groups)
    blocks = [6 if group[3] else 4 for group in groups]
    modes = [mode for value, mode in given]
    values = [value for value, mode in given]
    landed = [
        value.shape if mode == "swap" else (N_OWN,) + value.shape for value, mode in given
    ]
    many = max(len(given), 1)
    return pl.pallas_call(
        partial(spread_kernel, groups, modes),
        in_specs=[spec] * (len(owns) + len(given)),
        out_specs=[spec] * (len(shapes) + len(given)),
        out_shape=[jax.ShapeDtypeStruct(shape, jnp.bfloat16) for shape in shapes]
        + [jax.ShapeDtypeStruct(shape, value.dtype) for shape, value in zip(landed, values)],
        scratch_shapes=[
            pltpu.VMEM((len(group[0]), count, own.shape[0] // count, D), jnp.bfloat16)
            for own, group, count in zip(owns, groups, blocks)
        ]
        + [pltpu.VMEM(value.shape, value.dtype) for value in values]
        + [pltpu.VMEM(shape, value.dtype) for shape, value in zip(landed, values)]
        + [
            pltpu.SemaphoreType.DMA((len(owns),)),
            pltpu.SemaphoreType.DMA((len(owns), N_OWN, 6)),
            pltpu.SemaphoreType.DMA((len(owns), N_OWN, 6)),
            pltpu.SemaphoreType.DMA((n_stores,)),
            pltpu.SemaphoreType.DMA((many, 3)),
            pltpu.SemaphoreType.DMA((many, N_OWN - 1)),
            pltpu.SemaphoreType.DMA((many, N_OWN - 1)),
        ],
        compiler_params=pltpu.CompilerParams(
            collective_id=collective, has_side_effects=True, vmem_limit_bytes=50 * 1024 * 1024
        ),
        cost_estimate=pl.CostEstimate(
            flops=0, bytes_accessed=200 * 1000 * 1000, transcendentals=0
        ),
    )(*[own.reshape(count, own.shape[0] // count, D) for own, count in zip(owns, blocks)], *values)


LAG = 4


def collect_kernel(first, last, chunks, small, part, out, small_out, part_out, scratch):
    bufs, extra, locals_, finals, result = scratch[:2], scratch[2], scratch[3:5], scratch[5:7], scratch[7]
    ring_send, ring_recv, x_send, x_recv, end_send, end_recv, load_sem, own_sem = scratch[8:16]
    if small is not None:
        sums, arrived, small_send, small_recv = scratch[16:]
    if part is not None:
        frames, part_send, part_recv = scratch[16:]
    frame, clip = lax.axis_index("frame"), lax.axis_index("clip")
    x, core = frame // CORES, frame % CORES
    place = ring_place(clip)
    right, left, over_x, other = partners(frame, clip)
    swaps = [
        other,
        over_x,
        {"clip": clip + 1 - 2 * (clip % 2)},
        {"clip": clip + 2 - 4 * (clip // 2 % 2)},
        {"clip": clip + 4 - 8 * (clip // 4)},
    ]
    greet((right, left) + (tuple(swaps) if small is not None else (over_x, other)))
    f, l = first // 2, last // 2
    toward = (right, left)

    def owner(way, step):
        moved = N_OWN - 1 - step if way == 0 else 1 + step
        return clip_at((place + moved) % N_OWN)

    def f_rows(side, way):
        return pl.ds(pl.multiple_of(side * first + way * f, 8), f)

    def l_rows(way):
        return pl.ds(2 * first + way * l, l)

    def remote(src, dst, send_sem, recv_sem, device):
        return pltpu.make_async_remote_copy(
            src_ref=src,
            dst_ref=dst,
            send_sem=send_sem,
            recv_sem=recv_sem,
            device_id=device,
            device_id_type=pl.DeviceIdType.MESH,
        )

    def x_copy(way, step):
        return remote(
            chunks.at[owner(way, step), f_rows(1 - x, way)],
            extra.at[way, step],
            x_send.at[way, step],
            x_recv.at[way, step],
            over_x,
        )

    def load(kind, way, step):
        to = bufs[kind].at[way, 0] if step == 0 else locals_[kind].at[way, step % 2]
        rows = l_rows(way) if kind == 0 else f_rows(x, way)
        return pltpu.make_async_copy(
            chunks.at[owner(way, step), rows], to, load_sem.at[kind, way, step % 2]
        )

    def ring_copy(kind, way, step):
        return remote(
            bufs[kind].at[way, step],
            bufs[kind].at[way, step + 1],
            ring_send.at[kind, way, step],
            ring_recv.at[kind, way, step],
            toward[way],
        )

    def final_copy(kind, way):
        return remote(
            bufs[kind].at[way, N_OWN - 1],
            finals[kind].at[way],
            end_send.at[kind, way],
            end_recv.at[kind, way],
            over_x,
        )

    def small_copy(stage):
        return remote(
            sums.at[stage], arrived.at[stage], small_send.at[stage], small_recv.at[stage], swaps[stage]
        )

    flip_x = (1 - x) * CORES + core

    def part_copy(number, block=None):
        block = (frame, frame, flip_x)[number] if block is None else block
        return remote(
            frames.at[block],
            frames.at[block],
            part_send.at[number],
            part_recv.at[number],
            (over_x, other, other)[number],
        )

    def over_rows(start, count, work):
        def body(number, carry):
            work(pl.multiple_of(start + number * 8, 8))
            return carry

        lax.fori_loop(0, count // 8, body, 0)

    def small_load():
        return pltpu.make_async_copy(small, sums.at[0], own_sem.at[7])

    def part_load():
        return pltpu.make_async_copy(part, frames.at[frame], own_sem.at[7])

    for kind in range(2):
        for way in range(2):
            load(kind, way, 0).start()
    for way in range(2):
        x_copy(way, 0).start()
    if small is not None:
        small_load().start()
    if part is not None:
        part_load().start()

    def ring_step(kind, way, step):
        load(kind, way, step).wait()
        if step + 1 < N_OWN:
            load(kind, way, step + 1).start()
        if kind == 1:
            x_copy(way, step).wait_recv()
        if step > 0:
            ring_copy(kind, way, step - 1).wait_recv()
        buf, local = bufs[kind], locals_[kind]

        def add(row):
            at = pl.ds(row, 8)
            total = buf[way, step, at]
            if kind == 1:
                total = total + extra[way, step, at]
            if step > 0:
                total = total + local[way, step % 2, at]
            buf[way, step, at] = total

        if kind == 1 or step > 0:
            over_rows(0, f if kind == 1 else l, add)
        if step + 1 < N_OWN:
            ring_copy(kind, way, step).start()
        else:
            final_copy(kind, way).start()

    def own_half(kind):
        return pl.ds(2 * first, last) if kind == 0 else pl.ds(0, 2 * first)

    def core_swap(kind, to):
        return remote(
            result.at[own_half(kind)],
            out.at[to, own_half(kind)],
            own_sem.at[kind],
            own_sem.at[2 + kind],
            other,
        )

    def own_store(kind):
        return pltpu.make_async_copy(
            result.at[own_half(kind)], out.at[core, own_half(kind)], own_sem.at[4 + kind]
        )

    def finish(kind):
        for way in range(2):
            final_copy(kind, way).wait_recv()
            buf, final = bufs[kind], finals[kind]

            def put(row):
                at = pl.ds(row, 8)
                if kind == 0:
                    to = pl.multiple_of(2 * first + way * l + row, 8)
                    result[pl.ds(to, 8)] = buf[way, N_OWN - 1, at] + final[way, at]
                else:
                    to = pl.multiple_of(x * first + way * f + row, 8)
                    back = pl.multiple_of((1 - x) * first + way * f + row, 8)
                    result[pl.ds(to, 8)] = buf[way, N_OWN - 1, at]
                    result[pl.ds(back, 8)] = final[way, at]

            over_rows(0, l if kind == 0 else f, put)
        core_swap(kind, core).start()
        own_store(kind).start()

    for tick in range(N_OWN + LAG):
        if small is not None and tick < len(swaps) + 1:
            if tick == 0:
                small_load().wait()
            else:
                small_copy(tick - 1).wait_recv()

                def add_small(row):
                    at = pl.ds(row, 8)
                    sums[tick, at] = sums[tick - 1, at] + arrived[tick - 1, at]

                over_rows(0, small.shape[0], add_small)
            if tick < len(swaps):
                small_copy(tick).start()
        if 0 < tick < N_OWN:
            for way in range(2):
                x_copy(way, tick).start()
        if part is not None and tick == N_OWN - 1:
            part_load().wait()
            part_copy(0).start()
            part_copy(1).start()
        for way in range(2):
            if tick < N_OWN:
                ring_step(0, way, tick)
            if tick >= LAG:
                ring_step(1, way, tick - LAG)
    if small is not None:
        small_store = pltpu.make_async_copy(sums.at[len(swaps)], small_out, own_sem.at[6])
        small_store.start()
    finish(0)
    if part is not None:
        part_copy(0, flip_x).wait_recv()
        part_copy(2).start()
    finish(1)
    if part is not None:
        part_copy(1, x * CORES + 1 - core).wait_recv()
        part_copy(2, (1 - x) * CORES + 1 - core).wait_recv()
        part_store = pltpu.make_async_copy(frames, part_out, own_sem.at[6])
        part_store.start()
        part_store.wait()
        for number in range(3):
            part_copy(number).wait_send()
    if small is not None:
        small_store.wait()
        for stage in range(len(swaps)):
            small_copy(stage).wait_send()
    for way in range(2):
        for step in range(N_OWN):
            x_copy(way, step).wait_send()
    for kind in range(2):
        for way in range(2):
            for step in range(N_OWN - 1):
                ring_copy(kind, way, step).wait_send()
            final_copy(kind, way).wait_send()
        core_swap(kind, 1 - core).wait_recv()
        core_swap(kind, core).wait_send()
        own_store(kind).wait()


def collect_shard(chunks, first, collective, small=None, part=None):
    rows = chunks.shape[1]
    last = rows - 2 * first
    spec = pl.BlockSpec(memory_space=pl.ANY)
    out_shape = [jax.ShapeDtypeStruct((2, rows, D), jnp.float32)]
    beside = small if part is None else part
    if part is None:
        out_shape.append(jax.ShapeDtypeStruct(small.shape, jnp.float32))
        more = [
            pltpu.VMEM((6,) + small.shape, jnp.float32),
            pltpu.VMEM((5,) + small.shape, jnp.float32),
            pltpu.SemaphoreType.DMA((5,)),
            pltpu.SemaphoreType.DMA((5,)),
        ]
    else:
        out_shape.append(jax.ShapeDtypeStruct((4,) + part.shape, jnp.float32))
        more = [
            pltpu.VMEM((4,) + part.shape, jnp.float32),
            pltpu.SemaphoreType.DMA((3,)),
            pltpu.SemaphoreType.DMA((3,)),
        ]

    def kernel(chunks, beside, out, beside_out, *scratch):
        if part is None:
            collect_kernel(first, last, chunks, beside, None, out, beside_out, None, scratch)
        else:
            collect_kernel(first, last, chunks, None, beside, out, None, beside_out, scratch)

    return pl.pallas_call(
        kernel,
        in_specs=[spec] * 2,
        out_specs=[spec] * 2,
        out_shape=out_shape,
        scratch_shapes=[
            pltpu.VMEM((2, N_OWN, last // 2, D), jnp.float32),
            pltpu.VMEM((2, N_OWN, first // 2, D), jnp.float32),
            pltpu.VMEM((2, N_OWN, first // 2, D), jnp.float32),
            pltpu.VMEM((2, 2, last // 2, D), jnp.float32),
            pltpu.VMEM((2, 2, first // 2, D), jnp.float32),
            pltpu.VMEM((2, last // 2, D), jnp.float32),
            pltpu.VMEM((2, first // 2, D), jnp.float32),
            pltpu.VMEM((rows, D), jnp.float32),
            pltpu.SemaphoreType.DMA((2, 2, N_OWN)),
            pltpu.SemaphoreType.DMA((2, 2, N_OWN)),
            pltpu.SemaphoreType.DMA((2, N_OWN)),
            pltpu.SemaphoreType.DMA((2, N_OWN)),
            pltpu.SemaphoreType.DMA((2, 2)),
            pltpu.SemaphoreType.DMA((2, 2)),
            pltpu.SemaphoreType.DMA((2, 2, 2)),
            pltpu.SemaphoreType.DMA((8,)),
        ]
        + more,
        compiler_params=pltpu.CompilerParams(
            collective_id=collective, has_side_effects=True, vmem_limit_bytes=58 * 1024 * 1024
        ),
        cost_estimate=pl.CostEstimate(
            flops=0, bytes_accessed=800 * 1000 * 1000, transcendentals=0
        ),
    )(chunks, beside)


def matrix_plan(matrices, segments):
    shapes = [(rows, wide * D) for name, rows, wide in matrices]
    names = [name for name, rows, wide in matrices]
    stores = []
    for owner in range(N_OWN):
        offset = 0
        for name, first, count, wide in segments[owner]:
            for j in range(wide):
                stores.append((names.index(name), first, j * D, owner, offset, count))
                offset += count
    return shapes, stores


GRAD_COLUMNS = 384


def grad_plan(matrices, segments, lefts, rights):
    squares = {}
    for owner in range(N_OWN):
        row = 0
        for name, first, count, wide in segments[owner]:
            for j in range(wide):
                block, inner = divmod(first, D)
                piece = (inner, count // 2, owner, row)
                squares.setdefault((name, block, j), []).append(piece)
                row += count // 2
    plan = []
    for name, rows, wide in matrices:
        for block in range(rows // D):
            for j in range(wide):
                right, column = rights[name][j]
                plan.append((lefts[name], block * D, right, column, squares[name, block, j]))
    return plan


def grad_kernel(plan, parts, n_left, core_ref, *refs):
    n_in = sum(parts)
    ins, out = refs[:n_in], refs[n_in]
    left_buf, right_buf, made, left_sem, right_sem, out_sem = refs[n_in + 1 :]
    core = core_ref[0]
    place = [sum(parts[:k]) for k in range(len(parts))]

    def left_copies(square, slot):
        left, row = square[:2]
        return [
            pltpu.make_async_copy(
                ins[place[left] + part].at[pl.ds(row, D)],
                left_buf.at[slot, part, :, pl.ds(0, ins[place[left]].shape[1])],
                left_sem.at[slot, part],
            )
            for part in range(parts[left])
        ]

    def right_copies(square, slot):
        right, column = n_left + square[2], square[3]
        return [
            pltpu.make_async_copy(
                ins[place[right] + part].at[:, pl.ds(column, D)],
                right_buf.at[slot, part, pl.ds(0, ins[place[right]].shape[0])],
                right_sem.at[slot, part],
            )
            for part in range(parts[right])
        ]

    def out_copies(number):
        row, copies = 0, []
        for k, (first, count, owner, to) in enumerate(plan[number][4]):
            copies.append(
                pltpu.make_async_copy(
                    made.at[number % 2, pl.ds(row, count)],
                    out.at[owner, pl.ds(to, count)],
                    out_sem.at[number % 2, k],
                )
            )
            row += count
        return copies

    slots = []
    for number, square in enumerate(plan):
        if number == 0:
            slots.append((0, True, 0, True))
            continue
        left, _, right, _ = slots[-1]
        new_left = square[:2] != plan[number - 1][:2]
        new_right = square[2:4] != plan[number - 1][2:4]
        slots.append((left ^ new_left, new_left, right ^ new_right, new_right))

    def operands(number):
        left, new_left, right, new_right = slots[number]
        copies = left_copies(plan[number], left) if new_left else []
        return copies + (right_copies(plan[number], right) if new_right else [])

    for copy in operands(0):
        copy.start()
    for number, square in enumerate(plan):
        for copy in operands(number):
            copy.wait()
        if number + 1 < len(plan):
            for copy in operands(number + 1):
                copy.start()
        if number >= 2:
            for copy in out_copies(number - 2):
                copy.wait()
        left, _, right, _ = slots[number]
        depth = ins[place[square[0]]].shape[1]

        def some_columns(step, carry):
            columns = pl.ds(pl.multiple_of(step * GRAD_COLUMNS, LANES), GRAD_COLUMNS)
            row = 0
            for first, count, owner, to in square[4]:
                rows = pl.ds(pl.multiple_of(first + core * count, 16), count)
                total = 0.0
                for part in range(parts[square[0]]):
                    total = total + jnp.dot(
                        left_buf[left, part, rows, :depth],
                        right_buf[right, part, :depth, columns],
                        preferred_element_type=jnp.float32,
                    )
                made[number % 2, row : row + count, columns] = total
                row += count
            return carry

        lax.fori_loop(0, D // GRAD_COLUMNS, some_columns, 0)
        for copy in out_copies(number):
            copy.start()
    for number in range(max(len(plan) - 2, 0), len(plan)):
        for copy in out_copies(number):
            copy.wait()


def core_chunks(plan, core, lefts, rights, n_rows):
    operands = list(lefts) + list(rights)
    parts = [len(arrays) for arrays in operands]
    tokens = max(arrays[0].shape[1] for arrays in lefts)
    spec = pl.BlockSpec(memory_space=pl.ANY)
    return pl.pallas_call(
        partial(grad_kernel, plan, parts, len(lefts)),
        in_specs=[pl.BlockSpec(memory_space=pltpu.SMEM)] + [spec] * sum(parts),
        out_specs=spec,
        out_shape=jax.ShapeDtypeStruct((N_OWN, n_rows // 2, D), jnp.float32),
        scratch_shapes=[
            pltpu.VMEM((2, 2, D, tokens), jnp.bfloat16),
            pltpu.VMEM((2, 2, tokens, D), jnp.bfloat16),
            pltpu.VMEM((2, D // 2, D), jnp.float32),
            pltpu.SemaphoreType.DMA((2, 2)),
            pltpu.SemaphoreType.DMA((2, 2)),
            pltpu.SemaphoreType.DMA((2, N_OWN)),
        ],
        compiler_params=pltpu.CompilerParams(vmem_limit_bytes=36 * 1024 * 1024),
    )(core.astype(jnp.int32).reshape(1), *[array for arrays in operands for array in arrays])


def step_values(master, grad, first, second, average):
    keep = min(AVERAGE_KEEP, (1.0 + STEP) / (10.0 + STEP))
    first = BETA_FIRST * first + (1.0 - BETA_FIRST) * grad
    second = BETA_SECOND * second + (1.0 - BETA_SECOND) * grad * grad
    moved = (
        first
        / (1.0 - BETA_FIRST**STEP)
        / (jnp.sqrt(second / (1.0 - BETA_SECOND**STEP)) + ADAM_FLOOR)
    )
    master = master - LEARN_RATE * (moved + WEIGHT_DECAY * master)
    return (master, first, second, keep * average + (1.0 - keep) * master)


STEP_ROWS = 144


def step_kernel(widths, table, factor, grad, *refs):
    olds, news, (shard, flat, sem) = refs[:4], refs[4:8], refs[8:]
    block = pl.program_id(0)

    @pl.when(block == 0)
    def _():
        copy = pltpu.make_async_copy(grad, shard, sem)
        copy.start()
        copy.wait()

    for wide in widths:
        count = STEP_BLOCK // wide

        @pl.when(table[block, 0] == wide)
        def _():
            for slab in range(wide):
                row = pl.multiple_of(table[block, 1] + slab * table[block, 2], 8)
                for tile in range(LANE_TILES):
                    flat[pl.ds(LANE_TILES * slab + tile, count, stride=LANE_TILES * wide), :] = shard[
                        pl.ds(row, count), tile * LANES : (tile + 1) * LANES
                    ]

    scale = factor[0]

    def some_rows(number, carry):
        at = pl.ds(pl.multiple_of(number * STEP_ROWS, 8), STEP_ROWS)
        old = [ref[at, :] for ref in olds]
        made = step_values(old[0], flat[at, :] * scale, old[1], old[2], old[3])
        for ref, value in zip(news, made):
            ref[at, :] = value
        return carry

    lax.fori_loop(0, STEP_BLOCK * LANE_TILES // STEP_ROWS, some_rows, 0)


def step_shard(grad, table, widths, n_rows, factor, olds):
    units = STEP_BLOCK * LANE_TILES
    block_spec = pl.BlockSpec((units, LANES), lambda b, t, f: (b, 0))
    flat_shape = jax.ShapeDtypeStruct((n_rows * LANE_TILES, LANES), jnp.float32)
    made = pl.pallas_call(
        partial(step_kernel, widths),
        grid_spec=pltpu.PrefetchScalarGridSpec(
            num_scalar_prefetch=2,
            grid=(n_rows // STEP_BLOCK,),
            in_specs=[pl.BlockSpec(memory_space=pl.ANY)] + [block_spec] * 4,
            out_specs=[block_spec] * 4,
            scratch_shapes=[
                pltpu.VMEM((n_rows, D), jnp.float32),
                pltpu.VMEM((units, LANES), jnp.float32),
                pltpu.SemaphoreType.DMA,
            ],
        ),
        out_shape=[flat_shape] * 4,
        compiler_params=pltpu.CompilerParams(vmem_limit_bytes=50 * 1024 * 1024),
    )(table, factor, grad, *[old.reshape(-1, LANES) for old in olds])
    return [value.reshape(-1) for value in made]


def head_span(head):
    width = D // HEADS
    start = head * width // LANES * LANES
    stop = -(-(head + 1) * width // LANES) * LANES
    lane = start + lax.broadcasted_iota(jnp.int32, (1, stop - start), 1)
    ones = (lane >= head * width) & (lane < (head + 1) * width)
    return slice(start, stop), ones.astype(jnp.float32).astype(jnp.bfloat16)


def dot_rows(left, right):
    return lax.dot_general(left, right, (((1,), (1,)), ((), ())), preferred_element_type=jnp.float32)


def dot_down(left, right):
    return lax.dot_general(left, right, (((0,), (0,)), ((), ())), preferred_element_type=jnp.float32)


def live_keys(mode, live, n_queries, n_keys):
    key = lax.broadcasted_iota(jnp.int32, (n_queries, n_keys), 1)
    if mode == "cross":
        return key < live[0]
    if mode == "all":
        return None
    query = lax.broadcasted_iota(jnp.int32, (n_queries, n_keys), 0)
    return query // mode == key // mode


def head_scores(queries, keys, valid):
    scores = dot_rows(queries, keys) * (D // HEADS) ** (-0.5)
    return scores if valid is None else jnp.where(valid, scores, MASKED_SCORE)


def heads_kernel(mode, live, queries, keys, values, out, log_total, total):
    n_queries, n_keys = queries.shape[0], keys.shape[0]
    valid = live_keys(mode, live, n_queries, n_keys)
    lane = lax.broadcasted_iota(jnp.int32, (1, LANES), 1)
    total[...] = jnp.zeros_like(total)
    log_total[...] = jnp.zeros_like(log_total)
    for head in range(HEADS):
        span, ones = head_span(head)
        scores = head_scores(queries[:, span], keys[:, span] * ones, valid)
        summit = jnp.max(scores, -1, keepdims=True)
        powers = jnp.exp(scores - summit)
        sums = jnp.sum(powers, -1, keepdims=True)
        probs = (powers / sums).astype(jnp.bfloat16)
        total[:, span] += jnp.dot(
            probs, values[:, span] * ones, preferred_element_type=jnp.float32
        )
        log_total[...] += jnp.where(lane == head, summit + jnp.log(sums), 0.0)
    out[...] = total[...].astype(jnp.bfloat16)


def heads_back_kernel(
    mode, live, queries, keys, values, log_total, grad_out, grad_q, grad_k, grad_v, sum_q, sum_k, sum_v
):
    n_queries, n_keys = queries.shape[0], keys.shape[0]
    valid = live_keys(mode, live, n_queries, n_keys)
    scale = (D // HEADS) ** (-0.5)
    block, last = pl.program_id(0), pl.num_programs(0) - 1
    sum_q[...] = jnp.zeros_like(sum_q)

    @pl.when((block == 0) | (mode != "cross"))
    def _():
        sum_k[...] = jnp.zeros_like(sum_k)
        sum_v[...] = jnp.zeros_like(sum_v)

    for head in range(HEADS):
        span, ones = head_span(head)
        some_keys = keys[:, span] * ones
        scores = head_scores(queries[:, span], some_keys, valid)
        probs = jnp.exp(scores - log_total[:, head : head + 1])
        grad_probs = dot_rows(grad_out[:, span], values[:, span] * ones)
        row = jnp.sum(probs * grad_probs, -1, keepdims=True)
        grad_scores = (probs * (grad_probs - row)).astype(jnp.bfloat16)
        sum_q[:, span] += jnp.dot(grad_scores, some_keys, preferred_element_type=jnp.float32)
        sum_k[:, span] += dot_down(grad_scores, queries[:, span] * ones)
        sum_v[:, span] += dot_down(probs.astype(jnp.bfloat16), grad_out[:, span] * ones)
    grad_q[...] = (sum_q[...] * scale).astype(grad_q.dtype)

    @pl.when((block == last) | (mode != "cross"))
    def _():
        grad_k[...] = (sum_k[...] * scale).astype(grad_k.dtype)
        grad_v[...] = sum_v[...].astype(grad_v.dtype)


HEAD_ROWS = 256


def heads_specs(mode, keys):
    own = pl.BlockSpec((HEAD_ROWS, D), lambda b: (b, 0))
    side = pl.BlockSpec((HEAD_ROWS, LANES), lambda b: (b, 0))
    shared = pl.BlockSpec(keys.shape, lambda b: (0, 0)) if mode == "cross" else own
    return own, side, shared


def heads_forward(mode, queries, keys, values, live):
    own, side, shared = heads_specs(mode, keys)
    n_keys = keys.shape[0] if mode == "cross" else HEAD_ROWS
    return pl.pallas_call(
        partial(heads_kernel, mode),
        grid=(queries.shape[0] // HEAD_ROWS,),
        in_specs=[pl.BlockSpec(memory_space=pltpu.SMEM), own, shared, shared],
        out_specs=[own, side],
        out_shape=[
            jax.ShapeDtypeStruct(queries.shape, jnp.bfloat16),
            jax.ShapeDtypeStruct((queries.shape[0], LANES), jnp.float32),
        ],
        scratch_shapes=[pltpu.VMEM((HEAD_ROWS, D), jnp.float32)],
        compiler_params=pltpu.CompilerParams(vmem_limit_bytes=32 * 1024 * 1024),
    )(live, queries, keys, values)


def heads_backward(mode, queries, keys, values, live, log_total, grad_out):
    own, side, shared = heads_specs(mode, keys)
    n_keys = keys.shape[0] if mode == "cross" else HEAD_ROWS
    kind = jnp.float32 if mode == "cross" else jnp.bfloat16
    return pl.pallas_call(
        partial(heads_back_kernel, mode),
        grid=(queries.shape[0] // HEAD_ROWS,),
        in_specs=[pl.BlockSpec(memory_space=pltpu.SMEM), own, shared, shared, side, own],
        out_specs=[own, shared, shared],
        out_shape=[
            jax.ShapeDtypeStruct(queries.shape, jnp.bfloat16),
            jax.ShapeDtypeStruct(keys.shape, kind),
            jax.ShapeDtypeStruct(keys.shape, kind),
        ],
        scratch_shapes=[
            pltpu.VMEM((HEAD_ROWS, D), jnp.float32),
            pltpu.VMEM((n_keys, D), jnp.float32),
            pltpu.VMEM((n_keys, D), jnp.float32),
        ],
        compiler_params=pltpu.CompilerParams(vmem_limit_bytes=40 * 1024 * 1024),
    )(live, queries, keys, values, log_total, grad_out)


ROW_TIME_ONE = PATCH_VALUES
ROW_TIME_TWO = ROW_TIME_ONE + TFREQ
ROW_BLOCK = ROW_TIME_TWO + D
ROW_CAP_ONE = ROW_BLOCK + 6 * D
ROW_CAP_TWO = ROW_CAP_ONE + CAPW
ROW_FINAL = ROW_CAP_TWO + D
ROW_NULL = ROW_FINAL + PATCH_VALUES
EMB_UNITS = 16158720 // LANES // N_OWN
EMB_FIRST = [EMB_UNITS * c // LANE_TILES for c in range(N_OWN)]
EMB_SHIFT = [EMB_UNITS * c % LANE_TILES for c in range(N_OWN)]


def two_parts(product, value):
    both = product(jnp.concatenate(halves(value), 0))
    return both[: value.shape[0]] + both[value.shape[0] :]


def shards_block(
    latents,
    noise,
    timesteps,
    captions,
    cap_lengths,
    null_flags,
    sample_weight,
    embed_w,
    attend_w,
    dense_w,
    vector_w,
    embed_m,
    attend_m,
    dense_m,
    vector_m,
    embed_v,
    attend_v,
    dense_v,
    vector_v,
    embed_e,
    attend_e,
    dense_e,
    vector_e,
):
    clip_dev, frame_dev, patches = (latents.shape[0], latents.shape[1], latents.shape[2])
    n_frame = lax.axis_size("frame")
    n_clip = lax.axis_size("clip")
    local_pos = patches // n_frame
    tokens = frame_dev * patches
    frame_id = lax.axis_index("frame")
    clip_id = lax.axis_index("clip")
    x_id, core_id = frame_id // CORES, frame_id % CORES
    z_id, y_id = clip_id // Y_SIZE, clip_id % Y_SIZE

    emb_first = jnp.asarray(EMB_FIRST, jnp.int32)[clip_id]
    emb_shift = jnp.asarray(EMB_SHIFT, jnp.int32)[clip_id]
    emb_rows = flat_to_rows(embed_w.reshape(-1, LANES), EMB_PAD, emb_shift, jnp.bfloat16)
    dense_cast = cast_shard(
        dense_w, jnp.asarray(cast_table(DENSE_SEGS, CAST_BLOCK))[clip_id], (1, 4), DENSE_ROWS
    )
    cap_owners = range(4, N_OWN)
    cap_plan = (
        [(EMB_PAD * len(cap_owners), D)],
        [(0, EMB_PAD * k, 0, owner, 0, EMB_PAD) for k, owner in enumerate(cap_owners)],
    )
    own_clip = jnp.arange(n_clip) == clip_id
    facts = jnp.stack([timesteps.astype(jnp.float32)[0], sample_weight[0], null_flags.astype(jnp.float32)[0]])
    facts = jnp.broadcast_to(jnp.pad(facts, (0, LANES - 3))[None], (8, LANES))
    cap_weights, fc_in, fc_out, facts = spread_shards(
        [emb_rows, dense_cast],
        [(cap_owners,) + cap_plan + (True,), (range(N_OWN),) + matrix_plan(DENSE, DENSE_SEGS) + (True,)],
        2,
        given=[(facts, "gather")],
    )
    facts = facts[:, 0, :3]
    last = N_OWN - 1
    cap_last = cap_weights[EMB_PAD * (len(cap_owners) - 1) :]
    null_end = 16158720 - ROW_NULL * D
    null_first, final_first = ROW_NULL - EMB_FIRST[last], ROW_FINAL - EMB_FIRST[last]
    null_caption = (
        cap_last[null_first : null_first - (-null_end // D)]
        .reshape(-1)[:null_end]
        .reshape(L_CAP, CAPW)
    )
    final_w = cap_last[final_first : final_first + PATCH_VALUES].reshape(D, PATCH_VALUES)
    two_first = ROW_CAP_TWO - EMB_FIRST[last]

    def to_cap_rows(value):
        padded = jnp.pad(value, ((0, 0), (EMB_PAD, EMB_PAD)))
        starts = [EMB_FIRST[owner] - ROW_CAP_ONE + EMB_PAD for owner in cap_owners]
        return jnp.concatenate([padded[:, start : start + EMB_PAD] for start in starts], 1)

    def from_cap_rows(value):
        total = 0.0
        for k, owner in enumerate(cap_owners):
            start = EMB_FIRST[owner] - ROW_CAP_ONE
            low, high = max(0, -start), min(EMB_PAD, CAPW - start)
            part = value[:, EMB_PAD * k + low : EMB_PAD * k + high]
            total = total + jnp.pad(part, ((0, 0), (start + low, CAPW - start - high)))
        return total

    (
        patch_b,
        time_b1,
        time_b2,
        block_b,
        cap_b1,
        cap_b2,
        space_bq,
        space_bv,
        space_bo,
        time_bq,
        time_bv,
        time_bo,
        cross_bq,
        cross_bv,
        cross_bo,
        fc_in_b,
        fc_out_b,
        final_b,
        table,
        final_table,
    ) = split_flat(vector_w, vector_shapes())

    all_steps, all_null = facts[:, 0], facts[:, 2] == 1.0
    angle = (all_steps / 1000.0 + 0.008) / 1.008 * (math.pi / 2)
    signal = jnp.cos(angle) ** 2
    ratio = signal / (1.0 - signal)
    all_weights = facts[:, 1] * jnp.minimum(ratio, SNR_LIMIT) / ratio
    weight_total = jnp.sum(all_weights)
    signal = lax.dynamic_slice_in_dim(signal, clip_id, 1, 0)
    loss_weight = lax.dynamic_slice_in_dim(all_weights, clip_id, 1, 0)

    freq_in = sincos(all_steps, TFREQ).astype(jnp.bfloat16)
    at_start = clip_id == 0
    time_one = emb_rows[ROW_TIME_ONE:ROW_TIME_TWO]
    time_two = emb_rows[ROW_TIME_TWO:ROW_BLOCK]
    pre_one = matmul_low(freq_in, time_one) + time_b1
    act_one = jax.nn.silu(pre_one).astype(jnp.bfloat16)
    time_embed = matmul_low(act_one, time_two) + time_b2
    early = jnp.concatenate(
        [pre_one, time_embed, emb_rows[:ROW_TIME_ONE].astype(jnp.float32)], 0
    )
    is_null = null_flags == 1
    cap_in = jnp.where(is_null[:, None, None], null_caption[None], captions)
    cap_pre = (matmul_low(to_cap_rows(cap_in[0]), cap_weights) + cap_b1)[None]
    cap_act = gelu_tanh(cap_pre).astype(jnp.bfloat16)
    act_rows = jnp.pad(cap_act[0], ((0, 0), (two_first, EMB_PAD - two_first - D)))
    cap_rows = (matmul_low(act_rows, cap_last) + cap_b2).astype(jnp.bfloat16)[None]
    live_len = jnp.where(is_null, L_CAP, cap_lengths)
    cap_wide = jnp.concatenate([cap_in[0], cap_act[0]], -1)
    cap_wide = jnp.pad(cap_wide, ((0, 0), (EMB_PAD, EMB_PAD)))
    wanted = []
    for owner in range(n_clip):
        start = EMB_FIRST[owner] - ROW_CAP_ONE + EMB_PAD
        if start + EMB_PAD <= EMB_PAD:
            wanted.append(jnp.zeros((L_CAP, EMB_PAD // 4), jnp.bfloat16))
        else:
            wanted.append(
                lax.dynamic_slice_in_dim(cap_wide, start + frame_id * (EMB_PAD // 4), EMB_PAD // 4, 1)
            )
    attend_cast = cast_shard(
        attend_w, jnp.asarray(cast_table(ATTEND_SEGS, CAST_BLOCK))[clip_id], (1, 2, 3), ATTEND_ROWS
    )
    space_qkv, space_out, time_qkv, time_out, cross_q, cross_kv, cross_out, early, cap_left = spread_shards(
        [attend_cast],
        [(range(N_OWN),) + matrix_plan(ATTEND, ATTEND_SEGS) + (True,)],
        1,
        given=[(early, "first"), (jnp.pad(jnp.stack(wanted), ((0, 0), (0, 128 - L_CAP), (0, 0))), "swap")],
    )
    early = early[0]
    cap_left = cap_left[:, :L_CAP].reshape(n_clip * L_CAP, EMB_PAD // 4)
    cap_left = jnp.where(clip_id >= cap_owners[0], cap_left, jnp.zeros_like(cap_left))
    pre_one, time_embed = early[:n_clip], early[n_clip : 2 * n_clip]
    patch_w = early[2 * n_clip :].astype(jnp.bfloat16)
    act_one = jax.nn.silu(pre_one).astype(jnp.bfloat16)
    silu_time = jax.nn.silu(time_embed).astype(jnp.bfloat16)
    local_row = emb_first + jnp.arange(EMB_PAD, dtype=jnp.int32)
    block_row = local_row - ROW_BLOCK
    in_block = (block_row >= 0) & (block_row < 6 * D)
    block_part = jnp.where(in_block, block_row % 6, -1)
    block_line = jnp.where(in_block, block_row // 6, -1)
    chooser = jnp.arange(D, dtype=jnp.int32)[:, None] == block_line[None]
    silu_rows = matmul_low(silu_time, chooser.astype(jnp.bfloat16)).astype(jnp.bfloat16)
    part_mask = jnp.arange(6, dtype=jnp.int32)[:, None] == block_part[None]
    block_left = jnp.where(part_mask[None], silu_rows[:, None], 0).reshape(n_clip * 6, EMB_PAD)
    block_out = sum_clips(matmul_low(block_left, emb_rows)).reshape(n_clip, 6, D)
    all_mods = table[None] + (block_out + block_b.reshape(6, D))
    mods = lax.dynamic_slice_in_dim(all_mods, clip_id, 1, 0)
    my_embed = lax.dynamic_slice_in_dim(time_embed, clip_id, 1, 0)

    keep_part = jnp.sqrt(signal)[:, None, None, None]
    fade_part = jnp.sqrt(1.0 - signal)[:, None, None, None]
    noisy = (keep_part * latents + fade_part * noise).astype(jnp.bfloat16)
    frame_ids = frame_id * frame_dev + jnp.arange(frame_dev)
    patch_ids = jnp.arange(patches)
    place = jnp.concatenate(
        [sincos(patch_ids // PGRID, D // 2), sincos(patch_ids % PGRID, D // 2)], -1
    )[None, None]
    hidden_zero = matmul_low(noisy, patch_w) + patch_b + place + sincos(frame_ids, D)[None, :, None]

    def mod_row(number):
        return mods[:, number][:, None, None, :]

    def flat2(value):
        return value.reshape(-1, value.shape[-1])

    space_in = modulate(hidden_zero, mod_row(0), mod_row(1)).astype(jnp.bfloat16)
    live = live_len.astype(jnp.int32)
    space_q, space_k, space_v = split_qkv(matmul_low(flat2(space_in), space_qkv), space_bq, space_bv)
    space_o, space_lse = heads_forward("all", space_q, space_k, space_v, live)
    space_flat = space_o.reshape(clip_dev, frame_dev, patches, D)
    space_res = matmul_low(space_flat, space_out) + space_bo
    hidden_one = hidden_zero + mod_row(2) * space_res
    time_in = lax.all_to_all(
        hidden_one.astype(jnp.bfloat16), "frame", split_axis=2, concat_axis=1, tiled=True
    )
    time_in = jnp.swapaxes(time_in, 1, 2)
    frames = time_in.shape[2]
    time_q, time_k, time_v = split_qkv(matmul_low(flat2(time_in), time_qkv), time_bq, time_bv)
    time_o, time_lse = heads_forward(frames, time_q, time_k, time_v, live)
    time_back = jnp.swapaxes(time_o.reshape(clip_dev, local_pos, frames, D), 1, 2)
    time_flat = lax.all_to_all(time_back, "frame", split_axis=1, concat_axis=2, tiled=True)
    time_res = matmul_low(time_flat, time_out) + time_bo
    hidden_two = hidden_one + mod_row(2) * time_res
    cross_in = hidden_two.astype(jnp.bfloat16)
    cross_query = (matmul_low(flat2(cross_in), cross_q) + cross_bq).astype(jnp.bfloat16)
    cross_merged = matmul_low(jnp.pad(cap_rows[0], ((0, -L_CAP % 16), (0, 0))), cross_kv)
    cross_k = cross_merged[..., :D].astype(jnp.bfloat16)
    cross_v = (cross_merged[..., D:] + cross_bv).astype(jnp.bfloat16)
    cross_o, cross_lse = heads_forward("cross", cross_query, cross_k, cross_v, live)
    cross_flat = cross_o.reshape(clip_dev, frame_dev, patches, D)
    hidden_three = hidden_two + matmul_low(cross_flat, cross_out) + cross_bo
    dense_in = modulate(hidden_three, mod_row(3), mod_row(4)).astype(jnp.bfloat16)
    dense_pre = matmul_low(dense_in, fc_in) + fc_in_b
    dense_act = gelu_tanh(dense_pre).astype(jnp.bfloat16)
    dense_res = matmul_low(dense_act, fc_out) + fc_out_b
    hidden_four = hidden_three + mod_row(5) * dense_res
    final_mod = final_table[None] + my_embed[:, None, :]
    final_shift = final_mod[:, 0][:, None, None, :]
    final_scale = final_mod[:, 1][:, None, None, :]
    final_in = modulate(hidden_four, final_shift, final_scale).astype(jnp.bfloat16)
    predicted = matmul_low(final_in, final_w) + final_b
    miss = predicted - noise
    clip_error = jnp.sum(jnp.mean(miss * miss, -1), (1, 2))
    local_loss = jnp.sum(loss_weight * clip_error)

    def two_cores(value):
        return [value, shift(value, SWAP_CORE)]

    lefts = {
        label: two_cores(flat2(value).T)
        for label, value in (
            ("space_qkv", space_in),
            ("space_out", space_flat),
            ("time_qkv", time_in),
            ("time_out", time_flat),
            ("cross_q", cross_in),
            ("cross_out", cross_flat),
            ("fc_in", dense_in),
            ("fc_out", dense_act),
        )
    }

    def chunks_of(matrices, segments, rights, n_rows):
        arrays, where = [], {}
        for label, blocks in rights.items():
            where[label] = []
            for value, column in blocks:
                known = [k for k, other in enumerate(arrays) if other is value]
                if not known:
                    arrays.append(value)
                where[label].append((known[0] if known else len(arrays) - 1, column))
        order = {label: number for number, (label, rows, wide) in enumerate(matrices)}
        plan = grad_plan(matrices, segments, order, where)
        return core_chunks(plan, core_id, [lefts[label] for label in order], arrays, n_rows)

    grad_pred = (
        2.0 / miss.shape[-1] * (loss_weight / weight_total)[:, None, None, None] * miss
    ).astype(jnp.bfloat16)
    g_final_w = weight_grad(final_in, grad_pred)
    g_final_b = bias_grad(grad_pred)
    unused, pullback = jax.vjp(modulate, hidden_four, final_shift, final_scale)
    grad_hidden, grad_fshift, grad_fscale = pullback(back_low(grad_pred, final_w))
    grad_fmod = jnp.concatenate([grad_fshift.reshape(1, D), grad_fscale.reshape(1, D)], 0)
    grad_dense = (grad_hidden * mod_row(5)).astype(jnp.bfloat16)
    grad_gate_b = jnp.sum(grad_hidden * dense_res, (1, 2))
    dense_both = two_cores(flat2(grad_dense))
    g_fc_out_b = bias_grad(grad_dense)
    unused, pullback = jax.vjp(gelu_tanh, dense_pre)
    grad_pre = pullback(back_low(grad_dense, fc_out))[0].astype(jnp.bfloat16)
    pre_both = two_cores(flat2(grad_pre))
    dense_chunks = chunks_of(
        DENSE,
        DENSE_SEGS,
        {"fc_in": [(pre_both, j * D) for j in range(MLP // D)], "fc_out": [(dense_both, 0)]},
        DENSE_ROWS,
    )
    rights = {}
    g_fc_in_b = bias_grad(grad_pre)
    unused, pullback = jax.vjp(modulate, hidden_three, mod_row(3), mod_row(4))
    grad_input, grad_shift_b, grad_scale_b = pullback(back_low(grad_pre, fc_in))
    grad_hidden = grad_hidden + grad_input
    grad_cross = grad_hidden.astype(jnp.bfloat16)
    rights["cross_out"] = [(two_cores(flat2(grad_cross)), 0)]
    g_cross_bo = bias_grad(grad_cross)
    grad_cross_o = back_low(flat2(grad_cross), cross_out).astype(jnp.bfloat16)
    grad_cq, grad_ck, grad_cv = heads_backward(
        "cross", cross_query, cross_k, cross_v, live, cross_lse, grad_cross_o
    )
    grad_cq = grad_cq.reshape(clip_dev, frame_dev, patches, D)
    rights["cross_q"] = [(two_cores(flat2(grad_cq)), 0)]
    g_cross_bq = bias_grad(grad_cq)
    grad_hidden = grad_hidden + back_low(grad_cq, cross_q)
    grad_cv = grad_cv[:L_CAP]
    grad_ckv = jnp.concatenate([grad_ck[:L_CAP], grad_cv], -1)
    g_cross_bv = bias_grad(grad_cv)
    grad_ckv = grad_ckv + shift(grad_ckv, SWAP_CORE)
    pad_rows = lambda value: jnp.pad(value, ((0, -L_CAP % LANES), (0, 0)))
    cap_twice = pad_rows(cap_rows[0]).T
    lefts["cross_kv"] = [jnp.concatenate([cap_twice, cap_twice], 1)]
    ckv_parts = [jnp.concatenate([pad_rows(part) for part in halves(grad_ckv)], 0)]
    rights["cross_kv"] = [(ckv_parts, 0), (ckv_parts, D)]
    grad_ckv = grad_ckv + shift(grad_ckv, SWAP_X)
    grad_cap_rows = two_parts(lambda part: back_low(part, cross_kv), grad_ckv)

    grad_time = (grad_hidden * mod_row(2)).astype(jnp.bfloat16)
    rights["time_out"] = [(two_cores(flat2(grad_time)), 0)]
    g_time_bo = bias_grad(grad_time)
    grad_time_o = lax.all_to_all(
        back_low(grad_time, time_out).astype(jnp.bfloat16),
        "frame",
        split_axis=2,
        concat_axis=1,
        tiled=True,
    )
    grad_time_o = flat2(jnp.swapaxes(grad_time_o, 1, 2))
    grad_tqkv = [
        piece.reshape(clip_dev, local_pos, frames, D)
        for piece in heads_backward(frames, time_q, time_k, time_v, live, time_lse, grad_time_o)
    ]
    rights["time_qkv"] = [(two_cores(flat2(part)), 0) for part in grad_tqkv]
    g_time_bq = bias_grad(grad_tqkv[0])
    g_time_bv = bias_grad(grad_tqkv[2])
    grad_tqkv = lax.all_to_all(
        jnp.swapaxes(jnp.concatenate(grad_tqkv, -1), 1, 2), "frame", split_axis=1, concat_axis=2, tiled=True
    )
    grad_gate_a = jnp.sum(grad_hidden * time_res, (1, 2))
    grad_hidden = grad_hidden + back_low(grad_tqkv, time_qkv)
    grad_gate_a = grad_gate_a + jnp.sum(grad_hidden * space_res, (1, 2))
    grad_space = (grad_hidden * mod_row(2)).astype(jnp.bfloat16)
    rights["space_out"] = [(two_cores(flat2(grad_space)), 0)]
    g_space_bo = bias_grad(grad_space)
    grad_space_o = back_low(flat2(grad_space), space_out).astype(jnp.bfloat16)
    grad_sqkv = [
        piece.reshape(clip_dev, frame_dev, patches, D)
        for piece in heads_backward("all", space_q, space_k, space_v, live, space_lse, grad_space_o)
    ]
    rights["space_qkv"] = [(two_cores(flat2(part)), 0) for part in grad_sqkv]
    attend_chunks = chunks_of(ATTEND, ATTEND_SEGS, rights, ATTEND_ROWS)
    g_space_bq = bias_grad(grad_sqkv[0])
    g_space_bv = bias_grad(grad_sqkv[2])
    grad_sqkv = jnp.concatenate(grad_sqkv, -1)
    unused, pullback = jax.vjp(modulate, hidden_zero, mod_row(0), mod_row(1))
    grad_input, grad_shift_a, grad_scale_a = pullback(back_low(grad_sqkv, space_qkv))
    grad_hidden = grad_hidden + grad_input
    g_patch_w = weight_split(noisy, grad_hidden)
    g_patch_b = bias_grad(grad_hidden)
    grad_mods = jnp.concatenate(
        [
            grad_shift_a.reshape(clip_dev, D),
            grad_scale_a.reshape(clip_dev, D),
            grad_gate_a,
            grad_shift_b.reshape(clip_dev, D),
            grad_scale_b.reshape(clip_dev, D),
            grad_gate_b,
            grad_fmod,
        ],
        0,
    )

    unused, pullback = jax.vjp(gelu_tanh, cap_pre[0])
    grad_cap_act = two_parts(lambda part: back_low(part, cap_last), grad_cap_rows)
    grad_cap_pre = pullback(grad_cap_act[:, two_first : two_first + D])[0]
    cap_right = lax.all_gather(
        jnp.stack([grad_cap_pre, grad_cap_rows]), "clip", axis=1, tiled=True
    )
    null_sum = jnp.sum(jnp.where(all_null[:, None, None], cap_right[0].reshape(n_clip, L_CAP, D), 0.0), 0)
    g_cap_b1 = bias_grad(grad_cap_pre)
    g_cap_b2 = bias_grad(grad_cap_rows)

    once = frame_id == 0
    gathered_mods = jnp.where(own_clip[:, None, None], grad_mods[None], 0.0)
    ends = jnp.concatenate([g_final_b, local_loss.reshape(1)])
    vector_rows = [
        g_patch_b,
        jnp.where(once, g_cap_b1, 0.0),
        jnp.where(once, g_cap_b2, 0.0),
        g_space_bq,
        g_space_bv,
        g_space_bo,
        g_time_bq,
        g_time_bv,
        g_time_bo,
        g_cross_bq,
        g_cross_bv,
        g_cross_bo,
        g_fc_in_b.reshape(-1, D),
        g_fc_out_b,
        jnp.pad(ends, (0, D - ends.shape[0])),
    ]
    small = [gathered_mods.reshape(-1, D), g_patch_w, g_final_w.reshape(PATCH_VALUES, D)]
    small = small + [value.reshape(-1, D) for value in vector_rows]
    spare = -sum(value.shape[0] for value in small) % 8
    small = jnp.concatenate(small + [jnp.zeros((spare, D), jnp.float32)] * (spare > 0), 0)
    dense_grad, small = collect_shard(
        dense_chunks,
        160,
        3,
        small=small,
    )
    dense_grad = dense_grad.reshape(DENSE_ROWS, D)
    at = 8 * n_clip
    gathered_mods = small[:at].reshape(n_clip, 8, D)
    g_patch_w = small[at : at + PATCH_VALUES]
    g_final_w = small[at + PATCH_VALUES : at + 2 * PATCH_VALUES]
    rest = small[at + 2 * PATCH_VALUES :]
    n_whole = 12 + MLP // D + 1
    loss_sum = rest[n_whole, PATCH_VALUES]
    vector_grad = jnp.concatenate([rest[:n_whole].reshape(-1), rest[n_whole, :PATCH_VALUES]])

    grad_zero = gathered_mods[:, :6]
    grad_final = gathered_mods[:, 6:]
    zero_rows = grad_zero.reshape(n_clip * 6, D)
    back_rows = two_parts(lambda part: back_low(part, emb_rows), zero_rows)
    back_rows = jnp.sum(jnp.where(part_mask[None], back_rows.reshape(n_clip, 6, EMB_PAD), 0.0), 1)
    grad_silu = lax.dot_general(
        back_rows,
        chooser.astype(jnp.float32),
        (((1,), (1,)), ((), ())),
        precision=lax.Precision.HIGHEST,
        preferred_element_type=jnp.float32,
    )
    grad_silu = sum_clips(grad_silu)
    unused, pullback = jax.vjp(jax.nn.silu, time_embed)
    grad_embed = grad_final[:, 0] + grad_final[:, 1] + pullback(grad_silu)[0]
    grad_act = two_parts(lambda part: back_low(part, time_two), grad_embed)
    grad_act = sum_clips(jnp.where(at_start, grad_act, 0.0))
    unused, pullback = jax.vjp(jax.nn.silu, pre_one)
    grad_one = pullback(grad_act)[0]
    g_table = jnp.sum(grad_zero, 0)
    vector_sum = flatten_all(
        [
            vector_grad[:D],
            jnp.sum(grad_one, 0),
            jnp.sum(grad_embed, 0),
            g_table,
            vector_grad[D:],
            g_table,
            jnp.sum(grad_final, 0),
        ]
    )

    per = EMB_PAD // 4
    quarter_row = emb_first + frame_id * per + jnp.arange(per, dtype=jnp.int32)
    time_left = jnp.concatenate(
        [
            jnp.pad(freq_in, ((0, 0), (ROW_TIME_ONE, EMB_PAD - ROW_TIME_TWO))),
            jnp.pad(act_one, ((0, 0), (ROW_TIME_TWO, EMB_PAD - ROW_BLOCK))),
        ],
        0,
    )
    time_left = jnp.where(at_start, time_left, jnp.zeros_like(time_left))
    small_left = lax.dynamic_slice_in_dim(
        jnp.concatenate([time_left, block_left], 0), frame_id * per, per, 1
    )
    small_right = jnp.concatenate([grad_one, grad_embed, zero_rows], 0)
    first_kind = (quarter_row < ROW_CAP_TWO)[None]
    no_left = jnp.zeros_like(cap_left)
    null_back = back_low(cap_weights, jnp.concatenate(halves(null_sum), 0))
    g_null = from_cap_rows((null_back[:, :L_CAP] + null_back[:, L_CAP:]).T)
    n_null = -(-null_end // D)
    n_known = -(-(2 * PATCH_VALUES + n_null) // 16) * 16
    null_rows = jnp.pad(g_null.reshape(-1), (0, (n_known - 2 * PATCH_VALUES) * D - null_end))
    known = jnp.concatenate([g_patch_w, g_final_w, null_rows.reshape(-1, D)], 0)
    known_row = np.concatenate(
        [np.arange(PATCH_VALUES), ROW_FINAL + np.arange(n_known - PATCH_VALUES)]
    ).astype(np.int32)
    known_left = (jnp.asarray(known_row)[:, None] == quarter_row[None]).astype(jnp.bfloat16)
    emb_left = jnp.concatenate(
        [
            small_left,
            jnp.where(first_kind, cap_left, no_left),
            jnp.where(first_kind, no_left, cap_left),
            known_left,
        ],
        0,
    )
    emb_right = jnp.concatenate([small_right, cap_right[0], cap_right[1], known], 0)
    emb_grad = weight_split(emb_left, emb_right)
    unit = (
        LANE_TILES * (frame_id * per + jnp.arange(per, dtype=jnp.int32))[:, None]
        + jnp.arange(D, dtype=jnp.int32)[None] // LANES
        - emb_shift
    )
    emb_grad = jnp.where((unit >= 0) & (unit < EMB_UNITS), emb_grad, 0.0)

    attend_grad, emb_whole = collect_shard(
        attend_chunks,
        208,
        4,
        part=emb_grad,
    )
    attend_grad = attend_grad.reshape(ATTEND_ROWS, D)
    local_square = sum(jnp.sum(value * value) for value in (dense_grad, attend_grad, emb_whole))
    vector_square = jnp.sum(vector_sum * vector_sum)
    grad_norm = jnp.sqrt(sum_clips(local_square.reshape(1))[0] + vector_square)
    factor = jnp.minimum(1.0, CLIP_LIMIT / (grad_norm + NORM_FLOOR))
    scale = factor.reshape(1)
    dense_r = step_shard(
        dense_grad,
        jnp.asarray(step_table(DENSE_SEGS, STEP_BLOCK, DENSE_ROWS))[clip_id],
        (1, 4),
        DENSE_ROWS,
        scale,
        (dense_w, dense_m, dense_v, dense_e),
    )
    attend_r = step_shard(
        attend_grad,
        jnp.asarray(step_table(ATTEND_SEGS, STEP_BLOCK, ATTEND_ROWS))[clip_id],
        (1, 2, 3),
        ATTEND_ROWS,
        scale,
        (attend_w, attend_m, attend_v, attend_e),
    )
    emb_flat = rows_to_flat(emb_whole.reshape(EMB_PAD, D))
    emb_owned = lax.dynamic_slice_in_dim(emb_flat, emb_shift, EMB_UNITS, 0).reshape(-1)
    embed_r = adam_step(embed_w, emb_owned, embed_m, embed_v, embed_e, factor)
    vector_r = adam_step(vector_w, vector_sum, vector_m, vector_v, vector_e, factor)
    return (
        loss_sum,
        weight_total,
        grad_norm,
        embed_r[0],
        attend_r[0],
        dense_r[0],
        vector_r[0],
        embed_r[1],
        attend_r[1],
        dense_r[1],
        vector_r[1],
        embed_r[2],
        attend_r[2],
        dense_r[2],
        vector_r[2],
        embed_r[3],
        attend_r[3],
        dense_r[3],
        vector_r[3],
    )


def pick_plan(mesh):
    if mesh.shape["frame"] == X_SIZE * CORES and mesh.shape["clip"] == N_OWN:
        return shards_block
    return shards


def solution(mesh):
    in_specs = (
        P("clip", "frame", None, None),
        P("clip", "frame", None, None),
        P("clip"),
        P("clip", None, None),
        P("clip"),
        P("clip"),
        P("clip"),
        P("clip"),
        P("clip"),
        P("clip"),
        P(),
        P("clip"),
        P("clip"),
        P("clip"),
        P(),
        P("clip"),
        P("clip"),
        P("clip"),
        P(),
        P("clip"),
        P("clip"),
        P("clip"),
        P(),
    )
    out_specs = (
        P(),
        P(),
        P(),
        P("clip"),
        P("clip"),
        P("clip"),
        P(),
        P("clip"),
        P("clip"),
        P("clip"),
        P(),
        P("clip"),
        P("clip"),
        P("clip"),
        P(),
        P("clip"),
        P("clip"),
        P("clip"),
        P(),
    )
    return jax.shard_map(pick_plan(mesh), mesh=mesh, in_specs=in_specs, out_specs=out_specs, check_vma=False)
```
